32 devices in a mesh: replica: 8 (over y, x, core), tensor: 4 (over z).
Axes of the slice: x: 2, y: 2, z: 4, core: 2. Of those that a mesh axis runs over, the one named last changes fastest.
Arguments:
- projection_inputs: bfloat16 [1024, 5120], P('replica', 'tensor'), may hold values from -6 to 6
- switch_logits_raw: bfloat16 [1024, 256], P('replica', 'tensor'), may hold values from -6 to 6
- inner_neuron_slope: bfloat16 [1024, 256], P('replica', 'tensor'), may hold values from -0.59765625 to 0.59765625
- expansion_matrix: bfloat16 [256, 5120], P('tensor'), may hold values from -3 to 3
- velocity_buffer: float32 [8, 256, 5120], P('replica', 'tensor'), may hold values from -6 to 6
- sent_spectral_lines: int32 [8, 4, 80, 8], P('replica', 'tensor'), may hold values from 0 to 63, as said below
- participant_mask: int32 [8], replicated, may hold values from 0 to 1, as said below
- token_tallies: int32 [8], replicated, may hold values from 64 to 256
Outputs:
- input_grad: bfloat16 [1024, 5120], P('replica', 'tensor')
- new_momentum: float32 [8, 256, 5120], P('replica', 'tensor')
- update: float32 [256, 5120], P('tensor')
The draws below stay inside these ranges and needn't reach their ends.
Inputs may be any that keep to these rules, and one draw needn't show every extreme that they name: `sent_spectral_lines`: the 8 rows of one replica and block are distinct. `participant_mask`: at least one replica survives.
All inputs are finite; a program needn't handle non-finite values.
Results may differ from the reference program's by a relative error of at most 0.005.
Values may be sent and summed in bfloat16 or wider, within the bound.
No kernel may reach another device: no remote copies, remote signals or barrier semaphores. Data moves between devices by JAX's collectives and lax.ppermute only.
A program may use at most 64 MiB of HBM per device.

```python
import jax
import jax.numpy as jnp
from jax import lax

D = 5120
TOK_DEV = 128
KEEP = 8
REPLICAS = 8
FFW = 256
TOKENS = 1024
ROW_BLOCKS = 4
COL_BLOCKS = 80


def draw_sent_spectral_lines(key, part):
    key = jax.random.fold_in(key, 11)
    scores = jax.random.randint(key, (REPLICAS, ROW_BLOCKS, COL_BLOCKS, 64), 0, 1 << 20)
    scores = scores * 64 + lax.iota(jnp.int32, 64)
    return lax.top_k(scores, KEEP)[1].astype(jnp.int32)


def draw_participant_mask(key, part):
    key = jax.random.fold_in(key, 5)
    first, second = jax.random.split(key)
    living = jax.random.randint(first, (REPLICAS,), 0, 2)
    chosen = jax.random.randint(second, (), 0, REPLICAS)
    return jnp.where(lax.iota(jnp.int32, REPLICAS) == chosen, 1, living).astype(jnp.int32)


def set_ends(values, key, least, top_value):
    extent = values.shape
    place = [jax.random.randint(jax.random.fold_in(key, axis), (), 0, extent[axis]) for axis in range(len(extent))]
    values = values.at[tuple(place)].set(least)
    longest = extent.index(max(extent))
    place[longest] = (place[longest] + 1) % extent[longest]
    return values.at[tuple(place)].set(top_value)


def level_of(rng, extent, pieces, least, high):
    def one(dim, shards_of):
        steps = jax.random.uniform(jax.random.fold_in(jax.random.fold_in(rng, 6), dim), (shards_of,), jnp.float32, least / len(pieces), high / len(pieces))
        return jnp.repeat(jnp.exp(steps), extent[dim] // shards_of).reshape((-1,) + (1,) * (len(extent) - dim - 1))

    factor_of = one(*pieces[0])
    for cut in pieces[1:]:
        factor_of = factor_of * one(*cut)
    return factor_of


def bell_draw(own_key, shape, spread, most, shards=(), held_as=jnp.bfloat16):
    entries = spread * jax.random.normal(own_key, shape, jnp.float32)
    if shards:
        entries = entries * level_of(own_key, shape, shards, -0.22, 0.18)
    return jnp.clip(entries, -most, most).astype(held_as)


def setup_inputs(seed: int = 0) -> dict:
    key_of = jax.random.split(jax.random.key(seed), 9)
    projection_inputs = bell_draw(key_of[0], (TOKENS, D), 1.0, 6.0, ((0, 8), (1, 4)))
    switch_logits_raw = bell_draw(key_of[1], (TOKENS, FFW), 1.0, 6.0, ((0, 8), (1, 4)))
    inner_neuron_slope = bell_draw(key_of[2], (TOKENS, FFW), 0.1, 0.59765625, ((0, 8), (1, 4)))
    expansion_matrix = bell_draw(key_of[3], (FFW, D), 0.5, 3.0, ((0, 4),))
    velocity_buffer = bell_draw(key_of[4], (REPLICAS, FFW, D), 1.0, 6.0, ((0, 8), (1, 4)), jnp.float32)
    sent_spectral_lines = draw_sent_spectral_lines(jax.random.fold_in(key_of[8], 71), 0)
    participant_mask = draw_participant_mask(jax.random.fold_in(key_of[8], 71), 0)
    token_tallies = set_ends(jax.random.randint(key_of[7], (REPLICAS,), 64, 257), jax.random.fold_in(key_of[7], 1), 64, 256).astype(jnp.int32)
    return dict(projection_inputs=projection_inputs, switch_logits_raw=switch_logits_raw, inner_neuron_slope=inner_neuron_slope, expansion_matrix=expansion_matrix, velocity_buffer=velocity_buffer, sent_spectral_lines=sent_spectral_lines, participant_mask=participant_mask, token_tallies=token_tallies)


momentum_decay = 0.9

def cosine_table():
    freqs = jnp.arange(64, dtype=jnp.float32)[:, None]
    places = jnp.arange(64, dtype=jnp.float32)[None, :]
    cosines = jnp.cos(jnp.pi * (places + 0.5) * freqs / 64.0) * jnp.sqrt(2.0 / 64.0)
    return cosines.at[0].multiply(jnp.sqrt(0.5))

def reference(projection_inputs, switch_logits_raw, inner_neuron_slope, expansion_matrix, velocity_buffer, sent_spectral_lines, participant_mask, token_tallies):
    highest = lax.Precision.HIGHEST
    up_grad = (inner_neuron_slope.astype(jnp.float32) * jax.nn.silu(switch_logits_raw.astype(jnp.float32))).astype(jnp.bfloat16)
    input_grad = jnp.dot(up_grad, expansion_matrix, preferred_element_type=jnp.float32).astype(jnp.bfloat16)
    cosines = cosine_table()
    worker_burdens = participant_mask.astype(jnp.float32) * token_tallies.astype(jnp.float32)
    worker_fractions = worker_burdens * (jnp.sum(participant_mask.astype(jnp.float32)) / jnp.sum(worker_burdens))
    freq_ids = jnp.arange(64, dtype=jnp.int32)

    def replica_step(combined, index):
        token_rows = lax.dynamic_slice_in_dim(projection_inputs, index * TOK_DEV, TOK_DEV, 0)
        up_rows = lax.dynamic_slice_in_dim(up_grad, index * TOK_DEV, TOK_DEV, 0)
        grad_w = jnp.dot(up_rows.T, token_rows, preferred_element_type=jnp.float32)
        moment = momentum_decay * velocity_buffer[index] + grad_w
        blocks = moment.reshape(ROW_BLOCKS, 64, COL_BLOCKS, 64).transpose(0, 2, 1, 3)
        coefficients = jnp.einsum('fa,ijab,gb->ijfg', cosines, blocks, cosines, precision=highest)
        chosen = (sent_spectral_lines[index][..., None] == freq_ids).astype(jnp.float32)
        shipped = jnp.einsum('ijkf,ijfg->ijkg', chosen, coefficients, precision=highest).astype(jnp.bfloat16)
        spectrum = jnp.einsum('ijkf,ijkg->ijfg', chosen, shipped.astype(jnp.float32), precision=highest)
        returned = jnp.einsum('fa,ijfg,gb->ijab', cosines, spectrum, cosines, precision=highest)
        new_moment = moment - returned.transpose(0, 2, 1, 3).reshape(FFW, D)
        return (combined + worker_fractions[index] * spectrum, new_moment)
    start = jnp.zeros((ROW_BLOCKS, COL_BLOCKS, 64, 64), jnp.float32)
    combined, new_momentum = lax.scan(replica_step, start, jnp.arange(REPLICAS, dtype=jnp.int32))
    update = jnp.einsum('fa,ijfg,gb->ijab', cosines, combined, cosines, precision=highest)
    update = update.transpose(0, 2, 1, 3).reshape(FFW, D)
    return (input_grad, new_momentum, update)
```

```python
import functools

import jax
import jax.numpy as jnp
import numpy as np
from jax import lax
from jax.experimental import pallas as pl
from jax.experimental.pallas import tpu as pltpu
from jax.sharding import PartitionSpec as P

momentum_decay = 0.9
B = 64
G = 256
F32 = jnp.float32
BF16 = jnp.bfloat16
VMEM_LIMIT = 48 * 1024 * 1024

VM = pl.BlockSpec(memory_space=pltpu.VMEM)
SM = pl.BlockSpec(memory_space=pltpu.SMEM)


def cosine_table():
    freqs = jnp.arange(64, dtype=jnp.float32)[:, None]
    places = jnp.arange(64, dtype=jnp.float32)[None, :]
    cosines = jnp.cos(jnp.pi * (places + 0.5) * freqs / 64.0) * jnp.sqrt(2.0 / 64.0)
    return cosines.at[0].multiply(jnp.sqrt(0.5))


def cosine_np():
    f = np.arange(B)[:, None]
    a = np.arange(B)[None, :]
    c = np.cos(np.pi * (a + 0.5) * f / B) * np.sqrt(2.0 / B)
    c[0] *= np.sqrt(0.5)
    return c


def halves(c):
    hi = np.asarray(c, dtype=np.float32).astype(jnp.bfloat16)
    lo = (np.asarray(c, np.float64) - hi.astype(np.float64)).astype(np.float32).astype(jnp.bfloat16)
    return hi, lo


def constants():
    c = cosine_np()
    hi, lo = halves(c)
    stack = lambda h, l: np.block([[h, h], [l, l]])
    left = stack(hi, lo)
    left_t = stack(hi.T, lo.T)
    eye = np.eye(G // B)
    fwd = np.stack([np.kron(eye, np.asarray(x.T, np.float32)).astype(jnp.bfloat16) for x in (hi, lo)])
    inv = np.stack([np.kron(eye, np.asarray(x, np.float32)).astype(jnp.bfloat16) for x in (hi, lo)])
    tall = np.concatenate([hi.T, lo.T], axis=0)
    return [jnp.asarray(x) for x in (left, left_t, fwd, inv, tall)]


def dot(a, b):
    return jnp.dot(a, b, preferred_element_type=F32)


def split(x):
    hi = x.astype(BF16)
    return hi, (x - hi.astype(F32)).astype(BF16)


def left_mul(stacked, x):
    hi, lo = split(x)
    y = dot(stacked, jnp.concatenate([hi, lo], axis=0))
    return y[:B] + y[B:]


def call(body, out_shape, ins, in_specs, out_specs, scratch=(), flops=0, nbytes=0, name=None):
    return pl.pallas_call(
        body,
        out_shape=out_shape,
        in_specs=in_specs,
        out_specs=out_specs,
        scratch_shapes=scratch,
        compiler_params=pltpu.CompilerParams(vmem_limit_bytes=VMEM_LIMIT),
        cost_estimate=pl.CostEstimate(flops=flops, bytes_accessed=nbytes, transcendentals=0),
        name=name,
    )(*ins)


def cut_body(n_t, rp, cp, cols, pos, exp_ref, *outs):
    rep, ten = pos[0], pos[1]
    nr, nc = B // rp, cols // cp
    r0 = pl.multiple_of((rep // cp) * nr, nr)
    for k in range(n_t):
        dest = lax.rem(ten + k, n_t)
        c0 = pl.multiple_of(dest * cols + lax.rem(rep, cp) * nc, 128)
        outs[k][...] = exp_ref[pl.ds(r0, nr), pl.ds(c0, nc)]


def grads_body(n_t, *refs):
    ups, act, outs = refs[:n_t], refs[n_t], refs[n_t + 1 :]
    up = jnp.concatenate([u[...] for u in ups], axis=0)
    cols = act.shape[1]
    for c in range(0, cols, G):
        g = dot(up, act[:, c : c + G])
        for k in range(n_t):
            outs[k][:, c : c + G] = g[k * B : (k + 1) * B].astype(outs[k].dtype)


def moment_body(n_t, pos, vel, idx, left, left_t, fwd, inv, *refs):
    grads, (new_ref, ship_ref) = refs[:n_t], refs[n_t:]
    ten = pos[1]
    cols = grads[0].shape[1]
    keep = idx.shape[0]
    ng = cols // G
    blocks = idx.shape[1]
    idx_f = idx[...].astype(F32).astype(BF16)
    for k in range(n_t):
        c0 = pl.multiple_of(lax.rem(ten + k, n_t) * cols, 128)
        block = lax.broadcasted_iota(jnp.int32, (blocks, cols), 0)
        lane = lax.broadcasted_iota(jnp.int32, (blocks, cols), 1) + c0
        spread = jnp.where(lane // B == block, 1.0, 0.0).astype(BF16)
        rows = dot(idx_f, spread).astype(jnp.int32)
        moments = momentum_decay * vel[:, pl.ds(c0, cols)] + grads[k][...].astype(F32)
        sel = []
        for g in range(ng):
            coef = left_mul(left[...], moments[:, g * G : (g + 1) * G])
            num = rows[:, g * G : (g + 1) * G]
            got = jnp.zeros((keep, G), F32)
            for f in range(B):
                got = jnp.where(num == f, coef[f : f + 1], got)
            sel.append(got)
        sel = jnp.concatenate(sel, axis=0)
        hi, lo = split(sel)
        n = ng * keep
        y = dot(jnp.concatenate([hi, lo], axis=0), fwd[0])
        ship = (y[:n] + y[n:] + dot(hi, fwd[1])).astype(BF16)
        q = dot(ship, inv[0]) + dot(ship, inv[1])
        shipf = ship.astype(F32)
        freq = lax.broadcasted_iota(jnp.int32, (B, G), 0)
        ship_ref[:, pl.ds(c0, cols)] = jnp.concatenate(
            [shipf[g * keep : (g + 1) * keep] for g in range(ng)], axis=1
        ).astype(BF16)
        for g in range(ng):
            num = rows[:, g * G : (g + 1) * G]
            spec = jnp.zeros((B, G), F32)
            for s in range(keep):
                r = g * keep + s
                spec = jnp.where(freq == num[s : s + 1], q[r : r + 1], spec)
            back = left_mul(left_t[...], spec)
            at = pl.multiple_of(c0 + g * G, 128)
            new_ref[:, pl.ds(at, G)] = moments[:, g * G : (g + 1) * G] - back


def places_body(n_r, keep, mask, tally, idx_row, tall, hi_ref, lo_ref):
    total, alive = jnp.float32(0), jnp.float32(0)
    burdens = []
    for r in range(n_r):
        m = mask[r].astype(F32)
        burdens.append(m * tally[r].astype(F32))
        total = total + burdens[r]
        alive = alive + m
    rep = (lax.broadcasted_iota(jnp.int32, (1, G), 1) // keep) % n_r
    w = jnp.zeros((1, G), F32)
    for r in range(n_r):
        w = jnp.where(rep == r, burdens[r], w)
    w = w * (jnp.full((1, G), alive) / jnp.full((1, G), total))
    freq = lax.broadcasted_iota(jnp.int32, (B, G), 0)
    for c in range(0, idx_row.shape[1], G):
        hot = jnp.where(freq == idx_row[:, c : c + G], 1.0, 0.0).astype(BF16)
        y = dot(tall[...], hot)
        hi, lo = split((y[:B] + y[B:]) * w)
        hi_ref[:, c : c + G] = hi
        lo_ref[:, c : c + G] = lo


def update_body(n_r, keep, pos, p_hi, p_lo, inv, *refs):
    ships, out, held = refs[:n_r], refs[n_r], refs[n_r + 1]
    rep = pos[0]
    for m in range(n_r):
        q = pl.multiple_of((rep ^ m) * keep, keep)
        held[pl.ds(q, keep), :] = ships[m][...].astype(F32)
    per = n_r * keep
    nb = G // B
    width = nb * per
    lane_block = lax.broadcasted_iota(jnp.int32, (per, G), 1) // B
    for g in range(out.shape[1] // G):
        s = held[:, g * G : (g + 1) * G]
        w = jnp.concatenate(
            [jnp.where(lane_block == j, s, 0.0).astype(BF16) for j in range(nb)], axis=0
        )
        cut = slice(g * width, (g + 1) * width)
        y = dot(jnp.concatenate([p_hi[:, cut], p_lo[:, cut]], axis=0), w)
        hi, lo = split(y[:B] + y[B:])
        z = dot(jnp.concatenate([hi, lo], axis=0), inv[0])
        out[:, g * G : (g + 1) * G] = z[:B] + z[B:] + dot(hi, inv[1])


def input_grad_body(n_t, rp, cp, exp_ref, *refs):
    ups, out, held = refs[:n_t], refs[n_t], refs[n_t + 1]
    nr = B // rp
    nc = out.shape[1] // cp
    for i in range(rp):
        for j in range(cp):
            for k in range(n_t):
                held[k * B + i * nr : k * B + (i + 1) * nr, j * nc : (j + 1) * nc] = exp_ref[i * cp + j, k]
    up = jnp.concatenate([u[...] for u in ups], axis=0).T
    for c in range(0, out.shape[1], G):
        out[:, c : c + G] = dot(up, held[:, c : c + G]).astype(BF16)


def per_device(n_t, n_r, act, switch, slope, exp, vel, lines, mask, tally):
    cols = act.shape[1]
    width = exp.shape[1]
    tok = act.shape[0]
    keep = lines.shape[3]
    blocks = width // B
    cp = 2
    rp = n_r // cp
    left, left_t, fwd, inv, tall = constants()
    rep = lax.axis_index("replica")
    ten = lax.axis_index("tensor")
    pos = jnp.stack([rep, ten]).astype(jnp.int32)

    shift = lambda x, k: lax.ppermute(x, "tensor", [(i, (i + k) % n_t) for i in range(n_t)]) if k % n_t else x
    swap = lambda x, m: lax.ppermute(x, "replica", [(i, i ^ m) for i in range(n_r)]) if m else x

    up = (slope.astype(F32) * jax.nn.silu(switch.astype(F32))).astype(BF16).T
    ups = [shift(up, k) for k in range(n_t)]

    pieces = call(
        functools.partial(cut_body, n_t, rp, cp, cols),
        [jax.ShapeDtypeStruct((B // rp, cols // cp), BF16)] * n_t,
        (pos, exp),
        [SM, VM],
        [VM] * n_t,
        nbytes=exp.size * 2,
        name="cut_expansion",
    )
    pieces = jnp.stack([shift(pieces[k], k) for k in range(n_t)])
    exp_all = lax.all_gather(pieces, "replica", axis=0)

    own = lines[0, 0].T
    idx_all = lax.all_gather(own, "replica", axis=0)
    idx_row = idx_all.reshape(n_r * keep, blocks).T.reshape(1, blocks * n_r * keep)

    grads = call(
        functools.partial(grads_body, n_t),
        [jax.ShapeDtypeStruct((B, cols), F32)] + [jax.ShapeDtypeStruct((B, cols), BF16)] * (n_t - 1),
        (*ups, act),
        [VM] * (n_t + 1),
        [VM] * n_t,
        flops=2 * n_t * B * tok * cols,
        nbytes=act.size * 2 + n_t * B * cols * 2,
        name="weight_grads",
    )
    grads = [shift(grads[k], -k) for k in range(n_t)]

    p_hi, p_lo = call(
        functools.partial(places_body, n_r, keep),
        [jax.ShapeDtypeStruct((B, blocks * n_r * keep), BF16)] * 2,
        (mask, tally, idx_row, tall),
        [SM, SM, VM, VM],
        [VM, VM],
        flops=4 * B * B * blocks * n_r * keep,
        nbytes=4 * B * blocks * n_r * keep,
        name="places",
    )

    new, ship = call(
        functools.partial(moment_body, n_t),
        [jax.ShapeDtypeStruct((B, width), F32), jax.ShapeDtypeStruct((keep, width), BF16)],
        (pos, vel[0], own, left, left_t, fwd, inv, *grads),
        [SM] + [VM] * (6 + n_t),
        [VM, VM],
        flops=12 * B * B * width,
        nbytes=B * width * 12,
        name="moments",
    )
    ships = [swap(ship, m) for m in range(n_r)]

    input_grad = call(
        functools.partial(input_grad_body, n_t, rp, cp),
        jax.ShapeDtypeStruct((tok, cols), BF16),
        (exp_all, *ups),
        [VM] * (1 + n_t),
        VM,
        scratch=[pltpu.VMEM((n_t * B, cols), BF16)],
        flops=2 * tok * n_t * B * cols,
        nbytes=(n_t * B * cols + tok * cols) * 2,
        name="input_grads",
    )

    update = call(
        functools.partial(update_body, n_r, keep),
        jax.ShapeDtypeStruct((B, width), F32),
        (pos, p_hi, p_lo, inv, *ships),
        [SM] + [VM] * (3 + n_r),
        VM,
        scratch=[pltpu.VMEM((n_r * keep, width), F32)],
        flops=8 * B * G * width,
        nbytes=B * width * 8,
        name="updates",
    )
    return input_grad, new[None], update


def per_device_plain(
    projection_inputs,
    switch_logits_raw,
    inner_neuron_slope,
    expansion_matrix,
    velocity_buffer,
    sent_spectral_lines,
    participant_mask,
    token_tallies,
):
    highest = lax.Precision.HIGHEST
    up_grad = (
        inner_neuron_slope.astype(jnp.float32) * jax.nn.silu(switch_logits_raw.astype(jnp.float32))
    ).astype(jnp.bfloat16)
    partial_terms = jnp.dot(up_grad, expansion_matrix, preferred_element_type=jnp.float32)
    input_grad = lax.psum_scatter(partial_terms, "tensor", scatter_dimension=1, tiled=True).astype(
        jnp.bfloat16
    )
    grad_w = lax.dot_general(
        up_grad,
        lax.all_gather(projection_inputs, "tensor", axis=1, tiled=True),
        (((0,), (0,)), ((), ())),
        preferred_element_type=jnp.float32,
    )
    row_total_count = expansion_matrix.shape[0] // 64
    col_count = expansion_matrix.shape[1] // 64
    moment = momentum_decay * velocity_buffer[0] + grad_w
    cosines = cosine_table()
    blocks = moment.reshape(row_total_count, 64, col_count, 64).transpose(0, 2, 1, 3)
    coefficients = jnp.einsum("fa,ijab,gb->ijfg", cosines, blocks, cosines, precision=highest)
    freq_ids = jnp.arange(64, dtype=jnp.int32)
    own_rows = sent_spectral_lines[0]
    chosen = (own_rows[..., None] == freq_ids).astype(jnp.float32)
    shipped = jnp.einsum("ijkf,ijfg->ijkg", chosen, coefficients, precision=highest).astype(
        jnp.bfloat16
    )
    spectrum = jnp.einsum("ijkf,ijkg->ijfg", chosen, shipped.astype(jnp.float32), precision=highest)
    returned = jnp.einsum("fa,ijfg,gb->ijab", cosines, spectrum, cosines, precision=highest)
    new_moment = moment - returned.transpose(0, 2, 1, 3).reshape(moment.shape)
    worker_burdens = participant_mask.astype(jnp.float32) * token_tallies.astype(jnp.float32)
    worker_fractions = worker_burdens * (
        jnp.sum(participant_mask.astype(jnp.float32)) / jnp.sum(worker_burdens)
    )
    myself = lax.axis_index("replica")
    combined = lax.psum(worker_fractions[myself] * spectrum, "replica")
    update = jnp.einsum("fa,ijfg,gb->ijab", cosines, combined, cosines, precision=highest)
    update = update.transpose(0, 2, 1, 3).reshape(moment.shape)
    return (input_grad, new_moment[None], update)


def solution(mesh):
    n_t, n_r = mesh.shape["tensor"], mesh.shape["replica"]

    def device(*args):
        act, exp, lines = args[0], args[3], args[5]
        fits = (
            act.shape[1] % G == 0
            and act.shape[0] % 128 == 0
            and exp.shape[0] == B
            and lines.shape[3] == 8
            and n_r == 8
        )
        if not fits:
            return per_device_plain(*args)
        return per_device(n_t, n_r, *args)

    return jax.shard_map(
        device,
        mesh=mesh,
        in_specs=(
            P("replica", "tensor"),
            P("replica", "tensor"),
            P("replica", "tensor"),
            P("tensor", None),
            P("replica", "tensor", None),
            P("replica", "tensor", None, None),
            P(),
            P(),
        ),
        out_specs=(P("replica", "tensor"), P("replica", "tensor", None), P("tensor", None)),
        check_vma=False,
    )
```

```python
import functools

import jax
import jax.numpy as jnp
import numpy as np
from jax import lax
from jax.experimental import pallas as pl
from jax.experimental.pallas import tpu as pltpu
from jax.sharding import PartitionSpec as P

momentum_decay = 0.9
B = 64
G = 256
F32 = jnp.float32
BF16 = jnp.bfloat16
VMEM_LIMIT = 48 * 1024 * 1024

VM = pl.BlockSpec(memory_space=pltpu.VMEM)
SM = pl.BlockSpec(memory_space=pltpu.SMEM)


def cosine_table():
    freqs = jnp.arange(64, dtype=jnp.float32)[:, None]
    places = jnp.arange(64, dtype=jnp.float32)[None, :]
    cosines = jnp.cos(jnp.pi * (places + 0.5) * freqs / 64.0) * jnp.sqrt(2.0 / 64.0)
    return cosines.at[0].multiply(jnp.sqrt(0.5))


def cosine_np():
    f = np.arange(B)[:, None]
    a = np.arange(B)[None, :]
    c = np.cos(np.pi * (a + 0.5) * f / B) * np.sqrt(2.0 / B)
    c[0] *= np.sqrt(0.5)
    return c


def halves(c):
    hi = np.asarray(c, dtype=np.float32).astype(jnp.bfloat16)
    lo = (np.asarray(c, np.float64) - hi.astype(np.float64)).astype(np.float32).astype(jnp.bfloat16)
    return hi, lo


def constants():
    hi, lo = halves(cosine_np())
    eye = np.eye(G // B)
    kron = lambda x: np.kron(eye, np.asarray(x, np.float32)).astype(jnp.bfloat16)
    tall = np.zeros((2 * B, G), jnp.bfloat16)
    tall[:B, :B], tall[B:, :B] = hi.T, lo.T
    return jnp.asarray(np.concatenate([kron(hi.T), kron(lo.T), kron(hi), kron(lo), tall], axis=0))


def fwd(tab, i):
    return tab[i * G : (i + 1) * G, :]


def inv(tab, i):
    return tab[(2 + i) * G : (3 + i) * G, :]


def tall(tab):
    return tab[4 * G : 4 * G + 2 * B, :B]


def dot(a, b):
    return jnp.dot(a, b, preferred_element_type=F32)


def split(x):
    hi = x.astype(BF16)
    return hi, (x - hi.astype(F32)).astype(BF16)


def call(body, out_shape, ins, in_specs, out_specs, scratch=(), flops=0, nbytes=0, name=None):
    return pl.pallas_call(
        body,
        out_shape=out_shape,
        in_specs=in_specs,
        out_specs=out_specs,
        scratch_shapes=scratch,
        compiler_params=pltpu.CompilerParams(vmem_limit_bytes=VMEM_LIMIT),
        cost_estimate=pl.CostEstimate(flops=flops, bytes_accessed=nbytes, transcendentals=0),
        name=name,
    )(*ins)


def cut_body(n_t, rp, cp, cols, pos, exp_ref, out):
    rep = pos[0]
    nr, nc = B // rp, cols // cp
    r0 = pl.multiple_of((rep // cp) * nr, nr)
    for k in range(n_t):
        c0 = pl.multiple_of(k * cols + lax.rem(rep, cp) * nc, 128)
        out[k] = exp_ref[pl.ds(r0, nr), pl.ds(c0, nc)]


def grads_body(n_t, ups, act, out):
    up = ups[...].reshape(n_t * B, ups.shape[2])
    for c in range(0, act.shape[1], G):
        g = dot(up, act[:, c : c + G]).astype(BF16)
        for k in range(n_t):
            out[k, :, c : c + G] = g[k * B : (k + 1) * B]


def own_body(rows, tab, p_ref, a_ref):
    freq = lax.broadcasted_iota(jnp.int32, (B, 2 * B), 0)
    term = lax.broadcasted_iota(jnp.int32, (B, 2 * B), 1) // (B // 2)
    for g in range(rows.shape[0]):
        hot = jnp.where(freq == rows[g : g + 1, :], 1.0, 0.0).astype(BF16)
        y = dot(tall(tab), hot)
        p = jnp.where(term == 3, 0.0, jnp.where(term == 1, y[B:], y[:B]))
        p_ref[:, g * 2 * B : (g + 1) * 2 * B] = p.astype(BF16)
        a_ref[g * B : (g + 1) * B, :] = jnp.concatenate([p, p], axis=0).T[:B].astype(BF16)


def kept_body(keep, vel, a_ref, tab, grads, ship_ref):
    cols = grads.shape[2]
    ng = vel.shape[1] // G
    lane_block = lax.broadcasted_iota(jnp.int32, (keep, G), 1) // B
    sel = []
    for g in range(ng):
        k, c = divmod(g * G, cols)
        cut = slice(g * G, (g + 1) * G)
        hi, lo = split(momentum_decay * vel[:, cut] + grads[k, :, c : c + G].astype(F32))
        y = dot(a_ref[g * B : (g + 1) * B, :], jnp.concatenate([hi, lo], axis=0))
        y = y[: B // 2] + y[B // 2 :]
        got = y[:keep]
        for j in range(1, G // B):
            got = jnp.where(lane_block == j, y[j * keep : (j + 1) * keep], got)
        sel.append(got)
    hi, lo = split(jnp.concatenate(sel, axis=0))
    n = ng * keep
    y = dot(jnp.concatenate([hi, lo], axis=0), fwd(tab, 0))
    y = y[:n] + y[n:] + dot(hi, fwd(tab, 1))
    ship_ref[...] = jnp.concatenate(
        [y[g * keep : (g + 1) * keep] for g in range(ng)], axis=1
    ).astype(BF16)


def return_body(keep, vel, p_ref, tab, grads, ship, new_ref):
    cols = grads.shape[2]
    ng = vel.shape[1] // G
    lane_block = lax.broadcasted_iota(jnp.int32, (keep, G), 1) // B
    kept = ship[...].astype(F32)
    kept = jnp.concatenate([kept[:, g * G : (g + 1) * G] for g in range(ng)], axis=0).astype(BF16)
    q = dot(kept, inv(tab, 0)) + dot(kept, inv(tab, 1))
    for g in range(ng):
        k, c = divmod(g * G, cols)
        cut = slice(g * G, (g + 1) * G)
        own = q[g * keep : (g + 1) * keep]
        spread = jnp.concatenate(
            [jnp.where(lane_block == j, own, 0.0) for j in range(G // B)], axis=0
        )
        hi, lo = split(spread)
        w = jnp.concatenate([hi, hi, lo, jnp.zeros_like(lo)], axis=0)
        back = dot(p_ref[:, g * 2 * B : (g + 1) * 2 * B], w)
        new_ref[:, cut] = momentum_decay * vel[:, cut] + grads[k, :, c : c + G].astype(F32) - back


def places_body(n_r, keep, mask, tally, idx_row, tab, hi_ref, lo_ref):
    total, alive = jnp.float32(0), jnp.float32(0)
    burdens = []
    for r in range(n_r):
        m = mask[r].astype(F32)
        burdens.append(m * tally[r].astype(F32))
        total = total + burdens[r]
        alive = alive + m
    rep = (lax.broadcasted_iota(jnp.int32, (1, G), 1) // keep) % n_r
    w = jnp.zeros((1, G), F32)
    for r in range(n_r):
        w = jnp.where(rep == r, burdens[r], w)
    w = w * (jnp.full((1, G), alive) / jnp.full((1, G), total))
    freq = lax.broadcasted_iota(jnp.int32, (B, G), 0)
    for c in range(0, idx_row.shape[1], G):
        hot = jnp.where(freq == idx_row[:, c : c + G], 1.0, 0.0).astype(BF16)
        y = dot(tall(tab), hot)
        hi, lo = split((y[:B] + y[B:]) * w)
        hi_ref[:, c : c + G] = hi
        lo_ref[:, c : c + G] = lo


def update_body(n_r, keep, p_hi, p_lo, tab, ships, out):
    per = n_r * keep
    nb = G // B
    width = nb * per
    lane_block = lax.broadcasted_iota(jnp.int32, (per, G), 1) // B
    for g in range(out.shape[1] // G):
        cut = slice(g * G, (g + 1) * G)
        s = jnp.concatenate([ships[r, :, cut].astype(F32) for r in range(n_r)], axis=0)
        w = jnp.concatenate(
            [jnp.where(lane_block == j, s, 0.0).astype(BF16) for j in range(nb)], axis=0
        )
        wide = slice(g * width, (g + 1) * width)
        y = dot(jnp.concatenate([p_hi[:, wide], p_lo[:, wide]], axis=0), w)
        hi, lo = split(y[:B] + y[B:])
        z = dot(jnp.concatenate([hi, lo], axis=0), inv(tab, 0))
        out[:, cut] = z[:B] + z[B:] + dot(hi, inv(tab, 1))


def input_grad_body(n_t, rp, cp, exp_ref, ups, out, held):
    nr = B // rp
    nc = out.shape[1] // cp
    for i in range(rp):
        for j in range(cp):
            for k in range(n_t):
                held[k * B + i * nr : k * B + (i + 1) * nr, j * nc : (j + 1) * nc] = exp_ref[
                    i * cp + j, k * nr : (k + 1) * nr, :
                ]
    up = ups[...].reshape(n_t * B, ups.shape[2]).T
    for c in range(0, out.shape[1], G):
        out[:, c : c + G] = dot(up, held[:, c : c + G]).astype(BF16)


def per_device(n_t, n_r, act, switch, slope, exp, vel, lines, mask, tally):
    cols = act.shape[1]
    width = exp.shape[1]
    tok = act.shape[0]
    keep = lines.shape[3]
    blocks = width // B
    groups = width // G
    cp = 2
    rp = n_r // cp
    tab = constants()
    pos = lax.axis_index("replica").astype(jnp.int32).reshape(1)

    def trade(x, axis):
        return lax.all_to_all(x, axis, split_axis=0, concat_axis=0)

    def spread(x, axis, n):
        return trade(jnp.broadcast_to(x[None], (n,) + x.shape), axis)

    up = (slope.astype(F32) * jax.nn.silu(switch.astype(F32))).astype(BF16).T
    ups = spread(up, "tensor", n_t)

    grads = call(
        functools.partial(grads_body, n_t),
        jax.ShapeDtypeStruct((n_t, B, cols), BF16),
        (ups, act),
        [VM] * 2,
        VM,
        flops=2 * n_t * B * tok * cols,
        nbytes=act.size * 2 + n_t * B * cols * 2,
        name="weight_grads",
    )
    grads = trade(grads, "tensor")

    pieces = call(
        functools.partial(cut_body, n_t, rp, cp, cols),
        jax.ShapeDtypeStruct((n_t, B // rp, cols // cp), BF16),
        (pos, exp),
        [SM, VM],
        VM,
        nbytes=exp.size * 2,
        name="cut_expansion",
    )
    pieces = trade(pieces, "tensor").reshape(n_t * (B // rp), cols // cp)
    own = lines[0, 0].T
    lines_bf = jnp.pad(own.astype(BF16), ((0, 16 - keep), (0, cols // cp - blocks)))
    shared = spread(jnp.concatenate([pieces, lines_bf], axis=0), "replica", n_r)
    idx_all = shared[:, n_t * (B // rp) :][:, :keep, :blocks].astype(jnp.int32)
    idx_row = idx_all.reshape(n_r * keep, blocks).T.reshape(1, blocks * n_r * keep)

    own_rows = jnp.concatenate([lines[0, 0].reshape(groups, B // 2)] * 4, axis=1)
    p_own, a_own = call(
        own_body,
        [
            jax.ShapeDtypeStruct((B, groups * 2 * B), BF16),
            jax.ShapeDtypeStruct((groups * B, 2 * B), BF16),
        ],
        (own_rows, tab),
        [VM, VM],
        [VM, VM],
        flops=groups * 4 * B**3 * 4,
        nbytes=groups * B * B * 8,
        name="own_places",
    )
    p_hi, p_lo = call(
        functools.partial(places_body, n_r, keep),
        [jax.ShapeDtypeStruct((B, blocks * n_r * keep), BF16)] * 2,
        (mask, tally, idx_row, tab),
        [SM, SM, VM, VM],
        [VM, VM],
        flops=4 * B * B * blocks * n_r * keep,
        nbytes=4 * B * blocks * n_r * keep,
        name="places",
    )

    ship = call(
        functools.partial(kept_body, keep),
        jax.ShapeDtypeStruct((keep, width), BF16),
        (vel[0], a_own, tab, grads),
        [VM] * 4,
        VM,
        flops=6 * B * B * width,
        nbytes=B * width * 6,
        name="kept_rows",
    )
    ships = spread(ship, "replica", n_r)
    new = call(
        functools.partial(return_body, keep),
        jax.ShapeDtypeStruct((B, width), F32),
        (vel[0], p_own, tab, grads, ship),
        [VM] * 5,
        VM,
        flops=6 * B * B * width,
        nbytes=B * width * 10,
        name="new_momentums",
    )

    input_grad = call(
        functools.partial(input_grad_body, n_t, rp, cp),
        jax.ShapeDtypeStruct((tok, cols), BF16),
        (shared, ups),
        [VM] * 2,
        VM,
        scratch=[pltpu.VMEM((n_t * B, cols), BF16)],
        flops=2 * tok * n_t * B * cols,
        nbytes=(n_t * B * cols + tok * cols) * 2,
        name="input_grads",
    )

    update = call(
        functools.partial(update_body, n_r, keep),
        jax.ShapeDtypeStruct((B, width), F32),
        (p_hi, p_lo, tab, ships),
        [VM] * 4,
        VM,
        flops=8 * B * G * width,
        nbytes=B * width * 8,
        name="updates",
    )
    return input_grad, new[None], update


def per_device_plain(
    projection_inputs,
    switch_logits_raw,
    inner_neuron_slope,
    expansion_matrix,
    velocity_buffer,
    sent_spectral_lines,
    participant_mask,
    token_tallies,
):
    highest = lax.Precision.HIGHEST
    up_grad = (
        inner_neuron_slope.astype(jnp.float32) * jax.nn.silu(switch_logits_raw.astype(jnp.float32))
    ).astype(jnp.bfloat16)
    partial_terms = jnp.dot(up_grad, expansion_matrix, preferred_element_type=jnp.float32)
    input_grad = lax.psum_scatter(partial_terms, "tensor", scatter_dimension=1, tiled=True).astype(
        jnp.bfloat16
    )
    grad_w = lax.dot_general(
        up_grad,
        lax.all_gather(projection_inputs, "tensor", axis=1, tiled=True),
        (((0,), (0,)), ((), ())),
        preferred_element_type=jnp.float32,
    )
    row_total_count = expansion_matrix.shape[0] // 64
    col_count = expansion_matrix.shape[1] // 64
    moment = momentum_decay * velocity_buffer[0] + grad_w
    cosines = cosine_table()
    blocks = moment.reshape(row_total_count, 64, col_count, 64).transpose(0, 2, 1, 3)
    coefficients = jnp.einsum("fa,ijab,gb->ijfg", cosines, blocks, cosines, precision=highest)
    freq_ids = jnp.arange(64, dtype=jnp.int32)
    own_rows = sent_spectral_lines[0]
    chosen = (own_rows[..., None] == freq_ids).astype(jnp.float32)
    shipped = jnp.einsum("ijkf,ijfg->ijkg", chosen, coefficients, precision=highest).astype(
        jnp.bfloat16
    )
    spectrum = jnp.einsum("ijkf,ijkg->ijfg", chosen, shipped.astype(jnp.float32), precision=highest)
    returned = jnp.einsum("fa,ijfg,gb->ijab", cosines, spectrum, cosines, precision=highest)
    new_moment = moment - returned.transpose(0, 2, 1, 3).reshape(moment.shape)
    worker_burdens = participant_mask.astype(jnp.float32) * token_tallies.astype(jnp.float32)
    worker_fractions = worker_burdens * (
        jnp.sum(participant_mask.astype(jnp.float32)) / jnp.sum(worker_burdens)
    )
    myself = lax.axis_index("replica")
    combined = lax.psum(worker_fractions[myself] * spectrum, "replica")
    update = jnp.einsum("fa,ijfg,gb->ijab", cosines, combined, cosines, precision=highest)
    update = update.transpose(0, 2, 1, 3).reshape(moment.shape)
    return (input_grad, new_moment[None], update)


def solution(mesh):
    n_t, n_r = mesh.shape["tensor"], mesh.shape["replica"]

    def device(*args):
        act, exp, lines = args[0], args[3], args[5]
        fits = (
            act.shape[1] % G == 0
            and act.shape[0] % 128 == 0
            and exp.shape[0] == B
            and lines.shape[3] == 8
            and n_r == 8
        )
        if not fits:
            return per_device_plain(*args)
        return per_device(n_t, n_r, *args)

    return jax.shard_map(
        device,
        mesh=mesh,
        in_specs=(
            P("replica", "tensor"),
            P("replica", "tensor"),
            P("replica", "tensor"),
            P("tensor", None),
            P("replica", "tensor", None),
            P("replica", "tensor", None, None),
            P(),
            P(),
        ),
        out_specs=(P("replica", "tensor"), P("replica", "tensor", None), P("tensor", None)),
        check_vma=False,
    )
```

```python
import functools

import jax
import jax.numpy as jnp
import numpy as np
from jax import lax
from jax.experimental import pallas as pl
from jax.experimental.pallas import tpu as pltpu
from jax.sharding import PartitionSpec as P

momentum_decay = 0.9
B = 64
G = 256
F32 = jnp.float32
BF16 = jnp.bfloat16
VMEM_LIMIT = 24 * 1024 * 1024
FIRST_LIMIT = 63 * 1024 * 1024

VM = pl.BlockSpec(memory_space=pltpu.VMEM)
SM = pl.BlockSpec(memory_space=pltpu.SMEM)
ANY = pl.BlockSpec(memory_space=pl.ANY)


def cosine_table():
    freqs = jnp.arange(64, dtype=jnp.float32)[:, None]
    places = jnp.arange(64, dtype=jnp.float32)[None, :]
    cosines = jnp.cos(jnp.pi * (places + 0.5) * freqs / 64.0) * jnp.sqrt(2.0 / 64.0)
    return cosines.at[0].multiply(jnp.sqrt(0.5))


def cosine_np():
    f = np.arange(B)[:, None]
    a = np.arange(B)[None, :]
    c = np.cos(np.pi * (a + 0.5) * f / B) * np.sqrt(2.0 / B)
    c[0] *= np.sqrt(0.5)
    return c


def halves(c):
    hi = np.asarray(c, dtype=np.float32).astype(jnp.bfloat16)
    lo = (np.asarray(c, np.float64) - hi.astype(np.float64)).astype(np.float32).astype(jnp.bfloat16)
    return hi, lo


def constants():
    hi, lo = halves(cosine_np())
    eye = np.eye(G // B)
    kron = lambda x: np.kron(eye, np.asarray(x, np.float32)).astype(jnp.bfloat16)
    tall = np.zeros((2 * B, G), jnp.bfloat16)
    tall[:B, :B], tall[B:, :B] = hi.T, lo.T
    return jnp.asarray(np.concatenate([kron(hi.T), kron(lo.T), kron(hi), kron(lo), tall], axis=0))


def fwd(tab, i):
    return tab[i * G : (i + 1) * G, :]


def inv(tab, i):
    return tab[(2 + i) * G : (3 + i) * G, :]


def tall(tab):
    return tab[4 * G : 4 * G + 2 * B, :B]


def dot(a, b):
    return jnp.dot(a, b, preferred_element_type=F32)


def split(x):
    hi = x.astype(BF16)
    return hi, (x - hi.astype(F32)).astype(BF16)


def call(body, out_shape, ins, in_specs, out_specs, scratch=(), flops=0, nbytes=0, name=None, limit=VMEM_LIMIT):
    return pl.pallas_call(
        body,
        out_shape=out_shape,
        in_specs=in_specs,
        out_specs=out_specs,
        scratch_shapes=scratch,
        compiler_params=pltpu.CompilerParams(vmem_limit_bytes=limit),
        cost_estimate=pl.CostEstimate(flops=flops, bytes_accessed=nbytes, transcendentals=0),
        name=name,
    )(*ins)


def up_grad(switch, slope):
    v = switch.astype(F32)
    return (slope.astype(F32) * (v * jax.nn.sigmoid(v))).astype(BF16)


def first_body(n_t, cp, cols, nr, pos, switch, slope, exp_ref, *refs):
    outs = refs[:n_t]
    switch_v, slope_v, exp_v, sems = refs[n_t:]
    rep, ten = pos[0], pos[1]
    r0 = pl.multiple_of((rep // cp) * nr, nr)
    copies = [
        pltpu.make_async_copy(src, dst, sems.at[i])
        for i, (src, dst) in enumerate(
            [(switch, switch_v), (slope, slope_v), (exp_ref.at[pl.ds(r0, nr), :], exp_v)]
        )
    ]
    for copy in copies:
        copy.start()
    copies[0].wait()
    copies[1].wait()
    up = up_grad(switch_v[...], slope_v[...])
    for k in range(n_t):
        outs[k][:B, :] = up
    copies[2].wait()
    nc = cols // cp
    for k in range(n_t):
        c0 = lax.rem(ten + k, n_t) * cols + lax.rem(rep, cp) * nc
        for j in range(nc // 128):
            at = pl.multiple_of(c0 + j * 128, 128)
            outs[k][B + j * nr : B + (j + 1) * nr, :] = exp_v[:, pl.ds(at, 128)]


def grads_body(n_t, switch, slope, act, *refs):
    ups, outs = refs[: n_t - 1], refs[n_t - 1 :]
    up = jnp.concatenate([up_grad(switch[...], slope[...])] + [u[:B, :] for u in ups], axis=0)
    for c in range(0, act.shape[1], G):
        g = dot(up, act[:, c : c + G])
        for k in range(n_t):
            outs[k][:, c : c + G] = g[k * B : (k + 1) * B].astype(outs[k].dtype)


def bundle_body(n_t, keep, after, lines, *refs):
    parts, out = refs[:n_t], refs[n_t]
    n = parts[0].shape[0] - B
    for k in range(n_t):
        out[k * n : (k + 1) * n, :] = parts[k][B:, :]
    blocks = lines.shape[1]
    rows = jnp.concatenate([lines[...].astype(F32), jnp.zeros((keep, 128 - blocks), F32)], axis=1)
    out[n_t * n :, :] = jnp.concatenate([rows, jnp.zeros((16 - keep, 128), F32)], axis=0).astype(BF16)


def join_body(*refs):
    for i, ref in enumerate(refs[:-1]):
        refs[-1][i] = ref[...]


def own_body(n_r, keep, pos, mask, tally, rows, tab, p_ref, a_ref, tab_ref, w_ref, mask_s, tally_s, sems):
    copies = [pltpu.make_async_copy(mask, mask_s, sems.at[0]), pltpu.make_async_copy(tally, tally_s, sems.at[1])]
    for copy in copies:
        copy.start()
    tab_ref[...] = tab[...]
    freq = lax.broadcasted_iota(jnp.int32, (B, 2 * B), 0)
    term = lax.broadcasted_iota(jnp.int32, (B, 2 * B), 1) // (B // 2)
    for g in range(rows.shape[0]):
        hot = jnp.where(freq == rows[g : g + 1, :], 1.0, 0.0).astype(BF16)
        y = dot(tall(tab), hot)
        p = jnp.where(term == 3, 0.0, jnp.where(term == 1, y[B:], y[:B]))
        p_ref[:, g * 2 * B : (g + 1) * 2 * B] = p.astype(BF16)
        a_ref[g * B : (g + 1) * B, :] = jnp.concatenate([p, p], axis=0).T[:B].astype(BF16)
    for copy in copies:
        copy.wait()
    total, alive = jnp.float32(0), jnp.float32(0)
    for r in range(n_r):
        m = mask_s[r].astype(F32)
        total = total + m * tally_s[r].astype(F32)
        alive = alive + m
    half = n_r // 2
    place = (lax.broadcasted_iota(jnp.int32, (8, 2 * B), 1) // keep) % n_r
    w = jnp.zeros((8, 2 * B), F32)
    for i in range(n_r):
        r = pos[0] ^ (2 * (i % half) + i // half)
        w = jnp.where(place == i, mask_s[r].astype(F32) * tally_s[r].astype(F32), w)
    w_ref[...] = w * (jnp.full((8, 2 * B), alive) / jnp.full((8, 2 * B), total))


def kept_body(n_t, keep, pos, vel, a_ref, tab, after, *refs):
    grads, ship_ref = refs[:n_t], refs[n_t]
    cols = grads[0].shape[1]
    ng = cols // G
    lane_block = lax.broadcasted_iota(jnp.int32, (keep, G), 1) // B
    sel = []
    for k in range(n_t):
        c0 = lax.rem(pos[1] + k, n_t) * cols
        for i in range(ng):
            at = pl.multiple_of(c0 + i * G, G)
            moment = momentum_decay * vel[:, pl.ds(at, G)] + grads[k][:, i * G : (i + 1) * G].astype(F32)
            hi, lo = split(moment)
            y = dot(a_ref[pl.ds(pl.multiple_of(at // (G // B), B), B), :], jnp.concatenate([hi, lo], axis=0))
            y = y[: B // 2] + y[B // 2 :]
            got = y[:keep]
            for j in range(1, G // B):
                got = jnp.where(lane_block == j, y[j * keep : (j + 1) * keep], got)
            sel.append(got)
    hi, lo = split(jnp.concatenate(sel, axis=0))
    n = n_t * ng * keep
    y = dot(jnp.concatenate([hi, lo], axis=0), fwd(tab, 0))
    y = y[:n] + y[n:] + dot(hi, fwd(tab, 1))
    for k in range(n_t):
        c0 = pl.multiple_of(lax.rem(pos[1] + k, n_t) * cols, G)
        ship_ref[:, pl.ds(c0, cols)] = jnp.concatenate(
            [y[(k * ng + i) * keep : (k * ng + i + 1) * keep] for i in range(ng)], axis=1
        ).astype(BF16)


def return_body(n_t, keep, pos, vel, p_ref, tab, ship, *refs):
    grads, new_ref = refs[:n_t], refs[n_t]
    cols = grads[0].shape[1]
    ng = cols // G
    lane_block = lax.broadcasted_iota(jnp.int32, (keep, G), 1) // B
    kept = ship[...].astype(F32)
    total = kept.shape[1] // G
    kept = jnp.concatenate([kept[:, g * G : (g + 1) * G] for g in range(total)], axis=0).astype(BF16)
    q = dot(kept, inv(tab, 0)) + dot(kept, inv(tab, 1))
    for g in range(total):
        own = q[g * keep : (g + 1) * keep]
        spread = jnp.concatenate(
            [jnp.where(lane_block == j, own, 0.0) for j in range(G // B)], axis=0
        )
        hi, lo = split(spread)
        w = jnp.concatenate([hi, hi, lo, jnp.zeros_like(lo)], axis=0)
        back = dot(p_ref[:, g * 2 * B : (g + 1) * 2 * B], w)
        cut = slice(g * G, (g + 1) * G)
        new_ref[:, cut] = momentum_decay * vel[:, cut] - back
    for k in range(n_t):
        c0 = lax.rem(pos[1] + k, n_t) * cols
        for i in range(ng):
            at = pl.multiple_of(c0 + i * G, G)
            new_ref[:, pl.ds(at, G)] += grads[k][:, i * G : (i + 1) * G].astype(F32)


def places_body(n_r, keep, w_ref, mine, other, tab, hi_ref, lo_ref):
    half = n_r // 2
    w = w_ref[:1, :]
    last = mine.shape[1] - 16
    rows = [ref[i, last:, :].astype(F32)[:keep] for ref in (mine, other) for i in range(half)]
    rows = jnp.concatenate(rows + rows, axis=0).T
    freq = lax.broadcasted_iota(jnp.int32, (B, 2 * B), 0).astype(F32)
    first = lax.broadcasted_iota(jnp.int32, (1, 2 * B), 1) < B
    for c in range(hi_ref.shape[1] // (2 * B)):
        num = jnp.where(first, rows[2 * c : 2 * c + 1], rows[2 * c + 1 : 2 * c + 2])
        hot = jnp.where(freq == num, 1.0, 0.0).astype(BF16)
        y = dot(tall(tab), hot)
        hi, lo = split((y[:B] + y[B:]) * w)
        hi_ref[:, c * 2 * B : (c + 1) * 2 * B] = hi
        lo_ref[:, c * 2 * B : (c + 1) * 2 * B] = lo


def update_body(n_r, keep, p_hi, p_lo, tab, mine, other, out, hi_ref, lo_ref):
    per = n_r * keep
    nb = G // B
    width = nb * per
    half = n_r // 2
    ng = out.shape[1] // G
    lane_block = lax.broadcasted_iota(jnp.int32, (per, G), 1) // B
    for g in range(ng):
        cut = slice(g * G, (g + 1) * G)
        s = jnp.concatenate(
            [ref[i, :, cut].astype(F32) for ref in (mine, other) for i in range(half)], axis=0
        )
        w = jnp.concatenate(
            [jnp.where(lane_block == j, s, 0.0).astype(BF16) for j in range(nb)], axis=0
        )
        wide = slice(g * width, (g + 1) * width)
        y = dot(jnp.concatenate([p_hi[:, wide], p_lo[:, wide]], axis=0), w)
        hi, lo = split(y[:B] + y[B:])
        hi_ref[g * B : (g + 1) * B, :] = hi
        lo_ref[g * B : (g + 1) * B, :] = lo
    z = dot(hi_ref[...], inv(tab, 0)) + dot(lo_ref[...], inv(tab, 0)) + dot(hi_ref[...], inv(tab, 1))
    for g in range(ng):
        out[:, g * G : (g + 1) * G] = z[g * B : (g + 1) * B]


def input_grad_body(n_t, n_r, cp, pos, mine, other, *refs):
    ups, out, held = refs[:n_t], refs[n_t], refs[n_t + 1]
    nc = out.shape[1] // cp
    nr = B // (n_r // cp)
    tiles = nc // 128
    for h, ref in enumerate((mine, other)):
        for i in range(n_r // 2):
            src = pos[0] ^ (2 * i + h)
            r0 = (src // cp) * nr
            c0 = lax.rem(src, cp) * nc
            for k in range(n_t):
                for j in range(tiles):
                    at = (k * tiles + j) * nr
                    held[
                        pl.ds(pl.multiple_of(k * B + r0, nr), nr), pl.ds(pl.multiple_of(c0 + j * 128, 128), 128)
                    ] = ref[i, at : at + nr, :]
    up = jnp.concatenate([u[:B, :] for u in ups], axis=0).T
    for c in range(0, out.shape[1], G):
        out[:, c : c + G] = dot(up, held[:, c : c + G]).astype(BF16)


def per_device(n_t, n_r, act, switch, slope, exp, vel, lines, mask, tally):
    cols = act.shape[1]
    width = exp.shape[1]
    tok = act.shape[0]
    keep = lines.shape[3]
    blocks = width // B
    groups = width // G
    cp = 2
    rp = n_r // cp
    half = n_r // 2
    tab = constants()
    rep = lax.axis_index("replica").astype(jnp.int32)
    ten = lax.axis_index("tensor").astype(jnp.int32)
    pos = jnp.stack([rep, ten])

    def shift(x, k):
        return lax.ppermute(x, "tensor", [(i, (i + k) % n_t) for i in range(n_t)])

    def shifts(xs, sign):
        order = sorted(range(1, n_t), key=lambda k: -min(k, n_t - k))
        got = {0: xs[0]}
        for k in order:
            got[k] = shift(xs[k], sign * k)
        return [got[k] for k in range(n_t)]

    def swap(x, m):
        return lax.ppermute(x, "replica", [(i, i ^ m) for i in range(n_r)])

    def share(x, name):
        parts = [x] + [swap(x, 2 * i) for i in range(1, half)]
        mine = call(
            join_body,
            jax.ShapeDtypeStruct((half,) + x.shape, x.dtype),
            parts,
            [VM] * half,
            VM,
            name=name,
        )
        return mine, swap(mine, 1)

    tiles = cols // cp // 128
    nr = B // rp
    outs = call(
        functools.partial(first_body, n_t, cp, cols, nr),
        [jax.ShapeDtypeStruct((B + tiles * nr, 128), BF16)] * n_t,
        (pos, switch.T, slope.T, exp),
        [SM, ANY, ANY, ANY],
        [VM] * n_t,
        scratch=[
            pltpu.VMEM((B, tok), BF16),
            pltpu.VMEM((B, tok), BF16),
            pltpu.VMEM((nr, width), BF16),
            pltpu.SemaphoreType.DMA((3,)),
        ],
        flops=1 << 32,
        name="up_grads",
        limit=FIRST_LIMIT,
    )
    parts = shifts(outs, 1)

    grads = call(
        functools.partial(grads_body, n_t),
        [jax.ShapeDtypeStruct((B, cols), F32)] + [jax.ShapeDtypeStruct((B, cols), BF16)] * (n_t - 1),
        (switch.T, slope.T, act, *parts[1:]),
        [VM] * (n_t + 2),
        [VM] * n_t,
        flops=2 * n_t * B * tok * cols,
        nbytes=act.size * 2 + n_t * B * cols * 2,
        name="weight_grads",
    )
    made = grads[1]
    grads = shifts(grads, -1)

    own = lines[0, 0].T
    bundle = call(
        functools.partial(bundle_body, n_t, keep),
        jax.ShapeDtypeStruct((n_t * tiles * nr + 16, 128), BF16),
        (made, own, *parts),
        [ANY] + [VM] * (n_t + 1),
        VM,
        name="bundle",
    )
    mine, other = share(bundle, "join_bundles")

    own_rows = jnp.concatenate([lines[0, 0].reshape(groups, B // 2)] * 4, axis=1)
    p_own, a_own, tab, shares = call(
        functools.partial(own_body, n_r, keep),
        [
            jax.ShapeDtypeStruct((B, groups * 2 * B), BF16),
            jax.ShapeDtypeStruct((groups * B, 2 * B), BF16),
            jax.ShapeDtypeStruct(tab.shape, BF16),
            jax.ShapeDtypeStruct((8, 2 * B), F32),
        ],
        (pos, mask, tally, own_rows, tab),
        [SM, ANY, ANY, VM, VM],
        [VM] * 4,
        scratch=[pltpu.SMEM((n_r,), jnp.int32)] * 2 + [pltpu.SemaphoreType.DMA((2,))],
        name="own_places",
    )
    p_hi, p_lo = call(
        functools.partial(places_body, n_r, keep),
        [jax.ShapeDtypeStruct((B, blocks * n_r * keep), BF16)] * 2,
        (shares, mine, other, tab),
        [VM] * 4,
        [VM, VM],
        name="places",
    )
    input_grad = call(
        functools.partial(input_grad_body, n_t, n_r, cp),
        jax.ShapeDtypeStruct((tok, cols), BF16),
        (pos, mine, other, *parts),
        [SM] + [VM] * (2 + n_t),
        VM,
        scratch=[pltpu.VMEM((n_t * B, cols), BF16)],
        flops=2 * tok * n_t * B * cols,
        nbytes=(n_t * B * cols + tok * cols) * 2,
        name="input_grads",
    )

    ship = call(
        functools.partial(kept_body, n_t, keep),
        jax.ShapeDtypeStruct((keep, width), BF16),
        (pos, vel[0], a_own, tab, p_hi, *grads),
        [SM] + [VM] * 3 + [ANY] + [VM] * n_t,
        VM,
        flops=6 * B * B * width,
        nbytes=B * width * 6,
        name="kept_rows",
    )
    mine, other = share(ship, "join_kept")
    new = call(
        functools.partial(return_body, n_t, keep),
        jax.ShapeDtypeStruct((B, width), F32),
        (pos, vel[0], p_own, tab, ship, *grads),
        [SM] + [VM] * (4 + n_t),
        VM,
        flops=6 * B * B * width,
        nbytes=B * width * 10,
        name="new_momentums",
    )
    update = call(
        functools.partial(update_body, n_r, keep),
        jax.ShapeDtypeStruct((B, width), F32),
        (p_hi, p_lo, tab, mine, other),
        [VM] * 5,
        VM,
        scratch=[pltpu.VMEM((groups * B, G), BF16)] * 2,
        flops=8 * B * G * width,
        nbytes=B * width * 8,
        name="updates",
    )
    return input_grad, new[None], update


def per_device_plain(
    projection_inputs,
    switch_logits_raw,
    inner_neuron_slope,
    expansion_matrix,
    velocity_buffer,
    sent_spectral_lines,
    participant_mask,
    token_tallies,
):
    highest = lax.Precision.HIGHEST
    up_grad = (
        inner_neuron_slope.astype(jnp.float32) * jax.nn.silu(switch_logits_raw.astype(jnp.float32))
    ).astype(jnp.bfloat16)
    partial_terms = jnp.dot(up_grad, expansion_matrix, preferred_element_type=jnp.float32)
    input_grad = lax.psum_scatter(partial_terms, "tensor", scatter_dimension=1, tiled=True).astype(
        jnp.bfloat16
    )
    grad_w = lax.dot_general(
        up_grad,
        lax.all_gather(projection_inputs, "tensor", axis=1, tiled=True),
        (((0,), (0,)), ((), ())),
        preferred_element_type=jnp.float32,
    )
    row_total_count = expansion_matrix.shape[0] // 64
    col_count = expansion_matrix.shape[1] // 64
    moment = momentum_decay * velocity_buffer[0] + grad_w
    cosines = cosine_table()
    blocks = moment.reshape(row_total_count, 64, col_count, 64).transpose(0, 2, 1, 3)
    coefficients = jnp.einsum("fa,ijab,gb->ijfg", cosines, blocks, cosines, precision=highest)
    freq_ids = jnp.arange(64, dtype=jnp.int32)
    own_rows = sent_spectral_lines[0]
    chosen = (own_rows[..., None] == freq_ids).astype(jnp.float32)
    shipped = jnp.einsum("ijkf,ijfg->ijkg", chosen, coefficients, precision=highest).astype(
        jnp.bfloat16
    )
    spectrum = jnp.einsum("ijkf,ijkg->ijfg", chosen, shipped.astype(jnp.float32), precision=highest)
    returned = jnp.einsum("fa,ijfg,gb->ijab", cosines, spectrum, cosines, precision=highest)
    new_moment = moment - returned.transpose(0, 2, 1, 3).reshape(moment.shape)
    worker_burdens = participant_mask.astype(jnp.float32) * token_tallies.astype(jnp.float32)
    worker_fractions = worker_burdens * (
        jnp.sum(participant_mask.astype(jnp.float32)) / jnp.sum(worker_burdens)
    )
    myself = lax.axis_index("replica")
    combined = lax.psum(worker_fractions[myself] * spectrum, "replica")
    update = jnp.einsum("fa,ijfg,gb->ijab", cosines, combined, cosines, precision=highest)
    update = update.transpose(0, 2, 1, 3).reshape(moment.shape)
    return (input_grad, new_moment[None], update)


def solution(mesh):
    n_t, n_r = mesh.shape["tensor"], mesh.shape["replica"]

    def device(*args):
        act, exp, lines = args[0], args[3], args[5]
        fits = (
            act.shape[1] % G == 0
            and act.shape[0] % 128 == 0
            and exp.shape[0] == B
            and lines.shape[3] == 8
            and n_r == 8
        )
        if not fits:
            return per_device_plain(*args)
        return per_device(n_t, n_r, *args)

    return jax.shard_map(
        device,
        mesh=mesh,
        in_specs=(
            P("replica", "tensor"),
            P("replica", "tensor"),
            P("replica", "tensor"),
            P("tensor", None),
            P("replica", "tensor", None),
            P("replica", "tensor", None, None),
            P(),
            P(),
        ),
        out_specs=(P("replica", "tensor"), P("replica", "tensor", None), P("tensor", None)),
        check_vma=False,
    )
```

```python
import functools

import jax
import jax.numpy as jnp
import numpy as np
from jax import lax
from jax.experimental import pallas as pl
from jax.experimental.pallas import tpu as pltpu
from jax.sharding import PartitionSpec as P

momentum_decay = 0.9
B = 64
G = 256
F32 = jnp.float32
BF16 = jnp.bfloat16
VMEM_LIMIT = 24 * 1024 * 1024

VM = pl.BlockSpec(memory_space=pltpu.VMEM)
SM = pl.BlockSpec(memory_space=pltpu.SMEM)
ANY = pl.BlockSpec(memory_space=pl.ANY)


def cosine_table():
    freqs = jnp.arange(64, dtype=jnp.float32)[:, None]
    places = jnp.arange(64, dtype=jnp.float32)[None, :]
    cosines = jnp.cos(jnp.pi * (places + 0.5) * freqs / 64.0) * jnp.sqrt(2.0 / 64.0)
    return cosines.at[0].multiply(jnp.sqrt(0.5))


def cosine_np():
    f = np.arange(B)[:, None]
    a = np.arange(B)[None, :]
    c = np.cos(np.pi * (a + 0.5) * f / B) * np.sqrt(2.0 / B)
    c[0] *= np.sqrt(0.5)
    return c


def halves(c):
    hi = np.asarray(c, dtype=np.float32).astype(jnp.bfloat16)
    lo = (np.asarray(c, np.float64) - hi.astype(np.float64)).astype(np.float32).astype(jnp.bfloat16)
    return hi, lo


def constants():
    hi, lo = halves(cosine_np())
    eye = np.eye(G // B)
    kron = lambda x: np.kron(eye, np.asarray(x, np.float32)).astype(jnp.bfloat16)
    tall = np.zeros((2 * B, G), jnp.bfloat16)
    tall[:B, :B], tall[B:, :B] = hi.T, lo.T
    return jnp.asarray(np.concatenate([kron(hi.T), kron(lo.T), kron(hi), kron(lo), tall], axis=0))


def fwd(tab, i):
    return tab[i * G : (i + 1) * G, :]


def inv(tab, i):
    return tab[(2 + i) * G : (3 + i) * G, :]


def tall(tab):
    return tab[4 * G : 4 * G + 2 * B, :B]


def dot(a, b):
    return jnp.dot(a, b, preferred_element_type=F32)


def split(x):
    hi = x.astype(BF16)
    return hi, (x - hi.astype(F32)).astype(BF16)


def near(shape, dtype=BF16):
    return pltpu.VMEM(shape, dtype)


def far(x):
    return pltpu.with_memory_space_constraint(x, pltpu.HBM)


def call(body, out_shape, ins, in_specs, out_specs, scratch=(), flops=0, nbytes=0, name=None):
    return pl.pallas_call(
        body,
        out_shape=out_shape,
        in_specs=in_specs,
        out_specs=out_specs,
        scratch_shapes=scratch,
        compiler_params=pltpu.CompilerParams(vmem_limit_bytes=VMEM_LIMIT),
        cost_estimate=pl.CostEstimate(flops=flops, bytes_accessed=nbytes, transcendentals=0),
        name=name,
    )(*ins)


def first_body(n_t, cp, cols, nr, switch, slope, exp_ref, act, *refs):
    outs, act_out = refs[:n_t], refs[n_t]
    switch_v, slope_v, exp_v, sems = refs[n_t + 1 :]
    rep, ten = lax.axis_index("replica"), lax.axis_index("tensor")
    r0 = pl.multiple_of((rep // cp) * nr, nr)
    copies = [
        pltpu.make_async_copy(src, dst, sems.at[i])
        for i, (src, dst) in enumerate(
            [(switch, switch_v), (slope, slope_v), (exp_ref.at[pl.ds(r0, nr), :], exp_v), (act, act_out)]
        )
    ]
    for copy in copies:
        copy.start()
    copies[0].wait()
    copies[1].wait()
    v = switch_v[...].astype(F32)
    up = (slope_v[...].astype(F32) * (v * jax.nn.sigmoid(v))).astype(BF16)
    for k in range(n_t):
        outs[k][:B, :] = up
    copies[2].wait()
    nc = cols // cp
    for k in range(n_t):
        c0 = lax.rem(ten + k, n_t) * cols + lax.rem(rep, cp) * nc
        for j in range(nc // 128):
            at = pl.multiple_of(c0 + j * 128, 128)
            outs[k][B + j * nr : B + (j + 1) * nr, :] = exp_v[:, pl.ds(at, 128)]
    copies[3].wait()


def grads_body(n_t, act, *refs):
    ups, outs = refs[:n_t], refs[n_t:]
    up = jnp.concatenate([u[:B, :] for u in ups], axis=0)
    for c in range(0, act.shape[1], G):
        g = dot(up, act[:, c : c + G])
        for k in range(n_t):
            outs[k][:, c : c + G] = g[k * B : (k + 1) * B].astype(outs[k].dtype)


def bundle_body(n_t, keep, after, lines, *refs):
    parts, out = refs[:n_t], refs[n_t]
    n = parts[0].shape[0] - B
    for k in range(n_t):
        out[k * n : (k + 1) * n, :] = parts[k][B:, :]
    blocks = lines.shape[1]
    rows = jnp.concatenate([lines[...].astype(F32), jnp.zeros((keep, 128 - blocks), F32)], axis=1)
    out[n_t * n :, :] = jnp.concatenate([rows, jnp.zeros((16 - keep, 128), F32)], axis=0).astype(BF16)


def join_body(after, *refs):
    for i, ref in enumerate(refs[:-1]):
        refs[-1][i] = ref[...]


def own_body(n_r, keep, after, mask, tally, lines, tab, p_ref, a_ref, tab_ref, w_ref, mask_s, tally_s, sems):
    copies = [
        pltpu.make_async_copy(src, dst, sems.at[i])
        for i, (src, dst) in enumerate([(mask, mask_s), (tally, tally_s), (tab, tab_ref)])
    ]
    for copy in copies:
        copy.start()
    blocks = lines.shape[1]
    rows = jnp.concatenate([lines[...].astype(F32), jnp.zeros((keep, 128 - blocks), F32)], axis=1)
    rows = jnp.concatenate([rows] * (2 * B // keep), axis=0).T
    freq = lax.broadcasted_iota(jnp.int32, (B, 2 * B), 0).astype(F32)
    block = (lax.broadcasted_iota(jnp.int32, (1, 2 * B), 1) // keep) % (G // B)
    term = lax.broadcasted_iota(jnp.int32, (B, 2 * B), 1) // (B // 2)
    for copy in copies:
        copy.wait()
    for g in range(blocks // (G // B)):
        num = rows[g * (G // B) : g * (G // B) + 1]
        for j in range(1, G // B):
            num = jnp.where(block == j, rows[g * (G // B) + j : g * (G // B) + j + 1], num)
        hot = jnp.where(freq == num, 1.0, 0.0).astype(BF16)
        y = dot(tall(tab_ref), hot)
        p = jnp.where(term == 3, 0.0, jnp.where(term == 1, y[B:], y[:B]))
        p_ref[:, g * 2 * B : (g + 1) * 2 * B] = p.astype(BF16)
        a_ref[g * B : (g + 1) * B, :] = jnp.concatenate([p, p], axis=0).T[:B].astype(BF16)
    total, alive = jnp.float32(0), jnp.float32(0)
    for r in range(n_r):
        m = mask_s[r].astype(F32)
        total = total + m * tally_s[r].astype(F32)
        alive = alive + m
    place = (lax.broadcasted_iota(jnp.int32, (8, 2 * B), 1) // keep) % n_r
    w = jnp.zeros((8, 2 * B), F32)
    for m in range(n_r):
        r = lax.axis_index("replica") ^ m
        w = jnp.where(place == m, mask_s[r].astype(F32) * tally_s[r].astype(F32), w)
    w_ref[...] = w * (jnp.full((8, 2 * B), alive) / jnp.full((8, 2 * B), total))


def kept_body(n_t, keep, vel, a_ref, tab, after, *refs):
    grads, ship_ref = refs[:n_t], refs[n_t]
    cols = grads[0].shape[1]
    ng = cols // G
    lane_block = lax.broadcasted_iota(jnp.int32, (keep, G), 1) // B
    sel = []
    for k in range(n_t):
        c0 = lax.rem(lax.axis_index("tensor") + k, n_t) * cols
        for i in range(ng):
            at = pl.multiple_of(c0 + i * G, G)
            moment = momentum_decay * vel[:, pl.ds(at, G)] + grads[k][:, i * G : (i + 1) * G].astype(F32)
            hi, lo = split(moment)
            y = dot(a_ref[pl.ds(pl.multiple_of(at // (G // B), B), B), :], jnp.concatenate([hi, lo], axis=0))
            y = y[: B // 2] + y[B // 2 :]
            got = y[:keep]
            for j in range(1, G // B):
                got = jnp.where(lane_block == j, y[j * keep : (j + 1) * keep], got)
            sel.append(got)
    hi, lo = split(jnp.concatenate(sel, axis=0))
    n = n_t * ng * keep
    y = dot(jnp.concatenate([hi, lo], axis=0), fwd(tab, 0))
    y = y[:n] + y[n:] + dot(hi, fwd(tab, 1))
    for k in range(n_t):
        c0 = pl.multiple_of(lax.rem(lax.axis_index("tensor") + k, n_t) * cols, G)
        ship_ref[:, pl.ds(c0, cols)] = jnp.concatenate(
            [y[(k * ng + i) * keep : (k * ng + i + 1) * keep] for i in range(ng)], axis=1
        ).astype(BF16)


def return_body(n_t, keep, vel, p_ref, tab, ship, *refs):
    grads, new_ref = refs[:n_t], refs[n_t]
    cols = grads[0].shape[1]
    ng = cols // G
    lane_block = lax.broadcasted_iota(jnp.int32, (keep, G), 1) // B
    kept = ship[...].astype(F32)
    total = kept.shape[1] // G
    kept = jnp.concatenate([kept[:, g * G : (g + 1) * G] for g in range(total)], axis=0).astype(BF16)
    q = dot(kept, inv(tab, 0)) + dot(kept, inv(tab, 1))
    for g in range(total):
        own = q[g * keep : (g + 1) * keep]
        spread = jnp.concatenate(
            [jnp.where(lane_block == j, own, 0.0) for j in range(G // B)], axis=0
        )
        hi, lo = split(spread)
        w = jnp.concatenate([hi, hi, lo, jnp.zeros_like(lo)], axis=0)
        back = dot(p_ref[:, g * 2 * B : (g + 1) * 2 * B], w)
        cut = slice(g * G, (g + 1) * G)
        new_ref[:, cut] = momentum_decay * vel[:, cut] - back
    for k in range(n_t):
        c0 = lax.rem(lax.axis_index("tensor") + k, n_t) * cols
        for i in range(ng):
            at = pl.multiple_of(c0 + i * G, G)
            new_ref[:, pl.ds(at, G)] += grads[k][:, i * G : (i + 1) * G].astype(F32)


def places_body(keep, w_ref, tab, bundles, hi_ref, lo_ref):
    w = w_ref[:1, :]
    n_r, last = bundles.shape[0], bundles.shape[1] - 16
    rep = lax.axis_index("replica")
    rows = [bundles[rep ^ m, last:, :].astype(F32)[:keep] for m in range(n_r)]
    rows = jnp.concatenate(rows + rows, axis=0).T
    freq = lax.broadcasted_iota(jnp.int32, (B, 2 * B), 0).astype(F32)
    first = lax.broadcasted_iota(jnp.int32, (1, 2 * B), 1) < B
    for c in range(hi_ref.shape[1] // (2 * B)):
        num = jnp.where(first, rows[2 * c : 2 * c + 1], rows[2 * c + 1 : 2 * c + 2])
        hot = jnp.where(freq == num, 1.0, 0.0).astype(BF16)
        y = dot(tall(tab), hot)
        hi, lo = split((y[:B] + y[B:]) * w)
        hi_ref[:, c * 2 * B : (c + 1) * 2 * B] = hi
        lo_ref[:, c * 2 * B : (c + 1) * 2 * B] = lo


def update_body(n_r, keep, p_hi, p_lo, tab, mine, other, out, hi_ref, lo_ref):
    per = n_r * keep
    nb = G // B
    width = nb * per
    half = n_r // 2
    ng = out.shape[1] // G
    lane_block = lax.broadcasted_iota(jnp.int32, (per, G), 1) // B
    for g in range(ng):
        cut = slice(g * G, (g + 1) * G)
        s = jnp.concatenate(
            [ref[i, :, cut].astype(F32) for i in range(half) for ref in (mine, other)], axis=0
        )
        w = jnp.concatenate(
            [jnp.where(lane_block == j, s, 0.0).astype(BF16) for j in range(nb)], axis=0
        )
        wide = slice(g * width, (g + 1) * width)
        y = dot(jnp.concatenate([p_hi[:, wide], p_lo[:, wide]], axis=0), w)
        hi, lo = split(y[:B] + y[B:])
        hi_ref[g * B : (g + 1) * B, :] = hi
        lo_ref[g * B : (g + 1) * B, :] = lo
    z = dot(hi_ref[...], inv(tab, 0)) + dot(lo_ref[...], inv(tab, 0)) + dot(hi_ref[...], inv(tab, 1))
    for g in range(ng):
        out[:, g * G : (g + 1) * G] = z[g * B : (g + 1) * B]


def input_grad_body(n_t, n_r, cp, bundles, *refs):
    ups, out, held = refs[:n_t], refs[n_t], refs[n_t + 1]
    nc = out.shape[1] // cp
    nr = B // (n_r // cp)
    tiles = nc // 128
    for r in range(n_r):
        r0, c0 = (r // cp) * nr, (r % cp) * nc
        for k in range(n_t):
            for j in range(tiles):
                at = (k * tiles + j) * nr
                held[k * B + r0 : k * B + r0 + nr, c0 + j * 128 : c0 + (j + 1) * 128] = bundles[r, at : at + nr, :]
    up = jnp.concatenate([u[:B, :] for u in ups], axis=0).T
    for c in range(0, out.shape[1], G):
        out[:, c : c + G] = dot(up, held[:, c : c + G]).astype(BF16)


def per_device(n_t, n_r, act, switch, slope, exp, vel, lines, mask, tally):
    cols = act.shape[1]
    width = exp.shape[1]
    tok = act.shape[0]
    keep = lines.shape[3]
    blocks = width // B
    groups = width // G
    cp = 2
    rp = n_r // cp
    half = n_r // 2
    tab = constants()
    def shift(x, k):
        return lax.ppermute(x, "tensor", [(i, (i + k) % n_t) for i in range(n_t)])

    def shifts(xs, sign):
        order = sorted(range(1, n_t), key=lambda k: -min(k, n_t - k))
        got = {0: xs[0]}
        for k in order:
            got[k] = shift(xs[k], sign * k)
        return [got[k] for k in range(n_t)]

    def swap(x, m):
        return lax.ppermute(x, "replica", [(i, i ^ m) for i in range(n_r)])

    tiles = cols // cp // 128
    nr = B // rp
    *parts, act = call(
        functools.partial(first_body, n_t, cp, cols, nr),
        [near((B + tiles * nr, 128))] * n_t + [near(act.shape)],
        (far(switch.T), far(slope.T), far(exp), far(act)),
        [ANY] * 4,
        [VM] * (n_t + 1),
        scratch=[
            pltpu.VMEM((B, tok), BF16),
            pltpu.VMEM((B, tok), BF16),
            pltpu.VMEM((nr, width), BF16),
            pltpu.SemaphoreType.DMA((4,)),
        ],
        nbytes=act.size * 4 + nr * width * 2,
        name="up_grads",
    )
    parts = shifts(parts, 1)

    grads = call(
        functools.partial(grads_body, n_t),
        [near((B, cols), F32)] + [near((B, cols))] * (n_t - 1),
        (act, *parts),
        [VM] * (n_t + 1),
        [VM] * n_t,
        nbytes=act.size * 2 + n_t * B * cols * 2,
        name="weight_grads",
    )
    made = grads[1]
    grads = shifts(grads, -1)

    own = lines[0, 0].T
    bundle = call(
        functools.partial(bundle_body, n_t, keep),
        near((n_t * tiles * nr + 16, 128)),
        (made, own, *parts),
        [ANY] + [VM] * (n_t + 1),
        VM,
        name="bundle",
    )
    bundles = lax.all_gather(bundle, "replica", axis=0)

    p_own, a_own, tab, shares = call(
        functools.partial(own_body, n_r, keep),
        [
            near((B, groups * 2 * B)),
            near((groups * B, 2 * B)),
            near(tab.shape),
            near((8, 2 * B), F32),
        ],
        (made, far(mask), far(tally), own, far(tab)),
        [ANY, ANY, ANY, VM, ANY],
        [VM] * 4,
        scratch=[pltpu.SMEM((n_r,), jnp.int32)] * 2 + [pltpu.SemaphoreType.DMA((3,))],
        name="own_places",
    )
    p_hi, p_lo = call(
        functools.partial(places_body, keep),
        [near((B, blocks * n_r * keep))] * 2,
        (shares, tab, bundles),
        [VM] * 3,
        [VM, VM],
        name="places",
    )
    input_grad = call(
        functools.partial(input_grad_body, n_t, n_r, cp),
        jax.ShapeDtypeStruct((tok, cols), BF16),
        (bundles, *parts),
        [VM] * (1 + n_t),
        VM,
        scratch=[pltpu.VMEM((n_t * B, cols), BF16)],
        flops=2 * tok * n_t * B * cols,
        nbytes=(n_t * B * cols + tok * cols) * 2,
        name="input_grads",
    )

    ship = call(
        functools.partial(kept_body, n_t, keep),
        near((keep, width)),
        (vel[0], a_own, tab, p_hi, *grads),
        [VM] * 3 + [ANY] + [VM] * n_t,
        VM,
        flops=6 * B * B * width,
        nbytes=B * width * 6,
        name="kept_rows",
    )
    ships = [ship] + [swap(ship, 2 * i) for i in range(1, half)]
    new = call(
        functools.partial(return_body, n_t, keep),
        jax.ShapeDtypeStruct((B, width), F32),
        (vel[0], p_own, tab, ship, *grads),
        [VM] * (4 + n_t),
        VM,
        flops=6 * B * B * width,
        nbytes=B * width * 10,
        name="new_momentums",
    )
    mine = call(
        join_body,
        near((half, keep, width)),
        (far(new), *ships),
        [ANY] + [VM] * half,
        VM,
        name="join_kept",
    )
    other = swap(mine, 1)
    update = call(
        functools.partial(update_body, n_r, keep),
        jax.ShapeDtypeStruct((B, width), F32),
        (p_hi, p_lo, tab, mine, other),
        [VM] * 5,
        VM,
        scratch=[pltpu.VMEM((groups * B, G), BF16)] * 2,
        flops=8 * B * G * width,
        nbytes=B * width * 8,
        name="updates",
    )
    return input_grad, new[None], update


def per_device_plain(
    projection_inputs,
    switch_logits_raw,
    inner_neuron_slope,
    expansion_matrix,
    velocity_buffer,
    sent_spectral_lines,
    participant_mask,
    token_tallies,
):
    highest = lax.Precision.HIGHEST
    up_grad = (
        inner_neuron_slope.astype(jnp.float32) * jax.nn.silu(switch_logits_raw.astype(jnp.float32))
    ).astype(jnp.bfloat16)
    partial_terms = jnp.dot(up_grad, expansion_matrix, preferred_element_type=jnp.float32)
    input_grad = lax.psum_scatter(partial_terms, "tensor", scatter_dimension=1, tiled=True).astype(
        jnp.bfloat16
    )
    grad_w = lax.dot_general(
        up_grad,
        lax.all_gather(projection_inputs, "tensor", axis=1, tiled=True),
        (((0,), (0,)), ((), ())),
        preferred_element_type=jnp.float32,
    )
    row_total_count = expansion_matrix.shape[0] // 64
    col_count = expansion_matrix.shape[1] // 64
    moment = momentum_decay * velocity_buffer[0] + grad_w
    cosines = cosine_table()
    blocks = moment.reshape(row_total_count, 64, col_count, 64).transpose(0, 2, 1, 3)
    coefficients = jnp.einsum("fa,ijab,gb->ijfg", cosines, blocks, cosines, precision=highest)
    freq_ids = jnp.arange(64, dtype=jnp.int32)
    own_rows = sent_spectral_lines[0]
    chosen = (own_rows[..., None] == freq_ids).astype(jnp.float32)
    shipped = jnp.einsum("ijkf,ijfg->ijkg", chosen, coefficients, precision=highest).astype(
        jnp.bfloat16
    )
    spectrum = jnp.einsum("ijkf,ijkg->ijfg", chosen, shipped.astype(jnp.float32), precision=highest)
    returned = jnp.einsum("fa,ijfg,gb->ijab", cosines, spectrum, cosines, precision=highest)
    new_moment = moment - returned.transpose(0, 2, 1, 3).reshape(moment.shape)
    worker_burdens = participant_mask.astype(jnp.float32) * token_tallies.astype(jnp.float32)
    worker_fractions = worker_burdens * (
        jnp.sum(participant_mask.astype(jnp.float32)) / jnp.sum(worker_burdens)
    )
    myself = lax.axis_index("replica")
    combined = lax.psum(worker_fractions[myself] * spectrum, "replica")
    update = jnp.einsum("fa,ijfg,gb->ijab", cosines, combined, cosines, precision=highest)
    update = update.transpose(0, 2, 1, 3).reshape(moment.shape)
    return (input_grad, new_moment[None], update)


def solution(mesh):
    n_t, n_r = mesh.shape["tensor"], mesh.shape["replica"]

    def device(*args):
        act, exp, lines = args[0], args[3], args[5]
        fits = (
            act.shape[1] % G == 0
            and act.shape[0] % 128 == 0
            and exp.shape[0] == B
            and lines.shape[3] == 8
            and n_r == 8
        )
        if not fits:
            return per_device_plain(*args)
        return per_device(n_t, n_r, *args)

    return jax.shard_map(
        device,
        mesh=mesh,
        in_specs=(
            P("replica", "tensor"),
            P("replica", "tensor"),
            P("replica", "tensor"),
            P("tensor", None),
            P("replica", "tensor", None),
            P("replica", "tensor", None, None),
            P(),
            P(),
        ),
        out_specs=(P("replica", "tensor"), P("replica", "tensor", None), P("tensor", None)),
        check_vma=False,
    )
```

```python
import functools

import jax
import jax.numpy as jnp
import numpy as np
from jax import lax
from jax.experimental import pallas as pl
from jax.experimental.pallas import tpu as pltpu
from jax.sharding import PartitionSpec as P

momentum_decay = 0.9
B = 64
G = 256
F32 = jnp.float32
BF16 = jnp.bfloat16
VMEM_LIMIT = 24 * 1024 * 1024

VM = pl.BlockSpec(memory_space=pltpu.VMEM)
SM = pl.BlockSpec(memory_space=pltpu.SMEM)
ANY = pl.BlockSpec(memory_space=pl.ANY)


def cosine_table():
    freqs = jnp.arange(64, dtype=jnp.float32)[:, None]
    places = jnp.arange(64, dtype=jnp.float32)[None, :]
    cosines = jnp.cos(jnp.pi * (places + 0.5) * freqs / 64.0) * jnp.sqrt(2.0 / 64.0)
    return cosines.at[0].multiply(jnp.sqrt(0.5))


def cosine_np():
    f = np.arange(B)[:, None]
    a = np.arange(B)[None, :]
    c = np.cos(np.pi * (a + 0.5) * f / B) * np.sqrt(2.0 / B)
    c[0] *= np.sqrt(0.5)
    return c


def halves(c):
    hi = np.asarray(c, dtype=np.float32).astype(jnp.bfloat16)
    lo = (np.asarray(c, np.float64) - hi.astype(np.float64)).astype(np.float32).astype(jnp.bfloat16)
    return hi, lo


def constants():
    hi, lo = halves(cosine_np())
    eye = np.eye(G // B)
    kron = lambda x: np.kron(eye, np.asarray(x, np.float32)).astype(jnp.bfloat16)
    tall = np.zeros((2 * B, G), jnp.bfloat16)
    tall[:B, :B], tall[B:, :B] = hi.T, lo.T
    return jnp.asarray(np.concatenate([kron(hi.T), kron(lo.T), kron(hi), kron(lo), tall], axis=0))


def fwd(tab, i):
    return tab[i * G : (i + 1) * G, :]


def inv(tab, i):
    return tab[(2 + i) * G : (3 + i) * G, :]


def tall(tab):
    return tab[4 * G : 4 * G + 2 * B, :B]


def dot(a, b):
    return jnp.dot(a, b, preferred_element_type=F32)


def split(x):
    hi = x.astype(BF16)
    return hi, (x - hi.astype(F32)).astype(BF16)


def near(shape, dtype=BF16):
    return pltpu.VMEM(shape, dtype)


def far(x):
    return pltpu.with_memory_space_constraint(x, pltpu.HBM)


def call(body, out_shape, ins, in_specs, out_specs, scratch=(), flops=0, nbytes=0, name=None):
    return pl.pallas_call(
        body,
        out_shape=out_shape,
        in_specs=in_specs,
        out_specs=out_specs,
        scratch_shapes=scratch,
        compiler_params=pltpu.CompilerParams(vmem_limit_bytes=VMEM_LIMIT),
        cost_estimate=pl.CostEstimate(flops=flops, bytes_accessed=nbytes, transcendentals=0),
        name=name,
    )(*ins)


def first_body(n_t, cp, cols, nr, switch, slope, exp_ref, act, *refs):
    outs, act_out = refs[:n_t], refs[n_t]
    switch_v, slope_v, exp_v, sems = refs[n_t + 1 :]
    rep, ten = lax.axis_index("replica"), lax.axis_index("tensor")
    r0 = pl.multiple_of((rep // cp) * nr, nr)
    copies = [
        pltpu.make_async_copy(src, dst, sems.at[i])
        for i, (src, dst) in enumerate(
            [(switch, switch_v), (slope, slope_v), (exp_ref.at[pl.ds(r0, nr), :], exp_v), (act, act_out)]
        )
    ]
    for copy in copies:
        copy.start()
    copies[0].wait()
    copies[1].wait()
    v = switch_v[...].astype(F32)
    up = (slope_v[...].astype(F32) * (v * jax.nn.sigmoid(v))).astype(BF16)
    for k in range(n_t):
        outs[k][:B, :] = up
    copies[2].wait()
    nc = cols // cp
    for k in range(n_t):
        c0 = lax.rem(ten + k, n_t) * cols + lax.rem(rep, cp) * nc
        for j in range(nc // 128):
            at = pl.multiple_of(c0 + j * 128, 128)
            outs[k][B + j * nr : B + (j + 1) * nr, :] = exp_v[:, pl.ds(at, 128)]
    copies[3].wait()


def grads_body(n, act, after, *refs):
    ups, outs = refs[:n], refs[n:]
    up = jnp.concatenate([u[:B, :] for u in ups], axis=0)
    for c in range(0, act.shape[1], G):
        g = dot(up, act[:, c : c + G])
        for k in range(n):
            outs[k][:, c : c + G] = g[k * B : (k + 1) * B].astype(outs[k].dtype)


def bundle_body(n_t, keep, after, lines, *refs):
    parts, out = refs[:n_t], refs[n_t]
    n = parts[0].shape[0] - B
    for k in range(n_t):
        out[k * n : (k + 1) * n, :] = parts[k][B:, :]
    blocks = lines.shape[1]
    rows = jnp.concatenate([lines[...].astype(F32), jnp.zeros((keep, 128 - blocks), F32)], axis=1)
    out[n_t * n :, :] = jnp.concatenate([rows, jnp.zeros((16 - keep, 128), F32)], axis=0).astype(BF16)


def join_body(after, after_too, *refs):
    for i, ref in enumerate(refs[:-1]):
        refs[-1][i] = ref[...]


def own_body(n_r, keep, mask, tally, lines, tab, p_ref, a_ref, tab_ref, w_ref, mask_s, tally_s, sems):
    copies = [
        pltpu.make_async_copy(src, dst, sems.at[i])
        for i, (src, dst) in enumerate([(mask, mask_s), (tally, tally_s), (tab, tab_ref)])
    ]
    for copy in copies:
        copy.start()
    blocks = lines.shape[1]
    rows = jnp.concatenate([lines[...].astype(F32), jnp.zeros((keep, 128 - blocks), F32)], axis=1)
    rows = jnp.concatenate([rows] * (2 * B // keep), axis=0).T
    freq = lax.broadcasted_iota(jnp.int32, (B, 2 * B), 0).astype(F32)
    block = (lax.broadcasted_iota(jnp.int32, (1, 2 * B), 1) // keep) % (G // B)
    term = lax.broadcasted_iota(jnp.int32, (B, 2 * B), 1) // (B // 2)
    for copy in copies:
        copy.wait()
    for g in range(blocks // (G // B)):
        num = rows[g * (G // B) : g * (G // B) + 1]
        for j in range(1, G // B):
            num = jnp.where(block == j, rows[g * (G // B) + j : g * (G // B) + j + 1], num)
        hot = jnp.where(freq == num, 1.0, 0.0).astype(BF16)
        y = dot(tall(tab_ref), hot)
        p = jnp.where(term == 3, 0.0, jnp.where(term == 1, y[B:], y[:B]))
        p_ref[:, g * 2 * B : (g + 1) * 2 * B] = p.astype(BF16)
        a_ref[g * B : (g + 1) * B, :] = jnp.concatenate([p, p], axis=0).T[:B].astype(BF16)
    total, alive = jnp.float32(0), jnp.float32(0)
    for r in range(n_r):
        m = mask_s[r].astype(F32)
        total = total + m * tally_s[r].astype(F32)
        alive = alive + m
    place = (lax.broadcasted_iota(jnp.int32, (8, 2 * B), 1) // keep) % n_r
    w = jnp.zeros((8, 2 * B), F32)
    for m in range(n_r):
        r = lax.axis_index("replica") ^ m
        w = jnp.where(place == m, mask_s[r].astype(F32) * tally_s[r].astype(F32), w)
    w_ref[...] = w * (jnp.full((8, 2 * B), alive) / jnp.full((8, 2 * B), total))


def kept_body(n_t, keep, vel, a_ref, tab, after, *refs):
    grads, ship_ref = refs[:n_t], refs[n_t]
    cols = grads[0].shape[1]
    ng = cols // G
    lane_block = lax.broadcasted_iota(jnp.int32, (keep, G), 1) // B
    sel = []
    for k in range(n_t):
        c0 = lax.rem(lax.axis_index("tensor") + k, n_t) * cols
        for i in range(ng):
            at = pl.multiple_of(c0 + i * G, G)
            moment = momentum_decay * vel[:, pl.ds(at, G)] + grads[k][:, i * G : (i + 1) * G].astype(F32)
            hi, lo = split(moment)
            y = dot(a_ref[pl.ds(pl.multiple_of(at // (G // B), B), B), :], jnp.concatenate([hi, lo], axis=0))
            y = y[: B // 2] + y[B // 2 :]
            got = y[:keep]
            for j in range(1, G // B):
                got = jnp.where(lane_block == j, y[j * keep : (j + 1) * keep], got)
            sel.append(got)
    hi, lo = split(jnp.concatenate(sel, axis=0))
    n = n_t * ng * keep
    y = dot(jnp.concatenate([hi, lo], axis=0), fwd(tab, 0))
    y = y[:n] + y[n:] + dot(hi, fwd(tab, 1))
    for k in range(n_t):
        c0 = pl.multiple_of(lax.rem(lax.axis_index("tensor") + k, n_t) * cols, G)
        ship_ref[:, pl.ds(c0, cols)] = jnp.concatenate(
            [y[(k * ng + i) * keep : (k * ng + i + 1) * keep] for i in range(ng)], axis=1
        ).astype(BF16)


def return_body(n_t, keep, vel, p_ref, tab, ship, *refs):
    grads, new_ref = refs[:n_t], refs[n_t]
    cols = grads[0].shape[1]
    ng = cols // G
    lane_block = lax.broadcasted_iota(jnp.int32, (keep, G), 1) // B
    kept = ship[...].astype(F32)
    total = kept.shape[1] // G
    kept = jnp.concatenate([kept[:, g * G : (g + 1) * G] for g in range(total)], axis=0).astype(BF16)
    q = dot(kept, inv(tab, 0)) + dot(kept, inv(tab, 1))
    for g in range(total):
        own = q[g * keep : (g + 1) * keep]
        spread = jnp.concatenate(
            [jnp.where(lane_block == j, own, 0.0) for j in range(G // B)], axis=0
        )
        hi, lo = split(spread)
        w = jnp.concatenate([hi, hi, lo, jnp.zeros_like(lo)], axis=0)
        back = dot(p_ref[:, g * 2 * B : (g + 1) * 2 * B], w)
        cut = slice(g * G, (g + 1) * G)
        new_ref[:, cut] = momentum_decay * vel[:, cut] - back
    for k in range(n_t):
        c0 = lax.rem(lax.axis_index("tensor") + k, n_t) * cols
        for i in range(ng):
            at = pl.multiple_of(c0 + i * G, G)
            new_ref[:, pl.ds(at, G)] += grads[k][:, i * G : (i + 1) * G].astype(F32)


def places_body(keep, w_ref, tab, bundles, hi_ref, lo_ref):
    w = w_ref[:1, :]
    n_r, last = bundles.shape[0], bundles.shape[1] - 16
    rep = lax.axis_index("replica")
    rows = [bundles[rep ^ m, last:, :].astype(F32)[:keep] for m in range(n_r)]
    rows = jnp.concatenate(rows + rows, axis=0).T
    freq = lax.broadcasted_iota(jnp.int32, (B, 2 * B), 0).astype(F32)
    first = lax.broadcasted_iota(jnp.int32, (1, 2 * B), 1) < B
    for c in range(hi_ref.shape[1] // (2 * B)):
        num = jnp.where(first, rows[2 * c : 2 * c + 1], rows[2 * c + 1 : 2 * c + 2])
        hot = jnp.where(freq == num, 1.0, 0.0).astype(BF16)
        y = dot(tall(tab), hot)
        hi, lo = split((y[:B] + y[B:]) * w)
        hi_ref[:, c * 2 * B : (c + 1) * 2 * B] = hi
        lo_ref[:, c * 2 * B : (c + 1) * 2 * B] = lo


def update_body(n_r, keep, p_hi, p_lo, tab, mine, other, out, hi_ref, lo_ref):
    per = n_r * keep
    nb = G // B
    width = nb * per
    half = n_r // 2
    ng = out.shape[1] // G
    lane_block = lax.broadcasted_iota(jnp.int32, (per, G), 1) // B
    for g in range(ng):
        cut = slice(g * G, (g + 1) * G)
        s = jnp.concatenate(
            [ref[i, :, cut].astype(F32) for i in range(half) for ref in (mine, other)], axis=0
        )
        w = jnp.concatenate(
            [jnp.where(lane_block == j, s, 0.0).astype(BF16) for j in range(nb)], axis=0
        )
        wide = slice(g * width, (g + 1) * width)
        y = dot(jnp.concatenate([p_hi[:, wide], p_lo[:, wide]], axis=0), w)
        hi, lo = split(y[:B] + y[B:])
        hi_ref[g * B : (g + 1) * B, :] = hi
        lo_ref[g * B : (g + 1) * B, :] = lo
    z = dot(hi_ref[...], inv(tab, 0)) + dot(lo_ref[...], inv(tab, 0)) + dot(hi_ref[...], inv(tab, 1))
    for g in range(ng):
        out[:, g * G : (g + 1) * G] = z[g * B : (g + 1) * B]


def input_grad_body(n_t, n_r, cp, bundles, *refs):
    ups, out, held = refs[:n_t], refs[n_t], refs[n_t + 1]
    nc = out.shape[1] // cp
    nr = B // (n_r // cp)
    tiles = nc // 128
    for r in range(n_r):
        r0, c0 = (r // cp) * nr, (r % cp) * nc
        for k in range(n_t):
            for j in range(tiles):
                at = (k * tiles + j) * nr
                held[k * B + r0 : k * B + r0 + nr, c0 + j * 128 : c0 + (j + 1) * 128] = bundles[r, at : at + nr, :]
    up = jnp.concatenate([u[:B, :] for u in ups], axis=0).T
    for c in range(0, out.shape[1], G):
        out[:, c : c + G] = dot(up, held[:, c : c + G]).astype(BF16)


def per_device(n_t, n_r, act, switch, slope, exp, vel, lines, mask, tally):
    cols = act.shape[1]
    width = exp.shape[1]
    tok = act.shape[0]
    keep = lines.shape[3]
    blocks = width // B
    groups = width // G
    cp = 2
    rp = n_r // cp
    half = n_r // 2
    tab = constants()
    def shift(x, k):
        return lax.ppermute(x, "tensor", [(i, (i + k) % n_t) for i in range(n_t)])

    order = sorted(range(1, n_t), key=lambda k: -min(k, n_t - k))

    def swap(x, m):
        return lax.ppermute(x, "replica", [(i, i ^ m) for i in range(n_r)])

    own = lines[0, 0].T
    tiles = cols // cp // 128
    nr = B // rp
    *parts, act = call(
        functools.partial(first_body, n_t, cp, cols, nr),
        [near((B + tiles * nr, 128))] * n_t + [near(act.shape)],
        (far(switch.T), far(slope.T), far(exp), far(act)),
        [ANY] * 4,
        [VM] * (n_t + 1),
        scratch=[
            pltpu.VMEM((B, tok), BF16),
            pltpu.VMEM((B, tok), BF16),
            pltpu.VMEM((nr, width), BF16),
            pltpu.SemaphoreType.DMA((4,)),
        ],
        nbytes=act.size * 4 + nr * width * 2,
        name="up_grads",
    )
    parts = [parts[0]] + [shift(parts[k], k) for k in range(1, n_t)]

    p_own, a_own, tab, shares = call(
        functools.partial(own_body, n_r, keep),
        [
            near((B, groups * 2 * B)),
            near((groups * B, 2 * B)),
            near(tab.shape),
            near((8, 2 * B), F32),
        ],
        (far(mask), far(tally), own, far(tab)),
        [ANY, ANY, VM, ANY],
        [VM] * 4,
        scratch=[pltpu.SMEM((n_r,), jnp.int32)] * 2 + [pltpu.SemaphoreType.DMA((3,))],
        name="own_places",
    )

    def grads_of(ks, after):
        return call(
            functools.partial(grads_body, len(ks)),
            [near((B, cols), BF16 if k else F32) for k in ks],
            (act, after, *[parts[k] for k in ks]),
            [VM, ANY] + [VM] * len(ks),
            [VM] * len(ks),
            name="weight_grads",
        )

    grads = {}
    for k in order[:-1]:
        (grads[k],) = grads_of([k], act)
    made, grads[0] = grads_of([order[-1], 0], shares)
    grads[order[-1]] = made
    grads = [grads[0]] + [shift(grads[k], -k) for k in range(1, n_t)]

    bundle = call(
        functools.partial(bundle_body, n_t, keep),
        near((n_t * tiles * nr + 16, 128)),
        (made, own, *parts),
        [ANY] + [VM] * (n_t + 1),
        VM,
        name="bundle",
    )
    bundles = lax.all_gather(bundle, "replica", axis=0)

    p_hi, p_lo = call(
        functools.partial(places_body, keep),
        [near((B, blocks * n_r * keep))] * 2,
        (shares, tab, bundles),
        [VM] * 3,
        [VM, VM],
        name="places",
    )
    input_grad = call(
        functools.partial(input_grad_body, n_t, n_r, cp),
        jax.ShapeDtypeStruct((tok, cols), BF16),
        (bundles, *parts),
        [VM] * (1 + n_t),
        VM,
        scratch=[pltpu.VMEM((n_t * B, cols), BF16)],
        flops=2 * tok * n_t * B * cols,
        nbytes=(n_t * B * cols + tok * cols) * 2,
        name="input_grads",
    )

    ship = call(
        functools.partial(kept_body, n_t, keep),
        near((keep, width)),
        (vel[0], a_own, tab, bundles, *grads),
        [VM] * 3 + [ANY] + [VM] * n_t,
        VM,
        flops=6 * B * B * width,
        nbytes=B * width * 6,
        name="kept_rows",
    )
    ships = [ship] + [swap(ship, 2 * i) for i in range(1, half)]
    new = call(
        functools.partial(return_body, n_t, keep),
        jax.ShapeDtypeStruct((B, width), F32),
        (vel[0], p_own, tab, ship, *grads),
        [VM] * (4 + n_t),
        VM,
        flops=6 * B * B * width,
        nbytes=B * width * 10,
        name="new_momentums",
    )
    mine = call(
        join_body,
        near((half, keep, width)),
        (far(new), p_hi, *ships),
        [ANY, ANY] + [VM] * half,
        VM,
        name="join_kept",
    )
    other = swap(mine, 1)
    update = call(
        functools.partial(update_body, n_r, keep),
        jax.ShapeDtypeStruct((B, width), F32),
        (p_hi, p_lo, tab, mine, other),
        [VM] * 5,
        VM,
        scratch=[pltpu.VMEM((groups * B, G), BF16)] * 2,
        flops=8 * B * G * width,
        nbytes=B * width * 8,
        name="updates",
    )
    return input_grad, new[None], update


def per_device_plain(
    projection_inputs,
    switch_logits_raw,
    inner_neuron_slope,
    expansion_matrix,
    velocity_buffer,
    sent_spectral_lines,
    participant_mask,
    token_tallies,
):
    highest = lax.Precision.HIGHEST
    up_grad = (
        inner_neuron_slope.astype(jnp.float32) * jax.nn.silu(switch_logits_raw.astype(jnp.float32))
    ).astype(jnp.bfloat16)
    partial_terms = jnp.dot(up_grad, expansion_matrix, preferred_element_type=jnp.float32)
    input_grad = lax.psum_scatter(partial_terms, "tensor", scatter_dimension=1, tiled=True).astype(
        jnp.bfloat16
    )
    grad_w = lax.dot_general(
        up_grad,
        lax.all_gather(projection_inputs, "tensor", axis=1, tiled=True),
        (((0,), (0,)), ((), ())),
        preferred_element_type=jnp.float32,
    )
    row_total_count = expansion_matrix.shape[0] // 64
    col_count = expansion_matrix.shape[1] // 64
    moment = momentum_decay * velocity_buffer[0] + grad_w
    cosines = cosine_table()
    blocks = moment.reshape(row_total_count, 64, col_count, 64).transpose(0, 2, 1, 3)
    coefficients = jnp.einsum("fa,ijab,gb->ijfg", cosines, blocks, cosines, precision=highest)
    freq_ids = jnp.arange(64, dtype=jnp.int32)
    own_rows = sent_spectral_lines[0]
    chosen = (own_rows[..., None] == freq_ids).astype(jnp.float32)
    shipped = jnp.einsum("ijkf,ijfg->ijkg", chosen, coefficients, precision=highest).astype(
        jnp.bfloat16
    )
    spectrum = jnp.einsum("ijkf,ijkg->ijfg", chosen, shipped.astype(jnp.float32), precision=highest)
    returned = jnp.einsum("fa,ijfg,gb->ijab", cosines, spectrum, cosines, precision=highest)
    new_moment = moment - returned.transpose(0, 2, 1, 3).reshape(moment.shape)
    worker_burdens = participant_mask.astype(jnp.float32) * token_tallies.astype(jnp.float32)
    worker_fractions = worker_burdens * (
        jnp.sum(participant_mask.astype(jnp.float32)) / jnp.sum(worker_burdens)
    )
    myself = lax.axis_index("replica")
    combined = lax.psum(worker_fractions[myself] * spectrum, "replica")
    update = jnp.einsum("fa,ijfg,gb->ijab", cosines, combined, cosines, precision=highest)
    update = update.transpose(0, 2, 1, 3).reshape(moment.shape)
    return (input_grad, new_moment[None], update)


def solution(mesh):
    n_t, n_r = mesh.shape["tensor"], mesh.shape["replica"]

    def device(*args):
        act, exp, lines = args[0], args[3], args[5]
        fits = (
            act.shape[1] % G == 0
            and act.shape[0] % 128 == 0
            and exp.shape[0] == B
            and lines.shape[3] == 8
            and n_r == 8
        )
        if not fits:
            return per_device_plain(*args)
        return per_device(n_t, n_r, *args)

    return jax.shard_map(
        device,
        mesh=mesh,
        in_specs=(
            P("replica", "tensor"),
            P("replica", "tensor"),
            P("replica", "tensor"),
            P("tensor", None),
            P("replica", "tensor", None),
            P("replica", "tensor", None, None),
            P(),
            P(),
        ),
        out_specs=(P("replica", "tensor"), P("replica", "tensor", None), P("tensor", None)),
        check_vma=False,
    )
```

```python
import functools

import jax
import jax.numpy as jnp
import numpy as np
from jax import lax
from jax.experimental import pallas as pl
from jax.experimental.pallas import tpu as pltpu
from jax.sharding import PartitionSpec as P

momentum_decay = 0.9
B = 64
G = 256
F32 = jnp.float32
BF16 = jnp.bfloat16
VMEM_LIMIT = 24 * 1024 * 1024

VM = pl.BlockSpec(memory_space=pltpu.VMEM)
SM = pl.BlockSpec(memory_space=pltpu.SMEM)
ANY = pl.BlockSpec(memory_space=pl.ANY)


def cosine_table():
    freqs = jnp.arange(64, dtype=jnp.float32)[:, None]
    places = jnp.arange(64, dtype=jnp.float32)[None, :]
    cosines = jnp.cos(jnp.pi * (places + 0.5) * freqs / 64.0) * jnp.sqrt(2.0 / 64.0)
    return cosines.at[0].multiply(jnp.sqrt(0.5))


def cosine_np():
    f = np.arange(B)[:, None]
    a = np.arange(B)[None, :]
    c = np.cos(np.pi * (a + 0.5) * f / B) * np.sqrt(2.0 / B)
    c[0] *= np.sqrt(0.5)
    return c


def halves(c):
    hi = np.asarray(c, dtype=np.float32).astype(jnp.bfloat16)
    lo = (np.asarray(c, np.float64) - hi.astype(np.float64)).astype(np.float32).astype(jnp.bfloat16)
    return hi, lo


def constants():
    hi, lo = halves(cosine_np())
    eye = np.eye(G // B)
    kron = lambda x: np.kron(eye, np.asarray(x, np.float32)).astype(jnp.bfloat16)
    tall = np.zeros((2 * B, G), jnp.bfloat16)
    tall[:B, :B], tall[B:, :B] = hi.T, lo.T
    return jnp.asarray(np.concatenate([kron(hi.T), kron(lo.T), kron(hi), kron(lo), tall], axis=0))


def fwd(tab, i):
    return tab[i * G : (i + 1) * G, :]


def inv(tab, i):
    return tab[(2 + i) * G : (3 + i) * G, :]


def tall(tab):
    return tab[4 * G : 4 * G + 2 * B, :B]


def dot(a, b):
    return jnp.dot(a, b, preferred_element_type=F32)


def split(x):
    hi = x.astype(BF16)
    return hi, (x - hi.astype(F32)).astype(BF16)


def near(shape, dtype=BF16):
    return pltpu.VMEM(shape, dtype)


def far(x):
    return pltpu.with_memory_space_constraint(x, pltpu.HBM)


def call(body, out_shape, ins, in_specs, out_specs, scratch=(), flops=0, nbytes=0, name=None):
    return pl.pallas_call(
        body,
        out_shape=out_shape,
        in_specs=in_specs,
        out_specs=out_specs,
        scratch_shapes=scratch,
        compiler_params=pltpu.CompilerParams(vmem_limit_bytes=VMEM_LIMIT),
        cost_estimate=pl.CostEstimate(flops=flops, bytes_accessed=nbytes, transcendentals=0),
        name=name,
    )(*ins)


def first_body(n_t, cp, cols, nr, switch, slope, exp_ref, act, lines, tab, *refs):
    outs, (act_out, lines_out, tab_out) = refs[:n_t], refs[n_t : n_t + 3]
    switch_v, slope_v, exp_v, sems = refs[n_t + 3 :]
    rep, ten = lax.axis_index("replica"), lax.axis_index("tensor")
    r0 = pl.multiple_of((rep // cp) * nr, nr)
    copies = [
        pltpu.make_async_copy(src, dst, sems.at[i])
        for i, (src, dst) in enumerate(
            [
                (switch, switch_v),
                (slope, slope_v),
                (exp_ref.at[pl.ds(r0, nr), :], exp_v),
                (act, act_out),
                (lines, lines_out),
                (tab, tab_out),
            ]
        )
    ]
    for copy in copies:
        copy.start()
    copies[0].wait()
    copies[1].wait()
    v = switch_v[...].astype(F32)
    up = (slope_v[...].astype(F32) * (v * jax.nn.sigmoid(v))).astype(BF16)
    for k in range(n_t):
        outs[k][:B, :] = up
    copies[2].wait()
    nc = cols // cp
    for k in range(n_t):
        c0 = lax.rem(ten + k, n_t) * cols + lax.rem(rep, cp) * nc
        for j in range(nc // 128):
            at = pl.multiple_of(c0 + j * 128, 128)
            outs[k][B + j * nr : B + (j + 1) * nr, :] = exp_v[:, pl.ds(at, 128)]
    for copy in copies[3:]:
        copy.wait()


def grads_body(n, act, after, *refs):
    ups, outs = refs[:n], refs[n:]
    up = jnp.concatenate([u[:B, :] for u in ups], axis=0)
    for c in range(0, act.shape[1], G):
        g = dot(up, act[:, c : c + G])
        for k in range(n):
            outs[k][:, c : c + G] = g[k * B : (k + 1) * B].astype(outs[k].dtype)


def bundle_body(n_t, keep, after, lines, *refs):
    parts, out = refs[:n_t], refs[n_t]
    n = parts[0].shape[0] - B
    for k in range(n_t):
        out[k * n : (k + 1) * n, :] = parts[k][B:, :]
    blocks = lines.shape[1]
    rows = jnp.concatenate([lines[...].astype(F32), jnp.zeros((keep, 128 - blocks), F32)], axis=1)
    out[n_t * n :, :] = jnp.concatenate([rows, jnp.zeros((16 - keep, 128), F32)], axis=0).astype(BF16)


def join_body(after, *refs):
    for i, ref in enumerate(refs[:-1]):
        refs[-1][i] = ref[...]


def own_body(n_r, keep, mask, tally, lines, tab, p_ref, a_ref, w_ref, mask_s, tally_s, sems):
    copies = [
        pltpu.make_async_copy(src, dst, sems.at[i])
        for i, (src, dst) in enumerate([(mask, mask_s), (tally, tally_s)])
    ]
    for copy in copies:
        copy.start()
    blocks = lines.shape[1]
    rows = jnp.concatenate([lines[...].astype(F32), jnp.zeros((keep, 128 - blocks), F32)], axis=1)
    rows = jnp.concatenate([rows] * (2 * B // keep), axis=0).T
    freq = lax.broadcasted_iota(jnp.int32, (B, 2 * B), 0).astype(F32)
    block = (lax.broadcasted_iota(jnp.int32, (1, 2 * B), 1) // keep) % (G // B)
    term = lax.broadcasted_iota(jnp.int32, (B, 2 * B), 1) // (B // 2)
    for g in range(blocks // (G // B)):
        num = rows[g * (G // B) : g * (G // B) + 1]
        for j in range(1, G // B):
            num = jnp.where(block == j, rows[g * (G // B) + j : g * (G // B) + j + 1], num)
        hot = jnp.where(freq == num, 1.0, 0.0).astype(BF16)
        y = dot(tall(tab), hot)
        p = jnp.where(term == 3, 0.0, jnp.where(term == 1, y[B:], y[:B]))
        p_ref[:, g * 2 * B : (g + 1) * 2 * B] = p.astype(BF16)
        a_ref[g * B : (g + 1) * B, :] = jnp.concatenate([p, p], axis=0).T[:B].astype(BF16)
    for copy in copies:
        copy.wait()
    total, alive = jnp.float32(0), jnp.float32(0)
    for r in range(n_r):
        m = mask_s[r].astype(F32)
        total = total + m * tally_s[r].astype(F32)
        alive = alive + m
    half = n_r // 2
    place = (lax.broadcasted_iota(jnp.int32, (8, 2 * B), 1) // keep) % half
    scale = jnp.full((8, 2 * B), alive) / jnp.full((8, 2 * B), total)
    for h in range(2):
        w = jnp.zeros((8, 2 * B), F32)
        for i in range(half):
            r = lax.axis_index("replica") ^ (2 * i + h)
            w = jnp.where(place == i, mask_s[r].astype(F32) * tally_s[r].astype(F32), w)
        w_ref[h] = w * scale


def kept_body(n_t, keep, vel, a_ref, tab, after, after_too, *refs):
    grads, ship_ref = refs[:n_t], refs[n_t]
    cols = grads[0].shape[1]
    ng = cols // G
    lane_block = lax.broadcasted_iota(jnp.int32, (keep, G), 1) // B
    sel = []
    for k in range(n_t):
        c0 = lax.rem(lax.axis_index("tensor") + k, n_t) * cols
        for i in range(ng):
            at = pl.multiple_of(c0 + i * G, G)
            moment = momentum_decay * vel[:, pl.ds(at, G)] + grads[k][:, i * G : (i + 1) * G].astype(F32)
            hi, lo = split(moment)
            y = dot(a_ref[pl.ds(pl.multiple_of(at // (G // B), B), B), :], jnp.concatenate([hi, lo], axis=0))
            y = y[: B // 2] + y[B // 2 :]
            got = y[:keep]
            for j in range(1, G // B):
                got = jnp.where(lane_block == j, y[j * keep : (j + 1) * keep], got)
            sel.append(got)
    hi, lo = split(jnp.concatenate(sel, axis=0))
    n = n_t * ng * keep
    y = dot(jnp.concatenate([hi, lo], axis=0), fwd(tab, 0))
    y = y[:n] + y[n:] + dot(hi, fwd(tab, 1))
    for k in range(n_t):
        c0 = pl.multiple_of(lax.rem(lax.axis_index("tensor") + k, n_t) * cols, G)
        ship_ref[:, pl.ds(c0, cols)] = jnp.concatenate(
            [y[(k * ng + i) * keep : (k * ng + i + 1) * keep] for i in range(ng)], axis=1
        ).astype(BF16)


def return_body(n_t, keep, vel, p_ref, tab, ship, *refs):
    grads, (new_ref, held, sems) = refs[:n_t], refs[n_t:]
    cols = grads[0].shape[1]
    ng = cols // G
    lane_block = lax.broadcasted_iota(jnp.int32, (keep, G), 1) // B
    q = []
    for k in range(n_t):
        c0 = pl.multiple_of(lax.rem(lax.axis_index("tensor") + k, n_t) * cols, G)
        kept = ship[:, pl.ds(c0, cols)].astype(F32)
        q += [kept[:, i * G : (i + 1) * G] for i in range(ng)]
    q = jnp.concatenate(q, axis=0).astype(BF16)
    q = dot(q, inv(tab, 0)) + dot(q, inv(tab, 1))
    copies = []
    for k in range(n_t):
        c0 = pl.multiple_of(lax.rem(lax.axis_index("tensor") + k, n_t) * cols, G)
        for i in range(ng):
            at = pl.multiple_of(c0 + i * G, G)
            own = q[(k * ng + i) * keep : (k * ng + i + 1) * keep]
            spread = jnp.concatenate(
                [jnp.where(lane_block == j, own, 0.0) for j in range(G // B)], axis=0
            )
            hi, lo = split(spread)
            w = jnp.concatenate([hi, hi, lo, jnp.zeros_like(lo)], axis=0)
            back = dot(p_ref[:, pl.ds(pl.multiple_of(at // 2, 2 * B), 2 * B)], w)
            moment = momentum_decay * vel[:, pl.ds(at, G)] + grads[k][:, i * G : (i + 1) * G].astype(F32)
            held[:, pl.ds(at, G)] = moment - back
        cut = pl.ds(c0, cols)
        copies.append(pltpu.make_async_copy(held.at[:, cut], new_ref.at[:, cut], sems.at[k]))
        copies[-1].start()
    for copy in copies:
        copy.wait()


def places_body(keep, w_ref, tab, bundles, *p_refs):
    n_r, last = bundles.shape[0], bundles.shape[1] - 16
    half, nb = n_r // 2, G // B
    rep = lax.axis_index("replica")
    freq = lax.broadcasted_iota(jnp.int32, (B, 2 * B), 0).astype(F32)
    block = lax.broadcasted_iota(jnp.int32, (1, 2 * B), 1) // (half * keep)
    for h in range(2):
        hi_ref, lo_ref = p_refs[2 * h : 2 * h + 2]
        w = w_ref[h, :1, :]
        rows = [bundles[rep ^ (2 * i + h), last:, :].astype(F32)[:keep] for i in range(half)]
        rows = jnp.concatenate(rows * nb, axis=0).T
        for g in range(hi_ref.shape[1] // (2 * B)):
            num = rows[g * nb : g * nb + 1]
            for j in range(1, nb):
                num = jnp.where(block == j, rows[g * nb + j : g * nb + j + 1], num)
            hot = jnp.where(freq == num, 1.0, 0.0).astype(BF16)
            y = dot(tall(tab), hot)
            hi, lo = split((y[:B] + y[B:]) * w)
            hi_ref[:, g * 2 * B : (g + 1) * 2 * B] = hi
            lo_ref[:, g * 2 * B : (g + 1) * 2 * B] = lo


def spread_rows(p_hi, p_lo, ships, g):
    half, keep = ships.shape[0], ships.shape[1]
    lane_block = lax.broadcasted_iota(jnp.int32, (half * keep, G), 1) // B
    s = jnp.concatenate([ships[i, :, g * G : (g + 1) * G].astype(F32) for i in range(half)], axis=0)
    w = jnp.concatenate(
        [jnp.where(lane_block == j, s, 0.0).astype(BF16) for j in range(G // B)], axis=0
    )
    cut = slice(g * 2 * B, (g + 1) * 2 * B)
    y = dot(jnp.concatenate([p_hi[:, cut], p_lo[:, cut]], axis=0), w)
    return y[:B] + y[B:]


def half_update_body(p_hi, p_lo, mine, out):
    for g in range(out.shape[0] // B):
        out[g * B : (g + 1) * B, :] = spread_rows(p_hi, p_lo, mine, g)


def update_body(chunk, half_sum, p_hi, p_lo, tab, other, out, hi_ref, lo_ref, held, sems):
    ng = half_sum.shape[0] // B
    copies = []
    for c in range(0, ng, chunk):
        for g in range(c, c + chunk):
            at = slice(g * B, (g + 1) * B)
            hi_ref[at, :], lo_ref[at, :] = split(half_sum[at, :] + spread_rows(p_hi, p_lo, other, g))
        rows = slice(c * B, (c + chunk) * B)
        z = dot(hi_ref[rows, :], inv(tab, 0)) + dot(lo_ref[rows, :], inv(tab, 0)) + dot(hi_ref[rows, :], inv(tab, 1))
        for g in range(chunk):
            held[:, (c + g) * G : (c + g + 1) * G] = z[g * B : (g + 1) * B]
        cut = pl.ds(c * G, chunk * G)
        copies.append(pltpu.make_async_copy(held.at[:, cut], out.at[:, cut], sems.at[c // chunk]))
        copies[-1].start()
    for copy in copies:
        copy.wait()


def input_grad_body(n_t, n_r, cp, bundles, *refs):
    ups, out, held = refs[:n_t], refs[n_t], refs[n_t + 1]
    nc = out.shape[1] // cp
    nr = B // (n_r // cp)
    tiles = nc // 128
    for r in range(n_r):
        r0, c0 = (r // cp) * nr, (r % cp) * nc
        for k in range(n_t):
            for j in range(tiles):
                at = (k * tiles + j) * nr
                held[k * B + r0 : k * B + r0 + nr, c0 + j * 128 : c0 + (j + 1) * 128] = bundles[r, at : at + nr, :]
    up = jnp.concatenate([u[:B, :] for u in ups], axis=0).T
    for c in range(0, out.shape[1], G):
        out[:, c : c + G] = dot(up, held[:, c : c + G]).astype(BF16)


def per_device(n_t, n_r, act, switch, slope, exp, vel, lines, mask, tally):
    cols = act.shape[1]
    width = exp.shape[1]
    tok = act.shape[0]
    keep = lines.shape[3]
    blocks = width // B
    groups = width // G
    cp = 2
    rp = n_r // cp
    half = n_r // 2
    tab = constants()
    def shift(x, k):
        return lax.ppermute(x, "tensor", [(i, (i + k) % n_t) for i in range(n_t)])

    order = sorted(range(1, n_t), key=lambda k: -min(k, n_t - k))

    def swap(x, m):
        return lax.ppermute(x, "replica", [(i, i ^ m) for i in range(n_r)])

    own = lines[0, 0].T
    tiles = cols // cp // 128
    nr = B // rp
    *parts, act, own, tab = call(
        functools.partial(first_body, n_t, cp, cols, nr),
        [near((B + tiles * nr, 128))] * n_t
        + [near(act.shape), near(own.shape, jnp.int32), near(tab.shape)],
        (far(switch.T), far(slope.T), far(exp), far(act), far(own), far(tab)),
        [ANY] * 6,
        [VM] * (n_t + 3),
        scratch=[
            pltpu.VMEM((B, tok), BF16),
            pltpu.VMEM((B, tok), BF16),
            pltpu.VMEM((nr, width), BF16),
            pltpu.SemaphoreType.DMA((6,)),
        ],
        nbytes=act.size * 4 + nr * width * 2,
        name="up_grads",
    )
    parts = [parts[0]] + [shift(parts[k], k) for k in range(1, n_t)]

    p_own, a_own, shares = call(
        functools.partial(own_body, n_r, keep),
        [
            near((B, groups * 2 * B)),
            near((groups * B, 2 * B)),
            near((2, 8, 2 * B), F32),
        ],
        (far(mask), far(tally), own, tab),
        [ANY, ANY, VM, VM],
        [VM] * 3,
        scratch=[pltpu.SMEM((n_r,), jnp.int32)] * 2 + [pltpu.SemaphoreType.DMA((2,))],
        name="own_places",
    )

    def grads_of(ks, after):
        return call(
            functools.partial(grads_body, len(ks)),
            [near((B, cols), BF16 if k else F32) for k in ks],
            (act, after, *[parts[k] for k in ks]),
            [VM, ANY] + [VM] * len(ks),
            [VM] * len(ks),
            name="weight_grads",
        )

    grads = {}
    for k in order[:-1]:
        (grads[k],) = grads_of([k], act)
    made, grads[0] = grads_of([order[-1], 0], shares)
    grads[order[-1]] = made
    grads = [grads[0]] + [shift(grads[k], -k) for k in range(1, n_t)]

    bundle = call(
        functools.partial(bundle_body, n_t, keep),
        near((n_t * tiles * nr + 16, 128)),
        (made, own, *parts),
        [ANY] + [VM] * (n_t + 1),
        VM,
        name="bundle",
    )
    bundles = lax.all_gather(bundle, "replica", axis=0)

    places = call(
        functools.partial(places_body, keep),
        [near((B, blocks * half * keep))] * 4,
        (shares, tab, bundles),
        [VM] * 3,
        [VM] * 4,
        name="places",
    )
    input_grad = call(
        functools.partial(input_grad_body, n_t, n_r, cp),
        jax.ShapeDtypeStruct((tok, cols), BF16),
        (bundles, *parts),
        [VM] * (1 + n_t),
        VM,
        scratch=[pltpu.VMEM((n_t * B, cols), BF16)],
        flops=2 * tok * n_t * B * cols,
        nbytes=(n_t * B * cols + tok * cols) * 2,
        name="input_grads",
    )

    ship = call(
        functools.partial(kept_body, n_t, keep),
        near((keep, width)),
        (vel[0], a_own, tab, places[0], far(input_grad), *grads),
        [VM] * 3 + [ANY, ANY] + [VM] * n_t,
        VM,
        flops=6 * B * B * width,
        nbytes=B * width * 6,
        name="kept_rows",
    )
    ships = [ship] + [swap(ship, 2 * i) for i in range(1, half)]
    new = call(
        functools.partial(return_body, n_t, keep),
        jax.ShapeDtypeStruct((B, width), F32),
        (vel[0], p_own, tab, ship, *grads),
        [VM] * (4 + n_t),
        ANY,
        scratch=[pltpu.VMEM((B, width), F32), pltpu.SemaphoreType.DMA((n_t,))],
        flops=6 * B * B * width,
        nbytes=B * width * 10,
        name="new_momentums",
    )
    mine = call(
        join_body,
        near((half, keep, width)),
        (far(new), *ships),
        [ANY] + [VM] * half,
        VM,
        name="join_kept",
    )
    other = swap(mine, 1)
    half_sum = call(
        half_update_body,
        near((groups * B, G), F32),
        (*places[:2], mine),
        [VM] * 3,
        VM,
        name="half_updates",
    )
    chunk = next(c for c in (5, 4, 3, 2, 1) if groups % c == 0)
    update = call(
        functools.partial(update_body, chunk),
        jax.ShapeDtypeStruct((B, width), F32),
        (half_sum, *places[2:], tab, other),
        [VM] * 5,
        ANY,
        scratch=[
            pltpu.VMEM((groups * B, G), BF16),
            pltpu.VMEM((groups * B, G), BF16),
            pltpu.VMEM((B, width), F32),
            pltpu.SemaphoreType.DMA((groups // chunk,)),
        ],
        flops=8 * B * G * width,
        nbytes=B * width * 8,
        name="updates",
    )
    return input_grad, new[None], update


def per_device_plain(
    projection_inputs,
    switch_logits_raw,
    inner_neuron_slope,
    expansion_matrix,
    velocity_buffer,
    sent_spectral_lines,
    participant_mask,
    token_tallies,
):
    highest = lax.Precision.HIGHEST
    up_grad = (
        inner_neuron_slope.astype(jnp.float32) * jax.nn.silu(switch_logits_raw.astype(jnp.float32))
    ).astype(jnp.bfloat16)
    partial_terms = jnp.dot(up_grad, expansion_matrix, preferred_element_type=jnp.float32)
    input_grad = lax.psum_scatter(partial_terms, "tensor", scatter_dimension=1, tiled=True).astype(
        jnp.bfloat16
    )
    grad_w = lax.dot_general(
        up_grad,
        lax.all_gather(projection_inputs, "tensor", axis=1, tiled=True),
        (((0,), (0,)), ((), ())),
        preferred_element_type=jnp.float32,
    )
    row_total_count = expansion_matrix.shape[0] // 64
    col_count = expansion_matrix.shape[1] // 64
    moment = momentum_decay * velocity_buffer[0] + grad_w
    cosines = cosine_table()
    blocks = moment.reshape(row_total_count, 64, col_count, 64).transpose(0, 2, 1, 3)
    coefficients = jnp.einsum("fa,ijab,gb->ijfg", cosines, blocks, cosines, precision=highest)
    freq_ids = jnp.arange(64, dtype=jnp.int32)
    own_rows = sent_spectral_lines[0]
    chosen = (own_rows[..., None] == freq_ids).astype(jnp.float32)
    shipped = jnp.einsum("ijkf,ijfg->ijkg", chosen, coefficients, precision=highest).astype(
        jnp.bfloat16
    )
    spectrum = jnp.einsum("ijkf,ijkg->ijfg", chosen, shipped.astype(jnp.float32), precision=highest)
    returned = jnp.einsum("fa,ijfg,gb->ijab", cosines, spectrum, cosines, precision=highest)
    new_moment = moment - returned.transpose(0, 2, 1, 3).reshape(moment.shape)
    worker_burdens = participant_mask.astype(jnp.float32) * token_tallies.astype(jnp.float32)
    worker_fractions = worker_burdens * (
        jnp.sum(participant_mask.astype(jnp.float32)) / jnp.sum(worker_burdens)
    )
    myself = lax.axis_index("replica")
    combined = lax.psum(worker_fractions[myself] * spectrum, "replica")
    update = jnp.einsum("fa,ijfg,gb->ijab", cosines, combined, cosines, precision=highest)
    update = update.transpose(0, 2, 1, 3).reshape(moment.shape)
    return (input_grad, new_moment[None], update)


def solution(mesh):
    n_t, n_r = mesh.shape["tensor"], mesh.shape["replica"]

    def device(*args):
        act, exp, lines = args[0], args[3], args[5]
        fits = (
            act.shape[1] % G == 0
            and act.shape[0] % 128 == 0
            and exp.shape[0] == B
            and lines.shape[3] == 8
            and n_r == 8
        )
        if not fits:
            return per_device_plain(*args)
        return per_device(n_t, n_r, *args)

    return jax.shard_map(
        device,
        mesh=mesh,
        in_specs=(
            P("replica", "tensor"),
            P("replica", "tensor"),
            P("replica", "tensor"),
            P("tensor", None),
            P("replica", "tensor", None),
            P("replica", "tensor", None, None),
            P(),
            P(),
        ),
        out_specs=(P("replica", "tensor"), P("replica", "tensor", None), P("tensor", None)),
        check_vma=False,
    )
```

```python
import functools

import jax
import jax.numpy as jnp
import numpy as np
from jax import lax
from jax.experimental import pallas as pl
from jax.experimental.pallas import tpu as pltpu
from jax.sharding import PartitionSpec as P

momentum_decay = 0.9
B = 64
G = 256
F32 = jnp.float32
BF16 = jnp.bfloat16
VMEM_LIMIT = 24 * 1024 * 1024

VM = pl.BlockSpec(memory_space=pltpu.VMEM)
SM = pl.BlockSpec(memory_space=pltpu.SMEM)
ANY = pl.BlockSpec(memory_space=pl.ANY)


def cosine_table():
    freqs = jnp.arange(64, dtype=jnp.float32)[:, None]
    places = jnp.arange(64, dtype=jnp.float32)[None, :]
    cosines = jnp.cos(jnp.pi * (places + 0.5) * freqs / 64.0) * jnp.sqrt(2.0 / 64.0)
    return cosines.at[0].multiply(jnp.sqrt(0.5))


def cosine_np():
    f = np.arange(B)[:, None]
    a = np.arange(B)[None, :]
    c = np.cos(np.pi * (a + 0.5) * f / B) * np.sqrt(2.0 / B)
    c[0] *= np.sqrt(0.5)
    return c


def halves(c):
    hi = np.asarray(c, dtype=np.float32).astype(jnp.bfloat16)
    lo = (np.asarray(c, np.float64) - hi.astype(np.float64)).astype(np.float32).astype(jnp.bfloat16)
    return hi, lo


def constants():
    hi, lo = halves(cosine_np())
    eye = np.eye(G // B)
    kron = lambda x: np.kron(eye, np.asarray(x, np.float32)).astype(jnp.bfloat16)
    tall = np.zeros((2 * B, 2 * B), jnp.bfloat16)
    tall[:B, :B], tall[B:, :B] = hi.T, lo.T
    return jnp.asarray(np.concatenate([kron(x) for x in (hi.T, lo.T, hi, lo)], axis=0)), jnp.asarray(tall)


def fwd(tab, i):
    return tab[i * G : (i + 1) * G, :]


def inv(tab, i):
    return tab[(2 + i) * G : (3 + i) * G, :]


def dot(a, b):
    return jnp.dot(a, b, preferred_element_type=F32)


def split(x):
    hi = x.astype(BF16)
    return hi, (x - hi.astype(F32)).astype(BF16)


def near(shape, dtype=BF16):
    return pltpu.VMEM(shape, dtype)


def far(x):
    return pltpu.with_memory_space_constraint(x, pltpu.HBM)


def call(body, out_shape, ins, in_specs, out_specs, scratch=(), flops=0, nbytes=0, name=None):
    return pl.pallas_call(
        body,
        out_shape=out_shape,
        in_specs=in_specs,
        out_specs=out_specs,
        scratch_shapes=scratch,
        compiler_params=pltpu.CompilerParams(vmem_limit_bytes=VMEM_LIMIT),
        cost_estimate=pl.CostEstimate(flops=flops, bytes_accessed=nbytes, transcendentals=0),
        name=name,
    )(*ins)


def first_body(n_t, cp, cols, nr, switch, slope, exp_ref, act, lines, tall, *refs):
    outs, (act_out, lines_out, tall_out) = refs[:n_t], refs[n_t : n_t + 3]
    switch_v, slope_v, exp_v, sems = refs[n_t + 3 :]
    rep, ten = lax.axis_index("replica"), lax.axis_index("tensor")
    r0 = pl.multiple_of((rep // cp) * nr, nr)
    copies = [
        pltpu.make_async_copy(src, dst, sems.at[i])
        for i, (src, dst) in enumerate(
            [
                (switch, switch_v),
                (slope, slope_v),
                (exp_ref.at[pl.ds(r0, nr), :], exp_v),
                (act, act_out),
                (lines, lines_out),
                (tall, tall_out),
            ]
        )
    ]
    for copy in copies:
        copy.start()
    copies[0].wait()
    copies[1].wait()
    v = switch_v[...].astype(F32)
    up = (slope_v[...].astype(F32) * (v * jax.nn.sigmoid(v))).astype(BF16)
    for k in range(n_t):
        outs[k][:B, :] = up
    copies[2].wait()
    nc = cols // cp
    for k in range(n_t):
        c0 = lax.rem(ten + k, n_t) * cols + lax.rem(rep, cp) * nc
        for j in range(nc // 128):
            at = pl.multiple_of(c0 + j * 128, 128)
            outs[k][B + j * nr : B + (j + 1) * nr, :] = exp_v[:, pl.ds(at, 128)]
    for copy in copies[3:]:
        copy.wait()


def grads_body(n, act, *refs):
    ups, outs = refs[:n], refs[n:]
    up = jnp.concatenate([u[:B, :] for u in ups], axis=0)
    for c in range(0, act.shape[1], G):
        g = dot(up, act[:, c : c + G])
        for k in range(n):
            outs[k][:, c : c + G] = g[k * B : (k + 1) * B].astype(outs[k].dtype)


def bundle_body(n_t, keep, after, lines, *refs):
    parts, out = refs[:n_t], refs[n_t]
    n = parts[0].shape[0] - B
    for k in range(n_t):
        out[k * n : (k + 1) * n, :] = parts[k][B:, :]
    blocks = lines.shape[1]
    rows = jnp.concatenate([lines[...].astype(F32), jnp.zeros((keep, 128 - blocks), F32)], axis=1)
    out[n_t * n :, :] = jnp.concatenate([rows, jnp.zeros((16 - keep, 128), F32)], axis=0).astype(BF16)


def join_body(n, *refs):
    for i, ref in enumerate(refs[:n]):
        refs[-1][i] = ref[...]


def own_body(n_r, keep, mask, tally, tab, lines, tall, p_ref, a_ref, w_ref, tab_ref, mask_s, tally_s, sems):
    copies = [
        pltpu.make_async_copy(src, dst, sems.at[i])
        for i, (src, dst) in enumerate([(mask, mask_s), (tally, tally_s), (tab, tab_ref)])
    ]
    for copy in copies:
        copy.start()
    blocks = lines.shape[1]
    rows = jnp.concatenate([lines[...].astype(F32), jnp.zeros((keep, 128 - blocks), F32)], axis=1)
    rows = jnp.concatenate([rows] * (2 * B // keep), axis=0).T
    freq = lax.broadcasted_iota(jnp.int32, (B, 2 * B), 0).astype(F32)
    block = (lax.broadcasted_iota(jnp.int32, (1, 2 * B), 1) // keep) % (G // B)
    term = lax.broadcasted_iota(jnp.int32, (B, 2 * B), 1) // (B // 2)
    for g in range(blocks // (G // B)):
        num = rows[g * (G // B) : g * (G // B) + 1]
        for j in range(1, G // B):
            num = jnp.where(block == j, rows[g * (G // B) + j : g * (G // B) + j + 1], num)
        hot = jnp.where(freq == num, 1.0, 0.0).astype(BF16)
        y = dot(tall[:, :B], hot)
        p = jnp.where(term == 3, 0.0, jnp.where(term == 1, y[B:], y[:B]))
        p_ref[:, g * 2 * B : (g + 1) * 2 * B] = p.astype(BF16)
        a_ref[g * B : (g + 1) * B, :] = jnp.concatenate([p, p], axis=0).T[:B].astype(BF16)
    for copy in copies:
        copy.wait()
    total, alive = jnp.float32(0), jnp.float32(0)
    for r in range(n_r):
        m = mask_s[r].astype(F32)
        total = total + m * tally_s[r].astype(F32)
        alive = alive + m
    half = n_r // 2
    place = (lax.broadcasted_iota(jnp.int32, (8, 2 * B), 1) // keep) % half
    scale = jnp.full((8, 2 * B), alive) / jnp.full((8, 2 * B), total)
    for h in range(2):
        w = jnp.zeros((8, 2 * B), F32)
        for i in range(half):
            r = lax.axis_index("replica") ^ (2 * i + h)
            w = jnp.where(place == i, mask_s[r].astype(F32) * tally_s[r].astype(F32), w)
        w_ref[h] = w * scale


def kept_body(n_t, keep, vel, a_ref, tab, after, *refs):
    grads, (send_ref, own_ref) = refs[:n_t], refs[n_t:]
    cols = grads[0].shape[1]
    ng = cols // G
    lane_block = lax.broadcasted_iota(jnp.int32, (keep, G), 1) // B
    sel = []
    for k in range(n_t):
        c0 = lax.rem(lax.axis_index("tensor") + k, n_t) * cols
        for i in range(ng):
            at = pl.multiple_of(c0 + i * G, G)
            moment = momentum_decay * vel[:, pl.ds(at, G)] + grads[k][:, i * G : (i + 1) * G].astype(F32)
            hi, lo = split(moment)
            y = dot(a_ref[pl.ds(pl.multiple_of(at // (G // B), B), B), :], jnp.concatenate([hi, lo], axis=0))
            y = y[: B // 2] + y[B // 2 :]
            got = y[:keep]
            for j in range(1, G // B):
                got = jnp.where(lane_block == j, y[j * keep : (j + 1) * keep], got)
            sel.append(got)
    hi, lo = split(jnp.concatenate(sel, axis=0))
    n = n_t * ng * keep
    y = dot(jnp.concatenate([hi, lo], axis=0), fwd(tab, 0))
    kept = (y[:n] + y[n:] + dot(hi, fwd(tab, 1))).astype(BF16)
    q = dot(kept, inv(tab, 0)) + dot(kept, inv(tab, 1))
    for k in range(n_t):
        c0 = pl.multiple_of(lax.rem(lax.axis_index("tensor") + k, n_t) * cols, G)
        part = jnp.concatenate([q[(k * ng + i) * keep : (k * ng + i + 1) * keep] for i in range(ng)], axis=1)
        own_ref[:, pl.ds(c0, cols)] = part
        send_ref[:, pl.ds(c0, cols)] = part.astype(BF16)


def return_body(n_t, keep, vel, p_ref, q, *refs):
    grads, (new_ref, held, sems) = refs[:n_t], refs[n_t:]
    cols = grads[0].shape[1]
    ng = cols // G
    lane_block = lax.broadcasted_iota(jnp.int32, (keep, G), 1) // B
    copies = []
    for k in range(n_t):
        c0 = pl.multiple_of(lax.rem(lax.axis_index("tensor") + k, n_t) * cols, G)
        for i in range(ng):
            at = pl.multiple_of(c0 + i * G, G)
            own = q[:, pl.ds(at, G)]
            spread = jnp.concatenate(
                [jnp.where(lane_block == j, own, 0.0) for j in range(G // B)], axis=0
            )
            hi, lo = split(spread)
            w = jnp.concatenate([hi, hi, lo, jnp.zeros_like(lo)], axis=0)
            back = dot(p_ref[:, pl.ds(pl.multiple_of(at // 2, 2 * B), 2 * B)], w)
            moment = momentum_decay * vel[:, pl.ds(at, G)] + grads[k][:, i * G : (i + 1) * G].astype(F32)
            held[:, pl.ds(at, G)] = moment - back
        cut = pl.ds(c0, cols)
        copies.append(pltpu.make_async_copy(held.at[:, cut], new_ref.at[:, cut], sems.at[k]))
        copies[-1].start()
    for copy in copies:
        copy.wait()


def places_body(keep, w_ref, tall, bundles, *p_refs):
    n_r, last = bundles.shape[0], bundles.shape[1] - 16
    half, nb = n_r // 2, G // B
    rep = lax.axis_index("replica")
    freq = lax.broadcasted_iota(jnp.int32, (B, 2 * B), 0).astype(F32)
    block = lax.broadcasted_iota(jnp.int32, (1, 2 * B), 1) // (half * keep)
    for h in range(2):
        hi_ref, lo_ref = p_refs[2 * h : 2 * h + 2]
        w = w_ref[h, :1, :]
        rows = [bundles[rep ^ (2 * i + h), last:, :].astype(F32)[:keep] for i in range(half)]
        rows = jnp.concatenate(rows * nb, axis=0).T
        for g in range(hi_ref.shape[1] // (2 * B)):
            num = rows[g * nb : g * nb + 1]
            for j in range(1, nb):
                num = jnp.where(block == j, rows[g * nb + j : g * nb + j + 1], num)
            hot = jnp.where(freq == num, 1.0, 0.0).astype(BF16)
            y = dot(tall[:, :B], hot)
            hi, lo = split((y[:B] + y[B:]) * w)
            hi_ref[:, g * 2 * B : (g + 1) * 2 * B] = hi
            lo_ref[:, g * 2 * B : (g + 1) * 2 * B] = lo


def spread_rows(p_hi, p_lo, ships, g):
    half, keep = ships.shape[0], ships.shape[1]
    lane_block = lax.broadcasted_iota(jnp.int32, (half * keep, G), 1) // B
    s = jnp.concatenate([ships[i, :, g * G : (g + 1) * G].astype(F32) for i in range(half)], axis=0)
    w = jnp.concatenate(
        [jnp.where(lane_block == j, s, 0.0).astype(BF16) for j in range(G // B)], axis=0
    )
    cut = slice(g * 2 * B, (g + 1) * 2 * B)
    y = dot(jnp.concatenate([p_hi[:, cut], p_lo[:, cut]], axis=0), w)
    return y[:B] + y[B:]


def half_update_body(p_hi, p_lo, mine, out):
    for g in range(out.shape[0] // B):
        out[g * B : (g + 1) * B, :] = spread_rows(p_hi, p_lo, mine, g)


def update_body(chunk, half_sum, p_hi, p_lo, other, out, held, sems):
    ng = half_sum.shape[0] // B
    copies = []
    for c in range(0, ng, chunk):
        for g in range(c, c + chunk):
            held[:, g * G : (g + 1) * G] = half_sum[g * B : (g + 1) * B, :] + spread_rows(p_hi, p_lo, other, g)
        cut = pl.ds(c * G, chunk * G)
        copies.append(pltpu.make_async_copy(held.at[:, cut], out.at[:, cut], sems.at[c // chunk]))
        copies[-1].start()
    for copy in copies:
        copy.wait()


def input_grad_body(n_t, n_r, cp, bundles, *refs):
    ups, out, held = refs[:n_t], refs[n_t], refs[n_t + 1]
    nc = out.shape[1] // cp
    nr = B // (n_r // cp)
    tiles = nc // 128
    for r in range(n_r):
        r0, c0 = (r // cp) * nr, (r % cp) * nc
        for k in range(n_t):
            for j in range(tiles):
                at = (k * tiles + j) * nr
                held[k * B + r0 : k * B + r0 + nr, c0 + j * 128 : c0 + (j + 1) * 128] = bundles[r, at : at + nr, :]
    up = jnp.concatenate([u[:B, :] for u in ups], axis=0).T
    for c in range(0, out.shape[1], G):
        out[:, c : c + G] = dot(up, held[:, c : c + G]).astype(BF16)


def per_device(n_t, n_r, act, switch, slope, exp, vel, lines, mask, tally):
    cols = act.shape[1]
    width = exp.shape[1]
    tok = act.shape[0]
    keep = lines.shape[3]
    blocks = width // B
    groups = width // G
    cp = 2
    rp = n_r // cp
    half = n_r // 2
    tab, tall = constants()
    def shift(x, k):
        return lax.ppermute(x, "tensor", [(i, (i + k) % n_t) for i in range(n_t)])

    order = sorted(range(1, n_t), key=lambda k: -min(k, n_t - k))

    def swap(x, m):
        return lax.ppermute(x, "replica", [(i, i ^ m) for i in range(n_r)])

    own = lines[0, 0].T
    tiles = cols // cp // 128
    nr = B // rp
    *parts, act, own, tall = call(
        functools.partial(first_body, n_t, cp, cols, nr),
        [near((B + tiles * nr, 128))] * n_t
        + [near(act.shape), near(own.shape, jnp.int32), near(tall.shape)],
        (far(switch.T), far(slope.T), far(exp), far(act), far(own), far(tall)),
        [ANY] * 6,
        [VM] * (n_t + 3),
        scratch=[
            pltpu.VMEM((B, tok), BF16),
            pltpu.VMEM((B, tok), BF16),
            pltpu.VMEM((nr, width), BF16),
            pltpu.SemaphoreType.DMA((6,)),
        ],
        nbytes=act.size * 4 + nr * width * 2,
        name="up_grads",
    )
    parts = [parts[0]] + [shift(parts[k], k) for k in range(1, n_t)]

    p_own, a_own, shares, tab = call(
        functools.partial(own_body, n_r, keep),
        [
            near((B, groups * 2 * B)),
            near((groups * B, 2 * B)),
            near((2, 8, 2 * B), F32),
            near(tab.shape),
        ],
        (far(mask), far(tally), far(tab), own, tall),
        [ANY, ANY, ANY, VM, VM],
        [VM] * 4,
        scratch=[pltpu.SMEM((n_r,), jnp.int32)] * 2 + [pltpu.SemaphoreType.DMA((3,))],
        name="own_places",
    )

    def grads_of(ks):
        return call(
            functools.partial(grads_body, len(ks)),
            [near((B, cols), BF16 if k else F32) for k in ks],
            (act, *[parts[k] for k in ks]),
            [VM] * (1 + len(ks)),
            [VM] * len(ks),
            name="weight_grads",
        )

    grads = {}
    for k in order[:-1]:
        (grads[k],) = grads_of([k])
    made, grads[0] = grads_of([order[-1], 0])
    grads[order[-1]] = made
    grads = [grads[0]] + [shift(grads[k], -k) for k in range(1, n_t)]

    bundle = call(
        functools.partial(bundle_body, n_t, keep),
        near((n_t * tiles * nr + 16, 128)),
        (made, own, *parts),
        [ANY] + [VM] * (n_t + 1),
        VM,
        name="bundle",
    )
    bundles = lax.all_gather(bundle, "replica", axis=0)

    places = call(
        functools.partial(places_body, keep),
        [near((B, blocks * half * keep))] * 4,
        (shares, tall, bundles),
        [VM] * 3,
        [VM] * 4,
        name="places",
    )
    input_grad = call(
        functools.partial(input_grad_body, n_t, n_r, cp),
        jax.ShapeDtypeStruct((tok, cols), BF16),
        (bundles, *parts),
        [VM] * (1 + n_t),
        VM,
        scratch=[pltpu.VMEM((n_t * B, cols), BF16)],
        flops=2 * tok * n_t * B * cols,
        nbytes=(n_t * B * cols + tok * cols) * 2,
        name="input_grads",
    )

    ship, q_own = call(
        functools.partial(kept_body, n_t, keep),
        [near((keep, width)), near((keep, width), F32)],
        (vel[0], a_own, tab, bundles, *grads),
        [VM] * 3 + [ANY] + [VM] * n_t,
        [VM] * 2,
        flops=6 * B * B * width,
        nbytes=B * width * 6,
        name="kept_rows",
    )
    ships = [ship] + [swap(ship, 2 * i) for i in range(1, half)]
    new = call(
        functools.partial(return_body, n_t, keep),
        jax.ShapeDtypeStruct((B, width), F32),
        (vel[0], p_own, q_own, *grads),
        [VM] * (3 + n_t),
        ANY,
        scratch=[pltpu.VMEM((B, width), F32), pltpu.SemaphoreType.DMA((n_t,))],
        flops=6 * B * B * width,
        nbytes=B * width * 10,
        name="new_momentums",
    )
    mine = call(
        functools.partial(join_body, half),
        near((half, keep, width)),
        (*ships, far(new), far(input_grad), places[0]),
        [VM] * half + [ANY] * 3,
        VM,
        name="join_kept",
    )
    other = swap(mine, 1)
    half_sum = call(
        half_update_body,
        near((groups * B, G), F32),
        (*places[:2], mine),
        [VM] * 3,
        VM,
        name="half_updates",
    )
    chunk = next(c for c in (5, 4, 3, 2, 1) if groups % c == 0)
    update = call(
        functools.partial(update_body, chunk),
        jax.ShapeDtypeStruct((B, width), F32),
        (half_sum, *places[2:], other),
        [VM] * 4,
        ANY,
        scratch=[
            pltpu.VMEM((B, width), F32),
            pltpu.SemaphoreType.DMA((groups // chunk,)),
        ],
        flops=8 * B * G * width,
        nbytes=B * width * 8,
        name="updates",
    )
    return input_grad, new[None], update


def per_device_plain(
    projection_inputs,
    switch_logits_raw,
    inner_neuron_slope,
    expansion_matrix,
    velocity_buffer,
    sent_spectral_lines,
    participant_mask,
    token_tallies,
):
    highest = lax.Precision.HIGHEST
    up_grad = (
        inner_neuron_slope.astype(jnp.float32) * jax.nn.silu(switch_logits_raw.astype(jnp.float32))
    ).astype(jnp.bfloat16)
    partial_terms = jnp.dot(up_grad, expansion_matrix, preferred_element_type=jnp.float32)
    input_grad = lax.psum_scatter(partial_terms, "tensor", scatter_dimension=1, tiled=True).astype(
        jnp.bfloat16
    )
    grad_w = lax.dot_general(
        up_grad,
        lax.all_gather(projection_inputs, "tensor", axis=1, tiled=True),
        (((0,), (0,)), ((), ())),
        preferred_element_type=jnp.float32,
    )
    row_total_count = expansion_matrix.shape[0] // 64
    col_count = expansion_matrix.shape[1] // 64
    moment = momentum_decay * velocity_buffer[0] + grad_w
    cosines = cosine_table()
    blocks = moment.reshape(row_total_count, 64, col_count, 64).transpose(0, 2, 1, 3)
    coefficients = jnp.einsum("fa,ijab,gb->ijfg", cosines, blocks, cosines, precision=highest)
    freq_ids = jnp.arange(64, dtype=jnp.int32)
    own_rows = sent_spectral_lines[0]
    chosen = (own_rows[..., None] == freq_ids).astype(jnp.float32)
    shipped = jnp.einsum("ijkf,ijfg->ijkg", chosen, coefficients, precision=highest).astype(
        jnp.bfloat16
    )
    spectrum = jnp.einsum("ijkf,ijkg->ijfg", chosen, shipped.astype(jnp.float32), precision=highest)
    returned = jnp.einsum("fa,ijfg,gb->ijab", cosines, spectrum, cosines, precision=highest)
    new_moment = moment - returned.transpose(0, 2, 1, 3).reshape(moment.shape)
    worker_burdens = participant_mask.astype(jnp.float32) * token_tallies.astype(jnp.float32)
    worker_fractions = worker_burdens * (
        jnp.sum(participant_mask.astype(jnp.float32)) / jnp.sum(worker_burdens)
    )
    myself = lax.axis_index("replica")
    combined = lax.psum(worker_fractions[myself] * spectrum, "replica")
    update = jnp.einsum("fa,ijfg,gb->ijab", cosines, combined, cosines, precision=highest)
    update = update.transpose(0, 2, 1, 3).reshape(moment.shape)
    return (input_grad, new_moment[None], update)


def solution(mesh):
    n_t, n_r = mesh.shape["tensor"], mesh.shape["replica"]

    def device(*args):
        act, exp, lines = args[0], args[3], args[5]
        fits = (
            act.shape[1] % G == 0
            and act.shape[0] % 128 == 0
            and exp.shape[0] == B
            and lines.shape[3] == 8
            and n_r == 8
        )
        if not fits:
            return per_device_plain(*args)
        return per_device(n_t, n_r, *args)

    return jax.shard_map(
        device,
        mesh=mesh,
        in_specs=(
            P("replica", "tensor"),
            P("replica", "tensor"),
            P("replica", "tensor"),
            P("tensor", None),
            P("replica", "tensor", None),
            P("replica", "tensor", None, None),
            P(),
            P(),
        ),
        out_specs=(P("replica", "tensor"), P("replica", "tensor", None), P("tensor", None)),
        check_vma=False,
    )
```

```python
import functools

import jax
import jax.numpy as jnp
import numpy as np
from jax import lax
from jax.experimental import pallas as pl
from jax.experimental.pallas import tpu as pltpu
from jax.sharding import PartitionSpec as P

momentum_decay = 0.9
B = 64
G = 256
F32 = jnp.float32
BF16 = jnp.bfloat16
VMEM_LIMIT = 24 * 1024 * 1024

VM = pl.BlockSpec(memory_space=pltpu.VMEM)
SM = pl.BlockSpec(memory_space=pltpu.SMEM)
ANY = pl.BlockSpec(memory_space=pl.ANY)


def cosine_table():
    freqs = jnp.arange(64, dtype=jnp.float32)[:, None]
    places = jnp.arange(64, dtype=jnp.float32)[None, :]
    cosines = jnp.cos(jnp.pi * (places + 0.5) * freqs / 64.0) * jnp.sqrt(2.0 / 64.0)
    return cosines.at[0].multiply(jnp.sqrt(0.5))


def cosine_np():
    f = np.arange(B)[:, None]
    a = np.arange(B)[None, :]
    c = np.cos(np.pi * (a + 0.5) * f / B) * np.sqrt(2.0 / B)
    c[0] *= np.sqrt(0.5)
    return c


def halves(c):
    hi = np.asarray(c, dtype=np.float32).astype(jnp.bfloat16)
    lo = (np.asarray(c, np.float64) - hi.astype(np.float64)).astype(np.float32).astype(jnp.bfloat16)
    return hi, lo


def constants():
    hi, lo = halves(cosine_np())
    eye = np.eye(G // B)
    kron = lambda x: np.kron(eye, np.asarray(x, np.float32)).astype(jnp.bfloat16)
    tall = np.zeros((2 * B, 2 * B), jnp.bfloat16)
    tall[:B, :B], tall[B:, :B] = hi.T, lo.T
    return jnp.asarray(np.concatenate([kron(x) for x in (hi.T, lo.T, hi, lo)], axis=0)), jnp.asarray(tall)


def fwd(tab, i):
    return tab[i * G : (i + 1) * G, :]


def inv(tab, i):
    return tab[(2 + i) * G : (3 + i) * G, :]


def dot(a, b):
    return jnp.dot(a, b, preferred_element_type=F32)


def split(x):
    hi = x.astype(BF16)
    return hi, (x - hi.astype(F32)).astype(BF16)


def near(shape, dtype=BF16):
    return pltpu.VMEM(shape, dtype)


def far(x):
    return pltpu.with_memory_space_constraint(x, pltpu.HBM)


def call(body, out_shape, ins, in_specs, out_specs, scratch=(), flops=0, nbytes=0, name=None, alias={}):
    return pl.pallas_call(
        body,
        out_shape=out_shape,
        in_specs=in_specs,
        out_specs=out_specs,
        scratch_shapes=scratch,
        input_output_aliases=alias,
        compiler_params=pltpu.CompilerParams(vmem_limit_bytes=VMEM_LIMIT),
        cost_estimate=pl.CostEstimate(flops=flops, bytes_accessed=nbytes, transcendentals=0),
        name=name,
    )(*ins)


def first_body(n_t, cp, cols, nr, switch, slope, exp_ref, act, lines, tall, *refs):
    outs, (act_out, lines_out, tall_out) = refs[:n_t], refs[n_t : n_t + 3]
    switch_v, slope_v, exp_v, sems = refs[n_t + 3 :]
    rep, ten = lax.axis_index("replica"), lax.axis_index("tensor")
    r0 = pl.multiple_of((rep // cp) * nr, nr)
    copies = [
        pltpu.make_async_copy(src, dst, sems.at[i])
        for i, (src, dst) in enumerate(
            [
                (switch, switch_v),
                (slope, slope_v),
                (exp_ref.at[pl.ds(r0, nr), :], exp_v),
                (act, act_out),
                (lines, lines_out),
                (tall, tall_out),
            ]
        )
    ]
    for copy in copies:
        copy.start()
    copies[0].wait()
    copies[1].wait()
    v = switch_v[...].astype(F32)
    up = (slope_v[...].astype(F32) * (v * jax.nn.sigmoid(v))).astype(BF16)
    for k in range(n_t):
        outs[k][:B, :] = up
    copies[2].wait()
    nc = cols // cp
    for k in range(n_t):
        c0 = lax.rem(ten + k, n_t) * cols + lax.rem(rep, cp) * nc
        for j in range(nc // 128):
            at = pl.multiple_of(c0 + j * 128, 128)
            outs[k][B + j * nr : B + (j + 1) * nr, :] = exp_v[:, pl.ds(at, 128)]
    for copy in copies[3:]:
        copy.wait()


def grads_body(n, act, after, *refs):
    ups, outs = refs[:n], refs[n:]
    up = jnp.concatenate([u[:B, :] for u in ups], axis=0)
    for c in range(0, act.shape[1], G):
        g = dot(up, act[:, c : c + G])
        for k in range(n):
            outs[k][:, c : c + G] = g[k * B : (k + 1) * B].astype(outs[k].dtype)


def bundle_body(n_t, keep, after, lines, *refs):
    parts, out = refs[:n_t], refs[n_t]
    n = parts[0].shape[0] - B
    for k in range(n_t):
        out[k * n : (k + 1) * n, :] = parts[k][B:, :]
    blocks = lines.shape[1]
    rows = jnp.concatenate([lines[...].astype(F32), jnp.zeros((keep, 128 - blocks), F32)], axis=1)
    out[n_t * n :, :] = jnp.concatenate([rows, jnp.zeros((16 - keep, 128), F32)], axis=0).astype(BF16)


def join_body(n, *refs):
    for i, ref in enumerate(refs[:n]):
        refs[-1][i] = ref[...]


def own_body(n_r, keep, after, mask, tally, tab, lines, tall, p_ref, a_ref, w_ref, tab_ref, mask_s, tally_s, sems):
    copies = [
        pltpu.make_async_copy(src, dst, sems.at[i])
        for i, (src, dst) in enumerate([(mask, mask_s), (tally, tally_s), (tab, tab_ref)])
    ]
    for copy in copies:
        copy.start()
    blocks = lines.shape[1]
    rows = jnp.concatenate([lines[...].astype(F32), jnp.zeros((keep, 128 - blocks), F32)], axis=1)
    rows = jnp.concatenate([rows] * (2 * B // keep), axis=0).T
    freq = lax.broadcasted_iota(jnp.int32, (B, 2 * B), 0).astype(F32)
    block = (lax.broadcasted_iota(jnp.int32, (1, 2 * B), 1) // keep) % (G // B)
    term = lax.broadcasted_iota(jnp.int32, (B, 2 * B), 1) // (B // 2)
    for g in range(blocks // (G // B)):
        num = rows[g * (G // B) : g * (G // B) + 1]
        for j in range(1, G // B):
            num = jnp.where(block == j, rows[g * (G // B) + j : g * (G // B) + j + 1], num)
        hot = jnp.where(freq == num, 1.0, 0.0).astype(BF16)
        y = dot(tall[:, :B], hot)
        p = jnp.where(term == 3, 0.0, jnp.where(term == 1, y[B:], y[:B]))
        p_ref[:, g * 2 * B : (g + 1) * 2 * B] = p.astype(BF16)
        a_ref[g * B : (g + 1) * B, :] = jnp.concatenate([p, p], axis=0).T[:B].astype(BF16)
    for copy in copies:
        copy.wait()
    total, alive = jnp.float32(0), jnp.float32(0)
    for r in range(n_r):
        m = mask_s[r].astype(F32)
        total = total + m * tally_s[r].astype(F32)
        alive = alive + m
    half = n_r // 2
    place = (lax.broadcasted_iota(jnp.int32, (8, 2 * B), 1) // keep) % half
    scale = jnp.full((8, 2 * B), alive) / jnp.full((8, 2 * B), total)
    for h in range(2):
        w = jnp.zeros((8, 2 * B), F32)
        for i in range(half):
            r = lax.axis_index("replica") ^ (2 * i + h)
            w = jnp.where(place == i, mask_s[r].astype(F32) * tally_s[r].astype(F32), w)
        w_ref[h] = w * scale


def kept_body(ks, n_t, keep, vel, a_ref, tab, *refs):
    grads, (send_ref, own_ref) = refs[: len(ks)], refs[-2:]
    cols = grads[0].shape[1]
    ng = cols // G
    lane_block = lax.broadcasted_iota(jnp.int32, (keep, G), 1) // B
    sel = []
    for n, k in enumerate(ks):
        c0 = lax.rem(lax.axis_index("tensor") + k, n_t) * cols
        for i in range(ng):
            at = pl.multiple_of(c0 + i * G, G)
            moment = momentum_decay * vel[:, pl.ds(at, G)] + grads[n][:, i * G : (i + 1) * G].astype(F32)
            hi, lo = split(moment)
            y = dot(a_ref[pl.ds(pl.multiple_of(at // (G // B), B), B), :], jnp.concatenate([hi, lo], axis=0))
            y = y[: B // 2] + y[B // 2 :]
            got = y[:keep]
            for j in range(1, G // B):
                got = jnp.where(lane_block == j, y[j * keep : (j + 1) * keep], got)
            sel.append(got)
    hi, lo = split(jnp.concatenate(sel, axis=0))
    n = len(ks) * ng * keep
    y = dot(jnp.concatenate([hi, lo], axis=0), fwd(tab, 0))
    kept = (y[:n] + y[n:] + dot(hi, fwd(tab, 1))).astype(BF16)
    q = dot(kept, inv(tab, 0)) + dot(kept, inv(tab, 1))
    for n, k in enumerate(ks):
        c0 = pl.multiple_of(lax.rem(lax.axis_index("tensor") + k, n_t) * cols, G)
        part = jnp.concatenate([q[(n * ng + i) * keep : (n * ng + i + 1) * keep] for i in range(ng)], axis=1)
        own_ref[:, pl.ds(c0, cols)] = part
        send_ref[:, pl.ds(c0, cols)] = part.astype(BF16)


def return_body(n_t, keep, vel, p_ref, q, *refs):
    grads, (new_ref, held, sems) = refs[:n_t], refs[n_t:]
    cols = grads[0].shape[1]
    ng = cols // G
    lane_block = lax.broadcasted_iota(jnp.int32, (keep, G), 1) // B
    copies = []
    for k in range(n_t):
        c0 = pl.multiple_of(lax.rem(lax.axis_index("tensor") + k, n_t) * cols, G)
        for i in range(ng):
            at = pl.multiple_of(c0 + i * G, G)
            own = q[:, pl.ds(at, G)]
            spread = jnp.concatenate(
                [jnp.where(lane_block == j, own, 0.0) for j in range(G // B)], axis=0
            )
            hi, lo = split(spread)
            w = jnp.concatenate([hi, hi, lo, jnp.zeros_like(lo)], axis=0)
            back = dot(p_ref[:, pl.ds(pl.multiple_of(at // 2, 2 * B), 2 * B)], w)
            moment = momentum_decay * vel[:, pl.ds(at, G)] + grads[k][:, i * G : (i + 1) * G].astype(F32)
            held[:, pl.ds(at, G)] = moment - back
        cut = pl.ds(c0, cols)
        copies.append(pltpu.make_async_copy(held.at[:, cut], new_ref.at[:, cut], sems.at[k]))
        copies[-1].start()
    for copy in copies:
        copy.wait()


def places_body(keep, w_ref, tall, bundles, *p_refs):
    n_r, last = bundles.shape[0], bundles.shape[1] - 16
    half, nb = n_r // 2, G // B
    rep = lax.axis_index("replica")
    freq = lax.broadcasted_iota(jnp.int32, (B, 2 * B), 0).astype(F32)
    block = lax.broadcasted_iota(jnp.int32, (1, 2 * B), 1) // (half * keep)
    for h in range(2):
        hi_ref, lo_ref = p_refs[2 * h : 2 * h + 2]
        w = w_ref[h, :1, :]
        rows = [bundles[rep ^ (2 * i + h), last:, :].astype(F32)[:keep] for i in range(half)]
        rows = jnp.concatenate(rows * nb, axis=0).T
        for g in range(hi_ref.shape[1] // (2 * B)):
            num = rows[g * nb : g * nb + 1]
            for j in range(1, nb):
                num = jnp.where(block == j, rows[g * nb + j : g * nb + j + 1], num)
            hot = jnp.where(freq == num, 1.0, 0.0).astype(BF16)
            y = dot(tall[:, :B], hot)
            hi, lo = split((y[:B] + y[B:]) * w)
            hi_ref[:, g * 2 * B : (g + 1) * 2 * B] = hi
            lo_ref[:, g * 2 * B : (g + 1) * 2 * B] = lo


def spread_rows(p_hi, p_lo, ships, g):
    half, keep = ships.shape[0], ships.shape[1]
    lane_block = lax.broadcasted_iota(jnp.int32, (half * keep, G), 1) // B
    s = jnp.concatenate([ships[i, :, g * G : (g + 1) * G].astype(F32) for i in range(half)], axis=0)
    w = jnp.concatenate(
        [jnp.where(lane_block == j, s, 0.0).astype(BF16) for j in range(G // B)], axis=0
    )
    cut = slice(g * 2 * B, (g + 1) * 2 * B)
    y = dot(jnp.concatenate([p_hi[:, cut], p_lo[:, cut]], axis=0), w)
    return y[:B] + y[B:]


def half_update_body(p_hi, p_lo, mine, out):
    for g in range(out.shape[0] // B):
        out[g * B : (g + 1) * B, :] = spread_rows(p_hi, p_lo, mine, g)


def update_body(chunk, half_sum, p_hi, p_lo, other, out, held, sems):
    ng = half_sum.shape[0] // B
    copies = []
    for c in range(0, ng, chunk):
        for g in range(c, c + chunk):
            held[:, g * G : (g + 1) * G] = half_sum[g * B : (g + 1) * B, :] + spread_rows(p_hi, p_lo, other, g)
        cut = pl.ds(c * G, chunk * G)
        copies.append(pltpu.make_async_copy(held.at[:, cut], out.at[:, cut], sems.at[c // chunk]))
        copies[-1].start()
    for copy in copies:
        copy.wait()


def input_grad_body(n_t, n_r, cp, bundles, *refs):
    ups, out, held = refs[:n_t], refs[n_t], refs[n_t + 1]
    nc = out.shape[1] // cp
    nr = B // (n_r // cp)
    tiles = nc // 128
    for r in range(n_r):
        r0, c0 = (r // cp) * nr, (r % cp) * nc
        for k in range(n_t):
            for j in range(tiles):
                at = (k * tiles + j) * nr
                held[k * B + r0 : k * B + r0 + nr, c0 + j * 128 : c0 + (j + 1) * 128] = bundles[r, at : at + nr, :]
    up = jnp.concatenate([u[:B, :] for u in ups], axis=0).T
    for c in range(0, out.shape[1], G):
        out[:, c : c + G] = dot(up, held[:, c : c + G]).astype(BF16)


def per_device(n_t, n_r, act, switch, slope, exp, vel, lines, mask, tally):
    cols = act.shape[1]
    width = exp.shape[1]
    tok = act.shape[0]
    keep = lines.shape[3]
    blocks = width // B
    groups = width // G
    cp = 2
    rp = n_r // cp
    half = n_r // 2
    tab, tall = constants()
    def shift(x, k):
        return lax.ppermute(x, "tensor", [(i, (i + k) % n_t) for i in range(n_t)])

    def swap(x, m):
        return lax.ppermute(x, "replica", [(i, i ^ m) for i in range(n_r)])

    own = lines[0, 0].T
    tiles = cols // cp // 128
    nr = B // rp
    *parts, act, own, tall = call(
        functools.partial(first_body, n_t, cp, cols, nr),
        [near((B + tiles * nr, 128))] * n_t
        + [near(act.shape), near(own.shape, jnp.int32), near(tall.shape)],
        (far(switch.T), far(slope.T), far(exp), far(act), far(own), far(tall)),
        [ANY] * 6,
        [VM] * (n_t + 3),
        scratch=[
            pltpu.VMEM((B, tok), BF16),
            pltpu.VMEM((B, tok), BF16),
            pltpu.VMEM((nr, width), BF16),
            pltpu.SemaphoreType.DMA((6,)),
        ],
        nbytes=act.size * 4 + nr * width * 2,
        name="up_grads",
    )
    parts = [parts[0]] + [shift(parts[k], k) for k in range(1, n_t)]

    def grads_of(ks, after):
        return call(
            functools.partial(grads_body, len(ks)),
            [near((B, cols), BF16 if k else F32) for k in ks],
            (act, after, *[parts[k] for k in ks]),
            [VM, ANY] + [VM] * len(ks),
            [VM] * len(ks),
            name="weight_grads",
        )

    grads = {}
    made = act
    for k in range(1, n_t - 1):
        (made,) = grads_of([k], made)
        grads[k] = made
    made, grads[0] = grads_of([n_t - 1, 0], made)
    grads[n_t - 1] = made
    grads = [grads[0]] + [shift(grads[k], -k) for k in range(1, n_t)]

    bundle = call(
        functools.partial(bundle_body, n_t, keep),
        near((n_t * tiles * nr + 16, 128)),
        (made, own, *parts),
        [ANY] + [VM] * (n_t + 1),
        VM,
        name="bundle",
    )
    bundles = lax.all_gather(bundle, "replica", axis=0)

    p_own, a_own, shares, tab = call(
        functools.partial(own_body, n_r, keep),
        [
            near((B, groups * 2 * B)),
            near((groups * B, 2 * B)),
            near((2, 8, 2 * B), F32),
            near(tab.shape),
        ],
        (bundles, far(mask), far(tally), far(tab), own, tall),
        [ANY, ANY, ANY, ANY, VM, VM],
        [VM] * 4,
        scratch=[pltpu.SMEM((n_r,), jnp.int32)] * 2 + [pltpu.SemaphoreType.DMA((3,))],
        name="own_places",
    )
    places = call(
        functools.partial(places_body, keep),
        [near((B, blocks * half * keep))] * 4,
        (shares, tall, bundles),
        [VM] * 3,
        [VM] * 4,
        name="places",
    )
    input_grad = call(
        functools.partial(input_grad_body, n_t, n_r, cp),
        jax.ShapeDtypeStruct((tok, cols), BF16),
        (bundles, *parts),
        [VM] * (1 + n_t),
        VM,
        scratch=[pltpu.VMEM((n_t * B, cols), BF16)],
        flops=2 * tok * n_t * B * cols,
        nbytes=(n_t * B * cols + tok * cols) * 2,
        name="input_grads",
    )

    rows = []
    for ks in (list(range(n_t - 1)), [n_t - 1]):
        rows = call(
            functools.partial(kept_body, ks, n_t, keep),
            [near((keep, width)), near((keep, width), F32)],
            (vel[0], a_own, tab, *[grads[k] for k in ks], *rows),
            [VM] * (3 + len(ks) + len(rows)),
            [VM] * 2,
            flops=6 * B * B * cols * len(ks),
            nbytes=B * cols * 6 * len(ks),
            name="kept_rows",
            alias={3 + len(ks): 0, 4 + len(ks): 1} if rows else {},
        )
    ship, q_own = rows
    ships = [ship] + [swap(ship, 2 * i) for i in range(1, half)]
    new = call(
        functools.partial(return_body, n_t, keep),
        jax.ShapeDtypeStruct((B, width), F32),
        (vel[0], p_own, q_own, *grads),
        [VM] * (3 + n_t),
        ANY,
        scratch=[pltpu.VMEM((B, width), F32), pltpu.SemaphoreType.DMA((n_t,))],
        flops=6 * B * B * width,
        nbytes=B * width * 10,
        name="new_momentums",
    )
    mine = call(
        functools.partial(join_body, half),
        near((half, keep, width)),
        (*ships, far(new), far(input_grad), places[0]),
        [VM] * half + [ANY] * 3,
        VM,
        name="join_kept",
    )
    other = swap(mine, 1)
    half_sum = call(
        half_update_body,
        near((groups * B, G), F32),
        (*places[:2], mine),
        [VM] * 3,
        VM,
        name="half_updates",
    )
    chunk = next(c for c in (5, 4, 3, 2, 1) if groups % c == 0)
    update = call(
        functools.partial(update_body, chunk),
        jax.ShapeDtypeStruct((B, width), F32),
        (half_sum, *places[2:], other),
        [VM] * 4,
        ANY,
        scratch=[
            pltpu.VMEM((B, width), F32),
            pltpu.SemaphoreType.DMA((groups // chunk,)),
        ],
        flops=8 * B * G * width,
        nbytes=B * width * 8,
        name="updates",
    )
    return input_grad, new[None], update


def per_device_plain(
    projection_inputs,
    switch_logits_raw,
    inner_neuron_slope,
    expansion_matrix,
    velocity_buffer,
    sent_spectral_lines,
    participant_mask,
    token_tallies,
):
    highest = lax.Precision.HIGHEST
    up_grad = (
        inner_neuron_slope.astype(jnp.float32) * jax.nn.silu(switch_logits_raw.astype(jnp.float32))
    ).astype(jnp.bfloat16)
    partial_terms = jnp.dot(up_grad, expansion_matrix, preferred_element_type=jnp.float32)
    input_grad = lax.psum_scatter(partial_terms, "tensor", scatter_dimension=1, tiled=True).astype(
        jnp.bfloat16
    )
    grad_w = lax.dot_general(
        up_grad,
        lax.all_gather(projection_inputs, "tensor", axis=1, tiled=True),
        (((0,), (0,)), ((), ())),
        preferred_element_type=jnp.float32,
    )
    row_total_count = expansion_matrix.shape[0] // 64
    col_count = expansion_matrix.shape[1] // 64
    moment = momentum_decay * velocity_buffer[0] + grad_w
    cosines = cosine_table()
    blocks = moment.reshape(row_total_count, 64, col_count, 64).transpose(0, 2, 1, 3)
    coefficients = jnp.einsum("fa,ijab,gb->ijfg", cosines, blocks, cosines, precision=highest)
    freq_ids = jnp.arange(64, dtype=jnp.int32)
    own_rows = sent_spectral_lines[0]
    chosen = (own_rows[..., None] == freq_ids).astype(jnp.float32)
    shipped = jnp.einsum("ijkf,ijfg->ijkg", chosen, coefficients, precision=highest).astype(
        jnp.bfloat16
    )
    spectrum = jnp.einsum("ijkf,ijkg->ijfg", chosen, shipped.astype(jnp.float32), precision=highest)
    returned = jnp.einsum("fa,ijfg,gb->ijab", cosines, spectrum, cosines, precision=highest)
    new_moment = moment - returned.transpose(0, 2, 1, 3).reshape(moment.shape)
    worker_burdens = participant_mask.astype(jnp.float32) * token_tallies.astype(jnp.float32)
    worker_fractions = worker_burdens * (
        jnp.sum(participant_mask.astype(jnp.float32)) / jnp.sum(worker_burdens)
    )
    myself = lax.axis_index("replica")
    combined = lax.psum(worker_fractions[myself] * spectrum, "replica")
    update = jnp.einsum("fa,ijfg,gb->ijab", cosines, combined, cosines, precision=highest)
    update = update.transpose(0, 2, 1, 3).reshape(moment.shape)
    return (input_grad, new_moment[None], update)


def solution(mesh):
    n_t, n_r = mesh.shape["tensor"], mesh.shape["replica"]

    def device(*args):
        act, exp, lines = args[0], args[3], args[5]
        fits = (
            act.shape[1] % G == 0
            and act.shape[0] % 128 == 0
            and exp.shape[0] == B
            and lines.shape[3] == 8
            and n_r == 8
        )
        if not fits:
            return per_device_plain(*args)
        return per_device(n_t, n_r, *args)

    return jax.shard_map(
        device,
        mesh=mesh,
        in_specs=(
            P("replica", "tensor"),
            P("replica", "tensor"),
            P("replica", "tensor"),
            P("tensor", None),
            P("replica", "tensor", None),
            P("replica", "tensor", None, None),
            P(),
            P(),
        ),
        out_specs=(P("replica", "tensor"), P("replica", "tensor", None), P("tensor", None)),
        check_vma=False,
    )
```

```python
import functools

import jax
import jax.numpy as jnp
import numpy as np
from jax import lax
from jax.experimental import pallas as pl
from jax.experimental.pallas import tpu as pltpu
from jax.sharding import PartitionSpec as P

momentum_decay = 0.9
B = 64
G = 256
F32 = jnp.float32
BF16 = jnp.bfloat16
VMEM_LIMIT = 24 * 1024 * 1024

VM = pl.BlockSpec(memory_space=pltpu.VMEM)
SM = pl.BlockSpec(memory_space=pltpu.SMEM)
ANY = pl.BlockSpec(memory_space=pl.ANY)


def cosine_table():
    freqs = jnp.arange(64, dtype=jnp.float32)[:, None]
    places = jnp.arange(64, dtype=jnp.float32)[None, :]
    cosines = jnp.cos(jnp.pi * (places + 0.5) * freqs / 64.0) * jnp.sqrt(2.0 / 64.0)
    return cosines.at[0].multiply(jnp.sqrt(0.5))


def cosine_np():
    f = np.arange(B)[:, None]
    a = np.arange(B)[None, :]
    c = np.cos(np.pi * (a + 0.5) * f / B) * np.sqrt(2.0 / B)
    c[0] *= np.sqrt(0.5)
    return c


def halves(c):
    hi = np.asarray(c, dtype=np.float32).astype(jnp.bfloat16)
    lo = (np.asarray(c, np.float64) - hi.astype(np.float64)).astype(np.float32).astype(jnp.bfloat16)
    return hi, lo


def constants():
    hi, lo = halves(cosine_np())
    eye = np.eye(G // B)
    kron = lambda x: np.kron(eye, np.asarray(x, np.float32)).astype(jnp.bfloat16)
    tall = np.zeros((2 * B, 2 * B), jnp.bfloat16)
    tall[:B, :B], tall[B:, :B] = hi.T, lo.T
    return jnp.asarray(np.concatenate([kron(x) for x in (hi.T, lo.T, hi, lo)], axis=0)), jnp.asarray(tall)


def fwd(tab, i):
    return tab[i * G : (i + 1) * G, :]


def inv(tab, i):
    return tab[(2 + i) * G : (3 + i) * G, :]


def dot(a, b):
    return jnp.dot(a, b, preferred_element_type=F32)


def split(x):
    hi = x.astype(BF16)
    return hi, (x - hi.astype(F32)).astype(BF16)


def near(shape, dtype=BF16):
    return pltpu.VMEM(shape, dtype)


def far(x):
    return pltpu.with_memory_space_constraint(x, pltpu.HBM)


def call(body, out_shape, ins, in_specs, out_specs, scratch=(), flops=0, nbytes=0, name=None, alias={}):
    return pl.pallas_call(
        body,
        out_shape=out_shape,
        in_specs=in_specs,
        out_specs=out_specs,
        scratch_shapes=scratch,
        input_output_aliases=alias,
        compiler_params=pltpu.CompilerParams(vmem_limit_bytes=VMEM_LIMIT),
        cost_estimate=pl.CostEstimate(flops=flops, bytes_accessed=nbytes, transcendentals=0),
        name=name,
    )(*ins)


def first_body(n_t, cp, cols, nr, switch, slope, exp_ref, act, lines, tall, *refs):
    outs, (act_out, lines_out, tall_out) = refs[:n_t], refs[n_t : n_t + 3]
    switch_v, slope_v, exp_v, sems = refs[n_t + 3 :]
    rep, ten = lax.axis_index("replica"), lax.axis_index("tensor")
    r0 = pl.multiple_of((rep // cp) * nr, nr)
    copies = [
        pltpu.make_async_copy(src, dst, sems.at[i])
        for i, (src, dst) in enumerate(
            [
                (switch, switch_v),
                (slope, slope_v),
                (exp_ref.at[pl.ds(r0, nr), :], exp_v),
                (act, act_out),
                (lines, lines_out),
                (tall, tall_out),
            ]
        )
    ]
    for copy in copies:
        copy.start()
    copies[0].wait()
    copies[1].wait()
    v = switch_v[...].astype(F32)
    up = (slope_v[...].astype(F32) * (v * jax.nn.sigmoid(v))).astype(BF16)
    for k in range(n_t):
        outs[k][:B, :] = up
    copies[2].wait()
    nc = cols // cp
    for k in range(n_t):
        c0 = lax.rem(ten + k, n_t) * cols + lax.rem(rep, cp) * nc
        for j in range(nc // 128):
            at = pl.multiple_of(c0 + j * 128, 128)
            outs[k][B + j * nr : B + (j + 1) * nr, :] = exp_v[:, pl.ds(at, 128)]
    for copy in copies[3:]:
        copy.wait()


def grads_body(n, act, after, *refs):
    ups, outs = refs[:n], refs[n:]
    up = jnp.concatenate([u[:B, :] for u in ups], axis=0)
    for c in range(0, act.shape[1], G):
        g = dot(up, act[:, c : c + G])
        for k in range(n):
            outs[k][:, c : c + G] = g[k * B : (k + 1) * B].astype(outs[k].dtype)


def bundle_body(n_t, keep, after, lines, *refs):
    parts, out = refs[:n_t], refs[n_t]
    n = parts[0].shape[0] - B
    for k in range(n_t):
        out[k * n : (k + 1) * n, :] = parts[k][B:, :]
    blocks = lines.shape[1]
    rows = jnp.concatenate([lines[...].astype(F32), jnp.zeros((keep, 128 - blocks), F32)], axis=1)
    out[n_t * n :, :] = jnp.concatenate([rows, jnp.zeros((16 - keep, 128), F32)], axis=0).astype(BF16)


def join_body(n, *refs):
    for i, ref in enumerate(refs[:n]):
        refs[-1][i] = ref[...]


def own_body(n_r, keep, mask, tally, tab, lines, tall, p_ref, a_ref, w_ref, tab_ref, mask_s, tally_s, sems):
    copies = [
        pltpu.make_async_copy(src, dst, sems.at[i])
        for i, (src, dst) in enumerate([(mask, mask_s), (tally, tally_s), (tab, tab_ref)])
    ]
    for copy in copies:
        copy.start()
    blocks = lines.shape[1]
    rows = jnp.concatenate([lines[...].astype(F32), jnp.zeros((keep, 128 - blocks), F32)], axis=1)
    rows = jnp.concatenate([rows] * (2 * B // keep), axis=0).T
    freq = lax.broadcasted_iota(jnp.int32, (B, 2 * B), 0).astype(F32)
    block = (lax.broadcasted_iota(jnp.int32, (1, 2 * B), 1) // keep) % (G // B)
    term = lax.broadcasted_iota(jnp.int32, (B, 2 * B), 1) // (B // 2)
    for g in range(blocks // (G // B)):
        num = rows[g * (G // B) : g * (G // B) + 1]
        for j in range(1, G // B):
            num = jnp.where(block == j, rows[g * (G // B) + j : g * (G // B) + j + 1], num)
        hot = jnp.where(freq == num, 1.0, 0.0).astype(BF16)
        y = dot(tall[:, :B], hot)
        p = jnp.where(term == 3, 0.0, jnp.where(term == 1, y[B:], y[:B]))
        p_ref[:, g * 2 * B : (g + 1) * 2 * B] = p.astype(BF16)
        a_ref[g * B : (g + 1) * B, :] = jnp.concatenate([p, p], axis=0).T[:B].astype(BF16)
    for copy in copies:
        copy.wait()
    total, alive = jnp.float32(0), jnp.float32(0)
    for r in range(n_r):
        m = mask_s[r].astype(F32)
        total = total + m * tally_s[r].astype(F32)
        alive = alive + m
    half = n_r // 2
    place = (lax.broadcasted_iota(jnp.int32, (8, 2 * B), 1) // keep) % half
    scale = jnp.full((8, 2 * B), alive) / jnp.full((8, 2 * B), total)
    for h in range(2):
        w = jnp.zeros((8, 2 * B), F32)
        for i in range(half):
            r = lax.axis_index("replica") ^ (2 * i + h)
            w = jnp.where(place == i, mask_s[r].astype(F32) * tally_s[r].astype(F32), w)
        w_ref[h] = w * scale


def kept_body(ks, n_t, keep, vel, a_ref, tab, *refs):
    grads, (send_ref, own_ref) = refs[: len(ks)], refs[-2:]
    cols = grads[0].shape[1]
    ng = cols // G
    lane_block = lax.broadcasted_iota(jnp.int32, (keep, G), 1) // B
    sel = []
    for n, k in enumerate(ks):
        c0 = lax.rem(lax.axis_index("tensor") + k, n_t) * cols
        for i in range(ng):
            at = pl.multiple_of(c0 + i * G, G)
            moment = momentum_decay * vel[:, pl.ds(at, G)] + grads[n][:, i * G : (i + 1) * G].astype(F32)
            hi, lo = split(moment)
            y = dot(a_ref[pl.ds(pl.multiple_of(at // (G // B), B), B), :], jnp.concatenate([hi, lo], axis=0))
            y = y[: B // 2] + y[B // 2 :]
            got = y[:keep]
            for j in range(1, G // B):
                got = jnp.where(lane_block == j, y[j * keep : (j + 1) * keep], got)
            sel.append(got)
    hi, lo = split(jnp.concatenate(sel, axis=0))
    n = len(ks) * ng * keep
    y = dot(jnp.concatenate([hi, lo], axis=0), fwd(tab, 0))
    kept = (y[:n] + y[n:] + dot(hi, fwd(tab, 1))).astype(BF16)
    q = dot(kept, inv(tab, 0)) + dot(kept, inv(tab, 1))
    for n, k in enumerate(ks):
        c0 = pl.multiple_of(lax.rem(lax.axis_index("tensor") + k, n_t) * cols, G)
        part = jnp.concatenate([q[(n * ng + i) * keep : (n * ng + i + 1) * keep] for i in range(ng)], axis=1)
        own_ref[:, pl.ds(c0, cols)] = part
        send_ref[:, pl.ds(c0, cols)] = part.astype(BF16)


def return_body(n_t, keep, vel, p_ref, q, *refs):
    grads, (new_ref, held, sems) = refs[:n_t], refs[n_t:]
    cols = grads[0].shape[1]
    ng = cols // G
    lane_block = lax.broadcasted_iota(jnp.int32, (keep, G), 1) // B
    copies = []
    for k in range(n_t):
        c0 = pl.multiple_of(lax.rem(lax.axis_index("tensor") + k, n_t) * cols, G)
        for i in range(ng):
            at = pl.multiple_of(c0 + i * G, G)
            own = q[:, pl.ds(at, G)]
            spread = jnp.concatenate(
                [jnp.where(lane_block == j, own, 0.0) for j in range(G // B)], axis=0
            )
            hi, lo = split(spread)
            w = jnp.concatenate([hi, hi, lo, jnp.zeros_like(lo)], axis=0)
            back = dot(p_ref[:, pl.ds(pl.multiple_of(at // 2, 2 * B), 2 * B)], w)
            moment = momentum_decay * vel[:, pl.ds(at, G)] + grads[k][:, i * G : (i + 1) * G].astype(F32)
            held[:, pl.ds(at, G)] = moment - back
        cut = pl.ds(c0, cols)
        copies.append(pltpu.make_async_copy(held.at[:, cut], new_ref.at[:, cut], sems.at[k]))
        copies[-1].start()
    for copy in copies:
        copy.wait()


def places_body(keep, h, w_ref, tall, bundles, hi_ref, lo_ref):
    half, last, nb = bundles.shape[0], bundles.shape[1] - 16, G // B
    freq = lax.broadcasted_iota(jnp.int32, (B, 2 * B), 0).astype(F32)
    block = lax.broadcasted_iota(jnp.int32, (1, 2 * B), 1) // (half * keep)
    w = w_ref[h, :1, :]
    rows = [bundles[i, last:, :].astype(F32)[:keep] for i in range(half)]
    rows = jnp.concatenate(rows * nb, axis=0).T
    for g in range(hi_ref.shape[1] // (2 * B)):
        num = rows[g * nb : g * nb + 1]
        for j in range(1, nb):
            num = jnp.where(block == j, rows[g * nb + j : g * nb + j + 1], num)
        hot = jnp.where(freq == num, 1.0, 0.0).astype(BF16)
        y = dot(tall[:, :B], hot)
        hi, lo = split((y[:B] + y[B:]) * w)
        hi_ref[:, g * 2 * B : (g + 1) * 2 * B] = hi
        lo_ref[:, g * 2 * B : (g + 1) * 2 * B] = lo


def spread_rows(p_hi, p_lo, ships, g):
    half, keep = ships.shape[0], ships.shape[1]
    lane_block = lax.broadcasted_iota(jnp.int32, (half * keep, G), 1) // B
    s = jnp.concatenate([ships[i, :, g * G : (g + 1) * G].astype(F32) for i in range(half)], axis=0)
    w = jnp.concatenate(
        [jnp.where(lane_block == j, s, 0.0).astype(BF16) for j in range(G // B)], axis=0
    )
    cut = slice(g * 2 * B, (g + 1) * 2 * B)
    y = dot(jnp.concatenate([p_hi[:, cut], p_lo[:, cut]], axis=0), w)
    return y[:B] + y[B:]


def half_update_body(p_hi, p_lo, mine, out):
    for g in range(out.shape[0] // B):
        out[g * B : (g + 1) * B, :] = spread_rows(p_hi, p_lo, mine, g)


def update_body(chunk, half_sum, p_hi, p_lo, other, out, held, sems):
    ng = half_sum.shape[0] // B
    copies = []
    for c in range(0, ng, chunk):
        for g in range(c, c + chunk):
            held[:, g * G : (g + 1) * G] = half_sum[g * B : (g + 1) * B, :] + spread_rows(p_hi, p_lo, other, g)
        cut = pl.ds(c * G, chunk * G)
        copies.append(pltpu.make_async_copy(held.at[:, cut], out.at[:, cut], sems.at[c // chunk]))
        copies[-1].start()
    for copy in copies:
        copy.wait()


def input_grad_body(n_t, n_r, cp, mine, other, *refs):
    ups, out, held = refs[:n_t], refs[n_t], refs[n_t + 1]
    nc = out.shape[1] // cp
    nr = B // (n_r // cp)
    tiles = nc // 128
    for m in range(n_r):
        src = lax.axis_index("replica") ^ m
        r0, c0 = (src // cp) * nr, lax.rem(src, cp) * nc
        ref = (mine, other)[m % 2]
        for k in range(n_t):
            row = pl.multiple_of(k * B + r0, nr)
            for j in range(tiles):
                at = (k * tiles + j) * nr
                held[pl.ds(row, nr), pl.ds(pl.multiple_of(c0 + j * 128, 128), 128)] = ref[m // 2, at : at + nr, :]
    up = jnp.concatenate([u[:B, :] for u in ups], axis=0).T
    for c in range(0, out.shape[1], G):
        out[:, c : c + G] = dot(up, held[:, c : c + G]).astype(BF16)


def per_device(n_t, n_r, act, switch, slope, exp, vel, lines, mask, tally):
    cols = act.shape[1]
    width = exp.shape[1]
    tok = act.shape[0]
    keep = lines.shape[3]
    blocks = width // B
    groups = width // G
    cp = 2
    rp = n_r // cp
    half = n_r // 2
    tab, tall = constants()
    def shift(x, k):
        return lax.ppermute(x, "tensor", [(i, (i + k) % n_t) for i in range(n_t)])

    def swap(x, m):
        return lax.ppermute(x, "replica", [(i, i ^ m) for i in range(n_r)])

    def share(x, name, after=()):
        mine = call(
            functools.partial(join_body, half),
            near((half,) + x.shape),
            (x, *[swap(x, 2 * i) for i in range(1, half)], *after),
            [VM] * half + [ANY] * len(after),
            VM,
            name=name,
        )
        return mine, swap(mine, 1)

    own = lines[0, 0].T
    tiles = cols // cp // 128
    nr = B // rp
    *parts, act, own, tall = call(
        functools.partial(first_body, n_t, cp, cols, nr),
        [near((B + tiles * nr, 128))] * n_t
        + [near(act.shape), near(own.shape, jnp.int32), near(tall.shape)],
        (far(switch.T), far(slope.T), far(exp), far(act), far(own), far(tall)),
        [ANY] * 6,
        [VM] * (n_t + 3),
        scratch=[
            pltpu.VMEM((B, tok), BF16),
            pltpu.VMEM((B, tok), BF16),
            pltpu.VMEM((nr, width), BF16),
            pltpu.SemaphoreType.DMA((6,)),
        ],
        nbytes=act.size * 4 + nr * width * 2,
        name="up_grads",
    )
    parts = [parts[0]] + [shift(parts[k], k) for k in range(1, n_t)]

    def grads_of(ks, after):
        return call(
            functools.partial(grads_body, len(ks)),
            [near((B, cols), BF16 if k else F32) for k in ks],
            (act, after, *[parts[k] for k in ks]),
            [VM, ANY] + [VM] * len(ks),
            [VM] * len(ks),
            name="weight_grads",
        )

    grads = {}
    made = act
    for k in range(1, n_t - 1):
        (made,) = grads_of([k], made)
        grads[k] = made
    made, grads[0] = grads_of([n_t - 1, 0], made)
    grads[n_t - 1] = made
    grads = [grads[0]] + [shift(grads[k], -k) for k in range(1, n_t)]

    bundle = call(
        functools.partial(bundle_body, n_t, keep),
        near((n_t * tiles * nr + 16, 128)),
        (made, own, *parts),
        [ANY] + [VM] * (n_t + 1),
        VM,
        name="bundle",
    )
    bundles = share(bundle, "join_bundles")

    p_own, a_own, shares, tab = call(
        functools.partial(own_body, n_r, keep),
        [
            near((B, groups * 2 * B)),
            near((groups * B, 2 * B)),
            near((2, 8, 2 * B), F32),
            near(tab.shape),
        ],
        (far(mask), far(tally), far(tab), own, tall),
        [ANY, ANY, ANY, VM, VM],
        [VM] * 4,
        scratch=[pltpu.SMEM((n_r,), jnp.int32)] * 2 + [pltpu.SemaphoreType.DMA((3,))],
        name="own_places",
    )
    places = [
        call(
            functools.partial(places_body, keep, h),
            [near((B, blocks * half * keep))] * 2,
            (shares, tall, bundles[h]),
            [VM] * 3,
            [VM] * 2,
            name="places",
        )
        for h in range(2)
    ]
    input_grad = call(
        functools.partial(input_grad_body, n_t, n_r, cp),
        jax.ShapeDtypeStruct((tok, cols), BF16),
        (*bundles, *parts),
        [VM] * (2 + n_t),
        VM,
        scratch=[pltpu.VMEM((n_t * B, cols), BF16)],
        flops=2 * tok * n_t * B * cols,
        nbytes=(n_t * B * cols + tok * cols) * 2,
        name="input_grads",
    )

    rows = []
    for ks in (list(range(n_t - 1)), [n_t - 1]):
        rows = call(
            functools.partial(kept_body, ks, n_t, keep),
            [near((keep, width)), near((keep, width), F32)],
            (vel[0], a_own, tab, *[grads[k] for k in ks], *rows),
            [VM] * (3 + len(ks) + len(rows)),
            [VM] * 2,
            flops=6 * B * B * cols * len(ks),
            nbytes=B * cols * 6 * len(ks),
            name="kept_rows",
            alias={3 + len(ks): 0, 4 + len(ks): 1} if rows else {},
        )
    ship, q_own = rows
    new = call(
        functools.partial(return_body, n_t, keep),
        jax.ShapeDtypeStruct((B, width), F32),
        (vel[0], p_own, q_own, *grads),
        [VM] * (3 + n_t),
        ANY,
        scratch=[pltpu.VMEM((B, width), F32), pltpu.SemaphoreType.DMA((n_t,))],
        flops=6 * B * B * width,
        nbytes=B * width * 10,
        name="new_momentums",
    )
    mine, other = share(ship, "join_kept", (far(new),))
    half_sum = call(
        half_update_body,
        near((groups * B, G), F32),
        (*places[0], mine),
        [VM] * 3,
        VM,
        name="half_updates",
    )
    chunk = next(c for c in (5, 4, 3, 2, 1) if groups % c == 0)
    update = call(
        functools.partial(update_body, chunk),
        jax.ShapeDtypeStruct((B, width), F32),
        (half_sum, *places[1], other),
        [VM] * 4,
        ANY,
        scratch=[
            pltpu.VMEM((B, width), F32),
            pltpu.SemaphoreType.DMA((groups // chunk,)),
        ],
        flops=8 * B * G * width,
        nbytes=B * width * 8,
        name="updates",
    )
    return input_grad, new[None], update


def per_device_plain(
    projection_inputs,
    switch_logits_raw,
    inner_neuron_slope,
    expansion_matrix,
    velocity_buffer,
    sent_spectral_lines,
    participant_mask,
    token_tallies,
):
    highest = lax.Precision.HIGHEST
    up_grad = (
        inner_neuron_slope.astype(jnp.float32) * jax.nn.silu(switch_logits_raw.astype(jnp.float32))
    ).astype(jnp.bfloat16)
    partial_terms = jnp.dot(up_grad, expansion_matrix, preferred_element_type=jnp.float32)
    input_grad = lax.psum_scatter(partial_terms, "tensor", scatter_dimension=1, tiled=True).astype(
        jnp.bfloat16
    )
    grad_w = lax.dot_general(
        up_grad,
        lax.all_gather(projection_inputs, "tensor", axis=1, tiled=True),
        (((0,), (0,)), ((), ())),
        preferred_element_type=jnp.float32,
    )
    row_total_count = expansion_matrix.shape[0] // 64
    col_count = expansion_matrix.shape[1] // 64
    moment = momentum_decay * velocity_buffer[0] + grad_w
    cosines = cosine_table()
    blocks = moment.reshape(row_total_count, 64, col_count, 64).transpose(0, 2, 1, 3)
    coefficients = jnp.einsum("fa,ijab,gb->ijfg", cosines, blocks, cosines, precision=highest)
    freq_ids = jnp.arange(64, dtype=jnp.int32)
    own_rows = sent_spectral_lines[0]
    chosen = (own_rows[..., None] == freq_ids).astype(jnp.float32)
    shipped = jnp.einsum("ijkf,ijfg->ijkg", chosen, coefficients, precision=highest).astype(
        jnp.bfloat16
    )
    spectrum = jnp.einsum("ijkf,ijkg->ijfg", chosen, shipped.astype(jnp.float32), precision=highest)
    returned = jnp.einsum("fa,ijfg,gb->ijab", cosines, spectrum, cosines, precision=highest)
    new_moment = moment - returned.transpose(0, 2, 1, 3).reshape(moment.shape)
    worker_burdens = participant_mask.astype(jnp.float32) * token_tallies.astype(jnp.float32)
    worker_fractions = worker_burdens * (
        jnp.sum(participant_mask.astype(jnp.float32)) / jnp.sum(worker_burdens)
    )
    myself = lax.axis_index("replica")
    combined = lax.psum(worker_fractions[myself] * spectrum, "replica")
    update = jnp.einsum("fa,ijfg,gb->ijab", cosines, combined, cosines, precision=highest)
    update = update.transpose(0, 2, 1, 3).reshape(moment.shape)
    return (input_grad, new_moment[None], update)


def solution(mesh):
    n_t, n_r = mesh.shape["tensor"], mesh.shape["replica"]

    def device(*args):
        act, exp, lines = args[0], args[3], args[5]
        fits = (
            act.shape[1] % G == 0
            and act.shape[0] % 128 == 0
            and exp.shape[0] == B
            and lines.shape[3] == 8
            and n_r == 8
        )
        if not fits:
            return per_device_plain(*args)
        return per_device(n_t, n_r, *args)

    return jax.shard_map(
        device,
        mesh=mesh,
        in_specs=(
            P("replica", "tensor"),
            P("replica", "tensor"),
            P("replica", "tensor"),
            P("tensor", None),
            P("replica", "tensor", None),
            P("replica", "tensor", None, None),
            P(),
            P(),
        ),
        out_specs=(P("replica", "tensor"), P("replica", "tensor", None), P("tensor", None)),
        check_vma=False,
    )
```

```python
import functools

import jax
import jax.numpy as jnp
import numpy as np
from jax import lax
from jax.experimental import pallas as pl
from jax.experimental.pallas import tpu as pltpu
from jax.sharding import PartitionSpec as P

momentum_decay = 0.9
B = 64
G = 256
F32 = jnp.float32
BF16 = jnp.bfloat16
VMEM_LIMIT = 24 * 1024 * 1024

VM = pl.BlockSpec(memory_space=pltpu.VMEM)
SM = pl.BlockSpec(memory_space=pltpu.SMEM)
ANY = pl.BlockSpec(memory_space=pl.ANY)


def cosine_table():
    freqs = jnp.arange(64, dtype=jnp.float32)[:, None]
    places = jnp.arange(64, dtype=jnp.float32)[None, :]
    cosines = jnp.cos(jnp.pi * (places + 0.5) * freqs / 64.0) * jnp.sqrt(2.0 / 64.0)
    return cosines.at[0].multiply(jnp.sqrt(0.5))


def cosine_np():
    f = np.arange(B)[:, None]
    a = np.arange(B)[None, :]
    c = np.cos(np.pi * (a + 0.5) * f / B) * np.sqrt(2.0 / B)
    c[0] *= np.sqrt(0.5)
    return c


def halves(c):
    hi = np.asarray(c, dtype=np.float32).astype(jnp.bfloat16)
    lo = (np.asarray(c, np.float64) - hi.astype(np.float64)).astype(np.float32).astype(jnp.bfloat16)
    return hi, lo


def constants():
    hi, lo = halves(cosine_np())
    eye = np.eye(G // B)
    kron = lambda x: np.kron(eye, np.asarray(x, np.float32)).astype(jnp.bfloat16)
    tall = np.zeros((2 * B, 2 * B), jnp.bfloat16)
    tall[:B, :B], tall[B:, :B] = hi.T, lo.T
    return jnp.asarray(np.concatenate([kron(x) for x in (hi.T, lo.T, hi, lo)], axis=0)), jnp.asarray(tall)


def fwd(tab, i):
    return tab[i * G : (i + 1) * G, :]


def inv(tab, i):
    return tab[(2 + i) * G : (3 + i) * G, :]


def dot(a, b):
    return jnp.dot(a, b, preferred_element_type=F32)


def split(x):
    hi = x.astype(BF16)
    return hi, (x - hi.astype(F32)).astype(BF16)


def near(shape, dtype=BF16):
    return pltpu.VMEM(shape, dtype)


def far(x):
    return pltpu.with_memory_space_constraint(x, pltpu.HBM)


def call(body, out_shape, ins, in_specs, out_specs, scratch=(), flops=0, nbytes=0, name=None, alias={}):
    return pl.pallas_call(
        body,
        out_shape=out_shape,
        in_specs=in_specs,
        out_specs=out_specs,
        scratch_shapes=scratch,
        input_output_aliases=alias,
        compiler_params=pltpu.CompilerParams(vmem_limit_bytes=VMEM_LIMIT),
        cost_estimate=pl.CostEstimate(flops=flops, bytes_accessed=nbytes, transcendentals=0),
        name=name,
    )(*ins)


def first_body(n_t, cp, cols, nr, switch, slope, exp_ref, act, lines, tall, *refs):
    outs, (act_out, lines_out, tall_out) = refs[:n_t], refs[n_t : n_t + 3]
    switch_v, slope_v, exp_v, sems = refs[n_t + 3 :]
    rep, ten = lax.axis_index("replica"), lax.axis_index("tensor")
    r0 = pl.multiple_of((rep // cp) * nr, nr)
    copies = [
        pltpu.make_async_copy(src, dst, sems.at[i])
        for i, (src, dst) in enumerate(
            [
                (switch, switch_v),
                (slope, slope_v),
                (exp_ref.at[pl.ds(r0, nr), :], exp_v),
                (act, act_out),
                (lines, lines_out),
                (tall, tall_out),
            ]
        )
    ]
    for copy in copies:
        copy.start()
    copies[0].wait()
    copies[1].wait()
    v = switch_v[...].astype(F32)
    up = (slope_v[...].astype(F32) * (v * jax.nn.sigmoid(v))).astype(BF16)
    for k in range(n_t):
        outs[k][:B, :] = up
    copies[2].wait()
    nc = cols // cp
    for k in range(n_t):
        c0 = lax.rem(ten + k, n_t) * cols + lax.rem(rep, cp) * nc
        for j in range(nc // 128):
            at = pl.multiple_of(c0 + j * 128, 128)
            outs[k][B + j * nr : B + (j + 1) * nr, :] = exp_v[:, pl.ds(at, 128)]
    for copy in copies[3:]:
        copy.wait()


def grads_body(n, act, after, *refs):
    ups, outs = refs[:n], refs[n:]
    up = jnp.concatenate([u[:B, :] for u in ups], axis=0)
    for c in range(0, act.shape[1], G):
        g = dot(up, act[:, c : c + G])
        for k in range(n):
            outs[k][:, c : c + G] = g[k * B : (k + 1) * B].astype(outs[k].dtype)


def bundle_body(n_t, keep, after, lines, *refs):
    parts, out = refs[:n_t], refs[n_t]
    n = parts[0].shape[0] - B
    for k in range(n_t):
        out[k * n : (k + 1) * n, :] = parts[k][B:, :]
    blocks = lines.shape[1]
    rows = jnp.concatenate([lines[...].astype(F32), jnp.zeros((keep, 128 - blocks), F32)], axis=1)
    out[n_t * n :, :] = jnp.concatenate([rows, jnp.zeros((16 - keep, 128), F32)], axis=0).astype(BF16)


def join_body(n, *refs):
    for i, ref in enumerate(refs[:n]):
        refs[-1][i] = ref[...]


def own_body(n_r, keep, mask, tally, lines, tall, p_ref, a_ref, w_ref, mask_s, tally_s, sems):
    copies = [
        pltpu.make_async_copy(src, dst, sems.at[i])
        for i, (src, dst) in enumerate([(mask, mask_s), (tally, tally_s)])
    ]
    for copy in copies:
        copy.start()
    blocks = lines.shape[1]
    rows = jnp.concatenate([lines[...].astype(F32), jnp.zeros((keep, 128 - blocks), F32)], axis=1)
    rows = jnp.concatenate([rows] * (2 * B // keep), axis=0).T
    freq = lax.broadcasted_iota(jnp.int32, (B, 2 * B), 0).astype(F32)
    block = (lax.broadcasted_iota(jnp.int32, (1, 2 * B), 1) // keep) % (G // B)
    term = lax.broadcasted_iota(jnp.int32, (B, 2 * B), 1) // (B // 2)
    for g in range(blocks // (G // B)):
        num = rows[g * (G // B) : g * (G // B) + 1]
        for j in range(1, G // B):
            num = jnp.where(block == j, rows[g * (G // B) + j : g * (G // B) + j + 1], num)
        hot = jnp.where(freq == num, 1.0, 0.0).astype(BF16)
        y = dot(tall[:, :B], hot)
        p = jnp.where(term == 3, 0.0, jnp.where(term == 1, y[B:], y[:B]))
        p_ref[:, g * 2 * B : (g + 1) * 2 * B] = p.astype(BF16)
        a_ref[g * B : (g + 1) * B, :] = jnp.concatenate([p, p], axis=0).T[:B].astype(BF16)
    for copy in copies:
        copy.wait()
    total, alive = jnp.float32(0), jnp.float32(0)
    for r in range(n_r):
        m = mask_s[r].astype(F32)
        total = total + m * tally_s[r].astype(F32)
        alive = alive + m
    half = n_r // 2
    place = (lax.broadcasted_iota(jnp.int32, (8, 2 * B), 1) // keep) % half
    scale = jnp.full((8, 2 * B), alive) / jnp.full((8, 2 * B), total)
    for h in range(2):
        w = jnp.zeros((8, 2 * B), F32)
        for i in range(half):
            r = lax.axis_index("replica") ^ (2 * i + h)
            w = jnp.where(place == i, mask_s[r].astype(F32) * tally_s[r].astype(F32), w)
        w_ref[h] = w * scale


def kept_body(ks, n_t, keep, vel, a_ref, tab, after, *refs):
    grads, (send_ref, own_ref) = refs[: len(ks)], refs[-2:]
    cols = grads[0].shape[1]
    ng = cols // G
    lane_block = lax.broadcasted_iota(jnp.int32, (keep, G), 1) // B
    sel = []
    for n, k in enumerate(ks):
        c0 = lax.rem(lax.axis_index("tensor") + k, n_t) * cols
        for i in range(ng):
            at = pl.multiple_of(c0 + i * G, G)
            moment = momentum_decay * vel[:, pl.ds(at, G)] + grads[n][:, i * G : (i + 1) * G].astype(F32)
            hi, lo = split(moment)
            y = dot(a_ref[pl.ds(pl.multiple_of(at // (G // B), B), B), :], jnp.concatenate([hi, lo], axis=0))
            y = y[: B // 2] + y[B // 2 :]
            got = y[:keep]
            for j in range(1, G // B):
                got = jnp.where(lane_block == j, y[j * keep : (j + 1) * keep], got)
            sel.append(got)
    hi, lo = split(jnp.concatenate(sel, axis=0))
    n = len(ks) * ng * keep
    y = dot(jnp.concatenate([hi, lo], axis=0), fwd(tab, 0))
    kept = (y[:n] + y[n:] + dot(hi, fwd(tab, 1))).astype(BF16)
    q = dot(kept, inv(tab, 0)) + dot(kept, inv(tab, 1))
    for n, k in enumerate(ks):
        c0 = pl.multiple_of(lax.rem(lax.axis_index("tensor") + k, n_t) * cols, G)
        part = jnp.concatenate([q[(n * ng + i) * keep : (n * ng + i + 1) * keep] for i in range(ng)], axis=1)
        own_ref[:, pl.ds(c0, cols)] = part
        send_ref[:, pl.ds(c0, cols)] = part.astype(BF16)


def return_body(n_t, keep, vel, p_ref, q, *refs):
    grads, (new_ref, held, sems) = refs[:n_t], refs[n_t:]
    cols = grads[0].shape[1]
    ng = cols // G
    lane_block = lax.broadcasted_iota(jnp.int32, (keep, G), 1) // B
    copies = []
    for k in range(n_t):
        c0 = pl.multiple_of(lax.rem(lax.axis_index("tensor") + k, n_t) * cols, G)
        for i in range(ng):
            at = pl.multiple_of(c0 + i * G, G)
            own = q[:, pl.ds(at, G)]
            spread = jnp.concatenate(
                [jnp.where(lane_block == j, own, 0.0) for j in range(G // B)], axis=0
            )
            hi, lo = split(spread)
            w = jnp.concatenate([hi, hi, lo, jnp.zeros_like(lo)], axis=0)
            back = dot(p_ref[:, pl.ds(pl.multiple_of(at // 2, 2 * B), 2 * B)], w)
            moment = momentum_decay * vel[:, pl.ds(at, G)] + grads[k][:, i * G : (i + 1) * G].astype(F32)
            held[:, pl.ds(at, G)] = moment - back
        cut = pl.ds(c0, cols)
        copies.append(pltpu.make_async_copy(held.at[:, cut], new_ref.at[:, cut], sems.at[k]))
        copies[-1].start()
    for copy in copies:
        copy.wait()


def places_body(keep, w_ref, tall, bundles, *p_refs):
    n_r, last = bundles.shape[0], bundles.shape[1] - 16
    half, nb = n_r // 2, G // B
    rep = lax.axis_index("replica")
    freq = lax.broadcasted_iota(jnp.int32, (B, 2 * B), 0).astype(F32)
    block = lax.broadcasted_iota(jnp.int32, (1, 2 * B), 1) // (half * keep)
    for h in range(2):
        hi_ref, lo_ref = p_refs[2 * h : 2 * h + 2]
        w = w_ref[h, :1, :]
        rows = [bundles[rep ^ (2 * i + h), last:, :].astype(F32)[:keep] for i in range(half)]
        rows = jnp.concatenate(rows * nb, axis=0).T
        for g in range(hi_ref.shape[1] // (2 * B)):
            num = rows[g * nb : g * nb + 1]
            for j in range(1, nb):
                num = jnp.where(block == j, rows[g * nb + j : g * nb + j + 1], num)
            hot = jnp.where(freq == num, 1.0, 0.0).astype(BF16)
            y = dot(tall[:, :B], hot)
            hi, lo = split((y[:B] + y[B:]) * w)
            hi_ref[:, g * 2 * B : (g + 1) * 2 * B] = hi
            lo_ref[:, g * 2 * B : (g + 1) * 2 * B] = lo


def spread_rows(p_hi, p_lo, ships, g):
    half, keep = ships.shape[0], ships.shape[1]
    lane_block = lax.broadcasted_iota(jnp.int32, (half * keep, G), 1) // B
    s = jnp.concatenate([ships[i, :, g * G : (g + 1) * G].astype(F32) for i in range(half)], axis=0)
    w = jnp.concatenate(
        [jnp.where(lane_block == j, s, 0.0).astype(BF16) for j in range(G // B)], axis=0
    )
    cut = slice(g * 2 * B, (g + 1) * 2 * B)
    y = dot(jnp.concatenate([p_hi[:, cut], p_lo[:, cut]], axis=0), w)
    return y[:B] + y[B:]


def half_update_body(p_hi, p_lo, mine, out):
    for g in range(out.shape[0] // B):
        out[g * B : (g + 1) * B, :] = spread_rows(p_hi, p_lo, mine, g)


def update_body(chunk, half_sum, p_hi, p_lo, other, out, held, sems):
    ng = half_sum.shape[0] // B
    copies = []
    for c in range(0, ng, chunk):
        for g in range(c, c + chunk):
            held[:, g * G : (g + 1) * G] = half_sum[g * B : (g + 1) * B, :] + spread_rows(p_hi, p_lo, other, g)
        cut = pl.ds(c * G, chunk * G)
        copies.append(pltpu.make_async_copy(held.at[:, cut], out.at[:, cut], sems.at[c // chunk]))
        copies[-1].start()
    for copy in copies:
        copy.wait()


def input_grad_body(n_t, n_r, cp, bundles, *refs):
    ups, out, held = refs[:n_t], refs[n_t], refs[n_t + 1]
    nc = out.shape[1] // cp
    nr = B // (n_r // cp)
    tiles = nc // 128
    for r in range(n_r):
        r0, c0 = (r // cp) * nr, (r % cp) * nc
        for k in range(n_t):
            for j in range(tiles):
                at = (k * tiles + j) * nr
                held[k * B + r0 : k * B + r0 + nr, c0 + j * 128 : c0 + (j + 1) * 128] = bundles[r, at : at + nr, :]
    up = jnp.concatenate([u[:B, :] for u in ups], axis=0).T
    for c in range(0, out.shape[1], G):
        out[:, c : c + G] = dot(up, held[:, c : c + G]).astype(BF16)


def per_device(n_t, n_r, act, switch, slope, exp, vel, lines, mask, tally):
    cols = act.shape[1]
    width = exp.shape[1]
    tok = act.shape[0]
    keep = lines.shape[3]
    blocks = width // B
    groups = width // G
    cp = 2
    rp = n_r // cp
    half = n_r // 2
    tab, tall = constants()
    def shift(x, k):
        return lax.ppermute(x, "tensor", [(i, (i + k) % n_t) for i in range(n_t)])

    def swap(x, m):
        return lax.ppermute(x, "replica", [(i, i ^ m) for i in range(n_r)])

    own = lines[0, 0].T
    tiles = cols // cp // 128
    nr = B // rp
    *parts, act, own, tall = call(
        functools.partial(first_body, n_t, cp, cols, nr),
        [near((B + tiles * nr, 128))] * n_t
        + [near(act.shape), near(own.shape, jnp.int32), near(tall.shape)],
        (far(switch.T), far(slope.T), far(exp), far(act), far(own), far(tall)),
        [ANY] * 6,
        [VM] * (n_t + 3),
        scratch=[
            pltpu.VMEM((B, tok), BF16),
            pltpu.VMEM((B, tok), BF16),
            pltpu.VMEM((nr, width), BF16),
            pltpu.SemaphoreType.DMA((6,)),
        ],
        nbytes=act.size * 4 + nr * width * 2,
        name="up_grads",
    )
    parts = [parts[0]] + [shift(parts[k], k) for k in range(1, n_t)]

    p_own, a_own, shares = call(
        functools.partial(own_body, n_r, keep),
        [
            near((B, groups * 2 * B)),
            near((groups * B, 2 * B)),
            near((2, 8, 2 * B), F32),
        ],
        (far(mask), far(tally), own, tall),
        [ANY, ANY, VM, VM],
        [VM] * 3,
        scratch=[pltpu.SMEM((n_r,), jnp.int32)] * 2 + [pltpu.SemaphoreType.DMA((2,))],
        name="own_places",
    )

    def grads_of(ks, after):
        return call(
            functools.partial(grads_body, len(ks)),
            [near((B, cols), BF16 if k else F32) for k in ks],
            (act, after, *[parts[k] for k in ks]),
            [VM, ANY] + [VM] * len(ks),
            [VM] * len(ks),
            name="weight_grads",
        )

    grads = {}
    for k in range(1, n_t - 1):
        (grads[k],) = grads_of([k], act)
    made, grads[0] = grads_of([n_t - 1, 0], shares)
    grads[n_t - 1] = made
    grads = [grads[0]] + [shift(grads[k], -k) for k in range(1, n_t)]

    bundle = call(
        functools.partial(bundle_body, n_t, keep),
        near((n_t * tiles * nr + 16, 128)),
        (made, own, *parts),
        [ANY] + [VM] * (n_t + 1),
        VM,
        name="bundle",
    )
    bundles = lax.all_gather(bundle, "replica", axis=0)

    places = call(
        functools.partial(places_body, keep),
        [near((B, blocks * half * keep))] * 4,
        (shares, tall, bundles),
        [VM] * 3,
        [VM] * 4,
        name="places",
    )
    input_grad = call(
        functools.partial(input_grad_body, n_t, n_r, cp),
        jax.ShapeDtypeStruct((tok, cols), BF16),
        (bundles, *parts),
        [VM] * (1 + n_t),
        VM,
        scratch=[pltpu.VMEM((n_t * B, cols), BF16)],
        flops=2 * tok * n_t * B * cols,
        nbytes=(n_t * B * cols + tok * cols) * 2,
        name="input_grads",
    )

    rows = []
    for ks in (list(range(n_t - 1)), [n_t - 1]):
        rows = call(
            functools.partial(kept_body, ks, n_t, keep),
            [near((keep, width)), near((keep, width), F32)],
            (vel[0], a_own, tab, bundles, *[grads[k] for k in ks], *rows),
            [VM] * 3 + [ANY] + [VM] * (len(ks) + len(rows)),
            [VM] * 2,
            flops=6 * B * B * cols * len(ks),
            nbytes=B * cols * 6 * len(ks),
            name="kept_rows",
            alias={4 + len(ks): 0, 5 + len(ks): 1} if rows else {},
        )
    ship, q_own = rows
    ships = [ship] + [swap(ship, 2 * i) for i in range(1, half)]
    new = call(
        functools.partial(return_body, n_t, keep),
        jax.ShapeDtypeStruct((B, width), F32),
        (vel[0], p_own, q_own, *grads),
        [VM] * (3 + n_t),
        ANY,
        scratch=[pltpu.VMEM((B, width), F32), pltpu.SemaphoreType.DMA((n_t,))],
        flops=6 * B * B * width,
        nbytes=B * width * 10,
        name="new_momentums",
    )
    mine = call(
        functools.partial(join_body, half),
        near((half, keep, width)),
        (*ships, far(new), far(input_grad), places[0]),
        [VM] * half + [ANY] * 3,
        VM,
        name="join_kept",
    )
    other = swap(mine, 1)
    half_sum = call(
        half_update_body,
        near((groups * B, G), F32),
        (*places[:2], mine),
        [VM] * 3,
        VM,
        name="half_updates",
    )
    chunk = next(c for c in (5, 4, 3, 2, 1) if groups % c == 0)
    update = call(
        functools.partial(update_body, chunk),
        jax.ShapeDtypeStruct((B, width), F32),
        (half_sum, *places[2:], other),
        [VM] * 4,
        ANY,
        scratch=[
            pltpu.VMEM((B, width), F32),
            pltpu.SemaphoreType.DMA((groups // chunk,)),
        ],
        flops=8 * B * G * width,
        nbytes=B * width * 8,
        name="updates",
    )
    return input_grad, new[None], update


def per_device_plain(
    projection_inputs,
    switch_logits_raw,
    inner_neuron_slope,
    expansion_matrix,
    velocity_buffer,
    sent_spectral_lines,
    participant_mask,
    token_tallies,
):
    highest = lax.Precision.HIGHEST
    up_grad = (
        inner_neuron_slope.astype(jnp.float32) * jax.nn.silu(switch_logits_raw.astype(jnp.float32))
    ).astype(jnp.bfloat16)
    partial_terms = jnp.dot(up_grad, expansion_matrix, preferred_element_type=jnp.float32)
    input_grad = lax.psum_scatter(partial_terms, "tensor", scatter_dimension=1, tiled=True).astype(
        jnp.bfloat16
    )
    grad_w = lax.dot_general(
        up_grad,
        lax.all_gather(projection_inputs, "tensor", axis=1, tiled=True),
        (((0,), (0,)), ((), ())),
        preferred_element_type=jnp.float32,
    )
    row_total_count = expansion_matrix.shape[0] // 64
    col_count = expansion_matrix.shape[1] // 64
    moment = momentum_decay * velocity_buffer[0] + grad_w
    cosines = cosine_table()
    blocks = moment.reshape(row_total_count, 64, col_count, 64).transpose(0, 2, 1, 3)
    coefficients = jnp.einsum("fa,ijab,gb->ijfg", cosines, blocks, cosines, precision=highest)
    freq_ids = jnp.arange(64, dtype=jnp.int32)
    own_rows = sent_spectral_lines[0]
    chosen = (own_rows[..., None] == freq_ids).astype(jnp.float32)
    shipped = jnp.einsum("ijkf,ijfg->ijkg", chosen, coefficients, precision=highest).astype(
        jnp.bfloat16
    )
    spectrum = jnp.einsum("ijkf,ijkg->ijfg", chosen, shipped.astype(jnp.float32), precision=highest)
    returned = jnp.einsum("fa,ijfg,gb->ijab", cosines, spectrum, cosines, precision=highest)
    new_moment = moment - returned.transpose(0, 2, 1, 3).reshape(moment.shape)
    worker_burdens = participant_mask.astype(jnp.float32) * token_tallies.astype(jnp.float32)
    worker_fractions = worker_burdens * (
        jnp.sum(participant_mask.astype(jnp.float32)) / jnp.sum(worker_burdens)
    )
    myself = lax.axis_index("replica")
    combined = lax.psum(worker_fractions[myself] * spectrum, "replica")
    update = jnp.einsum("fa,ijfg,gb->ijab", cosines, combined, cosines, precision=highest)
    update = update.transpose(0, 2, 1, 3).reshape(moment.shape)
    return (input_grad, new_moment[None], update)


def solution(mesh):
    n_t, n_r = mesh.shape["tensor"], mesh.shape["replica"]

    def device(*args):
        act, exp, lines = args[0], args[3], args[5]
        fits = (
            act.shape[1] % G == 0
            and act.shape[0] % 128 == 0
            and exp.shape[0] == B
            and lines.shape[3] == 8
            and n_r == 8
        )
        if not fits:
            return per_device_plain(*args)
        return per_device(n_t, n_r, *args)

    return jax.shard_map(
        device,
        mesh=mesh,
        in_specs=(
            P("replica", "tensor"),
            P("replica", "tensor"),
            P("replica", "tensor"),
            P("tensor", None),
            P("replica", "tensor", None),
            P("replica", "tensor", None, None),
            P(),
            P(),
        ),
        out_specs=(P("replica", "tensor"), P("replica", "tensor", None), P("tensor", None)),
        check_vma=False,
    )
```

```python
import functools

import jax
import jax.numpy as jnp
import numpy as np
from jax import lax
from jax.experimental import pallas as pl
from jax.experimental.pallas import tpu as pltpu
from jax.sharding import PartitionSpec as P

momentum_decay = 0.9
B = 64
G = 256
F32 = jnp.float32
BF16 = jnp.bfloat16
VMEM_LIMIT = 24 * 1024 * 1024

VM = pl.BlockSpec(memory_space=pltpu.VMEM)
SM = pl.BlockSpec(memory_space=pltpu.SMEM)
ANY = pl.BlockSpec(memory_space=pl.ANY)


def cosine_table():
    freqs = jnp.arange(64, dtype=jnp.float32)[:, None]
    places = jnp.arange(64, dtype=jnp.float32)[None, :]
    cosines = jnp.cos(jnp.pi * (places + 0.5) * freqs / 64.0) * jnp.sqrt(2.0 / 64.0)
    return cosines.at[0].multiply(jnp.sqrt(0.5))


def cosine_np():
    f = np.arange(B)[:, None]
    a = np.arange(B)[None, :]
    c = np.cos(np.pi * (a + 0.5) * f / B) * np.sqrt(2.0 / B)
    c[0] *= np.sqrt(0.5)
    return c


def halves(c):
    hi = np.asarray(c, dtype=np.float32).astype(jnp.bfloat16)
    lo = (np.asarray(c, np.float64) - hi.astype(np.float64)).astype(np.float32).astype(jnp.bfloat16)
    return hi, lo


def constants():
    hi, lo = halves(cosine_np())
    eye = np.eye(G // B)
    kron = lambda x: np.kron(eye, np.asarray(x, np.float32)).astype(jnp.bfloat16)
    tall = np.zeros((2 * B, 2 * B), jnp.bfloat16)
    tall[:B, :B], tall[B:, :B] = hi.T, lo.T
    return jnp.asarray(np.concatenate([kron(x) for x in (hi.T, lo.T, hi, lo)], axis=0)), jnp.asarray(tall)


def fwd(tab, i):
    return tab[i * G : (i + 1) * G, :]


def inv(tab, i):
    return tab[(2 + i) * G : (3 + i) * G, :]


def dot(a, b):
    return jnp.dot(a, b, preferred_element_type=F32)


def split(x):
    hi = x.astype(BF16)
    return hi, (x - hi.astype(F32)).astype(BF16)


def near(shape, dtype=BF16):
    return pltpu.VMEM(shape, dtype)


def far(x):
    return pltpu.with_memory_space_constraint(x, pltpu.HBM)


def call(body, out_shape, ins, in_specs, out_specs, scratch=(), flops=0, nbytes=0, name=None, alias={}):
    return pl.pallas_call(
        body,
        out_shape=out_shape,
        in_specs=in_specs,
        out_specs=out_specs,
        scratch_shapes=scratch,
        input_output_aliases=alias,
        compiler_params=pltpu.CompilerParams(vmem_limit_bytes=VMEM_LIMIT),
        cost_estimate=pl.CostEstimate(flops=flops, bytes_accessed=nbytes, transcendentals=0),
        name=name,
    )(*ins)


def first_body(n_t, cp, cols, nr, switch, slope, exp_ref, act, lines, tall, *refs):
    outs, (act_out, lines_out, tall_out) = refs[:n_t], refs[n_t : n_t + 3]
    switch_v, slope_v, exp_v, sems = refs[n_t + 3 :]
    rep, ten = lax.axis_index("replica"), lax.axis_index("tensor")
    r0 = pl.multiple_of((rep // cp) * nr, nr)
    copies = [
        pltpu.make_async_copy(src, dst, sems.at[i])
        for i, (src, dst) in enumerate(
            [
                (switch, switch_v),
                (slope, slope_v),
                (exp_ref.at[pl.ds(r0, nr), :], exp_v),
                (act, act_out),
                (lines, lines_out),
                (tall, tall_out),
            ]
        )
    ]
    for copy in copies:
        copy.start()
    copies[0].wait()
    copies[1].wait()
    v = switch_v[...].astype(F32)
    up = (slope_v[...].astype(F32) * (v * jax.nn.sigmoid(v))).astype(BF16)
    for k in range(n_t):
        outs[k][:B, :] = up
    copies[2].wait()
    nc = cols // cp
    for k in range(n_t):
        c0 = (ten ^ k) * cols + lax.rem(rep, cp) * nc
        for j in range(nc // 128):
            at = pl.multiple_of(c0 + j * 128, 128)
            outs[k][B + j * nr : B + (j + 1) * nr, :] = exp_v[:, pl.ds(at, 128)]
    for copy in copies[3:]:
        copy.wait()


def grads_body(n, act, after, *refs):
    ups, outs = refs[:n], refs[n:]
    up = jnp.concatenate([u[:B, :] for u in ups], axis=0)
    for c in range(0, act.shape[1], G):
        g = dot(up, act[:, c : c + G])
        for k in range(n):
            outs[k][:, c : c + G] = g[k * B : (k + 1) * B].astype(outs[k].dtype)


def bundle_body(n_t, keep, after, lines, *refs):
    parts, out = refs[:n_t], refs[n_t]
    n = parts[0].shape[0] - B
    for k in range(n_t):
        out[k * n : (k + 1) * n, :] = parts[k][B:, :]
    blocks = lines.shape[1]
    rows = jnp.concatenate([lines[...].astype(F32), jnp.zeros((keep, 128 - blocks), F32)], axis=1)
    out[n_t * n :, :] = jnp.concatenate([rows, jnp.zeros((16 - keep, 128), F32)], axis=0).astype(BF16)


def join_body(n, *refs):
    for i, ref in enumerate(refs[:n]):
        refs[-1][i] = ref[...]


def own_body(n_r, keep, mask, tally, lines, tall, p_ref, a_ref, w_ref, mask_s, tally_s, sems):
    copies = [
        pltpu.make_async_copy(src, dst, sems.at[i])
        for i, (src, dst) in enumerate([(mask, mask_s), (tally, tally_s)])
    ]
    for copy in copies:
        copy.start()
    blocks = lines.shape[1]
    rows = jnp.concatenate([lines[...].astype(F32), jnp.zeros((keep, 128 - blocks), F32)], axis=1)
    rows = jnp.concatenate([rows] * (2 * B // keep), axis=0).T
    freq = lax.broadcasted_iota(jnp.int32, (B, 2 * B), 0).astype(F32)
    block = (lax.broadcasted_iota(jnp.int32, (1, 2 * B), 1) // keep) % (G // B)
    term = lax.broadcasted_iota(jnp.int32, (B, 2 * B), 1) // (B // 2)
    for g in range(blocks // (G // B)):
        num = rows[g * (G // B) : g * (G // B) + 1]
        for j in range(1, G // B):
            num = jnp.where(block == j, rows[g * (G // B) + j : g * (G // B) + j + 1], num)
        hot = jnp.where(freq == num, 1.0, 0.0).astype(BF16)
        y = dot(tall[:, :B], hot)
        p = jnp.where(term == 3, 0.0, jnp.where(term == 1, y[B:], y[:B]))
        p_ref[:, g * 2 * B : (g + 1) * 2 * B] = p.astype(BF16)
        a_ref[g * B : (g + 1) * B, :] = jnp.concatenate([p, p], axis=0).T[:B].astype(BF16)
    for copy in copies:
        copy.wait()
    total, alive = jnp.float32(0), jnp.float32(0)
    for r in range(n_r):
        m = mask_s[r].astype(F32)
        total = total + m * tally_s[r].astype(F32)
        alive = alive + m
    half = n_r // 2
    place = (lax.broadcasted_iota(jnp.int32, (8, 2 * B), 1) // keep) % half
    scale = jnp.full((8, 2 * B), alive) / jnp.full((8, 2 * B), total)
    for h in range(2):
        w = jnp.zeros((8, 2 * B), F32)
        for i in range(half):
            r = lax.axis_index("replica") ^ (2 * i + h)
            w = jnp.where(place == i, mask_s[r].astype(F32) * tally_s[r].astype(F32), w)
        w_ref[h] = w * scale


def kept_body(ks, n_t, keep, vel, a_ref, tab, after, *refs):
    grads, (send_ref, own_ref) = refs[: len(ks)], refs[-2:]
    cols = grads[0].shape[1]
    ng = cols // G
    lane_block = lax.broadcasted_iota(jnp.int32, (keep, G), 1) // B
    sel = []
    for n, k in enumerate(ks):
        c0 = (lax.axis_index("tensor") ^ k) * cols
        for i in range(ng):
            at = pl.multiple_of(c0 + i * G, G)
            moment = momentum_decay * vel[:, pl.ds(at, G)] + grads[n][:, i * G : (i + 1) * G].astype(F32)
            hi, lo = split(moment)
            y = dot(a_ref[pl.ds(pl.multiple_of(at // (G // B), B), B), :], jnp.concatenate([hi, lo], axis=0))
            y = y[: B // 2] + y[B // 2 :]
            got = y[:keep]
            for j in range(1, G // B):
                got = jnp.where(lane_block == j, y[j * keep : (j + 1) * keep], got)
            sel.append(got)
    hi, lo = split(jnp.concatenate(sel, axis=0))
    n = len(ks) * ng * keep
    y = dot(jnp.concatenate([hi, lo], axis=0), fwd(tab, 0))
    kept = (y[:n] + y[n:] + dot(hi, fwd(tab, 1))).astype(BF16)
    q = dot(kept, inv(tab, 0)) + dot(kept, inv(tab, 1))
    for n, k in enumerate(ks):
        c0 = pl.multiple_of((lax.axis_index("tensor") ^ k) * cols, G)
        part = jnp.concatenate([q[(n * ng + i) * keep : (n * ng + i + 1) * keep] for i in range(ng)], axis=1)
        own_ref[:, pl.ds(c0, cols)] = part
        send_ref[:, pl.ds(c0, cols)] = part.astype(BF16)


def return_body(n_t, keep, vel, p_ref, q, *refs):
    grads, (new_ref, held, sems) = refs[:n_t], refs[n_t:]
    cols = grads[0].shape[1]
    ng = cols // G
    lane_block = lax.broadcasted_iota(jnp.int32, (keep, G), 1) // B
    copies = []
    for k in range(n_t):
        c0 = pl.multiple_of((lax.axis_index("tensor") ^ k) * cols, G)
        for i in range(ng):
            at = pl.multiple_of(c0 + i * G, G)
            own = q[:, pl.ds(at, G)]
            spread = jnp.concatenate(
                [jnp.where(lane_block == j, own, 0.0) for j in range(G // B)], axis=0
            )
            hi, lo = split(spread)
            w = jnp.concatenate([hi, hi, lo, jnp.zeros_like(lo)], axis=0)
            back = dot(p_ref[:, pl.ds(pl.multiple_of(at // 2, 2 * B), 2 * B)], w)
            moment = momentum_decay * vel[:, pl.ds(at, G)] + grads[k][:, i * G : (i + 1) * G].astype(F32)
            held[:, pl.ds(at, G)] = moment - back
        cut = pl.ds(c0, cols)
        copies.append(pltpu.make_async_copy(held.at[:, cut], new_ref.at[:, cut], sems.at[k]))
        copies[-1].start()
    for copy in copies:
        copy.wait()


def places_body(keep, w_ref, tall, bundles, *p_refs):
    n_r, last = bundles.shape[0], bundles.shape[1] - 16
    half, nb = n_r // 2, G // B
    rep = lax.axis_index("replica")
    freq = lax.broadcasted_iota(jnp.int32, (B, 2 * B), 0).astype(F32)
    block = lax.broadcasted_iota(jnp.int32, (1, 2 * B), 1) // (half * keep)
    for h in range(2):
        hi_ref, lo_ref = p_refs[2 * h : 2 * h + 2]
        w = w_ref[h, :1, :]
        rows = [bundles[rep ^ (2 * i + h), last:, :].astype(F32)[:keep] for i in range(half)]
        rows = jnp.concatenate(rows * nb, axis=0).T
        for g in range(hi_ref.shape[1] // (2 * B)):
            num = rows[g * nb : g * nb + 1]
            for j in range(1, nb):
                num = jnp.where(block == j, rows[g * nb + j : g * nb + j + 1], num)
            hot = jnp.where(freq == num, 1.0, 0.0).astype(BF16)
            y = dot(tall[:, :B], hot)
            hi, lo = split((y[:B] + y[B:]) * w)
            hi_ref[:, g * 2 * B : (g + 1) * 2 * B] = hi
            lo_ref[:, g * 2 * B : (g + 1) * 2 * B] = lo


def spread_rows(p_hi, p_lo, ships, g):
    half, keep = ships.shape[0], ships.shape[1]
    lane_block = lax.broadcasted_iota(jnp.int32, (half * keep, G), 1) // B
    s = jnp.concatenate([ships[i, :, g * G : (g + 1) * G].astype(F32) for i in range(half)], axis=0)
    w = jnp.concatenate(
        [jnp.where(lane_block == j, s, 0.0).astype(BF16) for j in range(G // B)], axis=0
    )
    cut = slice(g * 2 * B, (g + 1) * 2 * B)
    y = dot(jnp.concatenate([p_hi[:, cut], p_lo[:, cut]], axis=0), w)
    return y[:B] + y[B:]


def half_update_body(p_hi, p_lo, mine, out):
    for g in range(out.shape[0] // B):
        out[g * B : (g + 1) * B, :] = spread_rows(p_hi, p_lo, mine, g)


def update_body(chunk, half_sum, p_hi, p_lo, other, out, held, sems):
    ng = half_sum.shape[0] // B
    copies = []
    for c in range(0, ng, chunk):
        for g in range(c, c + chunk):
            held[:, g * G : (g + 1) * G] = half_sum[g * B : (g + 1) * B, :] + spread_rows(p_hi, p_lo, other, g)
        cut = pl.ds(c * G, chunk * G)
        copies.append(pltpu.make_async_copy(held.at[:, cut], out.at[:, cut], sems.at[c // chunk]))
        copies[-1].start()
    for copy in copies:
        copy.wait()


def input_grad_body(n_t, n_r, cp, bundles, *refs):
    ups, out, held = refs[:n_t], refs[n_t], refs[n_t + 1]
    nc = out.shape[1] // cp
    nr = B // (n_r // cp)
    tiles = nc // 128
    for r in range(n_r):
        r0, c0 = (r // cp) * nr, (r % cp) * nc
        for k in range(n_t):
            for j in range(tiles):
                at = (k * tiles + j) * nr
                held[k * B + r0 : k * B + r0 + nr, c0 + j * 128 : c0 + (j + 1) * 128] = bundles[r, at : at + nr, :]
    up = jnp.concatenate([u[:B, :] for u in ups], axis=0).T
    for c in range(0, out.shape[1], G):
        out[:, c : c + G] = dot(up, held[:, c : c + G]).astype(BF16)


def per_device(n_t, n_r, act, switch, slope, exp, vel, lines, mask, tally):
    cols = act.shape[1]
    width = exp.shape[1]
    tok = act.shape[0]
    keep = lines.shape[3]
    blocks = width // B
    groups = width // G
    cp = 2
    rp = n_r // cp
    half = n_r // 2
    tab, tall = constants()
    def trade(x, k):
        return lax.ppermute(x, "tensor", [(i, i ^ k) for i in range(n_t)])

    order = [*range(2, n_t), 1]

    def swap(x, m):
        return lax.ppermute(x, "replica", [(i, i ^ m) for i in range(n_r)])

    own = lines[0, 0].T
    tiles = cols // cp // 128
    nr = B // rp
    *parts, act, own, tall = call(
        functools.partial(first_body, n_t, cp, cols, nr),
        [near((B + tiles * nr, 128))] * n_t
        + [near(act.shape), near(own.shape, jnp.int32), near(tall.shape)],
        (far(switch.T), far(slope.T), far(exp), far(act), far(own), far(tall)),
        [ANY] * 6,
        [VM] * (n_t + 3),
        scratch=[
            pltpu.VMEM((B, tok), BF16),
            pltpu.VMEM((B, tok), BF16),
            pltpu.VMEM((nr, width), BF16),
            pltpu.SemaphoreType.DMA((6,)),
        ],
        nbytes=act.size * 4 + nr * width * 2,
        name="up_grads",
    )
    got = {k: trade(parts[k], k) for k in order}
    parts = [parts[0]] + [got[k] for k in range(1, n_t)]

    p_own, a_own, shares = call(
        functools.partial(own_body, n_r, keep),
        [
            near((B, groups * 2 * B)),
            near((groups * B, 2 * B)),
            near((2, 8, 2 * B), F32),
        ],
        (far(mask), far(tally), own, tall),
        [ANY, ANY, VM, VM],
        [VM] * 3,
        scratch=[pltpu.SMEM((n_r,), jnp.int32)] * 2 + [pltpu.SemaphoreType.DMA((2,))],
        name="own_places",
    )

    def grads_of(ks, after):
        return call(
            functools.partial(grads_body, len(ks)),
            [near((B, cols), BF16 if k else F32) for k in ks],
            (act, after, *[parts[k] for k in ks]),
            [VM, ANY] + [VM] * len(ks),
            [VM] * len(ks),
            name="weight_grads",
        )

    grads = {}
    for k in order[:-1]:
        (grads[k],) = grads_of([k], act)
    made, grads[0] = grads_of([order[-1], 0], shares)
    grads[order[-1]] = made
    grads.update({k: trade(grads[k], k) for k in order})

    bundle = call(
        functools.partial(bundle_body, n_t, keep),
        near((n_t * tiles * nr + 16, 128)),
        (made, own, *parts),
        [ANY] + [VM] * (n_t + 1),
        VM,
        name="bundle",
    )
    bundles = lax.all_gather(bundle, "replica", axis=0)

    places = call(
        functools.partial(places_body, keep),
        [near((B, blocks * half * keep))] * 4,
        (shares, tall, bundles),
        [VM] * 3,
        [VM] * 4,
        name="places",
    )
    input_grad = call(
        functools.partial(input_grad_body, n_t, n_r, cp),
        jax.ShapeDtypeStruct((tok, cols), BF16),
        (bundles, *parts),
        [VM] * (1 + n_t),
        VM,
        scratch=[pltpu.VMEM((n_t * B, cols), BF16)],
        flops=2 * tok * n_t * B * cols,
        nbytes=(n_t * B * cols + tok * cols) * 2,
        name="input_grads",
    )

    rows = []
    for ks in ([k for k in range(n_t) if k != n_t - 1], [n_t - 1]):
        rows = call(
            functools.partial(kept_body, ks, n_t, keep),
            [near((keep, width)), near((keep, width), F32)],
            (vel[0], a_own, tab, bundles, *[grads[k] for k in ks], *rows),
            [VM] * 3 + [ANY] + [VM] * (len(ks) + len(rows)),
            [VM] * 2,
            flops=6 * B * B * cols * len(ks),
            nbytes=B * cols * 6 * len(ks),
            name="kept_rows",
            alias={4 + len(ks): 0, 5 + len(ks): 1} if rows else {},
        )
    ship, q_own = rows
    ships = [ship] + [swap(ship, 2 * i) for i in range(1, half)]
    new = call(
        functools.partial(return_body, n_t, keep),
        jax.ShapeDtypeStruct((B, width), F32),
        (vel[0], p_own, q_own, *[grads[k] for k in range(n_t)]),
        [VM] * (3 + n_t),
        ANY,
        scratch=[pltpu.VMEM((B, width), F32), pltpu.SemaphoreType.DMA((n_t,))],
        flops=6 * B * B * width,
        nbytes=B * width * 10,
        name="new_momentums",
    )
    mine = call(
        functools.partial(join_body, half),
        near((half, keep, width)),
        (*ships, far(new), far(input_grad), places[0]),
        [VM] * half + [ANY] * 3,
        VM,
        name="join_kept",
    )
    other = swap(mine, 1)
    half_sum = call(
        half_update_body,
        near((groups * B, G), F32),
        (*places[:2], mine),
        [VM] * 3,
        VM,
        name="half_updates",
    )
    chunk = next(c for c in (5, 4, 3, 2, 1) if groups % c == 0)
    update = call(
        functools.partial(update_body, chunk),
        jax.ShapeDtypeStruct((B, width), F32),
        (half_sum, *places[2:], other),
        [VM] * 4,
        ANY,
        scratch=[
            pltpu.VMEM((B, width), F32),
            pltpu.SemaphoreType.DMA((groups // chunk,)),
        ],
        flops=8 * B * G * width,
        nbytes=B * width * 8,
        name="updates",
    )
    return input_grad, new[None], update


def per_device_plain(
    projection_inputs,
    switch_logits_raw,
    inner_neuron_slope,
    expansion_matrix,
    velocity_buffer,
    sent_spectral_lines,
    participant_mask,
    token_tallies,
):
    highest = lax.Precision.HIGHEST
    up_grad = (
        inner_neuron_slope.astype(jnp.float32) * jax.nn.silu(switch_logits_raw.astype(jnp.float32))
    ).astype(jnp.bfloat16)
    partial_terms = jnp.dot(up_grad, expansion_matrix, preferred_element_type=jnp.float32)
    input_grad = lax.psum_scatter(partial_terms, "tensor", scatter_dimension=1, tiled=True).astype(
        jnp.bfloat16
    )
    grad_w = lax.dot_general(
        up_grad,
        lax.all_gather(projection_inputs, "tensor", axis=1, tiled=True),
        (((0,), (0,)), ((), ())),
        preferred_element_type=jnp.float32,
    )
    row_total_count = expansion_matrix.shape[0] // 64
    col_count = expansion_matrix.shape[1] // 64
    moment = momentum_decay * velocity_buffer[0] + grad_w
    cosines = cosine_table()
    blocks = moment.reshape(row_total_count, 64, col_count, 64).transpose(0, 2, 1, 3)
    coefficients = jnp.einsum("fa,ijab,gb->ijfg", cosines, blocks, cosines, precision=highest)
    freq_ids = jnp.arange(64, dtype=jnp.int32)
    own_rows = sent_spectral_lines[0]
    chosen = (own_rows[..., None] == freq_ids).astype(jnp.float32)
    shipped = jnp.einsum("ijkf,ijfg->ijkg", chosen, coefficients, precision=highest).astype(
        jnp.bfloat16
    )
    spectrum = jnp.einsum("ijkf,ijkg->ijfg", chosen, shipped.astype(jnp.float32), precision=highest)
    returned = jnp.einsum("fa,ijfg,gb->ijab", cosines, spectrum, cosines, precision=highest)
    new_moment = moment - returned.transpose(0, 2, 1, 3).reshape(moment.shape)
    worker_burdens = participant_mask.astype(jnp.float32) * token_tallies.astype(jnp.float32)
    worker_fractions = worker_burdens * (
        jnp.sum(participant_mask.astype(jnp.float32)) / jnp.sum(worker_burdens)
    )
    myself = lax.axis_index("replica")
    combined = lax.psum(worker_fractions[myself] * spectrum, "replica")
    update = jnp.einsum("fa,ijfg,gb->ijab", cosines, combined, cosines, precision=highest)
    update = update.transpose(0, 2, 1, 3).reshape(moment.shape)
    return (input_grad, new_moment[None], update)


def solution(mesh):
    n_t, n_r = mesh.shape["tensor"], mesh.shape["replica"]

    def device(*args):
        act, exp, lines = args[0], args[3], args[5]
        fits = (
            act.shape[1] % G == 0
            and act.shape[0] % 128 == 0
            and exp.shape[0] == B
            and lines.shape[3] == 8
            and n_r == 8
            and n_t >= 2
            and n_t & (n_t - 1) == 0
        )
        if not fits:
            return per_device_plain(*args)
        return per_device(n_t, n_r, *args)

    return jax.shard_map(
        device,
        mesh=mesh,
        in_specs=(
            P("replica", "tensor"),
            P("replica", "tensor"),
            P("replica", "tensor"),
            P("tensor", None),
            P("replica", "tensor", None),
            P("replica", "tensor", None, None),
            P(),
            P(),
        ),
        out_specs=(P("replica", "tensor"), P("replica", "tensor", None), P("tensor", None)),
        check_vma=False,
    )
```

```python
import functools

import jax
import jax.numpy as jnp
import numpy as np
from jax import lax
from jax.experimental import pallas as pl
from jax.experimental.pallas import tpu as pltpu
from jax.sharding import PartitionSpec as P

momentum_decay = 0.9
B = 64
G = 256
F32 = jnp.float32
BF16 = jnp.bfloat16
VMEM_LIMIT = 24 * 1024 * 1024

VM = pl.BlockSpec(memory_space=pltpu.VMEM)
SM = pl.BlockSpec(memory_space=pltpu.SMEM)
ANY = pl.BlockSpec(memory_space=pl.ANY)


def cosine_table():
    freqs = jnp.arange(64, dtype=jnp.float32)[:, None]
    places = jnp.arange(64, dtype=jnp.float32)[None, :]
    cosines = jnp.cos(jnp.pi * (places + 0.5) * freqs / 64.0) * jnp.sqrt(2.0 / 64.0)
    return cosines.at[0].multiply(jnp.sqrt(0.5))


def cosine_np():
    f = np.arange(B)[:, None]
    a = np.arange(B)[None, :]
    c = np.cos(np.pi * (a + 0.5) * f / B) * np.sqrt(2.0 / B)
    c[0] *= np.sqrt(0.5)
    return c


def halves(c):
    hi = np.asarray(c, dtype=np.float32).astype(jnp.bfloat16)
    lo = (np.asarray(c, np.float64) - hi.astype(np.float64)).astype(np.float32).astype(jnp.bfloat16)
    return hi, lo


def constants():
    hi, lo = halves(cosine_np())
    eye = np.eye(G // B)
    kron = lambda x: np.kron(eye, np.asarray(x, np.float32)).astype(jnp.bfloat16)
    tall = np.zeros((2 * B, 2 * B), jnp.bfloat16)
    tall[:B, :B], tall[B:, :B] = hi.T, lo.T
    return jnp.asarray(np.concatenate([kron(x) for x in (hi.T, lo.T, hi, lo)], axis=0)), jnp.asarray(tall)


def fwd(tab, i):
    return tab[i * G : (i + 1) * G, :]


def inv(tab, i):
    return tab[(2 + i) * G : (3 + i) * G, :]


def dot(a, b):
    return jnp.dot(a, b, preferred_element_type=F32)


def split(x):
    hi = x.astype(BF16)
    return hi, (x - hi.astype(F32)).astype(BF16)


def near(shape, dtype=BF16):
    return pltpu.VMEM(shape, dtype)


def far(x):
    return pltpu.with_memory_space_constraint(x, pltpu.HBM)


def call(body, out_shape, ins, in_specs, out_specs, scratch=(), flops=0, nbytes=0, name=None, alias={}):
    return pl.pallas_call(
        body,
        out_shape=out_shape,
        in_specs=in_specs,
        out_specs=out_specs,
        scratch_shapes=scratch,
        input_output_aliases=alias,
        compiler_params=pltpu.CompilerParams(vmem_limit_bytes=VMEM_LIMIT),
        cost_estimate=pl.CostEstimate(flops=flops, bytes_accessed=nbytes, transcendentals=0),
        name=name,
    )(*ins)


def first_body(n_t, cp, cols, nr, switch, slope, exp_ref, act, lines, tall, *refs):
    outs, (act_out, lines_out, tall_out) = refs[:n_t], refs[n_t : n_t + 3]
    switch_v, slope_v, exp_v, sems = refs[n_t + 3 :]
    rep, ten = lax.axis_index("replica"), lax.axis_index("tensor")
    r0 = pl.multiple_of((rep // cp) * nr, nr)
    copies = [
        pltpu.make_async_copy(src, dst, sems.at[i])
        for i, (src, dst) in enumerate(
            [
                (switch, switch_v),
                (slope, slope_v),
                (exp_ref.at[pl.ds(r0, nr), :], exp_v),
                (act, act_out),
                (lines, lines_out),
                (tall, tall_out),
            ]
        )
    ]
    for copy in copies:
        copy.start()
    copies[0].wait()
    copies[1].wait()
    v = switch_v[...].astype(F32)
    up = (slope_v[...].astype(F32) * (v * jax.nn.sigmoid(v))).astype(BF16)
    for k in range(n_t):
        outs[k][:B, :] = up
    copies[2].wait()
    nc = cols // cp
    for k in range(n_t):
        c0 = (ten ^ k) * cols + lax.rem(rep, cp) * nc
        for j in range(nc // 128):
            at = pl.multiple_of(c0 + j * 128, 128)
            outs[k][B + j * nr : B + (j + 1) * nr, :] = exp_v[:, pl.ds(at, 128)]
    for copy in copies[3:]:
        copy.wait()


def grads_body(n, act, after, *refs):
    ups, outs = refs[:n], refs[n:]
    up = jnp.concatenate([u[:B, :] for u in ups], axis=0)
    for c in range(0, act.shape[1], G):
        g = dot(up, act[:, c : c + G])
        for k in range(n):
            outs[k][:, c : c + G] = g[k * B : (k + 1) * B].astype(outs[k].dtype)


def bundle_body(n_t, keep, after, lines, *refs):
    parts, out = refs[:n_t], refs[n_t]
    n = parts[0].shape[0] - B
    for k in range(n_t):
        out[k * n : (k + 1) * n, :] = parts[k][B:, :]
    blocks = lines.shape[1]
    rows = jnp.concatenate([lines[...].astype(F32), jnp.zeros((keep, 128 - blocks), F32)], axis=1)
    out[n_t * n :, :] = jnp.concatenate([rows, jnp.zeros((16 - keep, 128), F32)], axis=0).astype(BF16)


def join_body(n, *refs):
    for i, ref in enumerate(refs[:n]):
        refs[-1][i] = ref[...]


def own_body(n_r, keep, mask, tally, lines, tall, p_ref, a_ref, w_ref, mask_s, tally_s, sems):
    copies = [
        pltpu.make_async_copy(src, dst, sems.at[i])
        for i, (src, dst) in enumerate([(mask, mask_s), (tally, tally_s)])
    ]
    for copy in copies:
        copy.start()
    blocks = lines.shape[1]
    rows = jnp.concatenate([lines[...].astype(F32), jnp.zeros((keep, 128 - blocks), F32)], axis=1)
    rows = jnp.concatenate([rows] * (2 * B // keep), axis=0).T
    freq = lax.broadcasted_iota(jnp.int32, (B, 2 * B), 0).astype(F32)
    block = (lax.broadcasted_iota(jnp.int32, (1, 2 * B), 1) // keep) % (G // B)
    term = lax.broadcasted_iota(jnp.int32, (B, 2 * B), 1) // (B // 2)
    for g in range(blocks // (G // B)):
        num = rows[g * (G // B) : g * (G // B) + 1]
        for j in range(1, G // B):
            num = jnp.where(block == j, rows[g * (G // B) + j : g * (G // B) + j + 1], num)
        hot = jnp.where(freq == num, 1.0, 0.0).astype(BF16)
        y = dot(tall[:, :B], hot)
        p = jnp.where(term == 3, 0.0, jnp.where(term == 1, y[B:], y[:B]))
        p_ref[:, g * 2 * B : (g + 1) * 2 * B] = p.astype(BF16)
        a_ref[g * B : (g + 1) * B, :] = jnp.concatenate([p, p], axis=0).T[:B].astype(BF16)
    for copy in copies:
        copy.wait()
    total, alive = jnp.float32(0), jnp.float32(0)
    for r in range(n_r):
        m = mask_s[r].astype(F32)
        total = total + m * tally_s[r].astype(F32)
        alive = alive + m
    half = n_r // 2
    place = (lax.broadcasted_iota(jnp.int32, (8, 2 * B), 1) // keep) % half
    scale = jnp.full((8, 2 * B), alive) / jnp.full((8, 2 * B), total)
    for h in range(2):
        w = jnp.zeros((8, 2 * B), F32)
        for i in range(half):
            r = lax.axis_index("replica") ^ (2 * i + h)
            w = jnp.where(place == i, mask_s[r].astype(F32) * tally_s[r].astype(F32), w)
        w_ref[h] = w * scale


def kept_body(ks, n_t, keep, vel, a_ref, tab, after, *refs):
    grads, (send_ref, own_ref) = refs[: len(ks)], refs[-2:]
    cols = grads[0].shape[1]
    ng = cols // G
    lane_block = lax.broadcasted_iota(jnp.int32, (keep, G), 1) // B
    sel = []
    for n, k in enumerate(ks):
        c0 = (lax.axis_index("tensor") ^ k) * cols
        for i in range(ng):
            at = pl.multiple_of(c0 + i * G, G)
            moment = momentum_decay * vel[:, pl.ds(at, G)] + grads[n][:, i * G : (i + 1) * G].astype(F32)
            hi, lo = split(moment)
            y = dot(a_ref[pl.ds(pl.multiple_of(at // (G // B), B), B), :], jnp.concatenate([hi, lo], axis=0))
            y = y[: B // 2] + y[B // 2 :]
            got = y[:keep]
            for j in range(1, G // B):
                got = jnp.where(lane_block == j, y[j * keep : (j + 1) * keep], got)
            sel.append(got)
    hi, lo = split(jnp.concatenate(sel, axis=0))
    n = len(ks) * ng * keep
    y = dot(jnp.concatenate([hi, lo], axis=0), fwd(tab, 0))
    kept = (y[:n] + y[n:] + dot(hi, fwd(tab, 1))).astype(BF16)
    q = dot(kept, inv(tab, 0)) + dot(kept, inv(tab, 1))
    for n, k in enumerate(ks):
        c0 = pl.multiple_of((lax.axis_index("tensor") ^ k) * cols, G)
        part = jnp.concatenate([q[(n * ng + i) * keep : (n * ng + i + 1) * keep] for i in range(ng)], axis=1)
        own_ref[:, pl.ds(c0, cols)] = part
        send_ref[:, pl.ds(c0, cols)] = part.astype(BF16)


def return_body(n_t, keep, vel, p_ref, q, *refs):
    grads, (new_ref, held, sems) = refs[:n_t], refs[n_t:]
    cols = grads[0].shape[1]
    ng = cols // G
    lane_block = lax.broadcasted_iota(jnp.int32, (keep, G), 1) // B
    copies = []
    for k in range(n_t):
        c0 = pl.multiple_of((lax.axis_index("tensor") ^ k) * cols, G)
        for i in range(ng):
            at = pl.multiple_of(c0 + i * G, G)
            own = q[:, pl.ds(at, G)]
            spread = jnp.concatenate(
                [jnp.where(lane_block == j, own, 0.0) for j in range(G // B)], axis=0
            )
            hi, lo = split(spread)
            w = jnp.concatenate([hi, hi, lo, jnp.zeros_like(lo)], axis=0)
            back = dot(p_ref[:, pl.ds(pl.multiple_of(at // 2, 2 * B), 2 * B)], w)
            moment = momentum_decay * vel[:, pl.ds(at, G)] + grads[k][:, i * G : (i + 1) * G].astype(F32)
            held[:, pl.ds(at, G)] = moment - back
        cut = pl.ds(c0, cols)
        copies.append(pltpu.make_async_copy(held.at[:, cut], new_ref.at[:, cut], sems.at[k]))
        copies[-1].start()
    for copy in copies:
        copy.wait()


def places_body(keep, w_ref, tall, bundles, *p_refs):
    n_r, last = bundles.shape[0], bundles.shape[1] - 16
    half, nb = n_r // 2, G // B
    rep = lax.axis_index("replica")
    freq = lax.broadcasted_iota(jnp.int32, (B, 2 * B), 0).astype(F32)
    block = lax.broadcasted_iota(jnp.int32, (1, 2 * B), 1) // (half * keep)
    for h in range(2):
        hi_ref, lo_ref = p_refs[2 * h : 2 * h + 2]
        w = w_ref[h, :1, :]
        rows = [bundles[rep ^ (2 * i + h), last:, :].astype(F32)[:keep] for i in range(half)]
        rows = jnp.concatenate(rows * nb, axis=0).T
        for g in range(hi_ref.shape[1] // (2 * B)):
            num = rows[g * nb : g * nb + 1]
            for j in range(1, nb):
                num = jnp.where(block == j, rows[g * nb + j : g * nb + j + 1], num)
            hot = jnp.where(freq == num, 1.0, 0.0).astype(BF16)
            y = dot(tall[:, :B], hot)
            hi, lo = split((y[:B] + y[B:]) * w)
            hi_ref[:, g * 2 * B : (g + 1) * 2 * B] = hi
            lo_ref[:, g * 2 * B : (g + 1) * 2 * B] = lo


def spread_rows(p_hi, p_lo, ships, g):
    half, keep = ships.shape[0], ships.shape[1]
    lane_block = lax.broadcasted_iota(jnp.int32, (half * keep, G), 1) // B
    s = jnp.concatenate([ships[i, :, g * G : (g + 1) * G].astype(F32) for i in range(half)], axis=0)
    w = jnp.concatenate(
        [jnp.where(lane_block == j, s, 0.0).astype(BF16) for j in range(G // B)], axis=0
    )
    cut = slice(g * 2 * B, (g + 1) * 2 * B)
    y = dot(jnp.concatenate([p_hi[:, cut], p_lo[:, cut]], axis=0), w)
    return y[:B] + y[B:]


def half_update_body(p_hi, p_lo, mine, out):
    for g in range(out.shape[0] // B):
        out[g * B : (g + 1) * B, :] = spread_rows(p_hi, p_lo, mine, g)


def update_body(chunk, half_sum, p_hi, p_lo, other, out, held, sems):
    ng = half_sum.shape[0] // B
    copies = []
    for c in range(0, ng, chunk):
        for g in range(c, c + chunk):
            held[:, g * G : (g + 1) * G] = half_sum[g * B : (g + 1) * B, :] + spread_rows(p_hi, p_lo, other, g)
        cut = pl.ds(c * G, chunk * G)
        copies.append(pltpu.make_async_copy(held.at[:, cut], out.at[:, cut], sems.at[c // chunk]))
        copies[-1].start()
    for copy in copies:
        copy.wait()


def input_grad_body(n_t, n_r, cp, bundles, *refs):
    ups, out, held = refs[:n_t], refs[n_t], refs[n_t + 1]
    nc = out.shape[1] // cp
    nr = B // (n_r // cp)
    tiles = nc // 128
    for r in range(n_r):
        r0, c0 = (r // cp) * nr, (r % cp) * nc
        for k in range(n_t):
            for j in range(tiles):
                at = (k * tiles + j) * nr
                held[k * B + r0 : k * B + r0 + nr, c0 + j * 128 : c0 + (j + 1) * 128] = bundles[r, at : at + nr, :]
    up = jnp.concatenate([u[:B, :] for u in ups], axis=0).T
    for c in range(0, out.shape[1], G):
        out[:, c : c + G] = dot(up, held[:, c : c + G]).astype(BF16)


def per_device(n_t, n_r, act, switch, slope, exp, vel, lines, mask, tally):
    cols = act.shape[1]
    width = exp.shape[1]
    tok = act.shape[0]
    keep = lines.shape[3]
    blocks = width // B
    groups = width // G
    cp = 2
    rp = n_r // cp
    half = n_r // 2
    tab, tall = constants()
    def trade(x, k):
        return lax.ppermute(x, "tensor", [(i, i ^ k) for i in range(n_t)])

    order = [*range(2, n_t), 1]

    def swap(x, m):
        return lax.ppermute(x, "replica", [(i, i ^ m) for i in range(n_r)])

    own = lines[0, 0].T
    tiles = cols // cp // 128
    nr = B // rp
    *parts, act, own, tall = call(
        functools.partial(first_body, n_t, cp, cols, nr),
        [near((B + tiles * nr, 128))] * n_t
        + [near(act.shape), near(own.shape, jnp.int32), near(tall.shape)],
        (far(switch.T), far(slope.T), far(exp), far(act), far(own), far(tall)),
        [ANY] * 6,
        [VM] * (n_t + 3),
        scratch=[
            pltpu.VMEM((B, tok), BF16),
            pltpu.VMEM((B, tok), BF16),
            pltpu.VMEM((nr, width), BF16),
            pltpu.SemaphoreType.DMA((6,)),
        ],
        nbytes=act.size * 4 + nr * width * 2,
        name="up_grads",
    )
    got = {k: trade(parts[k], k) for k in order}
    parts = [parts[0]] + [got[k] for k in range(1, n_t)]

    p_own, a_own, shares = call(
        functools.partial(own_body, n_r, keep),
        [
            near((B, groups * 2 * B)),
            near((groups * B, 2 * B)),
            near((2, 8, 2 * B), F32),
        ],
        (far(mask), far(tally), own, tall),
        [ANY, ANY, VM, VM],
        [VM] * 3,
        scratch=[pltpu.SMEM((n_r,), jnp.int32)] * 2 + [pltpu.SemaphoreType.DMA((2,))],
        name="own_places",
    )

    def grads_of(ks, after):
        return call(
            functools.partial(grads_body, len(ks)),
            [near((B, cols), BF16 if k else F32) for k in ks],
            (act, after, *[parts[k] for k in ks]),
            [VM, ANY] + [VM] * len(ks),
            [VM] * len(ks),
            name="weight_grads",
        )

    grads = {}
    for k in order[:-1]:
        (grads[k],) = grads_of([k], act)
    made, grads[0] = grads_of([order[-1], 0], shares)
    grads[order[-1]] = made
    grads.update({k: trade(grads[k], k) for k in order})

    bundle = call(
        functools.partial(bundle_body, n_t, keep),
        near((n_t * tiles * nr + 16, 128)),
        (made, own, *parts),
        [ANY] + [VM] * (n_t + 1),
        VM,
        name="bundle",
    )
    bundles = lax.all_gather(bundle, "replica", axis=0)

    places = call(
        functools.partial(places_body, keep),
        [near((B, blocks * half * keep))] * 4,
        (shares, tall, bundles),
        [VM] * 3,
        [VM] * 4,
        name="places",
    )
    input_grad = call(
        functools.partial(input_grad_body, n_t, n_r, cp),
        jax.ShapeDtypeStruct((tok, cols), BF16),
        (bundles, *parts),
        [VM] * (1 + n_t),
        VM,
        scratch=[pltpu.VMEM((n_t * B, cols), BF16)],
        flops=2 * tok * n_t * B * cols,
        nbytes=(n_t * B * cols + tok * cols) * 2,
        name="input_grads",
    )

    rows = []
    for ks in ([0, *order[:-1]], order[-1:]):
        rows = call(
            functools.partial(kept_body, ks, n_t, keep),
            [near((keep, width)), near((keep, width), F32)],
            (vel[0], a_own, tab, bundles, *[grads[k] for k in ks], *rows),
            [VM] * 3 + [ANY] + [VM] * (len(ks) + len(rows)),
            [VM] * 2,
            flops=6 * B * B * cols * len(ks),
            nbytes=B * cols * 6 * len(ks),
            name="kept_rows",
            alias={4 + len(ks): 0, 5 + len(ks): 1} if rows else {},
        )
    ship, q_own = rows
    ships = [ship] + [swap(ship, 2 * i) for i in range(1, half)]
    new = call(
        functools.partial(return_body, n_t, keep),
        jax.ShapeDtypeStruct((B, width), F32),
        (vel[0], p_own, q_own, *[grads[k] for k in range(n_t)]),
        [VM] * (3 + n_t),
        ANY,
        scratch=[pltpu.VMEM((B, width), F32), pltpu.SemaphoreType.DMA((n_t,))],
        flops=6 * B * B * width,
        nbytes=B * width * 10,
        name="new_momentums",
    )
    mine = call(
        functools.partial(join_body, half),
        near((half, keep, width)),
        (*ships, far(new), far(input_grad), places[0]),
        [VM] * half + [ANY] * 3,
        VM,
        name="join_kept",
    )
    other = swap(mine, 1)
    half_sum = call(
        half_update_body,
        near((groups * B, G), F32),
        (*places[:2], mine),
        [VM] * 3,
        VM,
        name="half_updates",
    )
    chunk = next(c for c in (5, 4, 3, 2, 1) if groups % c == 0)
    update = call(
        functools.partial(update_body, chunk),
        jax.ShapeDtypeStruct((B, width), F32),
        (half_sum, *places[2:], other),
        [VM] * 4,
        ANY,
        scratch=[
            pltpu.VMEM((B, width), F32),
            pltpu.SemaphoreType.DMA((groups // chunk,)),
        ],
        flops=8 * B * G * width,
        nbytes=B * width * 8,
        name="updates",
    )
    return input_grad, new[None], update


def per_device_plain(
    projection_inputs,
    switch_logits_raw,
    inner_neuron_slope,
    expansion_matrix,
    velocity_buffer,
    sent_spectral_lines,
    participant_mask,
    token_tallies,
):
    highest = lax.Precision.HIGHEST
    up_grad = (
        inner_neuron_slope.astype(jnp.float32) * jax.nn.silu(switch_logits_raw.astype(jnp.float32))
    ).astype(jnp.bfloat16)
    partial_terms = jnp.dot(up_grad, expansion_matrix, preferred_element_type=jnp.float32)
    input_grad = lax.psum_scatter(partial_terms, "tensor", scatter_dimension=1, tiled=True).astype(
        jnp.bfloat16
    )
    grad_w = lax.dot_general(
        up_grad,
        lax.all_gather(projection_inputs, "tensor", axis=1, tiled=True),
        (((0,), (0,)), ((), ())),
        preferred_element_type=jnp.float32,
    )
    row_total_count = expansion_matrix.shape[0] // 64
    col_count = expansion_matrix.shape[1] // 64
    moment = momentum_decay * velocity_buffer[0] + grad_w
    cosines = cosine_table()
    blocks = moment.reshape(row_total_count, 64, col_count, 64).transpose(0, 2, 1, 3)
    coefficients = jnp.einsum("fa,ijab,gb->ijfg", cosines, blocks, cosines, precision=highest)
    freq_ids = jnp.arange(64, dtype=jnp.int32)
    own_rows = sent_spectral_lines[0]
    chosen = (own_rows[..., None] == freq_ids).astype(jnp.float32)
    shipped = jnp.einsum("ijkf,ijfg->ijkg", chosen, coefficients, precision=highest).astype(
        jnp.bfloat16
    )
    spectrum = jnp.einsum("ijkf,ijkg->ijfg", chosen, shipped.astype(jnp.float32), precision=highest)
    returned = jnp.einsum("fa,ijfg,gb->ijab", cosines, spectrum, cosines, precision=highest)
    new_moment = moment - returned.transpose(0, 2, 1, 3).reshape(moment.shape)
    worker_burdens = participant_mask.astype(jnp.float32) * token_tallies.astype(jnp.float32)
    worker_fractions = worker_burdens * (
        jnp.sum(participant_mask.astype(jnp.float32)) / jnp.sum(worker_burdens)
    )
    myself = lax.axis_index("replica")
    combined = lax.psum(worker_fractions[myself] * spectrum, "replica")
    update = jnp.einsum("fa,ijfg,gb->ijab", cosines, combined, cosines, precision=highest)
    update = update.transpose(0, 2, 1, 3).reshape(moment.shape)
    return (input_grad, new_moment[None], update)


def solution(mesh):
    n_t, n_r = mesh.shape["tensor"], mesh.shape["replica"]

    def device(*args):
        act, exp, lines = args[0], args[3], args[5]
        fits = (
            act.shape[1] % G == 0
            and act.shape[0] % 128 == 0
            and exp.shape[0] == B
            and lines.shape[3] == 8
            and n_r == 8
            and n_t >= 2
            and n_t & (n_t - 1) == 0
        )
        if not fits:
            return per_device_plain(*args)
        return per_device(n_t, n_r, *args)

    return jax.shard_map(
        device,
        mesh=mesh,
        in_specs=(
            P("replica", "tensor"),
            P("replica", "tensor"),
            P("replica", "tensor"),
            P("tensor", None),
            P("replica", "tensor", None),
            P("replica", "tensor", None, None),
            P(),
            P(),
        ),
        out_specs=(P("replica", "tensor"), P("replica", "tensor", None), P("tensor", None)),
        check_vma=False,
    )
```

```python
import functools

import jax
import jax.numpy as jnp
import numpy as np
from jax import lax
from jax.experimental import pallas as pl
from jax.experimental.pallas import tpu as pltpu
from jax.sharding import PartitionSpec as P

momentum_decay = 0.9
B = 64
G = 256
F32 = jnp.float32
BF16 = jnp.bfloat16
VMEM_LIMIT = 24 * 1024 * 1024

VM = pl.BlockSpec(memory_space=pltpu.VMEM)
SM = pl.BlockSpec(memory_space=pltpu.SMEM)
ANY = pl.BlockSpec(memory_space=pl.ANY)


def cosine_table():
    freqs = jnp.arange(64, dtype=jnp.float32)[:, None]
    places = jnp.arange(64, dtype=jnp.float32)[None, :]
    cosines = jnp.cos(jnp.pi * (places + 0.5) * freqs / 64.0) * jnp.sqrt(2.0 / 64.0)
    return cosines.at[0].multiply(jnp.sqrt(0.5))


def cosine_np():
    f = np.arange(B)[:, None]
    a = np.arange(B)[None, :]
    c = np.cos(np.pi * (a + 0.5) * f / B) * np.sqrt(2.0 / B)
    c[0] *= np.sqrt(0.5)
    return c


def halves(c):
    hi = np.asarray(c, dtype=np.float32).astype(jnp.bfloat16)
    lo = (np.asarray(c, np.float64) - hi.astype(np.float64)).astype(np.float32).astype(jnp.bfloat16)
    return hi, lo


def constants():
    hi, lo = halves(cosine_np())
    eye = np.eye(G // B)
    kron = lambda x: np.kron(eye, np.asarray(x, np.float32)).astype(jnp.bfloat16)
    tall = np.zeros((2 * B, 2 * B), jnp.bfloat16)
    tall[:B, :B], tall[B:, :B] = hi.T, lo.T
    return jnp.asarray(np.concatenate([kron(x) for x in (hi.T, lo.T, hi, lo)], axis=0)), jnp.asarray(tall)


def fwd(tab, i):
    return tab[i * G : (i + 1) * G, :]


def inv(tab, i):
    return tab[(2 + i) * G : (3 + i) * G, :]


def dot(a, b):
    return jnp.dot(a, b, preferred_element_type=F32)


def split(x):
    hi = x.astype(BF16)
    return hi, (x - hi.astype(F32)).astype(BF16)


def near(shape, dtype=BF16):
    return pltpu.VMEM(shape, dtype)


def far(x):
    return pltpu.with_memory_space_constraint(x, pltpu.HBM)


def call(body, out_shape, ins, in_specs, out_specs, scratch=(), flops=0, nbytes=0, name=None, alias={}):
    return pl.pallas_call(
        body,
        out_shape=out_shape,
        in_specs=in_specs,
        out_specs=out_specs,
        scratch_shapes=scratch,
        input_output_aliases=alias,
        compiler_params=pltpu.CompilerParams(vmem_limit_bytes=VMEM_LIMIT),
        cost_estimate=pl.CostEstimate(flops=flops, bytes_accessed=nbytes, transcendentals=0),
        name=name,
    )(*ins)


def first_body(n_t, cp, cols, nr, switch, slope, exp_ref, act, lines, tall, *refs):
    outs, (act_out, lines_out, tall_out) = refs[:n_t], refs[n_t : n_t + 3]
    switch_v, slope_v, exp_v, sems = refs[n_t + 3 :]
    rep, ten = lax.axis_index("replica"), lax.axis_index("tensor")
    r0 = pl.multiple_of((rep // cp) * nr, nr)
    copies = [
        pltpu.make_async_copy(src, dst, sems.at[i])
        for i, (src, dst) in enumerate(
            [
                (switch, switch_v),
                (slope, slope_v),
                (exp_ref.at[pl.ds(r0, nr), :], exp_v),
                (act, act_out),
                (lines, lines_out),
                (tall, tall_out),
            ]
        )
    ]
    for copy in copies:
        copy.start()
    copies[0].wait()
    copies[1].wait()
    v = switch_v[...].astype(F32)
    up = (slope_v[...].astype(F32) * (v * jax.nn.sigmoid(v))).astype(BF16)
    for k in range(n_t):
        outs[k][:B, :] = up
    copies[2].wait()
    nc = cols // cp
    for k in range(n_t):
        c0 = (ten ^ k) * cols + lax.rem(rep, cp) * nc
        for j in range(nc // 128):
            at = pl.multiple_of(c0 + j * 128, 128)
            outs[k][B + j * nr : B + (j + 1) * nr, :] = exp_v[:, pl.ds(at, 128)]
    for copy in copies[3:]:
        copy.wait()


def grads_body(n, act, *refs):
    ups, outs = refs[:n], refs[n:]
    up = jnp.concatenate([u[:B, :] for u in ups], axis=0)
    for c in range(0, act.shape[1], G):
        g = dot(up, act[:, c : c + G])
        for k in range(n):
            outs[k][:, c : c + G] = g[k * B : (k + 1) * B].astype(outs[k].dtype)


def bundle_body(n_t, keep, after, lines, *refs):
    parts, out = refs[:n_t], refs[n_t]
    n = parts[0].shape[0] - B
    for k in range(n_t):
        out[k * n : (k + 1) * n, :] = parts[k][B:, :]
    blocks = lines.shape[1]
    rows = jnp.concatenate([lines[...].astype(F32), jnp.zeros((keep, 128 - blocks), F32)], axis=1)
    out[n_t * n :, :] = jnp.concatenate([rows, jnp.zeros((16 - keep, 128), F32)], axis=0).astype(BF16)


def join_body(n, *refs):
    for i, ref in enumerate(refs[:n]):
        refs[-1][i] = ref[...]


def own_body(n_r, keep, mask, tally, tab, lines, tall, p_ref, a_ref, w_ref, tab_ref, mask_s, tally_s, sems):
    copies = [
        pltpu.make_async_copy(src, dst, sems.at[i])
        for i, (src, dst) in enumerate([(mask, mask_s), (tally, tally_s), (tab, tab_ref)])
    ]
    for copy in copies:
        copy.start()
    blocks = lines.shape[1]
    rows = jnp.concatenate([lines[...].astype(F32), jnp.zeros((keep, 128 - blocks), F32)], axis=1)
    rows = jnp.concatenate([rows] * (2 * B // keep), axis=0).T
    freq = lax.broadcasted_iota(jnp.int32, (B, 2 * B), 0).astype(F32)
    block = (lax.broadcasted_iota(jnp.int32, (1, 2 * B), 1) // keep) % (G // B)
    term = lax.broadcasted_iota(jnp.int32, (B, 2 * B), 1) // (B // 2)
    for g in range(blocks // (G // B)):
        num = rows[g * (G // B) : g * (G // B) + 1]
        for j in range(1, G // B):
            num = jnp.where(block == j, rows[g * (G // B) + j : g * (G // B) + j + 1], num)
        hot = jnp.where(freq == num, 1.0, 0.0).astype(BF16)
        y = dot(tall[:, :B], hot)
        p = jnp.where(term == 3, 0.0, jnp.where(term == 1, y[B:], y[:B]))
        p_ref[:, g * 2 * B : (g + 1) * 2 * B] = p.astype(BF16)
        a_ref[g * B : (g + 1) * B, :] = jnp.concatenate([p, p], axis=0).T[:B].astype(BF16)
    for copy in copies:
        copy.wait()
    total, alive = jnp.float32(0), jnp.float32(0)
    for r in range(n_r):
        m = mask_s[r].astype(F32)
        total = total + m * tally_s[r].astype(F32)
        alive = alive + m
    half = n_r // 2
    place = (lax.broadcasted_iota(jnp.int32, (8, 2 * B), 1) // keep) % half
    scale = jnp.full((8, 2 * B), alive) / jnp.full((8, 2 * B), total)
    for h in range(2):
        w = jnp.zeros((8, 2 * B), F32)
        for i in range(half):
            r = lax.axis_index("replica") ^ (2 * i + h)
            w = jnp.where(place == i, mask_s[r].astype(F32) * tally_s[r].astype(F32), w)
        w_ref[h] = w * scale


def kept_body(ks, n_t, keep, vel, a_ref, tab, *refs):
    grads, (send_ref, own_ref) = refs[: len(ks)], refs[-2:]
    cols = grads[0].shape[1]
    ng = cols // G
    lane_block = lax.broadcasted_iota(jnp.int32, (keep, G), 1) // B
    sel = []
    for n, k in enumerate(ks):
        c0 = (lax.axis_index("tensor") ^ k) * cols
        for i in range(ng):
            at = pl.multiple_of(c0 + i * G, G)
            moment = momentum_decay * vel[:, pl.ds(at, G)] + grads[n][:, i * G : (i + 1) * G].astype(F32)
            hi, lo = split(moment)
            y = dot(a_ref[pl.ds(pl.multiple_of(at // (G // B), B), B), :], jnp.concatenate([hi, lo], axis=0))
            y = y[: B // 2] + y[B // 2 :]
            got = y[:keep]
            for j in range(1, G // B):
                got = jnp.where(lane_block == j, y[j * keep : (j + 1) * keep], got)
            sel.append(got)
    hi, lo = split(jnp.concatenate(sel, axis=0))
    n = len(ks) * ng * keep
    y = dot(jnp.concatenate([hi, lo], axis=0), fwd(tab, 0))
    kept = (y[:n] + y[n:] + dot(hi, fwd(tab, 1))).astype(BF16)
    q = dot(kept, inv(tab, 0)) + dot(kept, inv(tab, 1))
    for n, k in enumerate(ks):
        c0 = pl.multiple_of((lax.axis_index("tensor") ^ k) * cols, G)
        part = jnp.concatenate([q[(n * ng + i) * keep : (n * ng + i + 1) * keep] for i in range(ng)], axis=1)
        own_ref[:, pl.ds(c0, cols)] = part
        send_ref[:, pl.ds(c0, cols)] = part.astype(BF16)


def return_body(n_t, keep, vel, p_ref, q, *refs):
    grads, (new_ref, held, sems) = refs[:n_t], refs[n_t:]
    cols = grads[0].shape[1]
    ng = cols // G
    lane_block = lax.broadcasted_iota(jnp.int32, (keep, G), 1) // B
    copies = []
    for k in range(n_t):
        c0 = pl.multiple_of((lax.axis_index("tensor") ^ k) * cols, G)
        for i in range(ng):
            at = pl.multiple_of(c0 + i * G, G)
            own = q[:, pl.ds(at, G)]
            spread = jnp.concatenate(
                [jnp.where(lane_block == j, own, 0.0) for j in range(G // B)], axis=0
            )
            hi, lo = split(spread)
            w = jnp.concatenate([hi, hi, lo, jnp.zeros_like(lo)], axis=0)
            back = dot(p_ref[:, pl.ds(pl.multiple_of(at // 2, 2 * B), 2 * B)], w)
            moment = momentum_decay * vel[:, pl.ds(at, G)] + grads[k][:, i * G : (i + 1) * G].astype(F32)
            held[:, pl.ds(at, G)] = moment - back
        cut = pl.ds(c0, cols)
        copies.append(pltpu.make_async_copy(held.at[:, cut], new_ref.at[:, cut], sems.at[k]))
        copies[-1].start()
    for copy in copies:
        copy.wait()


def places_body(keep, h, w_ref, tall, bundles, hi_ref, lo_ref):
    half, last, nb = bundles.shape[0], bundles.shape[1] - 16, G // B
    freq = lax.broadcasted_iota(jnp.int32, (B, 2 * B), 0).astype(F32)
    block = lax.broadcasted_iota(jnp.int32, (1, 2 * B), 1) // (half * keep)
    w = w_ref[h, :1, :]
    rows = [bundles[i, last:, :].astype(F32)[:keep] for i in range(half)]
    rows = jnp.concatenate(rows * nb, axis=0).T
    for g in range(hi_ref.shape[1] // (2 * B)):
        num = rows[g * nb : g * nb + 1]
        for j in range(1, nb):
            num = jnp.where(block == j, rows[g * nb + j : g * nb + j + 1], num)
        hot = jnp.where(freq == num, 1.0, 0.0).astype(BF16)
        y = dot(tall[:, :B], hot)
        hi, lo = split((y[:B] + y[B:]) * w)
        hi_ref[:, g * 2 * B : (g + 1) * 2 * B] = hi
        lo_ref[:, g * 2 * B : (g + 1) * 2 * B] = lo


def spread_rows(p_hi, p_lo, ships, g):
    half, keep = ships.shape[0], ships.shape[1]
    lane_block = lax.broadcasted_iota(jnp.int32, (half * keep, G), 1) // B
    s = jnp.concatenate([ships[i, :, g * G : (g + 1) * G].astype(F32) for i in range(half)], axis=0)
    w = jnp.concatenate(
        [jnp.where(lane_block == j, s, 0.0).astype(BF16) for j in range(G // B)], axis=0
    )
    cut = slice(g * 2 * B, (g + 1) * 2 * B)
    y = dot(jnp.concatenate([p_hi[:, cut], p_lo[:, cut]], axis=0), w)
    return y[:B] + y[B:]


def half_update_body(p_hi, p_lo, mine, out):
    for g in range(out.shape[0] // B):
        out[g * B : (g + 1) * B, :] = spread_rows(p_hi, p_lo, mine, g)


def update_body(chunk, half_sum, p_hi, p_lo, other, out, held, sems):
    ng = half_sum.shape[0] // B
    copies = []
    for c in range(0, ng, chunk):
        for g in range(c, c + chunk):
            held[:, g * G : (g + 1) * G] = half_sum[g * B : (g + 1) * B, :] + spread_rows(p_hi, p_lo, other, g)
        cut = pl.ds(c * G, chunk * G)
        copies.append(pltpu.make_async_copy(held.at[:, cut], out.at[:, cut], sems.at[c // chunk]))
        copies[-1].start()
    for copy in copies:
        copy.wait()


def input_grad_body(n_t, h, bundles, *refs):
    ups, (out, held, ready, sem) = refs[:n_t], refs[-4:]
    half = bundles.shape[0]
    nc, nr = held.shape[1], B // half
    tiles = nc // 128
    rep = lax.axis_index("replica")
    for i in range(half):
        r0 = ((rep ^ (2 * i + h)) // 2) * nr
        for k in range(n_t):
            row = pl.multiple_of(k * B + r0, nr)
            for j in range(tiles):
                at = (k * tiles + j) * nr
                held[pl.ds(row, nr), j * 128 : (j + 1) * 128] = bundles[i, at : at + nr, :]
    up = jnp.concatenate([u[:B, :] for u in ups], axis=0).T
    for c in range(0, nc, 128):
        ready[:, c : c + 128] = dot(up, held[:, c : c + 128]).astype(BF16)
    c0 = pl.multiple_of(lax.rem(rep ^ h, 2) * nc, 128)
    copy = pltpu.make_async_copy(ready, out.at[:, pl.ds(c0, nc)], sem)
    copy.start()
    copy.wait()


def per_device(n_t, n_r, act, switch, slope, exp, vel, lines, mask, tally):
    cols = act.shape[1]
    width = exp.shape[1]
    tok = act.shape[0]
    keep = lines.shape[3]
    blocks = width // B
    groups = width // G
    cp = 2
    rp = n_r // cp
    half = n_r // 2
    tab, tall = constants()
    def trade(x, k):
        return lax.ppermute(x, "tensor", [(i, i ^ k) for i in range(n_t)])

    order = [*range(2, n_t), 1]

    def swap(x, m):
        return lax.ppermute(x, "replica", [(i, i ^ m) for i in range(n_r)])

    def share(x, name, after=()):
        mine = call(
            functools.partial(join_body, half),
            near((half,) + x.shape),
            (x, *[swap(x, 2 * i) for i in range(1, half)], *after),
            [VM] * half + [ANY] * len(after),
            VM,
            name=name,
        )
        return mine, swap(mine, 1)

    own = lines[0, 0].T
    tiles = cols // cp // 128
    nr = B // rp
    *parts, act, own, tall = call(
        functools.partial(first_body, n_t, cp, cols, nr),
        [near((B + tiles * nr, 128))] * n_t
        + [near(act.shape), near(own.shape, jnp.int32), near(tall.shape)],
        (far(switch.T), far(slope.T), far(exp), far(act), far(own), far(tall)),
        [ANY] * 6,
        [VM] * (n_t + 3),
        scratch=[
            pltpu.VMEM((B, tok), BF16),
            pltpu.VMEM((B, tok), BF16),
            pltpu.VMEM((nr, width), BF16),
            pltpu.SemaphoreType.DMA((6,)),
        ],
        nbytes=act.size * 4 + nr * width * 2,
        name="up_grads",
    )
    got = {k: trade(parts[k], k) for k in order}
    parts = [parts[0]] + [got[k] for k in range(1, n_t)]

    def grads_of(ks):
        return call(
            functools.partial(grads_body, len(ks)),
            [near((B, cols), BF16 if k else F32) for k in ks],
            (act, *[parts[k] for k in ks]),
            [VM] * (1 + len(ks)),
            [VM] * len(ks),
            name="weight_grads",
        )

    grads = {}
    for k in order[:-1]:
        (grads[k],) = grads_of([k])
    made, grads[0] = grads_of([order[-1], 0])
    grads[order[-1]] = made
    grads.update({k: trade(grads[k], k) for k in order})

    bundle = call(
        functools.partial(bundle_body, n_t, keep),
        near((n_t * tiles * nr + 16, 128)),
        (made, own, *parts),
        [ANY] + [VM] * (n_t + 1),
        VM,
        name="bundle",
    )
    bundles = share(bundle, "join_bundles")

    p_own, a_own, shares, tab = call(
        functools.partial(own_body, n_r, keep),
        [
            near((B, groups * 2 * B)),
            near((groups * B, 2 * B)),
            near((2, 8, 2 * B), F32),
            near(tab.shape),
        ],
        (far(mask), far(tally), far(tab), own, tall),
        [ANY, ANY, ANY, VM, VM],
        [VM] * 4,
        scratch=[pltpu.SMEM((n_r,), jnp.int32)] * 2 + [pltpu.SemaphoreType.DMA((3,))],
        name="own_places",
    )
    places = [
        call(
            functools.partial(places_body, keep, h),
            [near((B, blocks * half * keep))] * 2,
            (shares, tall, bundles[h]),
            [VM] * 3,
            [VM] * 2,
            name="places",
        )
        for h in range(2)
    ]
    input_grad = []
    for h in range(2):
        input_grad = [
            call(
                functools.partial(input_grad_body, n_t, h),
                jax.ShapeDtypeStruct((tok, cols), BF16),
                (bundles[h], *parts, *[far(x) for x in input_grad]),
                [VM] * (1 + n_t) + [ANY] * len(input_grad),
                ANY,
                scratch=[
                    pltpu.VMEM((n_t * B, cols // cp), BF16),
                    pltpu.VMEM((tok, cols // cp), BF16),
                    pltpu.SemaphoreType.DMA,
                ],
                name="input_grads",
                alias={1 + n_t: 0} if input_grad else {},
            )
        ]
        first_half = input_grad[0] if h == 0 else first_half
    input_grad = input_grad[0]

    rows = []
    for ks in (list(range(n_t - 1)), [n_t - 1]):
        rows = call(
            functools.partial(kept_body, ks, n_t, keep),
            [near((keep, width)), near((keep, width), F32)],
            (vel[0], a_own, tab, *[grads[k] for k in ks], *rows),
            [VM] * (3 + len(ks) + len(rows)),
            [VM] * 2,
            flops=6 * B * B * cols * len(ks),
            nbytes=B * cols * 6 * len(ks),
            name="kept_rows",
            alias={3 + len(ks): 0, 4 + len(ks): 1} if rows else {},
        )
    ship, q_own = rows
    new = call(
        functools.partial(return_body, n_t, keep),
        jax.ShapeDtypeStruct((B, width), F32),
        (vel[0], p_own, q_own, *[grads[k] for k in range(n_t)]),
        [VM] * (3 + n_t),
        ANY,
        scratch=[pltpu.VMEM((B, width), F32), pltpu.SemaphoreType.DMA((n_t,))],
        flops=6 * B * B * width,
        nbytes=B * width * 10,
        name="new_momentums",
    )
    mine, other = share(ship, "join_kept", (far(new), places[0][0], far(first_half)))
    half_sum = call(
        half_update_body,
        near((groups * B, G), F32),
        (*places[0], mine),
        [VM] * 3,
        VM,
        name="half_updates",
    )
    chunk = next(c for c in (5, 4, 3, 2, 1) if groups % c == 0)
    update = call(
        functools.partial(update_body, chunk),
        jax.ShapeDtypeStruct((B, width), F32),
        (half_sum, *places[1], other),
        [VM] * 4,
        ANY,
        scratch=[
            pltpu.VMEM((B, width), F32),
            pltpu.SemaphoreType.DMA((groups // chunk,)),
        ],
        flops=8 * B * G * width,
        nbytes=B * width * 8,
        name="updates",
    )
    return input_grad, new[None], update


def per_device_plain(
    projection_inputs,
    switch_logits_raw,
    inner_neuron_slope,
    expansion_matrix,
    velocity_buffer,
    sent_spectral_lines,
    participant_mask,
    token_tallies,
):
    highest = lax.Precision.HIGHEST
    up_grad = (
        inner_neuron_slope.astype(jnp.float32) * jax.nn.silu(switch_logits_raw.astype(jnp.float32))
    ).astype(jnp.bfloat16)
    partial_terms = jnp.dot(up_grad, expansion_matrix, preferred_element_type=jnp.float32)
    input_grad = lax.psum_scatter(partial_terms, "tensor", scatter_dimension=1, tiled=True).astype(
        jnp.bfloat16
    )
    grad_w = lax.dot_general(
        up_grad,
        lax.all_gather(projection_inputs, "tensor", axis=1, tiled=True),
        (((0,), (0,)), ((), ())),
        preferred_element_type=jnp.float32,
    )
    row_total_count = expansion_matrix.shape[0] // 64
    col_count = expansion_matrix.shape[1] // 64
    moment = momentum_decay * velocity_buffer[0] + grad_w
    cosines = cosine_table()
    blocks = moment.reshape(row_total_count, 64, col_count, 64).transpose(0, 2, 1, 3)
    coefficients = jnp.einsum("fa,ijab,gb->ijfg", cosines, blocks, cosines, precision=highest)
    freq_ids = jnp.arange(64, dtype=jnp.int32)
    own_rows = sent_spectral_lines[0]
    chosen = (own_rows[..., None] == freq_ids).astype(jnp.float32)
    shipped = jnp.einsum("ijkf,ijfg->ijkg", chosen, coefficients, precision=highest).astype(
        jnp.bfloat16
    )
    spectrum = jnp.einsum("ijkf,ijkg->ijfg", chosen, shipped.astype(jnp.float32), precision=highest)
    returned = jnp.einsum("fa,ijfg,gb->ijab", cosines, spectrum, cosines, precision=highest)
    new_moment = moment - returned.transpose(0, 2, 1, 3).reshape(moment.shape)
    worker_burdens = participant_mask.astype(jnp.float32) * token_tallies.astype(jnp.float32)
    worker_fractions = worker_burdens * (
        jnp.sum(participant_mask.astype(jnp.float32)) / jnp.sum(worker_burdens)
    )
    myself = lax.axis_index("replica")
    combined = lax.psum(worker_fractions[myself] * spectrum, "replica")
    update = jnp.einsum("fa,ijfg,gb->ijab", cosines, combined, cosines, precision=highest)
    update = update.transpose(0, 2, 1, 3).reshape(moment.shape)
    return (input_grad, new_moment[None], update)


def solution(mesh):
    n_t, n_r = mesh.shape["tensor"], mesh.shape["replica"]

    def device(*args):
        act, exp, lines = args[0], args[3], args[5]
        fits = (
            act.shape[1] % G == 0
            and act.shape[0] % 128 == 0
            and exp.shape[0] == B
            and lines.shape[3] == 8
            and n_r == 8
            and n_t >= 2
            and n_t & (n_t - 1) == 0
        )
        if not fits:
            return per_device_plain(*args)
        return per_device(n_t, n_r, *args)

    return jax.shard_map(
        device,
        mesh=mesh,
        in_specs=(
            P("replica", "tensor"),
            P("replica", "tensor"),
            P("replica", "tensor"),
            P("tensor", None),
            P("replica", "tensor", None),
            P("replica", "tensor", None, None),
            P(),
            P(),
        ),
        out_specs=(P("replica", "tensor"), P("replica", "tensor", None), P("tensor", None)),
        check_vma=False,
    )
```

```python
import functools

import jax
import jax.numpy as jnp
import numpy as np
from jax import lax
from jax.experimental import pallas as pl
from jax.experimental.pallas import tpu as pltpu
from jax.sharding import PartitionSpec as P

momentum_decay = 0.9
B = 64
G = 256
F32 = jnp.float32
BF16 = jnp.bfloat16
VMEM_LIMIT = 24 * 1024 * 1024

VM = pl.BlockSpec(memory_space=pltpu.VMEM)
SM = pl.BlockSpec(memory_space=pltpu.SMEM)
ANY = pl.BlockSpec(memory_space=pl.ANY)


def cosine_table():
    freqs = jnp.arange(64, dtype=jnp.float32)[:, None]
    places = jnp.arange(64, dtype=jnp.float32)[None, :]
    cosines = jnp.cos(jnp.pi * (places + 0.5) * freqs / 64.0) * jnp.sqrt(2.0 / 64.0)
    return cosines.at[0].multiply(jnp.sqrt(0.5))


def cosine_np():
    f = np.arange(B)[:, None]
    a = np.arange(B)[None, :]
    c = np.cos(np.pi * (a + 0.5) * f / B) * np.sqrt(2.0 / B)
    c[0] *= np.sqrt(0.5)
    return c


def halves(c):
    hi = np.asarray(c, dtype=np.float32).astype(jnp.bfloat16)
    lo = (np.asarray(c, np.float64) - hi.astype(np.float64)).astype(np.float32).astype(jnp.bfloat16)
    return hi, lo


def constants():
    hi, lo = halves(cosine_np())
    eye = np.eye(G // B)
    kron = lambda x: np.kron(eye, np.asarray(x, np.float32)).astype(jnp.bfloat16)
    small = np.zeros((2 * B, 4 * B), jnp.bfloat16)
    for i, x in enumerate((hi, lo)):
        rows = slice(i * B, (i + 1) * B)
        small[rows, :B], small[rows, B : 2 * B], small[rows, 2 * B : 3 * B] = x, x, x.T
    return jnp.asarray(np.concatenate([kron(x) for x in (hi.T, lo.T, hi, lo)], axis=0)), jnp.asarray(small)


def fwd(tab, i):
    return tab[i * G : (i + 1) * G, :]


def inv(tab, i):
    return tab[(2 + i) * G : (3 + i) * G, :]


def dot(a, b):
    return jnp.dot(a, b, preferred_element_type=F32)


def split(x):
    hi = x.astype(BF16)
    return hi, (x - hi.astype(F32)).astype(BF16)


def near(shape, dtype=BF16):
    return pltpu.VMEM(shape, dtype)


def far(x):
    return pltpu.with_memory_space_constraint(x, pltpu.HBM)


def call(body, out_shape, ins, in_specs, out_specs, scratch=(), flops=0, nbytes=0, name=None, alias={}):
    return pl.pallas_call(
        body,
        out_shape=out_shape,
        in_specs=in_specs,
        out_specs=out_specs,
        scratch_shapes=scratch,
        input_output_aliases=alias,
        compiler_params=pltpu.CompilerParams(vmem_limit_bytes=VMEM_LIMIT),
        cost_estimate=pl.CostEstimate(flops=flops, bytes_accessed=nbytes, transcendentals=0),
        name=name,
    )(*ins)


def first_body(n_t, cp, cols, nr, switch, slope, exp_ref, act, lines, small, *refs):
    outs, (act_out, lines_out, small_out) = refs[:n_t], refs[n_t : n_t + 3]
    switch_v, slope_v, exp_v, sems = refs[n_t + 3 :]
    rep, ten = lax.axis_index("replica"), lax.axis_index("tensor")
    r0 = pl.multiple_of((rep // cp) * nr, nr)
    copies = [
        pltpu.make_async_copy(src, dst, sems.at[i])
        for i, (src, dst) in enumerate(
            [
                (switch, switch_v),
                (slope, slope_v),
                (exp_ref.at[pl.ds(r0, nr), :], exp_v),
                (act, act_out),
                (lines, lines_out),
                (small, small_out),
            ]
        )
    ]
    for copy in copies:
        copy.start()
    copies[0].wait()
    copies[1].wait()
    v = switch_v[...].astype(F32)
    up = (slope_v[...].astype(F32) * (v * jax.nn.sigmoid(v))).astype(BF16)
    for k in range(n_t):
        outs[k][:B, :] = up
    copies[2].wait()
    nc = cols // cp
    for k in range(1, n_t):
        c0 = (ten ^ k) * cols + lax.rem(rep, cp) * nc
        for j in range(nc // 128):
            at = pl.multiple_of(c0 + j * 128, 128)
            outs[k][B + j * nr : B + (j + 1) * nr, :] = exp_v[:, pl.ds(at, 128)]
    for copy in copies[3:]:
        copy.wait()


def grads_body(n, act, after, *refs):
    ups, outs = refs[:n], refs[n:]
    up = jnp.concatenate([u[:B, :] for u in ups], axis=0)
    for c in range(0, act.shape[1], G):
        g = dot(up, act[:, c : c + G])
        for k in range(n):
            outs[k][:, c : c + G] = g[k * B : (k + 1) * B].astype(outs[k].dtype)


def bundle_body(n_t, keep, after, lines, *refs):
    parts, out = refs[: n_t - 1], refs[n_t - 1]
    n = parts[0].shape[0] - B
    for k in range(n_t - 1):
        out[k * n : (k + 1) * n, :] = parts[k][B:, :]
    blocks = lines.shape[1]
    rows = jnp.concatenate([lines[...].astype(F32), jnp.zeros((keep, 128 - blocks), F32)], axis=1)
    out[(n_t - 1) * n :, :] = jnp.concatenate([rows, jnp.zeros((16 - keep, 128), F32)], axis=0).astype(BF16)


def join_body(n, *refs):
    for i, ref in enumerate(refs[:n]):
        refs[-1][i] = ref[...]


def own_body(keep, lines, small, p_ref, a_ref):
    blocks, nb = lines.shape[1], G // B
    rows = jnp.concatenate([lines[...].astype(F32), jnp.zeros((keep, 128 - blocks), F32)], axis=1)
    lane = lax.broadcasted_iota(jnp.int32, (nb * keep, 2 * B), 1).astype(F32)
    for g in range(blocks // nb):
        num = jnp.concatenate(
            [jnp.broadcast_to(rows[:, g * nb + j : g * nb + j + 1], (keep, 2 * B)) for j in range(nb)], axis=0
        )
        hot = jnp.concatenate(
            [jnp.where(lane == num, 1.0, 0.0), jnp.where(lane - B == num, 1.0, 0.0)], axis=0
        ).astype(BF16)
        a_ref[g * B : (g + 1) * B, :] = dot(hot, small[:, : 2 * B]).astype(BF16)
    rows = jnp.concatenate([rows] * (2 * B // keep), axis=0).T
    freq = lax.broadcasted_iota(jnp.int32, (B, 2 * B), 0).astype(F32)
    block = (lax.broadcasted_iota(jnp.int32, (1, 2 * B), 1) // keep) % nb
    term = lax.broadcasted_iota(jnp.int32, (B, 2 * B), 1) // (B // 2)
    for g in range(blocks // nb):
        num = rows[g * nb : g * nb + 1]
        for j in range(1, nb):
            num = jnp.where(block == j, rows[g * nb + j : g * nb + j + 1], num)
        hot = jnp.where(freq == num, 1.0, 0.0).astype(BF16)
        y = dot(small[:, 2 * B : 3 * B], hot)
        p = jnp.where(term == 3, 0.0, jnp.where(term == 1, y[B:], y[:B]))
        p_ref[:, g * 2 * B : (g + 1) * 2 * B] = p.astype(BF16)


def kept_body(ks, n_t, keep, vel, a_ref, tab, after, *refs):
    grads, (send_ref, own_ref) = refs[: len(ks)], refs[-2:]
    cols = grads[0].shape[1]
    ng = cols // G
    lane_block = lax.broadcasted_iota(jnp.int32, (keep, G), 1) // B
    sel = []
    for n, k in enumerate(ks):
        c0 = (lax.axis_index("tensor") ^ k) * cols
        for i in range(ng):
            at = pl.multiple_of(c0 + i * G, G)
            moment = momentum_decay * vel[:, pl.ds(at, G)] + grads[n][:, i * G : (i + 1) * G].astype(F32)
            hi, lo = split(moment)
            y = dot(a_ref[pl.ds(pl.multiple_of(at // (G // B), B), B), :], jnp.concatenate([hi, lo], axis=0))
            y = y[: B // 2] + y[B // 2 :]
            got = y[:keep]
            for j in range(1, G // B):
                got = jnp.where(lane_block == j, y[j * keep : (j + 1) * keep], got)
            sel.append(got)
    hi, lo = split(jnp.concatenate(sel, axis=0))
    n = len(ks) * ng * keep
    y = dot(jnp.concatenate([hi, lo], axis=0), fwd(tab, 0))
    kept = (y[:n] + y[n:] + dot(hi, fwd(tab, 1))).astype(BF16)
    q = dot(kept, inv(tab, 0)) + dot(kept, inv(tab, 1))
    for n, k in enumerate(ks):
        c0 = pl.multiple_of((lax.axis_index("tensor") ^ k) * cols, G)
        part = jnp.concatenate([q[(n * ng + i) * keep : (n * ng + i + 1) * keep] for i in range(ng)], axis=1)
        own_ref[:, pl.ds(c0, cols)] = part
        send_ref[:, pl.ds(c0, cols)] = part.astype(BF16)


def return_body(n_t, keep, vel, p_ref, q, *refs):
    grads, (new_ref, held, sems) = refs[:n_t], refs[n_t:]
    cols = grads[0].shape[1]
    ng = cols // G
    lane_block = lax.broadcasted_iota(jnp.int32, (keep, G), 1) // B
    copies = []
    for k in range(n_t):
        c0 = pl.multiple_of((lax.axis_index("tensor") ^ k) * cols, G)
        for i in range(ng):
            at = pl.multiple_of(c0 + i * G, G)
            own = q[:, pl.ds(at, G)]
            spread = jnp.concatenate(
                [jnp.where(lane_block == j, own, 0.0) for j in range(G // B)], axis=0
            )
            hi, lo = split(spread)
            w = jnp.concatenate([hi, hi, lo, jnp.zeros_like(lo)], axis=0)
            back = dot(p_ref[:, pl.ds(pl.multiple_of(at // 2, 2 * B), 2 * B)], w)
            moment = momentum_decay * vel[:, pl.ds(at, G)] + grads[k][:, i * G : (i + 1) * G].astype(F32)
            held[:, pl.ds(at, G)] = moment - back
        cut = pl.ds(c0, cols)
        copies.append(pltpu.make_async_copy(held.at[:, cut], new_ref.at[:, cut], sems.at[k]))
        copies[-1].start()
    for copy in copies:
        copy.wait()


def places_body(keep, mask, tally, small, bundles, *refs):
    p_refs, (mask_s, tally_s, sems) = refs[:4], refs[4:]
    copies = [
        pltpu.make_async_copy(src, dst, sems.at[i])
        for i, (src, dst) in enumerate([(mask, mask_s), (tally, tally_s)])
    ]
    for copy in copies:
        copy.start()
    n_r, last = bundles.shape[0], bundles.shape[1] - 16
    half, nb = n_r // 2, G // B
    rep = lax.axis_index("replica")
    freq = lax.broadcasted_iota(jnp.int32, (B, 2 * B), 0).astype(F32)
    lane = lax.broadcasted_iota(jnp.int32, (1, 2 * B), 1)
    block, place = lane // (half * keep), (lane // keep) % half
    cells = [
        jnp.concatenate(
            [bundles[rep ^ (2 * i + h), last:, :].astype(F32)[:keep] for i in range(half)] * nb, axis=0
        ).T
        for h in range(2)
    ]
    for copy in copies:
        copy.wait()
    total, alive = jnp.float32(0), jnp.float32(0)
    for r in range(n_r):
        m = mask_s[r].astype(F32)
        total = total + m * tally_s[r].astype(F32)
        alive = alive + m
    scale = jnp.full((1, 2 * B), alive) / jnp.full((1, 2 * B), total)
    for h, rows in enumerate(cells):
        w = jnp.zeros((1, 2 * B), F32)
        for i in range(half):
            r = rep ^ (2 * i + h)
            w = jnp.where(place == i, mask_s[r].astype(F32) * tally_s[r].astype(F32), w)
        w = w * scale
        hi_ref, lo_ref = p_refs[2 * h : 2 * h + 2]
        for g in range(hi_ref.shape[1] // (2 * B)):
            num = rows[g * nb : g * nb + 1]
            for j in range(1, nb):
                num = jnp.where(block == j, rows[g * nb + j : g * nb + j + 1], num)
            hot = jnp.where(freq == num, 1.0, 0.0).astype(BF16)
            y = dot(small[:, 2 * B : 3 * B], hot)
            hi, lo = split((y[:B] + y[B:]) * w)
            hi_ref[:, g * 2 * B : (g + 1) * 2 * B] = hi
            lo_ref[:, g * 2 * B : (g + 1) * 2 * B] = lo


def spread_rows(p_hi, p_lo, ships, g):
    half, keep = ships.shape[0], ships.shape[1]
    lane_block = lax.broadcasted_iota(jnp.int32, (half * keep, G), 1) // B
    s = jnp.concatenate([ships[i, :, g * G : (g + 1) * G].astype(F32) for i in range(half)], axis=0)
    w = jnp.concatenate(
        [jnp.where(lane_block == j, s, 0.0).astype(BF16) for j in range(G // B)], axis=0
    )
    cut = slice(g * 2 * B, (g + 1) * 2 * B)
    y = dot(jnp.concatenate([p_hi[:, cut], p_lo[:, cut]], axis=0), w)
    return y[:B] + y[B:]


def half_update_body(p_hi, p_lo, mine, out):
    for g in range(out.shape[0] // B):
        out[g * B : (g + 1) * B, :] = spread_rows(p_hi, p_lo, mine, g)


def update_body(chunk, half_sum, p_hi, p_lo, other, out, held, sems):
    ng = half_sum.shape[0] // B
    copies = []
    for c in range(0, ng, chunk):
        for g in range(c, c + chunk):
            held[:, g * G : (g + 1) * G] = half_sum[g * B : (g + 1) * B, :] + spread_rows(p_hi, p_lo, other, g)
        cut = pl.ds(c * G, chunk * G)
        copies.append(pltpu.make_async_copy(held.at[:, cut], out.at[:, cut], sems.at[c // chunk]))
        copies[-1].start()
    for copy in copies:
        copy.wait()


def input_grad_body(n_t, n_r, cp, exp_ref, bundles, *refs):
    ups, (out, held, sem) = refs[:n_t], refs[n_t:]
    cols = out.shape[1]
    c0 = pl.multiple_of(lax.axis_index("tensor") * cols, 128)
    copy = pltpu.make_async_copy(exp_ref.at[:, pl.ds(c0, cols)], held.at[pl.ds(0, B), :], sem)
    copy.start()
    nc = cols // cp
    nr = B // (n_r // cp)
    tiles = nc // 128
    for r in range(n_r):
        r0, c0 = (r // cp) * nr, (r % cp) * nc
        for k in range(1, n_t):
            for j in range(tiles):
                at = ((k - 1) * tiles + j) * nr
                held[k * B + r0 : k * B + r0 + nr, c0 + j * 128 : c0 + (j + 1) * 128] = bundles[r, at : at + nr, :]
    up = jnp.concatenate([u[:B, :] for u in ups], axis=0).T
    copy.wait()
    for c in range(0, cols, G):
        out[:, c : c + G] = dot(up, held[:, c : c + G]).astype(BF16)


def per_device(n_t, n_r, act, switch, slope, exp, vel, lines, mask, tally):
    cols = act.shape[1]
    width = exp.shape[1]
    tok = act.shape[0]
    keep = lines.shape[3]
    blocks = width // B
    groups = width // G
    cp = 2
    rp = n_r // cp
    half = n_r // 2
    tab, small = constants()
    def trade(x, k):
        return lax.ppermute(x, "tensor", [(i, i ^ k) for i in range(n_t)])

    order = [*range(2, n_t), 1]

    def swap(x, m):
        return lax.ppermute(x, "replica", [(i, i ^ m) for i in range(n_r)])

    own = lines[0, 0].T
    tiles = cols // cp // 128
    nr = B // rp
    *parts, act, own, small = call(
        functools.partial(first_body, n_t, cp, cols, nr),
        [near((B, tok))]
        + [near((B + tiles * nr, 128))] * (n_t - 1)
        + [near(act.shape), near(own.shape, jnp.int32), near(small.shape)],
        (far(switch.T), far(slope.T), far(exp), far(act), far(own), far(small)),
        [ANY] * 6,
        [VM] * (n_t + 3),
        scratch=[
            pltpu.VMEM((B, tok), BF16),
            pltpu.VMEM((B, tok), BF16),
            pltpu.VMEM((nr, width), BF16),
            pltpu.SemaphoreType.DMA((6,)),
        ],
        nbytes=act.size * 4 + nr * width * 2,
        name="up_grads",
    )
    got = {k: trade(parts[k], k) for k in order}
    parts = [parts[0]] + [got[k] for k in range(1, n_t)]

    p_own, a_own = call(
        functools.partial(own_body, keep),
        [near((B, groups * 2 * B)), near((groups * B, 2 * B))],
        (own, small),
        [VM, VM],
        [VM, VM],
        name="own_places",
    )

    def grads_of(ks, after):
        return call(
            functools.partial(grads_body, len(ks)),
            [near((B, cols), BF16 if k else F32) for k in ks],
            (act, after, *[parts[k] for k in ks]),
            [VM, ANY] + [VM] * len(ks),
            [VM] * len(ks),
            name="weight_grads",
        )

    grads = {}
    for k in order[:-1]:
        (grads[k],) = grads_of([k], act)
    made, grads[0] = grads_of([order[-1], 0], a_own)
    grads[order[-1]] = made
    grads.update({k: trade(grads[k], k) for k in order})

    bundle = call(
        functools.partial(bundle_body, n_t, keep),
        near(((n_t - 1) * tiles * nr + 16, 128)),
        (made, own, *parts[1:]),
        [ANY] + [VM] * n_t,
        VM,
        name="bundle",
    )
    bundles = lax.all_gather(bundle, "replica", axis=0)

    places = call(
        functools.partial(places_body, keep),
        [near((B, blocks * half * keep))] * 4,
        (far(mask), far(tally), small, bundles),
        [ANY, ANY, VM, VM],
        [VM] * 4,
        scratch=[pltpu.SMEM((n_r,), jnp.int32)] * 2 + [pltpu.SemaphoreType.DMA((2,))],
        name="places",
    )
    input_grad = call(
        functools.partial(input_grad_body, n_t, n_r, cp),
        jax.ShapeDtypeStruct((tok, cols), BF16),
        (far(exp), bundles, *parts),
        [ANY] + [VM] * (1 + n_t),
        VM,
        scratch=[pltpu.VMEM((n_t * B, cols), BF16), pltpu.SemaphoreType.DMA],
        flops=2 * tok * n_t * B * cols,
        nbytes=(n_t * B * cols + tok * cols) * 2,
        name="input_grads",
    )

    rows = []
    for ks in ([k for k in range(n_t) if k != n_t - 1], [n_t - 1]):
        rows = call(
            functools.partial(kept_body, ks, n_t, keep),
            [near((keep, width)), near((keep, width), F32)],
            (vel[0], a_own, tab, bundles, *[grads[k] for k in ks], *rows),
            [VM] * 3 + [ANY] + [VM] * (len(ks) + len(rows)),
            [VM] * 2,
            flops=6 * B * B * cols * len(ks),
            nbytes=B * cols * 6 * len(ks),
            name="kept_rows",
            alias={4 + len(ks): 0, 5 + len(ks): 1} if rows else {},
        )
    ship, q_own = rows
    ships = [ship] + [swap(ship, 2 * i) for i in range(1, half)]
    new = call(
        functools.partial(return_body, n_t, keep),
        jax.ShapeDtypeStruct((B, width), F32),
        (vel[0], p_own, q_own, *[grads[k] for k in range(n_t)]),
        [VM] * (3 + n_t),
        ANY,
        scratch=[pltpu.VMEM((B, width), F32), pltpu.SemaphoreType.DMA((n_t,))],
        flops=6 * B * B * width,
        nbytes=B * width * 10,
        name="new_momentums",
    )
    mine = call(
        functools.partial(join_body, half),
        near((half, keep, width)),
        (*ships, far(new), far(input_grad), places[0]),
        [VM] * half + [ANY] * 3,
        VM,
        name="join_kept",
    )
    other = swap(mine, 1)
    half_sum = call(
        half_update_body,
        near((groups * B, G), F32),
        (*places[:2], mine),
        [VM] * 3,
        VM,
        name="half_updates",
    )
    chunk = 2 if groups % 2 == 0 else 1
    update = call(
        functools.partial(update_body, chunk),
        jax.ShapeDtypeStruct((B, width), F32),
        (half_sum, *places[2:], other),
        [VM] * 4,
        ANY,
        scratch=[
            pltpu.VMEM((B, width), F32),
            pltpu.SemaphoreType.DMA((groups // chunk,)),
        ],
        flops=8 * B * G * width,
        nbytes=B * width * 8,
        name="updates",
    )
    return input_grad, new[None], update


def per_device_plain(
    projection_inputs,
    switch_logits_raw,
    inner_neuron_slope,
    expansion_matrix,
    velocity_buffer,
    sent_spectral_lines,
    participant_mask,
    token_tallies,
):
    highest = lax.Precision.HIGHEST
    up_grad = (
        inner_neuron_slope.astype(jnp.float32) * jax.nn.silu(switch_logits_raw.astype(jnp.float32))
    ).astype(jnp.bfloat16)
    partial_terms = jnp.dot(up_grad, expansion_matrix, preferred_element_type=jnp.float32)
    input_grad = lax.psum_scatter(partial_terms, "tensor", scatter_dimension=1, tiled=True).astype(
        jnp.bfloat16
    )
    grad_w = lax.dot_general(
        up_grad,
        lax.all_gather(projection_inputs, "tensor", axis=1, tiled=True),
        (((0,), (0,)), ((), ())),
        preferred_element_type=jnp.float32,
    )
    row_total_count = expansion_matrix.shape[0] // 64
    col_count = expansion_matrix.shape[1] // 64
    moment = momentum_decay * velocity_buffer[0] + grad_w
    cosines = cosine_table()
    blocks = moment.reshape(row_total_count, 64, col_count, 64).transpose(0, 2, 1, 3)
    coefficients = jnp.einsum("fa,ijab,gb->ijfg", cosines, blocks, cosines, precision=highest)
    freq_ids = jnp.arange(64, dtype=jnp.int32)
    own_rows = sent_spectral_lines[0]
    chosen = (own_rows[..., None] == freq_ids).astype(jnp.float32)
    shipped = jnp.einsum("ijkf,ijfg->ijkg", chosen, coefficients, precision=highest).astype(
        jnp.bfloat16
    )
    spectrum = jnp.einsum("ijkf,ijkg->ijfg", chosen, shipped.astype(jnp.float32), precision=highest)
    returned = jnp.einsum("fa,ijfg,gb->ijab", cosines, spectrum, cosines, precision=highest)
    new_moment = moment - returned.transpose(0, 2, 1, 3).reshape(moment.shape)
    worker_burdens = participant_mask.astype(jnp.float32) * token_tallies.astype(jnp.float32)
    worker_fractions = worker_burdens * (
        jnp.sum(participant_mask.astype(jnp.float32)) / jnp.sum(worker_burdens)
    )
    myself = lax.axis_index("replica")
    combined = lax.psum(worker_fractions[myself] * spectrum, "replica")
    update = jnp.einsum("fa,ijfg,gb->ijab", cosines, combined, cosines, precision=highest)
    update = update.transpose(0, 2, 1, 3).reshape(moment.shape)
    return (input_grad, new_moment[None], update)


def solution(mesh):
    n_t, n_r = mesh.shape["tensor"], mesh.shape["replica"]

    def device(*args):
        act, exp, lines = args[0], args[3], args[5]
        fits = (
            act.shape[1] % G == 0
            and act.shape[0] % 128 == 0
            and exp.shape[0] == B
            and lines.shape[3] == 8
            and n_r == 8
            and n_t >= 2
            and n_t & (n_t - 1) == 0
        )
        if not fits:
            return per_device_plain(*args)
        return per_device(n_t, n_r, *args)

    return jax.shard_map(
        device,
        mesh=mesh,
        in_specs=(
            P("replica", "tensor"),
            P("replica", "tensor"),
            P("replica", "tensor"),
            P("tensor", None),
            P("replica", "tensor", None),
            P("replica", "tensor", None, None),
            P(),
            P(),
        ),
        out_specs=(P("replica", "tensor"), P("replica", "tensor", None), P("tensor", None)),
        check_vma=False,
    )
```

```python
import functools

import jax
import jax.numpy as jnp
import numpy as np
from jax import lax
from jax.experimental import pallas as pl
from jax.experimental.pallas import tpu as pltpu
from jax.sharding import PartitionSpec as P

momentum_decay = 0.9
B = 64
G = 256
F32 = jnp.float32
BF16 = jnp.bfloat16
VMEM_LIMIT = 24 * 1024 * 1024

VM = pl.BlockSpec(memory_space=pltpu.VMEM)
SM = pl.BlockSpec(memory_space=pltpu.SMEM)
ANY = pl.BlockSpec(memory_space=pl.ANY)


def cosine_table():
    freqs = jnp.arange(64, dtype=jnp.float32)[:, None]
    places = jnp.arange(64, dtype=jnp.float32)[None, :]
    cosines = jnp.cos(jnp.pi * (places + 0.5) * freqs / 64.0) * jnp.sqrt(2.0 / 64.0)
    return cosines.at[0].multiply(jnp.sqrt(0.5))


def cosine_np():
    f = np.arange(B)[:, None]
    a = np.arange(B)[None, :]
    c = np.cos(np.pi * (a + 0.5) * f / B) * np.sqrt(2.0 / B)
    c[0] *= np.sqrt(0.5)
    return c


def halves(c):
    hi = np.asarray(c, dtype=np.float32).astype(jnp.bfloat16)
    lo = (np.asarray(c, np.float64) - hi.astype(np.float64)).astype(np.float32).astype(jnp.bfloat16)
    return hi, lo


def constants():
    hi, lo = halves(cosine_np())
    eye = np.eye(G // B)
    kron = lambda x: np.kron(eye, np.asarray(x, np.float32)).astype(jnp.bfloat16)
    small = np.zeros((2 * B, 4 * B), jnp.bfloat16)
    for i, x in enumerate((hi, lo)):
        rows = slice(i * B, (i + 1) * B)
        small[rows, :B], small[rows, B : 2 * B], small[rows, 2 * B : 3 * B] = x, x, x.T
    return jnp.asarray(np.concatenate([kron(x) for x in (hi.T, lo.T, hi, lo)], axis=0)), jnp.asarray(small)


def fwd(tab, i):
    return tab[i * G : (i + 1) * G, :]


def inv(tab, i):
    return tab[(2 + i) * G : (3 + i) * G, :]


def dot(a, b):
    return jnp.dot(a, b, preferred_element_type=F32)


def split(x):
    hi = x.astype(BF16)
    return hi, (x - hi.astype(F32)).astype(BF16)


def near(shape, dtype=BF16):
    return pltpu.VMEM(shape, dtype)


def far(x):
    return pltpu.with_memory_space_constraint(x, pltpu.HBM)


def call(body, out_shape, ins, in_specs, out_specs, scratch=(), flops=0, nbytes=0, name=None, alias={}):
    return pl.pallas_call(
        body,
        out_shape=out_shape,
        in_specs=in_specs,
        out_specs=out_specs,
        scratch_shapes=scratch,
        input_output_aliases=alias,
        compiler_params=pltpu.CompilerParams(vmem_limit_bytes=VMEM_LIMIT),
        cost_estimate=pl.CostEstimate(flops=flops, bytes_accessed=nbytes, transcendentals=0),
        name=name,
    )(*ins)


def first_body(n_t, cp, cols, nr, switch, slope, exp_ref, act, lines, small, *refs):
    outs, (act_out, lines_out, small_out) = refs[:n_t], refs[n_t : n_t + 3]
    switch_v, slope_v, exp_v, sems = refs[n_t + 3 :]
    rep, ten = lax.axis_index("replica"), lax.axis_index("tensor")
    r0 = pl.multiple_of((rep // cp) * nr, nr)
    copies = [
        pltpu.make_async_copy(src, dst, sems.at[i])
        for i, (src, dst) in enumerate(
            [
                (switch, switch_v),
                (slope, slope_v),
                (exp_ref.at[pl.ds(r0, nr), :], exp_v),
                (act, act_out),
                (lines, lines_out),
                (small, small_out),
            ]
        )
    ]
    for copy in copies:
        copy.start()
    copies[0].wait()
    copies[1].wait()
    v = switch_v[...].astype(F32)
    up = (slope_v[...].astype(F32) * (v * jax.nn.sigmoid(v))).astype(BF16)
    for k in range(n_t):
        outs[k][:B, :] = up
    copies[2].wait()
    nc = cols // cp
    for k in range(1, n_t):
        c0 = (ten ^ k) * cols + lax.rem(rep, cp) * nc
        for j in range(nc // 128):
            at = pl.multiple_of(c0 + j * 128, 128)
            outs[k][B + j * nr : B + (j + 1) * nr, :] = exp_v[:, pl.ds(at, 128)]
    for copy in copies[3:]:
        copy.wait()


def grads_body(n, act, after, *refs):
    ups, outs = refs[:n], refs[n:]
    up = jnp.concatenate([u[:B, :] for u in ups], axis=0)
    for c in range(0, act.shape[1], G):
        g = dot(up, act[:, c : c + G])
        for k in range(n):
            outs[k][:, c : c + G] = g[k * B : (k + 1) * B].astype(outs[k].dtype)


def bundle_body(n_t, keep, after, lines, *refs):
    parts, out = refs[: n_t - 1], refs[n_t - 1]
    n = parts[0].shape[0] - B
    for k in range(n_t - 1):
        out[k * n : (k + 1) * n, :] = parts[k][B:, :]
    blocks = lines.shape[1]
    rows = jnp.concatenate([lines[...].astype(F32), jnp.zeros((keep, 128 - blocks), F32)], axis=1)
    out[(n_t - 1) * n :, :] = jnp.concatenate([rows, jnp.zeros((16 - keep, 128), F32)], axis=0).astype(BF16)


def join_body(n, *refs):
    for i, ref in enumerate(refs[:n]):
        refs[-1][i] = ref[...]


def own_body(keep, lines, small, p_ref, a_ref):
    blocks, nb = lines.shape[1], G // B
    rows = jnp.concatenate([lines[...].astype(F32), jnp.zeros((keep, 128 - blocks), F32)], axis=1)
    lane = lax.broadcasted_iota(jnp.int32, (nb * keep, 2 * B), 1).astype(F32)
    for g in range(blocks // nb):
        num = jnp.concatenate(
            [jnp.broadcast_to(rows[:, g * nb + j : g * nb + j + 1], (keep, 2 * B)) for j in range(nb)], axis=0
        )
        hot = jnp.concatenate(
            [jnp.where(lane == num, 1.0, 0.0), jnp.where(lane - B == num, 1.0, 0.0)], axis=0
        ).astype(BF16)
        a_ref[g * B : (g + 1) * B, :] = dot(hot, small[:, : 2 * B]).astype(BF16)
    rows = jnp.concatenate([rows] * (2 * B // keep), axis=0).T
    freq = lax.broadcasted_iota(jnp.int32, (B, 2 * B), 0).astype(F32)
    block = (lax.broadcasted_iota(jnp.int32, (1, 2 * B), 1) // keep) % nb
    term = lax.broadcasted_iota(jnp.int32, (B, 2 * B), 1) // (B // 2)
    for g in range(blocks // nb):
        num = rows[g * nb : g * nb + 1]
        for j in range(1, nb):
            num = jnp.where(block == j, rows[g * nb + j : g * nb + j + 1], num)
        hot = jnp.where(freq == num, 1.0, 0.0).astype(BF16)
        y = dot(small[:, 2 * B : 3 * B], hot)
        p = jnp.where(term == 3, 0.0, jnp.where(term == 1, y[B:], y[:B]))
        p_ref[:, g * 2 * B : (g + 1) * 2 * B] = p.astype(BF16)


def share_rows(keep, mask, tally, w_ref):
    n_r = mask.shape[0]
    total, alive = jnp.float32(0), jnp.float32(0)
    for r in range(n_r):
        m = mask[r].astype(F32)
        total = total + m * tally[r].astype(F32)
        alive = alive + m
    half = n_r // 2
    place = (lax.broadcasted_iota(jnp.int32, (8, 2 * B), 1) // keep) % half
    scale = jnp.full((8, 2 * B), alive) / jnp.full((8, 2 * B), total)
    for h in range(2):
        w = jnp.zeros((8, 2 * B), F32)
        for i in range(half):
            r = lax.axis_index("replica") ^ (2 * i + h)
            w = jnp.where(place == i, mask[r].astype(F32) * tally[r].astype(F32), w)
        w_ref[h] = w * scale


def kept_body(ks, n_t, keep, vel, a_ref, tab, mask, tally, *refs):
    grads, (send_ref, own_ref, w_ref, mask_s, tally_s, sems) = refs[: len(ks)], refs[len(ks) + 1 :]
    copies = [
        pltpu.make_async_copy(src, dst, sems.at[i])
        for i, (src, dst) in enumerate([(mask, mask_s), (tally, tally_s)])
    ]
    for copy in copies:
        copy.start()
    keep_rows(ks, n_t, keep, vel, a_ref, tab, grads, send_ref, own_ref)
    for copy in copies:
        copy.wait()
    share_rows(keep, mask_s, tally_s, w_ref)


def kept_more_body(ks, n_t, keep, vel, a_ref, tab, *refs):
    keep_rows(ks, n_t, keep, vel, a_ref, tab, refs[: len(ks)], *refs[-2:])


def keep_rows(ks, n_t, keep, vel, a_ref, tab, grads, send_ref, own_ref):
    cols = grads[0].shape[1]
    ng = cols // G
    lane_block = lax.broadcasted_iota(jnp.int32, (keep, G), 1) // B
    sel = []
    for n, k in enumerate(ks):
        c0 = (lax.axis_index("tensor") ^ k) * cols
        for i in range(ng):
            at = pl.multiple_of(c0 + i * G, G)
            moment = momentum_decay * vel[:, pl.ds(at, G)] + grads[n][:, i * G : (i + 1) * G].astype(F32)
            hi, lo = split(moment)
            y = dot(a_ref[pl.ds(pl.multiple_of(at // (G // B), B), B), :], jnp.concatenate([hi, lo], axis=0))
            y = y[: B // 2] + y[B // 2 :]
            got = y[:keep]
            for j in range(1, G // B):
                got = jnp.where(lane_block == j, y[j * keep : (j + 1) * keep], got)
            sel.append(got)
    hi, lo = split(jnp.concatenate(sel, axis=0))
    n = len(ks) * ng * keep
    y = dot(jnp.concatenate([hi, lo], axis=0), fwd(tab, 0))
    kept = (y[:n] + y[n:] + dot(hi, fwd(tab, 1))).astype(BF16)
    q = dot(kept, inv(tab, 0)) + dot(kept, inv(tab, 1))
    for n, k in enumerate(ks):
        c0 = pl.multiple_of((lax.axis_index("tensor") ^ k) * cols, G)
        part = jnp.concatenate([q[(n * ng + i) * keep : (n * ng + i + 1) * keep] for i in range(ng)], axis=1)
        own_ref[:, pl.ds(c0, cols)] = part
        send_ref[:, pl.ds(c0, cols)] = part.astype(BF16)


def return_body(n_t, keep, vel, p_ref, q, *refs):
    grads, (new_ref, held, sems) = refs[:n_t], refs[n_t:]
    cols = grads[0].shape[1]
    ng = cols // G
    lane_block = lax.broadcasted_iota(jnp.int32, (keep, G), 1) // B
    copies = []
    for k in range(n_t):
        c0 = pl.multiple_of((lax.axis_index("tensor") ^ k) * cols, G)
        for i in range(ng):
            at = pl.multiple_of(c0 + i * G, G)
            own = q[:, pl.ds(at, G)]
            spread = jnp.concatenate(
                [jnp.where(lane_block == j, own, 0.0) for j in range(G // B)], axis=0
            )
            hi, lo = split(spread)
            w = jnp.concatenate([hi, hi, lo, jnp.zeros_like(lo)], axis=0)
            back = dot(p_ref[:, pl.ds(pl.multiple_of(at // 2, 2 * B), 2 * B)], w)
            moment = momentum_decay * vel[:, pl.ds(at, G)] + grads[k][:, i * G : (i + 1) * G].astype(F32)
            held[:, pl.ds(at, G)] = moment - back
        cut = pl.ds(c0, cols)
        copies.append(pltpu.make_async_copy(held.at[:, cut], new_ref.at[:, cut], sems.at[k]))
        copies[-1].start()
    for copy in copies:
        copy.wait()


def places_body(keep, w_ref, small, bundles, exp_ref, *refs):
    p_refs, (local, sem) = refs[:4], refs[4:]
    cols = local.shape[1]
    c0 = pl.multiple_of(lax.axis_index("tensor") * cols, 128)
    copy = pltpu.make_async_copy(exp_ref.at[:, pl.ds(c0, cols)], local, sem)
    copy.start()
    n_r, last = bundles.shape[0], bundles.shape[1] - 16
    half, nb = n_r // 2, G // B
    rep = lax.axis_index("replica")
    freq = lax.broadcasted_iota(jnp.int32, (B, 2 * B), 0).astype(F32)
    block = lax.broadcasted_iota(jnp.int32, (1, 2 * B), 1) // (half * keep)
    for h in range(2):
        hi_ref, lo_ref = p_refs[2 * h : 2 * h + 2]
        w = w_ref[h, :1, :]
        rows = [bundles[rep ^ (2 * i + h), last:, :].astype(F32)[:keep] for i in range(half)]
        rows = jnp.concatenate(rows * nb, axis=0).T
        for g in range(hi_ref.shape[1] // (2 * B)):
            num = rows[g * nb : g * nb + 1]
            for j in range(1, nb):
                num = jnp.where(block == j, rows[g * nb + j : g * nb + j + 1], num)
            hot = jnp.where(freq == num, 1.0, 0.0).astype(BF16)
            y = dot(small[:, 2 * B : 3 * B], hot)
            hi, lo = split((y[:B] + y[B:]) * w)
            hi_ref[:, g * 2 * B : (g + 1) * 2 * B] = hi
            lo_ref[:, g * 2 * B : (g + 1) * 2 * B] = lo
    copy.wait()


def spread_rows(p_hi, p_lo, ships, g):
    half, keep = ships.shape[0], ships.shape[1]
    lane_block = lax.broadcasted_iota(jnp.int32, (half * keep, G), 1) // B
    s = jnp.concatenate([ships[i, :, g * G : (g + 1) * G].astype(F32) for i in range(half)], axis=0)
    w = jnp.concatenate(
        [jnp.where(lane_block == j, s, 0.0).astype(BF16) for j in range(G // B)], axis=0
    )
    cut = slice(g * 2 * B, (g + 1) * 2 * B)
    y = dot(jnp.concatenate([p_hi[:, cut], p_lo[:, cut]], axis=0), w)
    return y[:B] + y[B:]


def half_update_body(p_hi, p_lo, mine, out):
    for g in range(out.shape[0] // B):
        out[g * B : (g + 1) * B, :] = spread_rows(p_hi, p_lo, mine, g)


def update_body(chunk, half_sum, p_hi, p_lo, other, out, held, sems):
    ng = half_sum.shape[0] // B
    copies = []
    for c in range(0, ng, chunk):
        for g in range(c, c + chunk):
            held[:, g * G : (g + 1) * G] = half_sum[g * B : (g + 1) * B, :] + spread_rows(p_hi, p_lo, other, g)
        cut = pl.ds(c * G, chunk * G)
        copies.append(pltpu.make_async_copy(held.at[:, cut], out.at[:, cut], sems.at[c // chunk]))
        copies[-1].start()
    for copy in copies:
        copy.wait()


def input_grad_body(n_t, n_r, cp, local, bundles, *refs):
    ups, (out, held) = refs[:n_t], refs[n_t:]
    cols = out.shape[1]
    held[:B, :] = local[...]
    nc = cols // cp
    nr = B // (n_r // cp)
    tiles = nc // 128
    for r in range(n_r):
        r0, c0 = (r // cp) * nr, (r % cp) * nc
        for k in range(1, n_t):
            for j in range(tiles):
                at = ((k - 1) * tiles + j) * nr
                held[k * B + r0 : k * B + r0 + nr, c0 + j * 128 : c0 + (j + 1) * 128] = bundles[r, at : at + nr, :]
    up = jnp.concatenate([u[:B, :] for u in ups], axis=0).T
    for c in range(0, cols, G):
        out[:, c : c + G] = dot(up, held[:, c : c + G]).astype(BF16)


def per_device(n_t, n_r, act, switch, slope, exp, vel, lines, mask, tally):
    cols = act.shape[1]
    width = exp.shape[1]
    tok = act.shape[0]
    keep = lines.shape[3]
    blocks = width // B
    groups = width // G
    cp = 2
    rp = n_r // cp
    half = n_r // 2
    tab, small = constants()
    def trade(x, k):
        return lax.ppermute(x, "tensor", [(i, i ^ k) for i in range(n_t)])

    order = [*range(2, n_t), 1]

    def swap(x, m):
        return lax.ppermute(x, "replica", [(i, i ^ m) for i in range(n_r)])

    own = lines[0, 0].T
    tiles = cols // cp // 128
    nr = B // rp
    *parts, act, own, small = call(
        functools.partial(first_body, n_t, cp, cols, nr),
        [near((B, tok))]
        + [near((B + tiles * nr, 128))] * (n_t - 1)
        + [near(act.shape), near(own.shape, jnp.int32), near(small.shape)],
        (far(switch.T), far(slope.T), far(exp), far(act), far(own), far(small)),
        [ANY] * 6,
        [VM] * (n_t + 3),
        scratch=[
            pltpu.VMEM((B, tok), BF16),
            pltpu.VMEM((B, tok), BF16),
            pltpu.VMEM((nr, width), BF16),
            pltpu.SemaphoreType.DMA((6,)),
        ],
        nbytes=act.size * 4 + nr * width * 2,
        name="up_grads",
    )
    got = {k: trade(parts[k], k) for k in order}
    parts = [parts[0]] + [got[k] for k in range(1, n_t)]

    p_own, a_own = call(
        functools.partial(own_body, keep),
        [near((B, groups * 2 * B)), near((groups * B, 2 * B))],
        (own, small),
        [VM, VM],
        [VM, VM],
        name="own_places",
    )

    def grads_of(ks, after):
        return call(
            functools.partial(grads_body, len(ks)),
            [near((B, cols), BF16 if k else F32) for k in ks],
            (act, after, *[parts[k] for k in ks]),
            [VM, ANY] + [VM] * len(ks),
            [VM] * len(ks),
            name="weight_grads",
        )

    grads = {}
    for k in order[:-1]:
        (grads[k],) = grads_of([k], act)
    made, grads[0] = grads_of([order[-1], 0], a_own)
    grads[order[-1]] = made
    grads.update({k: trade(grads[k], k) for k in order})

    bundle = call(
        functools.partial(bundle_body, n_t, keep),
        near(((n_t - 1) * tiles * nr + 16, 128)),
        (made, own, *parts[1:]),
        [ANY] + [VM] * n_t,
        VM,
        name="bundle",
    )
    bundles = lax.all_gather(bundle, "replica", axis=0)

    rows = []
    for ks in ([k for k in range(n_t) if k != n_t - 1], [n_t - 1]):
        n = len(ks)
        first = not rows
        rows = call(
            functools.partial(kept_body if first else kept_more_body, ks, n_t, keep),
            [near((keep, width)), near((keep, width), F32)] + [near((2, 8, 2 * B), F32)] * first,
            (vel[0], a_own, tab, *((far(mask), far(tally)) if first else ()), *[grads[k] for k in ks])
            + (bundles,) * first
            + tuple(rows[:2]),
            [VM] * 3 + [ANY] * 2 * first + [VM] * n + ([ANY] if first else [VM] * 2),
            [VM] * (2 + first),
            scratch=([pltpu.SMEM((n_r,), jnp.int32)] * 2 + [pltpu.SemaphoreType.DMA((2,))]) * first,
            flops=6 * B * B * cols * n,
            nbytes=B * cols * 6 * n,
            name="kept_rows",
            alias={} if first else {3 + n: 0, 4 + n: 1},
        )
        shares = rows[2] if first else shares
    ship, q_own = rows

    *places, local = call(
        functools.partial(places_body, keep),
        [near((B, blocks * half * keep))] * 4 + [near((B, cols))],
        (shares, small, bundles, far(exp)),
        [VM] * 3 + [ANY],
        [VM] * 5,
        scratch=[pltpu.SemaphoreType.DMA],
        name="places",
    )
    input_grad = call(
        functools.partial(input_grad_body, n_t, n_r, cp),
        jax.ShapeDtypeStruct((tok, cols), BF16),
        (local, bundles, *parts),
        [VM] * (2 + n_t),
        VM,
        scratch=[pltpu.VMEM((n_t * B, cols), BF16)],
        flops=2 * tok * n_t * B * cols,
        nbytes=(n_t * B * cols + tok * cols) * 2,
        name="input_grads",
    )

    ships = [ship] + [swap(ship, 2 * i) for i in range(1, half)]
    new = call(
        functools.partial(return_body, n_t, keep),
        jax.ShapeDtypeStruct((B, width), F32),
        (vel[0], p_own, q_own, *[grads[k] for k in range(n_t)]),
        [VM] * (3 + n_t),
        ANY,
        scratch=[pltpu.VMEM((B, width), F32), pltpu.SemaphoreType.DMA((n_t,))],
        flops=6 * B * B * width,
        nbytes=B * width * 10,
        name="new_momentums",
    )
    mine = call(
        functools.partial(join_body, half),
        near((half, keep, width)),
        (*ships, far(new), far(input_grad), places[0]),
        [VM] * half + [ANY] * 3,
        VM,
        name="join_kept",
    )
    other = swap(mine, 1)
    half_sum = call(
        half_update_body,
        near((groups * B, G), F32),
        (*places[:2], mine),
        [VM] * 3,
        VM,
        name="half_updates",
    )
    chunk = 2 if groups % 2 == 0 else 1
    update = call(
        functools.partial(update_body, chunk),
        jax.ShapeDtypeStruct((B, width), F32),
        (half_sum, *places[2:], other),
        [VM] * 4,
        ANY,
        scratch=[
            pltpu.VMEM((B, width), F32),
            pltpu.SemaphoreType.DMA((groups // chunk,)),
        ],
        flops=8 * B * G * width,
        nbytes=B * width * 8,
        name="updates",
    )
    return input_grad, new[None], update


def per_device_plain(
    projection_inputs,
    switch_logits_raw,
    inner_neuron_slope,
    expansion_matrix,
    velocity_buffer,
    sent_spectral_lines,
    participant_mask,
    token_tallies,
):
    highest = lax.Precision.HIGHEST
    up_grad = (
        inner_neuron_slope.astype(jnp.float32) * jax.nn.silu(switch_logits_raw.astype(jnp.float32))
    ).astype(jnp.bfloat16)
    partial_terms = jnp.dot(up_grad, expansion_matrix, preferred_element_type=jnp.float32)
    input_grad = lax.psum_scatter(partial_terms, "tensor", scatter_dimension=1, tiled=True).astype(
        jnp.bfloat16
    )
    grad_w = lax.dot_general(
        up_grad,
        lax.all_gather(projection_inputs, "tensor", axis=1, tiled=True),
        (((0,), (0,)), ((), ())),
        preferred_element_type=jnp.float32,
    )
    row_total_count = expansion_matrix.shape[0] // 64
    col_count = expansion_matrix.shape[1] // 64
    moment = momentum_decay * velocity_buffer[0] + grad_w
    cosines = cosine_table()
    blocks = moment.reshape(row_total_count, 64, col_count, 64).transpose(0, 2, 1, 3)
    coefficients = jnp.einsum("fa,ijab,gb->ijfg", cosines, blocks, cosines, precision=highest)
    freq_ids = jnp.arange(64, dtype=jnp.int32)
    own_rows = sent_spectral_lines[0]
    chosen = (own_rows[..., None] == freq_ids).astype(jnp.float32)
    shipped = jnp.einsum("ijkf,ijfg->ijkg", chosen, coefficients, precision=highest).astype(
        jnp.bfloat16
    )
    spectrum = jnp.einsum("ijkf,ijkg->ijfg", chosen, shipped.astype(jnp.float32), precision=highest)
    returned = jnp.einsum("fa,ijfg,gb->ijab", cosines, spectrum, cosines, precision=highest)
    new_moment = moment - returned.transpose(0, 2, 1, 3).reshape(moment.shape)
    worker_burdens = participant_mask.astype(jnp.float32) * token_tallies.astype(jnp.float32)
    worker_fractions = worker_burdens * (
        jnp.sum(participant_mask.astype(jnp.float32)) / jnp.sum(worker_burdens)
    )
    myself = lax.axis_index("replica")
    combined = lax.psum(worker_fractions[myself] * spectrum, "replica")
    update = jnp.einsum("fa,ijfg,gb->ijab", cosines, combined, cosines, precision=highest)
    update = update.transpose(0, 2, 1, 3).reshape(moment.shape)
    return (input_grad, new_moment[None], update)


def solution(mesh):
    n_t, n_r = mesh.shape["tensor"], mesh.shape["replica"]

    def device(*args):
        act, exp, lines = args[0], args[3], args[5]
        fits = (
            act.shape[1] % G == 0
            and act.shape[0] % 128 == 0
            and exp.shape[0] == B
            and lines.shape[3] == 8
            and n_r == 8
            and n_t >= 2
            and n_t & (n_t - 1) == 0
        )
        if not fits:
            return per_device_plain(*args)
        return per_device(n_t, n_r, *args)

    return jax.shard_map(
        device,
        mesh=mesh,
        in_specs=(
            P("replica", "tensor"),
            P("replica", "tensor"),
            P("replica", "tensor"),
            P("tensor", None),
            P("replica", "tensor", None),
            P("replica", "tensor", None, None),
            P(),
            P(),
        ),
        out_specs=(P("replica", "tensor"), P("replica", "tensor", None), P("tensor", None)),
        check_vma=False,
    )
```

```python
import functools

import jax
import jax.numpy as jnp
import numpy as np
from jax import lax
from jax.experimental import pallas as pl
from jax.experimental.pallas import tpu as pltpu
from jax.sharding import PartitionSpec as P

momentum_decay = 0.9
B = 64
G = 256
F32 = jnp.float32
BF16 = jnp.bfloat16
VMEM_LIMIT = 24 * 1024 * 1024

VM = pl.BlockSpec(memory_space=pltpu.VMEM)
SM = pl.BlockSpec(memory_space=pltpu.SMEM)
ANY = pl.BlockSpec(memory_space=pl.ANY)


def cosine_table():
    freqs = jnp.arange(64, dtype=jnp.float32)[:, None]
    places = jnp.arange(64, dtype=jnp.float32)[None, :]
    cosines = jnp.cos(jnp.pi * (places + 0.5) * freqs / 64.0) * jnp.sqrt(2.0 / 64.0)
    return cosines.at[0].multiply(jnp.sqrt(0.5))


def cosine_np():
    f = np.arange(B)[:, None]
    a = np.arange(B)[None, :]
    c = np.cos(np.pi * (a + 0.5) * f / B) * np.sqrt(2.0 / B)
    c[0] *= np.sqrt(0.5)
    return c


def halves(c):
    hi = np.asarray(c, dtype=np.float32).astype(jnp.bfloat16)
    lo = (np.asarray(c, np.float64) - hi.astype(np.float64)).astype(np.float32).astype(jnp.bfloat16)
    return hi, lo


def constants():
    hi, lo = halves(cosine_np())
    eye = np.eye(G // B)
    kron = lambda x: np.kron(eye, np.asarray(x, np.float32)).astype(jnp.bfloat16)
    small = np.zeros((2 * B, 4 * B), jnp.bfloat16)
    for i, x in enumerate((hi, lo)):
        rows = slice(i * B, (i + 1) * B)
        small[rows, :B], small[rows, B : 2 * B], small[rows, 2 * B : 3 * B] = x, x, x.T
    return jnp.asarray(np.concatenate([kron(x) for x in (hi.T, lo.T, hi, lo)], axis=0)), jnp.asarray(small)


def fwd(tab, i):
    return tab[i * G : (i + 1) * G, :]


def inv(tab, i):
    return tab[(2 + i) * G : (3 + i) * G, :]


def dot(a, b):
    return jnp.dot(a, b, preferred_element_type=F32)


def split(x):
    hi = x.astype(BF16)
    return hi, (x - hi.astype(F32)).astype(BF16)


def near(shape, dtype=BF16):
    return pltpu.VMEM(shape, dtype)


def far(x):
    return pltpu.with_memory_space_constraint(x, pltpu.HBM)


def call(body, out_shape, ins, in_specs, out_specs, scratch=(), flops=0, nbytes=0, name=None, alias={}):
    return pl.pallas_call(
        body,
        out_shape=out_shape,
        in_specs=in_specs,
        out_specs=out_specs,
        scratch_shapes=scratch,
        input_output_aliases=alias,
        compiler_params=pltpu.CompilerParams(vmem_limit_bytes=VMEM_LIMIT),
        cost_estimate=pl.CostEstimate(flops=flops, bytes_accessed=nbytes, transcendentals=0),
        name=name,
    )(*ins)


def first_body(n_t, cp, cols, nr, switch, slope, exp_ref, act, lines, small, *refs):
    outs, (act_out, lines_out, small_out) = refs[:n_t], refs[n_t : n_t + 3]
    switch_v, slope_v, exp_v, sems = refs[n_t + 3 :]
    rep, ten = lax.axis_index("replica"), lax.axis_index("tensor")
    r0 = pl.multiple_of((rep // cp) * nr, nr)
    copies = [
        pltpu.make_async_copy(src, dst, sems.at[i])
        for i, (src, dst) in enumerate(
            [
                (switch, switch_v),
                (slope, slope_v),
                (exp_ref.at[pl.ds(r0, nr), :], exp_v),
                (act, act_out),
                (lines, lines_out),
                (small, small_out),
            ]
        )
    ]
    for copy in copies:
        copy.start()
    copies[0].wait()
    copies[1].wait()
    v = switch_v[...].astype(F32)
    up = (slope_v[...].astype(F32) * (v * jax.nn.sigmoid(v))).astype(BF16)
    for k in range(n_t):
        outs[k][:B, :] = up
    copies[2].wait()
    nc = cols // cp
    for k in range(1, n_t):
        c0 = (ten ^ k) * cols + lax.rem(rep, cp) * nc
        for j in range(nc // 128):
            at = pl.multiple_of(c0 + j * 128, 128)
            outs[k][B + j * nr : B + (j + 1) * nr, :] = exp_v[:, pl.ds(at, 128)]
    for copy in copies[3:]:
        copy.wait()


def grads_body(n, act, after, *refs):
    ups, outs = refs[:n], refs[n:]
    up = jnp.concatenate([u[:B, :] for u in ups], axis=0)
    for c in range(0, act.shape[1], G):
        g = dot(up, act[:, c : c + G])
        for k in range(n):
            outs[k][:, c : c + G] = g[k * B : (k + 1) * B].astype(outs[k].dtype)


def bundle_body(n_t, keep, after, lines, *refs):
    parts, out = refs[: n_t - 1], refs[n_t - 1]
    n = parts[0].shape[0] - B
    for k in range(n_t - 1):
        out[k * n : (k + 1) * n, :] = parts[k][B:, :]
    blocks = lines.shape[1]
    rows = jnp.concatenate([lines[...].astype(F32), jnp.zeros((keep, 128 - blocks), F32)], axis=1)
    out[(n_t - 1) * n :, :] = jnp.concatenate([rows, jnp.zeros((16 - keep, 128), F32)], axis=0).astype(BF16)


def join_body(n, *refs):
    for i, ref in enumerate(refs[:n]):
        refs[-1][i] = ref[...]


def own_body(keep, lines, small, p_ref, a_ref):
    blocks, nb = lines.shape[1], G // B
    rows = jnp.concatenate([lines[...].astype(F32), jnp.zeros((keep, 128 - blocks), F32)], axis=1)
    lane = lax.broadcasted_iota(jnp.int32, (nb * keep, 2 * B), 1).astype(F32)
    for g in range(blocks // nb):
        num = jnp.concatenate(
            [jnp.broadcast_to(rows[:, g * nb + j : g * nb + j + 1], (keep, 2 * B)) for j in range(nb)], axis=0
        )
        hot = jnp.concatenate(
            [jnp.where(lane == num, 1.0, 0.0), jnp.where(lane - B == num, 1.0, 0.0)], axis=0
        ).astype(BF16)
        a_ref[g * B : (g + 1) * B, :] = dot(hot, small[:, : 2 * B]).astype(BF16)
    rows = jnp.concatenate([rows] * (2 * B // keep), axis=0).T
    freq = lax.broadcasted_iota(jnp.int32, (B, 2 * B), 0).astype(F32)
    block = (lax.broadcasted_iota(jnp.int32, (1, 2 * B), 1) // keep) % nb
    term = lax.broadcasted_iota(jnp.int32, (B, 2 * B), 1) // (B // 2)
    for g in range(blocks // nb):
        num = rows[g * nb : g * nb + 1]
        for j in range(1, nb):
            num = jnp.where(block == j, rows[g * nb + j : g * nb + j + 1], num)
        hot = jnp.where(freq == num, 1.0, 0.0).astype(BF16)
        y = dot(small[:, 2 * B : 3 * B], hot)
        p = jnp.where(term == 3, 0.0, jnp.where(term == 1, y[B:], y[:B]))
        p_ref[:, g * 2 * B : (g + 1) * 2 * B] = p.astype(BF16)


def kept_body(ks, n_t, keep, vel, a_ref, tab, after, *refs):
    keep_rows(ks, n_t, keep, vel, a_ref, tab, refs[: len(ks)], *refs[-2:])


def keep_rows(ks, n_t, keep, vel, a_ref, tab, grads, send_ref, own_ref):
    cols = grads[0].shape[1]
    ng = cols // G
    lane_block = lax.broadcasted_iota(jnp.int32, (keep, G), 1) // B
    sel = []
    for n, k in enumerate(ks):
        c0 = (lax.axis_index("tensor") ^ k) * cols
        for i in range(ng):
            at = pl.multiple_of(c0 + i * G, G)
            moment = momentum_decay * vel[:, pl.ds(at, G)] + grads[n][:, i * G : (i + 1) * G].astype(F32)
            hi, lo = split(moment)
            y = dot(a_ref[pl.ds(pl.multiple_of(at // (G // B), B), B), :], jnp.concatenate([hi, lo], axis=0))
            y = y[: B // 2] + y[B // 2 :]
            got = y[:keep]
            for j in range(1, G // B):
                got = jnp.where(lane_block == j, y[j * keep : (j + 1) * keep], got)
            sel.append(got)
    hi, lo = split(jnp.concatenate(sel, axis=0))
    n = len(ks) * ng * keep
    y = dot(jnp.concatenate([hi, lo], axis=0), fwd(tab, 0))
    kept = (y[:n] + y[n:] + dot(hi, fwd(tab, 1))).astype(BF16)
    q = dot(kept, inv(tab, 0)) + dot(kept, inv(tab, 1))
    for n, k in enumerate(ks):
        c0 = pl.multiple_of((lax.axis_index("tensor") ^ k) * cols, G)
        part = jnp.concatenate([q[(n * ng + i) * keep : (n * ng + i + 1) * keep] for i in range(ng)], axis=1)
        own_ref[:, pl.ds(c0, cols)] = part
        send_ref[:, pl.ds(c0, cols)] = part.astype(BF16)


def return_body(n_t, keep, vel, p_ref, q, *refs):
    grads, (new_ref, held, sems) = refs[:n_t], refs[n_t:]
    cols = grads[0].shape[1]
    ng = cols // G
    lane_block = lax.broadcasted_iota(jnp.int32, (keep, G), 1) // B
    copies = []
    for k in range(n_t):
        c0 = pl.multiple_of((lax.axis_index("tensor") ^ k) * cols, G)
        for i in range(ng):
            at = pl.multiple_of(c0 + i * G, G)
            own = q[:, pl.ds(at, G)]
            spread = jnp.concatenate(
                [jnp.where(lane_block == j, own, 0.0) for j in range(G // B)], axis=0
            )
            hi, lo = split(spread)
            w = jnp.concatenate([hi, hi, lo, jnp.zeros_like(lo)], axis=0)
            back = dot(p_ref[:, pl.ds(pl.multiple_of(at // 2, 2 * B), 2 * B)], w)
            moment = momentum_decay * vel[:, pl.ds(at, G)] + grads[k][:, i * G : (i + 1) * G].astype(F32)
            held[:, pl.ds(at, G)] = moment - back
        cut = pl.ds(c0, cols)
        copies.append(pltpu.make_async_copy(held.at[:, cut], new_ref.at[:, cut], sems.at[k]))
        copies[-1].start()
    for copy in copies:
        copy.wait()


def places_body(keep, mask, tally, small, bundles, *p_refs):
    n_r, last = bundles.shape[0], bundles.shape[1] - 16
    half, nb = n_r // 2, G // B
    rep = lax.axis_index("replica")
    total, alive = jnp.float32(0), jnp.float32(0)
    for r in range(n_r):
        m = mask[r].astype(F32)
        total = total + m * tally[r].astype(F32)
        alive = alive + m
    scale = jnp.full((1, 2 * B), alive) / jnp.full((1, 2 * B), total)
    freq = lax.broadcasted_iota(jnp.int32, (B, 2 * B), 0).astype(F32)
    lane = lax.broadcasted_iota(jnp.int32, (1, 2 * B), 1)
    block, place = lane // (half * keep), (lane // keep) % half
    for h in range(2):
        hi_ref, lo_ref = p_refs[2 * h : 2 * h + 2]
        w = jnp.zeros((1, 2 * B), F32)
        for i in range(half):
            r = rep ^ (2 * i + h)
            w = jnp.where(place == i, mask[r].astype(F32) * tally[r].astype(F32), w)
        w = w * scale
        rows = [bundles[rep ^ (2 * i + h), last:, :].astype(F32)[:keep] for i in range(half)]
        rows = jnp.concatenate(rows * nb, axis=0).T
        for g in range(hi_ref.shape[1] // (2 * B)):
            num = rows[g * nb : g * nb + 1]
            for j in range(1, nb):
                num = jnp.where(block == j, rows[g * nb + j : g * nb + j + 1], num)
            hot = jnp.where(freq == num, 1.0, 0.0).astype(BF16)
            y = dot(small[:, 2 * B : 3 * B], hot)
            hi, lo = split((y[:B] + y[B:]) * w)
            hi_ref[:, g * 2 * B : (g + 1) * 2 * B] = hi
            lo_ref[:, g * 2 * B : (g + 1) * 2 * B] = lo


def spread_rows(p_hi, p_lo, ships, g):
    half, keep = ships.shape[0], ships.shape[1]
    lane_block = lax.broadcasted_iota(jnp.int32, (half * keep, G), 1) // B
    s = jnp.concatenate([ships[i, :, g * G : (g + 1) * G].astype(F32) for i in range(half)], axis=0)
    w = jnp.concatenate(
        [jnp.where(lane_block == j, s, 0.0).astype(BF16) for j in range(G // B)], axis=0
    )
    cut = slice(g * 2 * B, (g + 1) * 2 * B)
    y = dot(jnp.concatenate([p_hi[:, cut], p_lo[:, cut]], axis=0), w)
    return y[:B] + y[B:]


def half_update_body(p_hi, p_lo, mine, out):
    for g in range(out.shape[0] // B):
        out[g * B : (g + 1) * B, :] = spread_rows(p_hi, p_lo, mine, g)


def update_body(chunk, half_sum, p_hi, p_lo, other, out, held, sems):
    ng = half_sum.shape[0] // B
    copies = []
    for c in range(0, ng, chunk):
        for g in range(c, c + chunk):
            held[:, g * G : (g + 1) * G] = half_sum[g * B : (g + 1) * B, :] + spread_rows(p_hi, p_lo, other, g)
        cut = pl.ds(c * G, chunk * G)
        copies.append(pltpu.make_async_copy(held.at[:, cut], out.at[:, cut], sems.at[c // chunk]))
        copies[-1].start()
    for copy in copies:
        copy.wait()


def input_grad_body(n_t, n_r, cp, exp_ref, bundles, *refs):
    ups, (out, held) = refs[:n_t], refs[n_t:]
    cols = out.shape[1]
    held[:B, :] = exp_ref[:, pl.ds(pl.multiple_of(lax.axis_index("tensor") * cols, 128), cols)]
    nc = cols // cp
    nr = B // (n_r // cp)
    tiles = nc // 128
    for r in range(n_r):
        r0, c0 = (r // cp) * nr, (r % cp) * nc
        for k in range(1, n_t):
            for j in range(tiles):
                at = ((k - 1) * tiles + j) * nr
                held[k * B + r0 : k * B + r0 + nr, c0 + j * 128 : c0 + (j + 1) * 128] = bundles[r, at : at + nr, :]
    up = jnp.concatenate([u[:B, :] for u in ups], axis=0).T
    for c in range(0, cols, G):
        out[:, c : c + G] = dot(up, held[:, c : c + G]).astype(BF16)


def per_device(n_t, n_r, act, switch, slope, exp, vel, lines, mask, tally):
    cols = act.shape[1]
    width = exp.shape[1]
    tok = act.shape[0]
    keep = lines.shape[3]
    blocks = width // B
    groups = width // G
    cp = 2
    rp = n_r // cp
    half = n_r // 2
    tab, small = constants()
    def trade(x, k):
        return lax.ppermute(x, "tensor", [(i, i ^ k) for i in range(n_t)])

    order = [*range(2, n_t), 1]

    def swap(x, m):
        return lax.ppermute(x, "replica", [(i, i ^ m) for i in range(n_r)])

    own = lines[0, 0].T
    tiles = cols // cp // 128
    nr = B // rp
    *parts, act, own, small = call(
        functools.partial(first_body, n_t, cp, cols, nr),
        [near((B, tok))]
        + [near((B + tiles * nr, 128))] * (n_t - 1)
        + [near(act.shape), near(own.shape, jnp.int32), near(small.shape)],
        (far(switch.T), far(slope.T), far(exp), far(act), far(own), far(small)),
        [ANY] * 6,
        [VM] * (n_t + 3),
        scratch=[
            pltpu.VMEM((B, tok), BF16),
            pltpu.VMEM((B, tok), BF16),
            pltpu.VMEM((nr, width), BF16),
            pltpu.SemaphoreType.DMA((6,)),
        ],
        nbytes=act.size * 4 + nr * width * 2,
        name="up_grads",
    )
    got = {k: trade(parts[k], k) for k in order}
    parts = [parts[0]] + [got[k] for k in range(1, n_t)]

    p_own, a_own = call(
        functools.partial(own_body, keep),
        [near((B, groups * 2 * B)), near((groups * B, 2 * B))],
        (own, small),
        [VM, VM],
        [VM, VM],
        name="own_places",
    )

    def grads_of(ks, after):
        return call(
            functools.partial(grads_body, len(ks)),
            [near((B, cols), BF16 if k else F32) for k in ks],
            (act, after, *[parts[k] for k in ks]),
            [VM, ANY] + [VM] * len(ks),
            [VM] * len(ks),
            name="weight_grads",
        )

    grads = {}
    for k in order[:-1]:
        (grads[k],) = grads_of([k], act)
    made, grads[0] = grads_of([order[-1], 0], a_own)
    grads[order[-1]] = made
    grads.update({k: trade(grads[k], k) for k in order})

    bundle = call(
        functools.partial(bundle_body, n_t, keep),
        near(((n_t - 1) * tiles * nr + 16, 128)),
        (made, own, *parts[1:]),
        [ANY] + [VM] * n_t,
        VM,
        name="bundle",
    )
    bundles = lax.all_gather(bundle, "replica", axis=0)

    rows = []
    for ks in ([k for k in range(n_t) if k != n_t - 1], [n_t - 1]):
        n = len(ks)
        rows = call(
            functools.partial(kept_body, ks, n_t, keep),
            [near((keep, width)), near((keep, width), F32)],
            (vel[0], a_own, tab, bundles, *[grads[k] for k in ks], *rows),
            [VM] * 3 + [ANY] + [VM] * (n + len(rows)),
            [VM] * 2,
            flops=6 * B * B * cols * n,
            nbytes=B * cols * 6 * n,
            name="kept_rows",
            alias={4 + n: 0, 5 + n: 1} if rows else {},
        )
    ship, q_own = rows

    places = call(
        functools.partial(places_body, keep),
        [near((B, blocks * half * keep))] * 4,
        (mask, tally, small, bundles),
        [SM, SM, VM, VM],
        [VM] * 4,
        name="places",
    )
    input_grad = call(
        functools.partial(input_grad_body, n_t, n_r, cp),
        jax.ShapeDtypeStruct((tok, cols), BF16),
        (exp, bundles, *parts),
        [VM] * (2 + n_t),
        VM,
        scratch=[pltpu.VMEM((n_t * B, cols), BF16)],
        flops=2 * tok * n_t * B * cols,
        nbytes=(n_t * B * cols + tok * cols) * 2,
        name="input_grads",
    )

    ships = [ship] + [swap(ship, 2 * i) for i in range(1, half)]
    new = call(
        functools.partial(return_body, n_t, keep),
        jax.ShapeDtypeStruct((B, width), F32),
        (vel[0], p_own, q_own, *[grads[k] for k in range(n_t)]),
        [VM] * (3 + n_t),
        ANY,
        scratch=[pltpu.VMEM((B, width), F32), pltpu.SemaphoreType.DMA((n_t,))],
        flops=6 * B * B * width,
        nbytes=B * width * 10,
        name="new_momentums",
    )
    mine = call(
        functools.partial(join_body, half),
        near((half, keep, width)),
        (*ships, far(new), far(input_grad), places[0]),
        [VM] * half + [ANY] * 3,
        VM,
        name="join_kept",
    )
    other = swap(mine, 1)
    half_sum = call(
        half_update_body,
        near((groups * B, G), F32),
        (*places[:2], mine),
        [VM] * 3,
        VM,
        name="half_updates",
    )
    chunk = 2 if groups % 2 == 0 else 1
    update = call(
        functools.partial(update_body, chunk),
        jax.ShapeDtypeStruct((B, width), F32),
        (half_sum, *places[2:], other),
        [VM] * 4,
        ANY,
        scratch=[
            pltpu.VMEM((B, width), F32),
            pltpu.SemaphoreType.DMA((groups // chunk,)),
        ],
        flops=8 * B * G * width,
        nbytes=B * width * 8,
        name="updates",
    )
    return input_grad, new[None], update


def per_device_plain(
    projection_inputs,
    switch_logits_raw,
    inner_neuron_slope,
    expansion_matrix,
    velocity_buffer,
    sent_spectral_lines,
    participant_mask,
    token_tallies,
):
    highest = lax.Precision.HIGHEST
    up_grad = (
        inner_neuron_slope.astype(jnp.float32) * jax.nn.silu(switch_logits_raw.astype(jnp.float32))
    ).astype(jnp.bfloat16)
    partial_terms = jnp.dot(up_grad, expansion_matrix, preferred_element_type=jnp.float32)
    input_grad = lax.psum_scatter(partial_terms, "tensor", scatter_dimension=1, tiled=True).astype(
        jnp.bfloat16
    )
    grad_w = lax.dot_general(
        up_grad,
        lax.all_gather(projection_inputs, "tensor", axis=1, tiled=True),
        (((0,), (0,)), ((), ())),
        preferred_element_type=jnp.float32,
    )
    row_total_count = expansion_matrix.shape[0] // 64
    col_count = expansion_matrix.shape[1] // 64
    moment = momentum_decay * velocity_buffer[0] + grad_w
    cosines = cosine_table()
    blocks = moment.reshape(row_total_count, 64, col_count, 64).transpose(0, 2, 1, 3)
    coefficients = jnp.einsum("fa,ijab,gb->ijfg", cosines, blocks, cosines, precision=highest)
    freq_ids = jnp.arange(64, dtype=jnp.int32)
    own_rows = sent_spectral_lines[0]
    chosen = (own_rows[..., None] == freq_ids).astype(jnp.float32)
    shipped = jnp.einsum("ijkf,ijfg->ijkg", chosen, coefficients, precision=highest).astype(
        jnp.bfloat16
    )
    spectrum = jnp.einsum("ijkf,ijkg->ijfg", chosen, shipped.astype(jnp.float32), precision=highest)
    returned = jnp.einsum("fa,ijfg,gb->ijab", cosines, spectrum, cosines, precision=highest)
    new_moment = moment - returned.transpose(0, 2, 1, 3).reshape(moment.shape)
    worker_burdens = participant_mask.astype(jnp.float32) * token_tallies.astype(jnp.float32)
    worker_fractions = worker_burdens * (
        jnp.sum(participant_mask.astype(jnp.float32)) / jnp.sum(worker_burdens)
    )
    myself = lax.axis_index("replica")
    combined = lax.psum(worker_fractions[myself] * spectrum, "replica")
    update = jnp.einsum("fa,ijfg,gb->ijab", cosines, combined, cosines, precision=highest)
    update = update.transpose(0, 2, 1, 3).reshape(moment.shape)
    return (input_grad, new_moment[None], update)


def solution(mesh):
    n_t, n_r = mesh.shape["tensor"], mesh.shape["replica"]

    def device(*args):
        act, exp, lines = args[0], args[3], args[5]
        fits = (
            act.shape[1] % G == 0
            and act.shape[0] % 128 == 0
            and exp.shape[0] == B
            and lines.shape[3] == 8
            and n_r == 8
            and n_t >= 2
            and n_t & (n_t - 1) == 0
        )
        if not fits:
            return per_device_plain(*args)
        return per_device(n_t, n_r, *args)

    return jax.shard_map(
        device,
        mesh=mesh,
        in_specs=(
            P("replica", "tensor"),
            P("replica", "tensor"),
            P("replica", "tensor"),
            P("tensor", None),
            P("replica", "tensor", None),
            P("replica", "tensor", None, None),
            P(),
            P(),
        ),
        out_specs=(P("replica", "tensor"), P("replica", "tensor", None), P("tensor", None)),
        check_vma=False,
    )
```

```python
import functools

import jax
import jax.numpy as jnp
import numpy as np
from jax import lax
from jax.experimental import pallas as pl
from jax.experimental.pallas import tpu as pltpu
from jax.sharding import PartitionSpec as P

momentum_decay = 0.9
B = 64
G = 256
F32 = jnp.float32
BF16 = jnp.bfloat16
VMEM_LIMIT = 24 * 1024 * 1024

VM = pl.BlockSpec(memory_space=pltpu.VMEM)
SM = pl.BlockSpec(memory_space=pltpu.SMEM)
ANY = pl.BlockSpec(memory_space=pl.ANY)


def cosine_table():
    freqs = jnp.arange(64, dtype=jnp.float32)[:, None]
    places = jnp.arange(64, dtype=jnp.float32)[None, :]
    cosines = jnp.cos(jnp.pi * (places + 0.5) * freqs / 64.0) * jnp.sqrt(2.0 / 64.0)
    return cosines.at[0].multiply(jnp.sqrt(0.5))


def cosine_np():
    f = np.arange(B)[:, None]
    a = np.arange(B)[None, :]
    c = np.cos(np.pi * (a + 0.5) * f / B) * np.sqrt(2.0 / B)
    c[0] *= np.sqrt(0.5)
    return c


def halves(c):
    hi = np.asarray(c, dtype=np.float32).astype(jnp.bfloat16)
    lo = (np.asarray(c, np.float64) - hi.astype(np.float64)).astype(np.float32).astype(jnp.bfloat16)
    return hi, lo


def constants():
    hi, lo = halves(cosine_np())
    eye = np.eye(G // B)
    kron = lambda x: np.kron(eye, np.asarray(x, np.float32)).astype(jnp.bfloat16)
    small = np.zeros((2 * B, 4 * B), jnp.bfloat16)
    for i, x in enumerate((hi, lo)):
        rows = slice(i * B, (i + 1) * B)
        small[rows, :B], small[rows, B : 2 * B], small[rows, 2 * B : 3 * B] = x, x, x.T
    return jnp.asarray(np.concatenate([kron(x) for x in (hi.T, lo.T, hi, lo)], axis=0)), jnp.asarray(small)


def fwd(tab, i):
    return tab[i * G : (i + 1) * G, :]


def inv(tab, i):
    return tab[(2 + i) * G : (3 + i) * G, :]


def dot(a, b):
    return jnp.dot(a, b, preferred_element_type=F32)


def split(x):
    hi = x.astype(BF16)
    return hi, (x - hi.astype(F32)).astype(BF16)


def near(shape, dtype=BF16):
    return pltpu.VMEM(shape, dtype)


def far(x):
    return pltpu.with_memory_space_constraint(x, pltpu.HBM)


def call(body, out_shape, ins, in_specs, out_specs, scratch=(), flops=0, nbytes=0, name=None, alias={}):
    return pl.pallas_call(
        body,
        out_shape=out_shape,
        in_specs=in_specs,
        out_specs=out_specs,
        scratch_shapes=scratch,
        input_output_aliases=alias,
        compiler_params=pltpu.CompilerParams(vmem_limit_bytes=VMEM_LIMIT),
        cost_estimate=pl.CostEstimate(flops=flops, bytes_accessed=nbytes, transcendentals=0),
        name=name,
    )(*ins)


def first_body(n_t, cp, cols, nr, switch, slope, exp_ref, act, lines, small, *refs):
    outs, (act_out, lines_out, small_out) = refs[:n_t], refs[n_t : n_t + 3]
    switch_v, slope_v, exp_v, sems = refs[n_t + 3 :]
    rep, ten = lax.axis_index("replica"), lax.axis_index("tensor")
    r0 = pl.multiple_of((rep // cp) * nr, nr)
    copies = [
        pltpu.make_async_copy(src, dst, sems.at[i])
        for i, (src, dst) in enumerate(
            [
                (switch, switch_v),
                (slope, slope_v),
                (exp_ref.at[pl.ds(r0, nr), :], exp_v),
                (act, act_out),
                (lines, lines_out),
                (small, small_out),
            ]
        )
    ]
    for copy in copies:
        copy.start()
    copies[0].wait()
    copies[1].wait()
    v = switch_v[...].astype(F32)
    up = (slope_v[...].astype(F32) * (v * jax.nn.sigmoid(v))).astype(BF16)
    for k in range(n_t):
        outs[k][:B, :] = up
    copies[2].wait()
    nc = cols // cp
    for k in range(1, n_t):
        c0 = (ten ^ k) * cols + lax.rem(rep, cp) * nc
        for j in range(nc // 128):
            at = pl.multiple_of(c0 + j * 128, 128)
            outs[k][B + j * nr : B + (j + 1) * nr, :] = exp_v[:, pl.ds(at, 128)]
    for copy in copies[3:]:
        copy.wait()


def grads_body(n, act, after, *refs):
    ups, outs = refs[:n], refs[n:]
    up = jnp.concatenate([u[:B, :] for u in ups], axis=0)
    for c in range(0, act.shape[1], G):
        g = dot(up, act[:, c : c + G])
        for k in range(n):
            outs[k][:, c : c + G] = g[k * B : (k + 1) * B].astype(outs[k].dtype)


def bundle_body(n_t, keep, after, lines, *refs):
    parts, out = refs[: n_t - 1], refs[n_t - 1]
    n = parts[0].shape[0] - B
    for k in range(n_t - 1):
        out[k * n : (k + 1) * n, :] = parts[k][B:, :]
    blocks = lines.shape[1]
    rows = jnp.concatenate([lines[...].astype(F32), jnp.zeros((keep, 128 - blocks), F32)], axis=1)
    out[(n_t - 1) * n :, :] = jnp.concatenate([rows, jnp.zeros((16 - keep, 128), F32)], axis=0).astype(BF16)


def join_body(n, *refs):
    for i, ref in enumerate(reversed(refs[:n])):
        refs[-1][i] = ref[...]


def own_body(keep, lines, small, p_ref, a_ref):
    blocks, nb = lines.shape[1], G // B
    rows = jnp.concatenate([lines[...].astype(F32), jnp.zeros((keep, 128 - blocks), F32)], axis=1)
    lane = lax.broadcasted_iota(jnp.int32, (nb * keep, 2 * B), 1).astype(F32)
    for g in range(blocks // nb):
        num = jnp.concatenate(
            [jnp.broadcast_to(rows[:, g * nb + j : g * nb + j + 1], (keep, 2 * B)) for j in range(nb)], axis=0
        )
        hot = jnp.concatenate(
            [jnp.where(lane == num, 1.0, 0.0), jnp.where(lane - B == num, 1.0, 0.0)], axis=0
        ).astype(BF16)
        a_ref[g * B : (g + 1) * B, :] = dot(hot, small[:, : 2 * B]).astype(BF16)
    rows = jnp.concatenate([rows] * (2 * B // keep), axis=0).T
    freq = lax.broadcasted_iota(jnp.int32, (B, 2 * B), 0).astype(F32)
    block = (lax.broadcasted_iota(jnp.int32, (1, 2 * B), 1) // keep) % nb
    term = lax.broadcasted_iota(jnp.int32, (B, 2 * B), 1) // (B // 2)
    for g in range(blocks // nb):
        num = rows[g * nb : g * nb + 1]
        for j in range(1, nb):
            num = jnp.where(block == j, rows[g * nb + j : g * nb + j + 1], num)
        hot = jnp.where(freq == num, 1.0, 0.0).astype(BF16)
        y = dot(small[:, 2 * B : 3 * B], hot)
        p = jnp.where(term == 3, 0.0, jnp.where(term == 1, y[B:], y[:B]))
        p_ref[:, g * 2 * B : (g + 1) * 2 * B] = p.astype(BF16)


def kept_body(ks, n_t, keep, vel, a_ref, tab, after, *refs):
    keep_rows(ks, n_t, keep, vel, a_ref, tab, refs[: len(ks)], *refs[-2:])


def keep_rows(ks, n_t, keep, vel, a_ref, tab, grads, send_ref, own_ref):
    cols = grads[0].shape[1]
    ng = cols // G
    lane_block = lax.broadcasted_iota(jnp.int32, (keep, G), 1) // B
    sel = []
    for n, k in enumerate(ks):
        c0 = (lax.axis_index("tensor") ^ k) * cols
        for i in range(ng):
            at = pl.multiple_of(c0 + i * G, G)
            moment = momentum_decay * vel[:, pl.ds(at, G)] + grads[n][:, i * G : (i + 1) * G].astype(F32)
            hi, lo = split(moment)
            y = dot(a_ref[pl.ds(pl.multiple_of(at // (G // B), B), B), :], jnp.concatenate([hi, lo], axis=0))
            y = y[: B // 2] + y[B // 2 :]
            got = y[:keep]
            for j in range(1, G // B):
                got = jnp.where(lane_block == j, y[j * keep : (j + 1) * keep], got)
            sel.append(got)
    hi, lo = split(jnp.concatenate(sel, axis=0))
    n = len(ks) * ng * keep
    y = dot(jnp.concatenate([hi, lo], axis=0), fwd(tab, 0))
    kept = (y[:n] + y[n:] + dot(hi, fwd(tab, 1))).astype(BF16)
    q = dot(kept, inv(tab, 0)) + dot(kept, inv(tab, 1))
    for n, k in enumerate(ks):
        c0 = pl.multiple_of((lax.axis_index("tensor") ^ k) * cols, G)
        part = jnp.concatenate([q[(n * ng + i) * keep : (n * ng + i + 1) * keep] for i in range(ng)], axis=1)
        own_ref[:, pl.ds(c0, cols)] = part
        send_ref[:, pl.ds(c0, cols)] = part.astype(BF16)


def return_body(n_t, keep, vel, p_ref, q, *refs):
    grads, (new_ref, held, sems) = refs[:n_t], refs[n_t:]
    cols = grads[0].shape[1]
    ng = cols // G
    lane_block = lax.broadcasted_iota(jnp.int32, (keep, G), 1) // B
    copies = []
    for k in range(n_t):
        c0 = pl.multiple_of((lax.axis_index("tensor") ^ k) * cols, G)
        for i in range(ng):
            at = pl.multiple_of(c0 + i * G, G)
            own = q[:, pl.ds(at, G)]
            spread = jnp.concatenate(
                [jnp.where(lane_block == j, own, 0.0) for j in range(G // B)], axis=0
            )
            hi, lo = split(spread)
            w = jnp.concatenate([hi, hi, lo, jnp.zeros_like(lo)], axis=0)
            back = dot(p_ref[:, pl.ds(pl.multiple_of(at // 2, 2 * B), 2 * B)], w)
            moment = momentum_decay * vel[:, pl.ds(at, G)] + grads[k][:, i * G : (i + 1) * G].astype(F32)
            held[:, pl.ds(at, G)] = moment - back
        cut = pl.ds(c0, cols)
        copies.append(pltpu.make_async_copy(held.at[:, cut], new_ref.at[:, cut], sems.at[k]))
        copies[-1].start()
    for copy in copies:
        copy.wait()


def places_body(keep, mask, tally, small, bundles, *p_refs):
    n_r, last = bundles.shape[0], bundles.shape[1] - 16
    half, nb = n_r // 2, G // B
    rep = lax.axis_index("replica")
    total, alive = jnp.float32(0), jnp.float32(0)
    for r in range(n_r):
        m = mask[r].astype(F32)
        total = total + m * tally[r].astype(F32)
        alive = alive + m
    scale = jnp.full((1, 2 * B), alive) / jnp.full((1, 2 * B), total)
    freq = lax.broadcasted_iota(jnp.int32, (B, 2 * B), 0).astype(F32)
    lane = lax.broadcasted_iota(jnp.int32, (1, 2 * B), 1)
    block, place = lane // (half * keep), (lane // keep) % half
    for h in range(2):
        hi_ref, lo_ref = p_refs[2 * h : 2 * h + 2]
        w = jnp.zeros((1, 2 * B), F32)
        for i in range(half):
            r = rep ^ (2 * i + h)
            w = jnp.where(place == i, mask[r].astype(F32) * tally[r].astype(F32), w)
        w = w * scale
        rows = [bundles[rep ^ (2 * i + h), last:, :].astype(F32)[:keep] for i in range(half)]
        rows = jnp.concatenate(rows * nb, axis=0).T
        for g in range(hi_ref.shape[1] // (2 * B)):
            num = rows[g * nb : g * nb + 1]
            for j in range(1, nb):
                num = jnp.where(block == j, rows[g * nb + j : g * nb + j + 1], num)
            hot = jnp.where(freq == num, 1.0, 0.0).astype(BF16)
            y = dot(small[:, 2 * B : 3 * B], hot)
            hi, lo = split((y[:B] + y[B:]) * w)
            hi_ref[:, g * 2 * B : (g + 1) * 2 * B] = hi
            lo_ref[:, g * 2 * B : (g + 1) * 2 * B] = lo


def spread_rows(p_hi, p_lo, ships, g):
    half, keep = ships.shape[0], ships.shape[1]
    lane_block = lax.broadcasted_iota(jnp.int32, (half * keep, G), 1) // B
    s = jnp.concatenate([ships[i, :, g * G : (g + 1) * G].astype(F32) for i in range(half)], axis=0)
    w = jnp.concatenate(
        [jnp.where(lane_block == j, s, 0.0).astype(BF16) for j in range(G // B)], axis=0
    )
    cut = slice(g * 2 * B, (g + 1) * 2 * B)
    y = dot(jnp.concatenate([p_hi[:, cut], p_lo[:, cut]], axis=0), w)
    return y[:B] + y[B:]


def half_update_body(p_hi, p_lo, mine, out):
    for g in range(out.shape[0] // B):
        out[g * B : (g + 1) * B, :] = spread_rows(p_hi, p_lo, mine, g)


def update_body(chunk, half_sum, p_hi, p_lo, other, out, held, sems):
    ng = half_sum.shape[0] // B
    copies = []
    for c in range(0, ng, chunk):
        for g in range(c, c + chunk):
            held[:, g * G : (g + 1) * G] = half_sum[g * B : (g + 1) * B, :] + spread_rows(p_hi, p_lo, other, g)
        cut = pl.ds(c * G, chunk * G)
        copies.append(pltpu.make_async_copy(held.at[:, cut], out.at[:, cut], sems.at[c // chunk]))
        copies[-1].start()
    for copy in copies:
        copy.wait()


def input_grad_body(n_t, n_r, cp, exp_ref, bundles, *refs):
    ups, (out, held) = refs[:n_t], refs[n_t:]
    cols = out.shape[1]
    held[:B, :] = exp_ref[:, pl.ds(pl.multiple_of(lax.axis_index("tensor") * cols, 128), cols)]
    nc = cols // cp
    nr = B // (n_r // cp)
    tiles = nc // 128
    for r in range(n_r):
        r0, c0 = (r // cp) * nr, (r % cp) * nc
        for k in range(1, n_t):
            for j in range(tiles):
                at = ((k - 1) * tiles + j) * nr
                held[k * B + r0 : k * B + r0 + nr, c0 + j * 128 : c0 + (j + 1) * 128] = bundles[r, at : at + nr, :]
    up = jnp.concatenate([u[:B, :] for u in ups], axis=0).T
    for c in range(0, cols, G):
        out[:, c : c + G] = dot(up, held[:, c : c + G]).astype(BF16)


def per_device(n_t, n_r, act, switch, slope, exp, vel, lines, mask, tally):
    cols = act.shape[1]
    width = exp.shape[1]
    tok = act.shape[0]
    keep = lines.shape[3]
    blocks = width // B
    groups = width // G
    cp = 2
    rp = n_r // cp
    half = n_r // 2
    tab, small = constants()
    def trade(x, k):
        return lax.ppermute(x, "tensor", [(i, i ^ k) for i in range(n_t)])

    order = [*range(2, n_t), 1]

    def swap(x, m):
        return lax.ppermute(x, "replica", [(i, i ^ m) for i in range(n_r)])

    own = lines[0, 0].T
    tiles = cols // cp // 128
    nr = B // rp
    *parts, act, own, small = call(
        functools.partial(first_body, n_t, cp, cols, nr),
        [near((B, tok))]
        + [near((B + tiles * nr, 128))] * (n_t - 1)
        + [near(act.shape), near(own.shape, jnp.int32), near(small.shape)],
        (far(switch.T), far(slope.T), far(exp), far(act), far(own), far(small)),
        [ANY] * 6,
        [VM] * (n_t + 3),
        scratch=[
            pltpu.VMEM((B, tok), BF16),
            pltpu.VMEM((B, tok), BF16),
            pltpu.VMEM((nr, width), BF16),
            pltpu.SemaphoreType.DMA((6,)),
        ],
        nbytes=act.size * 4 + nr * width * 2,
        name="up_grads",
    )
    got = {k: trade(parts[k], k) for k in order}
    parts = [parts[0]] + [got[k] for k in range(1, n_t)]

    p_own, a_own = call(
        functools.partial(own_body, keep),
        [near((B, groups * 2 * B)), near((groups * B, 2 * B))],
        (own, small),
        [VM, VM],
        [VM, VM],
        name="own_places",
    )

    def grads_of(ks, after):
        return call(
            functools.partial(grads_body, len(ks)),
            [near((B, cols), BF16 if k else F32) for k in ks],
            (act, after, *[parts[k] for k in ks]),
            [VM, ANY] + [VM] * len(ks),
            [VM] * len(ks),
            name="weight_grads",
        )

    grads = {}
    for k in order[:-1]:
        (grads[k],) = grads_of([k], act)
    made, grads[0] = grads_of([order[-1], 0], a_own)
    grads[order[-1]] = made
    grads.update({k: trade(grads[k], k) for k in order})

    bundle = call(
        functools.partial(bundle_body, n_t, keep),
        near(((n_t - 1) * tiles * nr + 16, 128)),
        (made, own, *parts[1:]),
        [ANY] + [VM] * n_t,
        VM,
        name="bundle",
    )
    bundles = lax.all_gather(bundle, "replica", axis=0)

    rows = []
    for ks in ([0, *order[:-2]], order[-2:]) if n_t > 2 else ([0], [1]):
        n = len(ks)
        rows = call(
            functools.partial(kept_body, ks, n_t, keep),
            [near((keep, width)), near((keep, width), F32)],
            (vel[0], a_own, tab, bundles, *[grads[k] for k in ks], *rows),
            [VM] * 3 + [ANY] + [VM] * (n + len(rows)),
            [VM] * 2,
            flops=6 * B * B * cols * n,
            nbytes=B * cols * 6 * n,
            name="kept_rows",
            alias={4 + n: 0, 5 + n: 1} if rows else {},
        )
    ship, q_own = rows

    places = call(
        functools.partial(places_body, keep),
        [near((B, blocks * half * keep))] * 4,
        (mask, tally, small, bundles),
        [SM, SM, VM, VM],
        [VM] * 4,
        name="places",
    )
    input_grad = call(
        functools.partial(input_grad_body, n_t, n_r, cp),
        jax.ShapeDtypeStruct((tok, cols), BF16),
        (exp, bundles, *parts),
        [VM] * (2 + n_t),
        VM,
        scratch=[pltpu.VMEM((n_t * B, cols), BF16)],
        flops=2 * tok * n_t * B * cols,
        nbytes=(n_t * B * cols + tok * cols) * 2,
        name="input_grads",
    )

    ships = [ship] + [swap(ship, 2 * i) for i in range(1, half)]
    new = call(
        functools.partial(return_body, n_t, keep),
        jax.ShapeDtypeStruct((B, width), F32),
        (vel[0], p_own, q_own, *[grads[k] for k in range(n_t)]),
        [VM] * (3 + n_t),
        ANY,
        scratch=[pltpu.VMEM((B, width), F32), pltpu.SemaphoreType.DMA((n_t,))],
        flops=6 * B * B * width,
        nbytes=B * width * 10,
        name="new_momentums",
    )
    mine = call(
        functools.partial(join_body, half),
        near((half, keep, width)),
        (*reversed(ships), far(new), far(input_grad), places[0]),
        [VM] * half + [ANY] * 3,
        VM,
        name="join_kept",
    )
    other = swap(mine, 1)
    half_sum = call(
        half_update_body,
        near((groups * B, G), F32),
        (*places[:2], mine),
        [VM] * 3,
        VM,
        name="half_updates",
    )
    chunk = 2 if groups % 2 == 0 else 1
    update = call(
        functools.partial(update_body, chunk),
        jax.ShapeDtypeStruct((B, width), F32),
        (half_sum, *places[2:], other),
        [VM] * 4,
        ANY,
        scratch=[
            pltpu.VMEM((B, width), F32),
            pltpu.SemaphoreType.DMA((groups // chunk,)),
        ],
        flops=8 * B * G * width,
        nbytes=B * width * 8,
        name="updates",
    )
    return input_grad, new[None], update


def per_device_plain(
    projection_inputs,
    switch_logits_raw,
    inner_neuron_slope,
    expansion_matrix,
    velocity_buffer,
    sent_spectral_lines,
    participant_mask,
    token_tallies,
):
    highest = lax.Precision.HIGHEST
    up_grad = (
        inner_neuron_slope.astype(jnp.float32) * jax.nn.silu(switch_logits_raw.astype(jnp.float32))
    ).astype(jnp.bfloat16)
    partial_terms = jnp.dot(up_grad, expansion_matrix, preferred_element_type=jnp.float32)
    input_grad = lax.psum_scatter(partial_terms, "tensor", scatter_dimension=1, tiled=True).astype(
        jnp.bfloat16
    )
    grad_w = lax.dot_general(
        up_grad,
        lax.all_gather(projection_inputs, "tensor", axis=1, tiled=True),
        (((0,), (0,)), ((), ())),
        preferred_element_type=jnp.float32,
    )
    row_total_count = expansion_matrix.shape[0] // 64
    col_count = expansion_matrix.shape[1] // 64
    moment = momentum_decay * velocity_buffer[0] + grad_w
    cosines = cosine_table()
    blocks = moment.reshape(row_total_count, 64, col_count, 64).transpose(0, 2, 1, 3)
    coefficients = jnp.einsum("fa,ijab,gb->ijfg", cosines, blocks, cosines, precision=highest)
    freq_ids = jnp.arange(64, dtype=jnp.int32)
    own_rows = sent_spectral_lines[0]
    chosen = (own_rows[..., None] == freq_ids).astype(jnp.float32)
    shipped = jnp.einsum("ijkf,ijfg->ijkg", chosen, coefficients, precision=highest).astype(
        jnp.bfloat16
    )
    spectrum = jnp.einsum("ijkf,ijkg->ijfg", chosen, shipped.astype(jnp.float32), precision=highest)
    returned = jnp.einsum("fa,ijfg,gb->ijab", cosines, spectrum, cosines, precision=highest)
    new_moment = moment - returned.transpose(0, 2, 1, 3).reshape(moment.shape)
    worker_burdens = participant_mask.astype(jnp.float32) * token_tallies.astype(jnp.float32)
    worker_fractions = worker_burdens * (
        jnp.sum(participant_mask.astype(jnp.float32)) / jnp.sum(worker_burdens)
    )
    myself = lax.axis_index("replica")
    combined = lax.psum(worker_fractions[myself] * spectrum, "replica")
    update = jnp.einsum("fa,ijfg,gb->ijab", cosines, combined, cosines, precision=highest)
    update = update.transpose(0, 2, 1, 3).reshape(moment.shape)
    return (input_grad, new_moment[None], update)


def solution(mesh):
    n_t, n_r = mesh.shape["tensor"], mesh.shape["replica"]

    def device(*args):
        act, exp, lines = args[0], args[3], args[5]
        fits = (
            act.shape[1] % G == 0
            and act.shape[0] % 128 == 0
            and exp.shape[0] == B
            and lines.shape[3] == 8
            and n_r == 8
            and n_t >= 2
            and n_t & (n_t - 1) == 0
        )
        if not fits:
            return per_device_plain(*args)
        return per_device(n_t, n_r, *args)

    return jax.shard_map(
        device,
        mesh=mesh,
        in_specs=(
            P("replica", "tensor"),
            P("replica", "tensor"),
            P("replica", "tensor"),
            P("tensor", None),
            P("replica", "tensor", None),
            P("replica", "tensor", None, None),
            P(),
            P(),
        ),
        out_specs=(P("replica", "tensor"), P("replica", "tensor", None), P("tensor", None)),
        check_vma=False,
    )
```

```python
import functools

import jax
import jax.numpy as jnp
import numpy as np
from jax import lax
from jax.experimental import pallas as pl
from jax.experimental.pallas import tpu as pltpu
from jax.sharding import PartitionSpec as P

momentum_decay = 0.9
B = 64
G = 256
F32 = jnp.float32
BF16 = jnp.bfloat16
VMEM_LIMIT = 24 * 1024 * 1024

VM = pl.BlockSpec(memory_space=pltpu.VMEM)
SM = pl.BlockSpec(memory_space=pltpu.SMEM)
ANY = pl.BlockSpec(memory_space=pl.ANY)


def cosine_table():
    freqs = jnp.arange(64, dtype=jnp.float32)[:, None]
    places = jnp.arange(64, dtype=jnp.float32)[None, :]
    cosines = jnp.cos(jnp.pi * (places + 0.5) * freqs / 64.0) * jnp.sqrt(2.0 / 64.0)
    return cosines.at[0].multiply(jnp.sqrt(0.5))


def cosine_np():
    f = np.arange(B)[:, None]
    a = np.arange(B)[None, :]
    c = np.cos(np.pi * (a + 0.5) * f / B) * np.sqrt(2.0 / B)
    c[0] *= np.sqrt(0.5)
    return c


def halves(c):
    hi = np.asarray(c, dtype=np.float32).astype(jnp.bfloat16)
    lo = (np.asarray(c, np.float64) - hi.astype(np.float64)).astype(np.float32).astype(jnp.bfloat16)
    return hi, lo


def constants():
    hi, lo = halves(cosine_np())
    eye = np.eye(G // B)
    kron = lambda x: np.kron(eye, np.asarray(x, np.float32)).astype(jnp.bfloat16)
    small = np.zeros((2 * B, 4 * B), jnp.bfloat16)
    for i, x in enumerate((hi, lo)):
        rows = slice(i * B, (i + 1) * B)
        small[rows, :B], small[rows, B : 2 * B], small[rows, 2 * B : 3 * B] = x, x, x.T
    return jnp.asarray(np.concatenate([kron(x) for x in (hi.T, lo.T, hi, lo)], axis=0)), jnp.asarray(small)


def fwd(tab, i):
    return tab[i * G : (i + 1) * G, :]


def inv(tab, i):
    return tab[(2 + i) * G : (3 + i) * G, :]


def dot(a, b):
    return jnp.dot(a, b, preferred_element_type=F32)


def split(x):
    hi = x.astype(BF16)
    return hi, (x - hi.astype(F32)).astype(BF16)


def near(shape, dtype=BF16):
    return pltpu.VMEM(shape, dtype)


def far(x):
    return pltpu.with_memory_space_constraint(x, pltpu.HBM)


def call(body, out_shape, ins, in_specs, out_specs, scratch=(), flops=0, nbytes=0, name=None, alias={}):
    return pl.pallas_call(
        body,
        out_shape=out_shape,
        in_specs=in_specs,
        out_specs=out_specs,
        scratch_shapes=scratch,
        input_output_aliases=alias,
        compiler_params=pltpu.CompilerParams(vmem_limit_bytes=VMEM_LIMIT),
        cost_estimate=pl.CostEstimate(flops=flops, bytes_accessed=nbytes, transcendentals=0),
        name=name,
    )(*ins)


def first_body(n_t, cp, cols, nr, switch, slope, exp_ref, act, lines, small, *refs):
    outs, (act_out, lines_out, small_out) = refs[:n_t], refs[n_t : n_t + 3]
    switch_v, slope_v, exp_v, sems = refs[n_t + 3 :]
    rep, ten = lax.axis_index("replica"), lax.axis_index("tensor")
    r0 = pl.multiple_of((rep // cp) * nr, nr)
    copies = [
        pltpu.make_async_copy(src, dst, sems.at[i])
        for i, (src, dst) in enumerate(
            [
                (switch, switch_v),
                (slope, slope_v),
                (exp_ref.at[pl.ds(r0, nr), :], exp_v),
                (act, act_out),
                (lines, lines_out),
                (small, small_out),
            ]
        )
    ]
    for copy in copies:
        copy.start()
    copies[0].wait()
    copies[1].wait()
    v = switch_v[...].astype(F32)
    up = (slope_v[...].astype(F32) * (v * jax.nn.sigmoid(v))).astype(BF16)
    for k in range(n_t):
        outs[k][:B, :] = up
    copies[2].wait()
    nc = cols // cp
    for k in range(1, n_t):
        c0 = (ten ^ k) * cols + lax.rem(rep, cp) * nc
        for j in range(nc // 128):
            at = pl.multiple_of(c0 + j * 128, 128)
            outs[k][B + j * nr : B + (j + 1) * nr, :] = exp_v[:, pl.ds(at, 128)]
    for copy in copies[3:]:
        copy.wait()


def grads_body(n, act, after, *refs):
    ups, outs = refs[:n], refs[n:]
    up = jnp.concatenate([u[:B, :] for u in ups], axis=0)
    for c in range(0, act.shape[1], G):
        g = dot(up, act[:, c : c + G])
        for k in range(n):
            outs[k][:, c : c + G] = g[k * B : (k + 1) * B].astype(outs[k].dtype)


def bundle_body(n_t, keep, after, lines, *refs):
    parts, out = refs[: n_t - 1], refs[n_t - 1]
    n = parts[0].shape[0] - B
    for k in range(n_t - 1):
        out[k * n : (k + 1) * n, :] = parts[k][B:, :]
    blocks = lines.shape[1]
    rows = jnp.concatenate([lines[...].astype(F32), jnp.zeros((keep, 128 - blocks), F32)], axis=1)
    out[(n_t - 1) * n :, :] = jnp.concatenate([rows, jnp.zeros((16 - keep, 128), F32)], axis=0).astype(BF16)


def join_body(n, *refs):
    for i, ref in enumerate(refs[:n]):
        refs[-1][i] = ref[...]


def own_body(keep, lines, small, p_ref, a_ref):
    blocks, nb = lines.shape[1], G // B
    rows = jnp.concatenate([lines[...].astype(F32), jnp.zeros((keep, 128 - blocks), F32)], axis=1)
    lane = lax.broadcasted_iota(jnp.int32, (nb * keep, 2 * B), 1).astype(F32)
    for g in range(blocks // nb):
        num = jnp.concatenate(
            [jnp.broadcast_to(rows[:, g * nb + j : g * nb + j + 1], (keep, 2 * B)) for j in range(nb)], axis=0
        )
        hot = jnp.concatenate(
            [jnp.where(lane == num, 1.0, 0.0), jnp.where(lane - B == num, 1.0, 0.0)], axis=0
        ).astype(BF16)
        a_ref[g * B : (g + 1) * B, :] = dot(hot, small[:, : 2 * B]).astype(BF16)
    rows = jnp.concatenate([rows] * (2 * B // keep), axis=0).T
    freq = lax.broadcasted_iota(jnp.int32, (B, 2 * B), 0).astype(F32)
    block = (lax.broadcasted_iota(jnp.int32, (1, 2 * B), 1) // keep) % nb
    term = lax.broadcasted_iota(jnp.int32, (B, 2 * B), 1) // (B // 2)
    for g in range(blocks // nb):
        num = rows[g * nb : g * nb + 1]
        for j in range(1, nb):
            num = jnp.where(block == j, rows[g * nb + j : g * nb + j + 1], num)
        hot = jnp.where(freq == num, 1.0, 0.0).astype(BF16)
        y = dot(small[:, 2 * B : 3 * B], hot)
        p = jnp.where(term == 3, 0.0, jnp.where(term == 1, y[B:], y[:B]))
        p_ref[:, g * 2 * B : (g + 1) * 2 * B] = p.astype(BF16)


def kept_body(ks, n_t, keep, vel, a_ref, tab, after, after_too, *refs):
    keep_rows(ks, n_t, keep, vel, a_ref, tab, refs[: len(ks)], *refs[-2:])


def keep_rows(ks, n_t, keep, vel, a_ref, tab, grads, send_ref, own_ref):
    cols = grads[0].shape[1]
    ng = cols // G
    lane_block = lax.broadcasted_iota(jnp.int32, (keep, G), 1) // B
    sel = []
    for n, k in enumerate(ks):
        c0 = (lax.axis_index("tensor") ^ k) * cols
        for i in range(ng):
            at = pl.multiple_of(c0 + i * G, G)
            moment = momentum_decay * vel[:, pl.ds(at, G)] + grads[n][:, i * G : (i + 1) * G].astype(F32)
            hi, lo = split(moment)
            y = dot(a_ref[pl.ds(pl.multiple_of(at // (G // B), B), B), :], jnp.concatenate([hi, lo], axis=0))
            y = y[: B // 2] + y[B // 2 :]
            got = y[:keep]
            for j in range(1, G // B):
                got = jnp.where(lane_block == j, y[j * keep : (j + 1) * keep], got)
            sel.append(got)
    hi, lo = split(jnp.concatenate(sel, axis=0))
    n = len(ks) * ng * keep
    y = dot(jnp.concatenate([hi, lo], axis=0), fwd(tab, 0))
    kept = (y[:n] + y[n:] + dot(hi, fwd(tab, 1))).astype(BF16)
    q = dot(kept, inv(tab, 0)) + dot(kept, inv(tab, 1))
    for n, k in enumerate(ks):
        c0 = pl.multiple_of((lax.axis_index("tensor") ^ k) * cols, G)
        part = jnp.concatenate([q[(n * ng + i) * keep : (n * ng + i + 1) * keep] for i in range(ng)], axis=1)
        own_ref[:, pl.ds(c0, cols)] = part
        send_ref[:, pl.ds(c0, cols)] = part.astype(BF16)


def return_body(n_t, keep, vel, p_ref, q, *refs):
    grads, (new_ref, held, sems) = refs[:n_t], refs[n_t:]
    cols = grads[0].shape[1]
    ng = cols // G
    lane_block = lax.broadcasted_iota(jnp.int32, (keep, G), 1) // B
    copies = []
    for k in range(n_t):
        c0 = pl.multiple_of((lax.axis_index("tensor") ^ k) * cols, G)
        for i in range(ng):
            at = pl.multiple_of(c0 + i * G, G)
            own = q[:, pl.ds(at, G)]
            spread = jnp.concatenate(
                [jnp.where(lane_block == j, own, 0.0) for j in range(G // B)], axis=0
            )
            hi, lo = split(spread)
            w = jnp.concatenate([hi, hi, lo, jnp.zeros_like(lo)], axis=0)
            back = dot(p_ref[:, pl.ds(pl.multiple_of(at // 2, 2 * B), 2 * B)], w)
            moment = momentum_decay * vel[:, pl.ds(at, G)] + grads[k][:, i * G : (i + 1) * G].astype(F32)
            held[:, pl.ds(at, G)] = moment - back
        cut = pl.ds(c0, cols)
        copies.append(pltpu.make_async_copy(held.at[:, cut], new_ref.at[:, cut], sems.at[k]))
        copies[-1].start()
    for copy in copies:
        copy.wait()


def places_body(keep, mask, tally, small, bundles, hi_ref, lo_ref, w_ref):
    half = bundles.shape[0]
    rep = lax.axis_index("replica")
    total, alive = jnp.float32(0), jnp.float32(0)
    for r in range(2 * half):
        m = mask[r].astype(F32)
        total = total + m * tally[r].astype(F32)
        alive = alive + m
    place = (lax.broadcasted_iota(jnp.int32, (8, 2 * B), 1) // keep) % half
    scale = jnp.full((8, 2 * B), alive) / jnp.full((8, 2 * B), total)
    ws = []
    for h in range(2):
        w = jnp.zeros((8, 2 * B), F32)
        for i in range(half):
            r = rep ^ (2 * i + h)
            w = jnp.where(place == i, mask[r].astype(F32) * tally[r].astype(F32), w)
        ws.append(w * scale)
    w_ref[...] = ws[1]
    side_places(keep, ws[0][:1], small, bundles, hi_ref, lo_ref)


def other_places_body(keep, w_ref, small, bundles, hi_ref, lo_ref):
    side_places(keep, w_ref[:1, :], small, bundles, hi_ref, lo_ref)


def side_places(keep, w, small, bundles, hi_ref, lo_ref):
    half, last, nb = bundles.shape[0], bundles.shape[1] - 16, G // B
    freq = lax.broadcasted_iota(jnp.int32, (B, 2 * B), 0).astype(F32)
    block = lax.broadcasted_iota(jnp.int32, (1, 2 * B), 1) // (half * keep)
    chip = lax.axis_index("replica") // 2
    rows = [bundles[chip ^ i, last:, :].astype(F32)[:keep] for i in range(half)]
    rows = jnp.concatenate(rows * nb, axis=0).T
    for g in range(hi_ref.shape[1] // (2 * B)):
        num = rows[g * nb : g * nb + 1]
        for j in range(1, nb):
            num = jnp.where(block == j, rows[g * nb + j : g * nb + j + 1], num)
        hot = jnp.where(freq == num, 1.0, 0.0).astype(BF16)
        y = dot(small[:, 2 * B : 3 * B], hot)
        hi, lo = split((y[:B] + y[B:]) * w)
        hi_ref[:, g * 2 * B : (g + 1) * 2 * B] = hi
        lo_ref[:, g * 2 * B : (g + 1) * 2 * B] = lo


def spread_rows(p_hi, p_lo, ships, g):
    half, keep = ships.shape[0], ships.shape[1]
    lane_block = lax.broadcasted_iota(jnp.int32, (half * keep, G), 1) // B
    s = jnp.concatenate([ships[i, :, g * G : (g + 1) * G].astype(F32) for i in range(half)], axis=0)
    w = jnp.concatenate(
        [jnp.where(lane_block == j, s, 0.0).astype(BF16) for j in range(G // B)], axis=0
    )
    cut = slice(g * 2 * B, (g + 1) * 2 * B)
    y = dot(jnp.concatenate([p_hi[:, cut], p_lo[:, cut]], axis=0), w)
    return y[:B] + y[B:]


def half_update_body(p_hi, p_lo, mine, out):
    for g in range(out.shape[0] // B):
        out[g * B : (g + 1) * B, :] = spread_rows(p_hi, p_lo, mine, g)


def update_body(chunk, half_sum, p_hi, p_lo, other, out, held, sems):
    ng = half_sum.shape[0] // B
    copies = []
    for c in range(0, ng, chunk):
        for g in range(c, c + chunk):
            held[:, g * G : (g + 1) * G] = half_sum[g * B : (g + 1) * B, :] + spread_rows(p_hi, p_lo, other, g)
        cut = pl.ds(c * G, chunk * G)
        copies.append(pltpu.make_async_copy(held.at[:, cut], out.at[:, cut], sems.at[c // chunk]))
        copies[-1].start()
    for copy in copies:
        copy.wait()


def input_grad_body(n_t, h, exp_ref, bundles, *refs):
    ups, (out, held, ready, sem) = refs[:n_t], refs[-4:]
    half = bundles.shape[0]
    nc, nr = held.shape[1], B // half
    tiles = nc // 128
    c0 = pl.multiple_of(lax.rem(lax.axis_index("replica") ^ h, 2) * nc, 128)
    held[:B, :] = exp_ref[:, pl.ds(pl.multiple_of(lax.axis_index("tensor") * 2 * nc + c0, 128), nc)]
    for i in range(half):
        for k in range(1, n_t):
            row = k * B + i * nr
            for j in range(tiles):
                at = ((k - 1) * tiles + j) * nr
                held[row : row + nr, j * 128 : (j + 1) * 128] = bundles[i, at : at + nr, :]
    up = jnp.concatenate([u[:B, :] for u in ups], axis=0).T
    for c in range(0, nc, 128):
        ready[:, c : c + 128] = dot(up, held[:, c : c + 128]).astype(BF16)
    copy = pltpu.make_async_copy(ready, out.at[:, pl.ds(c0, nc)], sem)
    copy.start()
    copy.wait()


def per_device(n_t, n_r, act, switch, slope, exp, vel, lines, mask, tally):
    cols = act.shape[1]
    width = exp.shape[1]
    tok = act.shape[0]
    keep = lines.shape[3]
    blocks = width // B
    groups = width // G
    cp = 2
    rp = n_r // cp
    half = n_r // 2
    tab, small = constants()
    def trade(x, k):
        return lax.ppermute(x, "tensor", [(i, i ^ k) for i in range(n_t)])

    order = [*range(2, n_t), 1]

    def swap(x, m):
        return lax.ppermute(x, "replica", [(i, i ^ m) for i in range(n_r)])

    own = lines[0, 0].T
    tiles = cols // cp // 128
    nr = B // rp
    *parts, act, own, small = call(
        functools.partial(first_body, n_t, cp, cols, nr),
        [near((B, tok))]
        + [near((B + tiles * nr, 128))] * (n_t - 1)
        + [near(act.shape), near(own.shape, jnp.int32), near(small.shape)],
        (far(switch.T), far(slope.T), far(exp), far(act), far(own), far(small)),
        [ANY] * 6,
        [VM] * (n_t + 3),
        scratch=[
            pltpu.VMEM((B, tok), BF16),
            pltpu.VMEM((B, tok), BF16),
            pltpu.VMEM((nr, width), BF16),
            pltpu.SemaphoreType.DMA((6,)),
        ],
        nbytes=act.size * 4 + nr * width * 2,
        name="up_grads",
    )
    got = {k: trade(parts[k], k) for k in order}
    parts = [parts[0]] + [got[k] for k in range(1, n_t)]

    p_own, a_own = call(
        functools.partial(own_body, keep),
        [near((B, groups * 2 * B)), near((groups * B, 2 * B))],
        (own, small),
        [VM, VM],
        [VM, VM],
        name="own_places",
    )

    def grads_of(ks, after):
        return call(
            functools.partial(grads_body, len(ks)),
            [near((B, cols), BF16 if k else F32) for k in ks],
            (act, after, *[parts[k] for k in ks]),
            [VM, ANY] + [VM] * len(ks),
            [VM] * len(ks),
            name="weight_grads",
        )

    grads = {}
    for k in order[:-1]:
        (grads[k],) = grads_of([k], act)
    made, grads[0] = grads_of([order[-1], 0], a_own)
    grads[order[-1]] = made
    grads.update({k: trade(grads[k], k) for k in order})

    bundle = call(
        functools.partial(bundle_body, n_t, keep),
        near(((n_t - 1) * tiles * nr + 16, 128)),
        (made, own, *parts[1:]),
        [ANY] + [VM] * n_t,
        VM,
        name="bundle",
    )
    sides = [[r for r in range(n_r) if r % 2 == h] for h in range(2)]
    bundles = [lax.all_gather(bundle, "replica", axis=0, axis_index_groups=sides)]
    bundles.append(swap(bundles[0], 1))

    *mine_at, shares = call(
        functools.partial(places_body, keep),
        [near((B, blocks * half * keep))] * 2 + [near((8, 2 * B), F32)],
        (mask, tally, small, bundles[0]),
        [SM, SM, VM, VM],
        [VM] * 3,
        name="places",
    )

    def columns_of(h, so_far=()):
        return call(
            functools.partial(input_grad_body, n_t, h),
            jax.ShapeDtypeStruct((tok, cols), BF16),
            (exp, bundles[h], *parts, *so_far),
            [VM] * (2 + n_t) + [ANY] * len(so_far),
            ANY,
            scratch=[
                pltpu.VMEM((n_t * B, cols // cp), BF16),
                pltpu.VMEM((tok, cols // cp), BF16),
                pltpu.SemaphoreType.DMA,
            ],
            name="input_grads",
            alias={2 + n_t: 0} if so_far else {},
        )

    first_columns = columns_of(0)

    rows = []
    for ks in ([k for k in range(n_t) if k != n_t - 1], [n_t - 1]):
        n = len(ks)
        rows = call(
            functools.partial(kept_body, ks, n_t, keep),
            [near((keep, width)), near((keep, width), F32)],
            (vel[0], a_own, tab, mine_at[0], far(first_columns), *[grads[k] for k in ks], *rows),
            [VM] * 3 + [ANY] * 2 + [VM] * (n + len(rows)),
            [VM] * 2,
            flops=6 * B * B * cols * n,
            nbytes=B * cols * 6 * n,
            name="kept_rows",
            alias={5 + n: 0, 6 + n: 1} if rows else {},
        )
    ship, q_own = rows


    other_at = call(
        functools.partial(other_places_body, keep),
        [near((B, blocks * half * keep))] * 2,
        (shares, small, bundles[1]),
        [VM] * 3,
        [VM] * 2,
        name="other_places",
    )
    input_grad = columns_of(1, (far(first_columns),))

    ships = [ship] + [swap(ship, 2 * i) for i in range(1, half)]
    new = call(
        functools.partial(return_body, n_t, keep),
        jax.ShapeDtypeStruct((B, width), F32),
        (vel[0], p_own, q_own, *[grads[k] for k in range(n_t)]),
        [VM] * (3 + n_t),
        ANY,
        scratch=[pltpu.VMEM((B, width), F32), pltpu.SemaphoreType.DMA((n_t,))],
        flops=6 * B * B * width,
        nbytes=B * width * 10,
        name="new_momentums",
    )
    mine = call(
        functools.partial(join_body, half),
        near((half, keep, width)),
        (*ships, far(new), other_at[0]),
        [VM] * half + [ANY] * 2,
        VM,
        name="join_kept",
    )
    other = swap(mine, 1)
    half_sum = call(
        half_update_body,
        near((groups * B, G), F32),
        (*mine_at, mine),
        [VM] * 3,
        VM,
        name="half_updates",
    )
    chunk = 2 if groups % 2 == 0 else 1
    update = call(
        functools.partial(update_body, chunk),
        jax.ShapeDtypeStruct((B, width), F32),
        (half_sum, *other_at, other),
        [VM] * 4,
        ANY,
        scratch=[
            pltpu.VMEM((B, width), F32),
            pltpu.SemaphoreType.DMA((groups // chunk,)),
        ],
        flops=8 * B * G * width,
        nbytes=B * width * 8,
        name="updates",
    )
    return input_grad, new[None], update


def per_device_plain(
    projection_inputs,
    switch_logits_raw,
    inner_neuron_slope,
    expansion_matrix,
    velocity_buffer,
    sent_spectral_lines,
    participant_mask,
    token_tallies,
):
    highest = lax.Precision.HIGHEST
    up_grad = (
        inner_neuron_slope.astype(jnp.float32) * jax.nn.silu(switch_logits_raw.astype(jnp.float32))
    ).astype(jnp.bfloat16)
    partial_terms = jnp.dot(up_grad, expansion_matrix, preferred_element_type=jnp.float32)
    input_grad = lax.psum_scatter(partial_terms, "tensor", scatter_dimension=1, tiled=True).astype(
        jnp.bfloat16
    )
    grad_w = lax.dot_general(
        up_grad,
        lax.all_gather(projection_inputs, "tensor", axis=1, tiled=True),
        (((0,), (0,)), ((), ())),
        preferred_element_type=jnp.float32,
    )
    row_total_count = expansion_matrix.shape[0] // 64
    col_count = expansion_matrix.shape[1] // 64
    moment = momentum_decay * velocity_buffer[0] + grad_w
    cosines = cosine_table()
    blocks = moment.reshape(row_total_count, 64, col_count, 64).transpose(0, 2, 1, 3)
    coefficients = jnp.einsum("fa,ijab,gb->ijfg", cosines, blocks, cosines, precision=highest)
    freq_ids = jnp.arange(64, dtype=jnp.int32)
    own_rows = sent_spectral_lines[0]
    chosen = (own_rows[..., None] == freq_ids).astype(jnp.float32)
    shipped = jnp.einsum("ijkf,ijfg->ijkg", chosen, coefficients, precision=highest).astype(
        jnp.bfloat16
    )
    spectrum = jnp.einsum("ijkf,ijkg->ijfg", chosen, shipped.astype(jnp.float32), precision=highest)
    returned = jnp.einsum("fa,ijfg,gb->ijab", cosines, spectrum, cosines, precision=highest)
    new_moment = moment - returned.transpose(0, 2, 1, 3).reshape(moment.shape)
    worker_burdens = participant_mask.astype(jnp.float32) * token_tallies.astype(jnp.float32)
    worker_fractions = worker_burdens * (
        jnp.sum(participant_mask.astype(jnp.float32)) / jnp.sum(worker_burdens)
    )
    myself = lax.axis_index("replica")
    combined = lax.psum(worker_fractions[myself] * spectrum, "replica")
    update = jnp.einsum("fa,ijfg,gb->ijab", cosines, combined, cosines, precision=highest)
    update = update.transpose(0, 2, 1, 3).reshape(moment.shape)
    return (input_grad, new_moment[None], update)


def solution(mesh):
    n_t, n_r = mesh.shape["tensor"], mesh.shape["replica"]

    def device(*args):
        act, exp, lines = args[0], args[3], args[5]
        fits = (
            act.shape[1] % G == 0
            and act.shape[0] % 128 == 0
            and exp.shape[0] == B
            and lines.shape[3] == 8
            and n_r == 8
            and n_t >= 2
            and n_t & (n_t - 1) == 0
        )
        if not fits:
            return per_device_plain(*args)
        return per_device(n_t, n_r, *args)

    return jax.shard_map(
        device,
        mesh=mesh,
        in_specs=(
            P("replica", "tensor"),
            P("replica", "tensor"),
            P("replica", "tensor"),
            P("tensor", None),
            P("replica", "tensor", None),
            P("replica", "tensor", None, None),
            P(),
            P(),
        ),
        out_specs=(P("replica", "tensor"), P("replica", "tensor", None), P("tensor", None)),
        check_vma=False,
    )
```

```python
import functools

import jax
import jax.numpy as jnp
import numpy as np
from jax import lax
from jax.experimental import pallas as pl
from jax.experimental.pallas import tpu as pltpu
from jax.sharding import PartitionSpec as P

momentum_decay = 0.9
B = 64
G = 256
F32 = jnp.float32
BF16 = jnp.bfloat16
VMEM_LIMIT = 24 * 1024 * 1024

VM = pl.BlockSpec(memory_space=pltpu.VMEM)
SM = pl.BlockSpec(memory_space=pltpu.SMEM)
ANY = pl.BlockSpec(memory_space=pl.ANY)


def cosine_table():
    freqs = jnp.arange(64, dtype=jnp.float32)[:, None]
    places = jnp.arange(64, dtype=jnp.float32)[None, :]
    cosines = jnp.cos(jnp.pi * (places + 0.5) * freqs / 64.0) * jnp.sqrt(2.0 / 64.0)
    return cosines.at[0].multiply(jnp.sqrt(0.5))


def cosine_np():
    f = np.arange(B)[:, None]
    a = np.arange(B)[None, :]
    c = np.cos(np.pi * (a + 0.5) * f / B) * np.sqrt(2.0 / B)
    c[0] *= np.sqrt(0.5)
    return c


def halves(c):
    hi = np.asarray(c, dtype=np.float32).astype(jnp.bfloat16)
    lo = (np.asarray(c, np.float64) - hi.astype(np.float64)).astype(np.float32).astype(jnp.bfloat16)
    return hi, lo


def constants():
    hi, lo = halves(cosine_np())
    eye = np.eye(G // B)
    kron = lambda x: np.kron(eye, np.asarray(x, np.float32)).astype(jnp.bfloat16)
    small = np.zeros((2 * B, 4 * B), jnp.bfloat16)
    for i, x in enumerate((hi, lo)):
        rows = slice(i * B, (i + 1) * B)
        small[rows, :B], small[rows, B : 2 * B], small[rows, 2 * B : 3 * B] = x, x, x.T
    return jnp.asarray(np.concatenate([kron(x) for x in (hi.T, lo.T, hi, lo)], axis=0)), jnp.asarray(small)


def fwd(tab, i):
    return tab[i * G : (i + 1) * G, :]


def inv(tab, i):
    return tab[(2 + i) * G : (3 + i) * G, :]


def dot(a, b):
    return jnp.dot(a, b, preferred_element_type=F32)


def split(x):
    hi = x.astype(BF16)
    return hi, (x - hi.astype(F32)).astype(BF16)


def near(shape, dtype=BF16):
    return pltpu.VMEM(shape, dtype)


def far(x):
    return pltpu.with_memory_space_constraint(x, pltpu.HBM)


def call(body, out_shape, ins, in_specs, out_specs, scratch=(), flops=0, nbytes=0, name=None, alias={}):
    return pl.pallas_call(
        body,
        out_shape=out_shape,
        in_specs=in_specs,
        out_specs=out_specs,
        scratch_shapes=scratch,
        input_output_aliases=alias,
        compiler_params=pltpu.CompilerParams(vmem_limit_bytes=VMEM_LIMIT),
        cost_estimate=pl.CostEstimate(flops=flops, bytes_accessed=nbytes, transcendentals=0),
        name=name,
    )(*ins)


def first_body(n_t, cp, cols, nr, switch, slope, exp_ref, act, lines, small, *refs):
    outs, (act_out, lines_out, small_out) = refs[:n_t], refs[n_t : n_t + 3]
    switch_v, slope_v, exp_v, sems = refs[n_t + 3 :]
    rep, ten = lax.axis_index("replica"), lax.axis_index("tensor")
    r0 = pl.multiple_of((rep // cp) * nr, nr)
    copies = [
        pltpu.make_async_copy(src, dst, sems.at[i])
        for i, (src, dst) in enumerate(
            [
                (switch, switch_v),
                (slope, slope_v),
                (exp_ref.at[pl.ds(r0, nr), :], exp_v),
                (act, act_out),
                (lines, lines_out),
                (small, small_out),
            ]
        )
    ]
    for copy in copies:
        copy.start()
    copies[0].wait()
    copies[1].wait()
    v = switch_v[...].astype(F32)
    up = (slope_v[...].astype(F32) * (v * jax.nn.sigmoid(v))).astype(BF16)
    for k in range(n_t):
        outs[k][:B, :] = up
    copies[2].wait()
    nc = cols // cp
    for k in range(1, n_t):
        c0 = (ten ^ k) * cols + lax.rem(rep, cp) * nc
        for j in range(nc // 128):
            at = pl.multiple_of(c0 + j * 128, 128)
            outs[k][B + j * nr : B + (j + 1) * nr, :] = exp_v[:, pl.ds(at, 128)]
    for copy in copies[3:]:
        copy.wait()


def grads_body(n, act, after, *refs):
    ups, outs = refs[:n], refs[n:]
    up = jnp.concatenate([u[:B, :] for u in ups], axis=0)
    for c in range(0, act.shape[1], G):
        g = dot(up, act[:, c : c + G])
        for k in range(n):
            outs[k][:, c : c + G] = g[k * B : (k + 1) * B].astype(outs[k].dtype)


def bundle_body(n_t, keep, after, lines, *refs):
    parts, out = refs[: n_t - 1], refs[n_t - 1]
    n = parts[0].shape[0] - B
    for k in range(n_t - 1):
        out[k * n : (k + 1) * n, :] = parts[k][B:, :]
    blocks = lines.shape[1]
    rows = jnp.concatenate([lines[...].astype(F32), jnp.zeros((keep, 128 - blocks), F32)], axis=1)
    out[(n_t - 1) * n :, :] = jnp.concatenate([rows, jnp.zeros((16 - keep, 128), F32)], axis=0).astype(BF16)


def join_body(n, *refs):
    for i, ref in enumerate(refs[:n]):
        refs[-1][i] = ref[...]


def own_body(keep, lines, small, p_ref, a_ref):
    blocks, nb = lines.shape[1], G // B
    rows = jnp.concatenate([lines[...].astype(F32), jnp.zeros((keep, 128 - blocks), F32)], axis=1)
    lane = lax.broadcasted_iota(jnp.int32, (nb * keep, 2 * B), 1).astype(F32)
    for g in range(blocks // nb):
        num = jnp.concatenate(
            [jnp.broadcast_to(rows[:, g * nb + j : g * nb + j + 1], (keep, 2 * B)) for j in range(nb)], axis=0
        )
        hot = jnp.concatenate(
            [jnp.where(lane == num, 1.0, 0.0), jnp.where(lane - B == num, 1.0, 0.0)], axis=0
        ).astype(BF16)
        a_ref[g * B : (g + 1) * B, :] = dot(hot, small[:, : 2 * B]).astype(BF16)
    rows = jnp.concatenate([rows] * (2 * B // keep), axis=0).T
    freq = lax.broadcasted_iota(jnp.int32, (B, 2 * B), 0).astype(F32)
    block = (lax.broadcasted_iota(jnp.int32, (1, 2 * B), 1) // keep) % nb
    term = lax.broadcasted_iota(jnp.int32, (B, 2 * B), 1) // (B // 2)
    for g in range(blocks // nb):
        num = rows[g * nb : g * nb + 1]
        for j in range(1, nb):
            num = jnp.where(block == j, rows[g * nb + j : g * nb + j + 1], num)
        hot = jnp.where(freq == num, 1.0, 0.0).astype(BF16)
        y = dot(small[:, 2 * B : 3 * B], hot)
        p = jnp.where(term == 3, 0.0, jnp.where(term == 1, y[B:], y[:B]))
        p_ref[:, g * 2 * B : (g + 1) * 2 * B] = p.astype(BF16)


def kept_body(ks, n_t, keep, vel, a_ref, tab, after, after_too, *refs):
    keep_rows(ks, n_t, keep, vel, a_ref, tab, refs[: len(ks)], *refs[-2:])


def keep_rows(ks, n_t, keep, vel, a_ref, tab, grads, send_ref, own_ref):
    cols = grads[0].shape[1]
    ng = cols // G
    lane_block = lax.broadcasted_iota(jnp.int32, (keep, G), 1) // B
    sel = []
    for n, k in enumerate(ks):
        c0 = (lax.axis_index("tensor") ^ k) * cols
        for i in range(ng):
            at = pl.multiple_of(c0 + i * G, G)
            moment = momentum_decay * vel[:, pl.ds(at, G)] + grads[n][:, i * G : (i + 1) * G].astype(F32)
            hi, lo = split(moment)
            y = dot(a_ref[pl.ds(pl.multiple_of(at // (G // B), B), B), :], jnp.concatenate([hi, lo], axis=0))
            y = y[: B // 2] + y[B // 2 :]
            got = y[:keep]
            for j in range(1, G // B):
                got = jnp.where(lane_block == j, y[j * keep : (j + 1) * keep], got)
            sel.append(got)
    hi, lo = split(jnp.concatenate(sel, axis=0))
    n = len(ks) * ng * keep
    y = dot(jnp.concatenate([hi, lo], axis=0), fwd(tab, 0))
    kept = (y[:n] + y[n:] + dot(hi, fwd(tab, 1))).astype(BF16)
    q = dot(kept, inv(tab, 0)) + dot(kept, inv(tab, 1))
    for n, k in enumerate(ks):
        c0 = pl.multiple_of((lax.axis_index("tensor") ^ k) * cols, G)
        part = jnp.concatenate([q[(n * ng + i) * keep : (n * ng + i + 1) * keep] for i in range(ng)], axis=1)
        own_ref[:, pl.ds(c0, cols)] = part
        send_ref[:, pl.ds(c0, cols)] = part.astype(BF16)


def return_body(n_t, keep, vel, p_ref, q, *refs):
    grads, (new_ref, held, sems) = refs[:n_t], refs[n_t:]
    cols = grads[0].shape[1]
    ng = cols // G
    lane_block = lax.broadcasted_iota(jnp.int32, (keep, G), 1) // B
    copies = []
    for k in range(n_t):
        c0 = pl.multiple_of((lax.axis_index("tensor") ^ k) * cols, G)
        for i in range(ng):
            at = pl.multiple_of(c0 + i * G, G)
            own = q[:, pl.ds(at, G)]
            spread = jnp.concatenate(
                [jnp.where(lane_block == j, own, 0.0) for j in range(G // B)], axis=0
            )
            hi, lo = split(spread)
            w = jnp.concatenate([hi, hi, lo, jnp.zeros_like(lo)], axis=0)
            back = dot(p_ref[:, pl.ds(pl.multiple_of(at // 2, 2 * B), 2 * B)], w)
            moment = momentum_decay * vel[:, pl.ds(at, G)] + grads[k][:, i * G : (i + 1) * G].astype(F32)
            held[:, pl.ds(at, G)] = moment - back
        cut = pl.ds(c0, cols)
        copies.append(pltpu.make_async_copy(held.at[:, cut], new_ref.at[:, cut], sems.at[k]))
        copies[-1].start()
    for copy in copies:
        copy.wait()


def places_body(keep, mask, tally, small, bundles, hi_ref, lo_ref, w_ref):
    half = bundles.shape[0]
    rep = lax.axis_index("replica")
    total, alive = jnp.float32(0), jnp.float32(0)
    for r in range(2 * half):
        m = mask[r].astype(F32)
        total = total + m * tally[r].astype(F32)
        alive = alive + m
    place = (lax.broadcasted_iota(jnp.int32, (8, 2 * B), 1) // keep) % half
    scale = jnp.full((8, 2 * B), alive) / jnp.full((8, 2 * B), total)
    ws = []
    for h in range(2):
        w = jnp.zeros((8, 2 * B), F32)
        for i in range(half):
            r = rep ^ (2 * i + h)
            w = jnp.where(place == i, mask[r].astype(F32) * tally[r].astype(F32), w)
        ws.append(w * scale)
    w_ref[...] = ws[1]
    side_places(keep, ws[0][:1], small, bundles, hi_ref, lo_ref)


def other_places_body(keep, w_ref, small, bundles, hi_ref, lo_ref):
    side_places(keep, w_ref[:1, :], small, bundles, hi_ref, lo_ref)


def side_places(keep, w, small, bundles, hi_ref, lo_ref):
    half, last, nb = bundles.shape[0], bundles.shape[1] - 16, G // B
    freq = lax.broadcasted_iota(jnp.int32, (B, 2 * B), 0).astype(F32)
    block = lax.broadcasted_iota(jnp.int32, (1, 2 * B), 1) // (half * keep)
    chip = lax.axis_index("replica") // 2
    rows = [bundles[chip ^ i, last:, :].astype(F32)[:keep] for i in range(half)]
    rows = jnp.concatenate(rows * nb, axis=0).T
    for g in range(hi_ref.shape[1] // (2 * B)):
        num = rows[g * nb : g * nb + 1]
        for j in range(1, nb):
            num = jnp.where(block == j, rows[g * nb + j : g * nb + j + 1], num)
        hot = jnp.where(freq == num, 1.0, 0.0).astype(BF16)
        y = dot(small[:, 2 * B : 3 * B], hot)
        hi, lo = split((y[:B] + y[B:]) * w)
        hi_ref[:, g * 2 * B : (g + 1) * 2 * B] = hi
        lo_ref[:, g * 2 * B : (g + 1) * 2 * B] = lo


def spread_rows(p_hi, p_lo, ships, g):
    half, keep = ships.shape[0], ships.shape[1]
    lane_block = lax.broadcasted_iota(jnp.int32, (half * keep, G), 1) // B
    s = jnp.concatenate([ships[i, :, g * G : (g + 1) * G].astype(F32) for i in range(half)], axis=0)
    w = jnp.concatenate(
        [jnp.where(lane_block == j, s, 0.0).astype(BF16) for j in range(G // B)], axis=0
    )
    cut = slice(g * 2 * B, (g + 1) * 2 * B)
    y = dot(jnp.concatenate([p_hi[:, cut], p_lo[:, cut]], axis=0), w)
    return y[:B] + y[B:]


def half_update_body(p_hi, p_lo, mine, out):
    for g in range(out.shape[0] // B):
        out[g * B : (g + 1) * B, :] = spread_rows(p_hi, p_lo, mine, g)


def update_body(chunk, half_sum, p_hi, p_lo, other, out, held, sems):
    ng = half_sum.shape[0] // B
    copies = []
    for c in range(0, ng, chunk):
        for g in range(c, c + chunk):
            held[:, g * G : (g + 1) * G] = half_sum[g * B : (g + 1) * B, :] + spread_rows(p_hi, p_lo, other, g)
        cut = pl.ds(c * G, chunk * G)
        copies.append(pltpu.make_async_copy(held.at[:, cut], out.at[:, cut], sems.at[c // chunk]))
        copies[-1].start()
    for copy in copies:
        copy.wait()


def input_grad_body(n_t, h, exp_ref, bundles, *refs):
    ups, (out, held, ready, sem) = refs[:n_t], refs[-4:]
    half = bundles.shape[0]
    nc, nr = held.shape[1], B // half
    tiles = nc // 128
    c0 = pl.multiple_of(lax.rem(lax.axis_index("replica") ^ h, 2) * nc, 128)
    held[:B, :] = exp_ref[:, pl.ds(pl.multiple_of(lax.axis_index("tensor") * 2 * nc + c0, 128), nc)]
    for i in range(half):
        for k in range(1, n_t):
            row = k * B + i * nr
            for j in range(tiles):
                at = ((k - 1) * tiles + j) * nr
                held[row : row + nr, j * 128 : (j + 1) * 128] = bundles[i, at : at + nr, :]
    up = jnp.concatenate([u[:B, :] for u in ups], axis=0).T
    for c in range(0, nc, 128):
        ready[:, c : c + 128] = dot(up, held[:, c : c + 128]).astype(BF16)
    copy = pltpu.make_async_copy(ready, out.at[:, pl.ds(c0, nc)], sem)
    copy.start()
    copy.wait()


def per_device(n_t, n_r, act, switch, slope, exp, vel, lines, mask, tally):
    cols = act.shape[1]
    width = exp.shape[1]
    tok = act.shape[0]
    keep = lines.shape[3]
    blocks = width // B
    groups = width // G
    cp = 2
    rp = n_r // cp
    half = n_r // 2
    tab, small = constants()
    def trade(x, k):
        return lax.ppermute(x, "tensor", [(i, i ^ k) for i in range(n_t)])

    order = [*range(2, n_t), 1]

    def swap(x, m):
        return lax.ppermute(x, "replica", [(i, i ^ m) for i in range(n_r)])

    own = lines[0, 0].T
    tiles = cols // cp // 128
    nr = B // rp
    *parts, act, own, small = call(
        functools.partial(first_body, n_t, cp, cols, nr),
        [near((B, tok))]
        + [near((B + tiles * nr, 128))] * (n_t - 1)
        + [near(act.shape), near(own.shape, jnp.int32), near(small.shape)],
        (far(switch.T), far(slope.T), far(exp), far(act), far(own), far(small)),
        [ANY] * 6,
        [VM] * (n_t + 3),
        scratch=[
            pltpu.VMEM((B, tok), BF16),
            pltpu.VMEM((B, tok), BF16),
            pltpu.VMEM((nr, width), BF16),
            pltpu.SemaphoreType.DMA((6,)),
        ],
        nbytes=act.size * 4 + nr * width * 2,
        name="up_grads",
    )
    got = {k: trade(parts[k], k) for k in order}
    parts = [parts[0]] + [got[k] for k in range(1, n_t)]

    p_own, a_own = call(
        functools.partial(own_body, keep),
        [near((B, groups * 2 * B)), near((groups * B, 2 * B))],
        (own, small),
        [VM, VM],
        [VM, VM],
        name="own_places",
    )

    def grads_of(ks, after):
        return call(
            functools.partial(grads_body, len(ks)),
            [near((B, cols), BF16 if k else F32) for k in ks],
            (act, after, *[parts[k] for k in ks]),
            [VM, ANY] + [VM] * len(ks),
            [VM] * len(ks),
            name="weight_grads",
        )

    grads = {}
    for k in order[:-1]:
        (grads[k],) = grads_of([k], act)
    made, grads[0] = grads_of([order[-1], 0], a_own)
    grads[order[-1]] = made
    grads.update({k: trade(grads[k], k) for k in order})

    bundle = call(
        functools.partial(bundle_body, n_t, keep),
        near(((n_t - 1) * tiles * nr + 16, 128)),
        (made, own, *parts[1:]),
        [ANY] + [VM] * n_t,
        VM,
        name="bundle",
    )
    sides = [[r for r in range(n_r) if r % 2 == h] for h in range(2)]
    bundles = [lax.all_gather(bundle, "replica", axis=0, axis_index_groups=sides)]
    bundles.append(swap(bundles[0], 1))

    *mine_at, shares = call(
        functools.partial(places_body, keep),
        [near((B, blocks * half * keep))] * 2 + [near((8, 2 * B), F32)],
        (mask, tally, small, bundles[0]),
        [SM, SM, VM, VM],
        [VM] * 3,
        name="places",
    )

    def columns_of(h, so_far=()):
        return call(
            functools.partial(input_grad_body, n_t, h),
            jax.ShapeDtypeStruct((tok, cols), BF16),
            (exp, bundles[h], *parts, *so_far),
            [VM] * (2 + n_t) + [ANY] * len(so_far),
            ANY,
            scratch=[
                pltpu.VMEM((n_t * B, cols // cp), BF16),
                pltpu.VMEM((tok, cols // cp), BF16),
                pltpu.SemaphoreType.DMA,
            ],
            name="input_grads",
            alias={2 + n_t: 0} if so_far else {},
        )

    first_columns = columns_of(0)

    rows = []
    for ks in ([k for k in range(n_t) if k != n_t - 1], [n_t - 1]):
        n = len(ks)
        rows = call(
            functools.partial(kept_body, ks, n_t, keep),
            [near((keep, width)), near((keep, width), F32)],
            (vel[0], a_own, tab, mine_at[0], far(first_columns), *[grads[k] for k in ks], *rows),
            [VM] * 3 + [ANY] * 2 + [VM] * (n + len(rows)),
            [VM] * 2,
            flops=6 * B * B * cols * n,
            nbytes=B * cols * 6 * n,
            name="kept_rows",
            alias={5 + n: 0, 6 + n: 1} if rows else {},
        )
    ship, q_own = rows


    other_at = call(
        functools.partial(other_places_body, keep),
        [near((B, blocks * half * keep))] * 2,
        (shares, small, bundles[1]),
        [VM] * 3,
        [VM] * 2,
        name="other_places",
    )
    input_grad = columns_of(1, (far(first_columns),))

    ships = [ship] + [swap(ship, 2 * i) for i in range(1, half)]
    new = call(
        functools.partial(return_body, n_t, keep),
        jax.ShapeDtypeStruct((B, width), F32),
        (vel[0], p_own, q_own, *[grads[k] for k in range(n_t)]),
        [VM] * (3 + n_t),
        ANY,
        scratch=[pltpu.VMEM((B, width), F32), pltpu.SemaphoreType.DMA((n_t,))],
        flops=1 << 33,
        nbytes=B * width * 10,
        name="new_momentums",
    )
    mine = call(
        functools.partial(join_body, half),
        near((half, keep, width)),
        (*ships, far(new), other_at[0]),
        [VM] * half + [ANY] * 2,
        VM,
        name="join_kept",
    )
    other = swap(mine, 1)
    half_sum = call(
        half_update_body,
        near((groups * B, G), F32),
        (*mine_at, mine),
        [VM] * 3,
        VM,
        name="half_updates",
    )
    chunk = 2 if groups % 2 == 0 else 1
    update = call(
        functools.partial(update_body, chunk),
        jax.ShapeDtypeStruct((B, width), F32),
        (half_sum, *other_at, other),
        [VM] * 4,
        ANY,
        scratch=[
            pltpu.VMEM((B, width), F32),
            pltpu.SemaphoreType.DMA((groups // chunk,)),
        ],
        flops=8 * B * G * width,
        nbytes=B * width * 8,
        name="updates",
    )
    return input_grad, new[None], update


def per_device_plain(
    projection_inputs,
    switch_logits_raw,
    inner_neuron_slope,
    expansion_matrix,
    velocity_buffer,
    sent_spectral_lines,
    participant_mask,
    token_tallies,
):
    highest = lax.Precision.HIGHEST
    up_grad = (
        inner_neuron_slope.astype(jnp.float32) * jax.nn.silu(switch_logits_raw.astype(jnp.float32))
    ).astype(jnp.bfloat16)
    partial_terms = jnp.dot(up_grad, expansion_matrix, preferred_element_type=jnp.float32)
    input_grad = lax.psum_scatter(partial_terms, "tensor", scatter_dimension=1, tiled=True).astype(
        jnp.bfloat16
    )
    grad_w = lax.dot_general(
        up_grad,
        lax.all_gather(projection_inputs, "tensor", axis=1, tiled=True),
        (((0,), (0,)), ((), ())),
        preferred_element_type=jnp.float32,
    )
    row_total_count = expansion_matrix.shape[0] // 64
    col_count = expansion_matrix.shape[1] // 64
    moment = momentum_decay * velocity_buffer[0] + grad_w
    cosines = cosine_table()
    blocks = moment.reshape(row_total_count, 64, col_count, 64).transpose(0, 2, 1, 3)
    coefficients = jnp.einsum("fa,ijab,gb->ijfg", cosines, blocks, cosines, precision=highest)
    freq_ids = jnp.arange(64, dtype=jnp.int32)
    own_rows = sent_spectral_lines[0]
    chosen = (own_rows[..., None] == freq_ids).astype(jnp.float32)
    shipped = jnp.einsum("ijkf,ijfg->ijkg", chosen, coefficients, precision=highest).astype(
        jnp.bfloat16
    )
    spectrum = jnp.einsum("ijkf,ijkg->ijfg", chosen, shipped.astype(jnp.float32), precision=highest)
    returned = jnp.einsum("fa,ijfg,gb->ijab", cosines, spectrum, cosines, precision=highest)
    new_moment = moment - returned.transpose(0, 2, 1, 3).reshape(moment.shape)
    worker_burdens = participant_mask.astype(jnp.float32) * token_tallies.astype(jnp.float32)
    worker_fractions = worker_burdens * (
        jnp.sum(participant_mask.astype(jnp.float32)) / jnp.sum(worker_burdens)
    )
    myself = lax.axis_index("replica")
    combined = lax.psum(worker_fractions[myself] * spectrum, "replica")
    update = jnp.einsum("fa,ijfg,gb->ijab", cosines, combined, cosines, precision=highest)
    update = update.transpose(0, 2, 1, 3).reshape(moment.shape)
    return (input_grad, new_moment[None], update)


def solution(mesh):
    n_t, n_r = mesh.shape["tensor"], mesh.shape["replica"]

    def device(*args):
        act, exp, lines = args[0], args[3], args[5]
        fits = (
            act.shape[1] % G == 0
            and act.shape[0] % 128 == 0
            and exp.shape[0] == B
            and lines.shape[3] == 8
            and n_r == 8
            and n_t >= 2
            and n_t & (n_t - 1) == 0
        )
        if not fits:
            return per_device_plain(*args)
        return per_device(n_t, n_r, *args)

    return jax.shard_map(
        device,
        mesh=mesh,
        in_specs=(
            P("replica", "tensor"),
            P("replica", "tensor"),
            P("replica", "tensor"),
            P("tensor", None),
            P("replica", "tensor", None),
            P("replica", "tensor", None, None),
            P(),
            P(),
        ),
        out_specs=(P("replica", "tensor"), P("replica", "tensor", None), P("tensor", None)),
        check_vma=False,
    )
```

```python
import functools

import jax
import jax.numpy as jnp
import numpy as np
from jax import lax
from jax.experimental import pallas as pl
from jax.experimental.pallas import tpu as pltpu
from jax.sharding import PartitionSpec as P

momentum_decay = 0.9
B = 64
G = 256
F32 = jnp.float32
BF16 = jnp.bfloat16
VMEM_LIMIT = 24 * 1024 * 1024

VM = pl.BlockSpec(memory_space=pltpu.VMEM)
SM = pl.BlockSpec(memory_space=pltpu.SMEM)
ANY = pl.BlockSpec(memory_space=pl.ANY)


def cosine_table():
    freqs = jnp.arange(64, dtype=jnp.float32)[:, None]
    places = jnp.arange(64, dtype=jnp.float32)[None, :]
    cosines = jnp.cos(jnp.pi * (places + 0.5) * freqs / 64.0) * jnp.sqrt(2.0 / 64.0)
    return cosines.at[0].multiply(jnp.sqrt(0.5))


def cosine_np():
    f = np.arange(B)[:, None]
    a = np.arange(B)[None, :]
    c = np.cos(np.pi * (a + 0.5) * f / B) * np.sqrt(2.0 / B)
    c[0] *= np.sqrt(0.5)
    return c


def halves(c):
    hi = np.asarray(c, dtype=np.float32).astype(jnp.bfloat16)
    lo = (np.asarray(c, np.float64) - hi.astype(np.float64)).astype(np.float32).astype(jnp.bfloat16)
    return hi, lo


def constants():
    hi, lo = halves(cosine_np())
    eye = np.eye(G // B)
    kron = lambda x: np.kron(eye, np.asarray(x, np.float32)).astype(jnp.bfloat16)
    small = np.zeros((2 * B, 4 * B), jnp.bfloat16)
    for i, x in enumerate((hi, lo)):
        rows = slice(i * B, (i + 1) * B)
        small[rows, :B], small[rows, B : 2 * B], small[rows, 2 * B : 3 * B] = x, x, x.T
    return jnp.asarray(np.concatenate([kron(x) for x in (hi.T, lo.T, hi, lo)], axis=0)), jnp.asarray(small)


def fwd(tab, i):
    return tab[i * G : (i + 1) * G, :]


def inv(tab, i):
    return tab[(2 + i) * G : (3 + i) * G, :]


def dot(a, b):
    return jnp.dot(a, b, preferred_element_type=F32)


def split(x):
    hi = x.astype(BF16)
    return hi, (x - hi.astype(F32)).astype(BF16)


def near(shape, dtype=BF16):
    return pltpu.VMEM(shape, dtype)


def far(x):
    return pltpu.with_memory_space_constraint(x, pltpu.HBM)


def call(body, out_shape, ins, in_specs, out_specs, scratch=(), flops=0, nbytes=0, name=None, alias={}):
    return pl.pallas_call(
        body,
        out_shape=out_shape,
        in_specs=in_specs,
        out_specs=out_specs,
        scratch_shapes=scratch,
        input_output_aliases=alias,
        compiler_params=pltpu.CompilerParams(vmem_limit_bytes=VMEM_LIMIT),
        cost_estimate=pl.CostEstimate(flops=flops, bytes_accessed=nbytes, transcendentals=0),
        name=name,
    )(*ins)


def first_body(n_t, cp, cols, nr, switch, slope, exp_ref, act, lines, small, *refs):
    outs, (act_out, lines_out, small_out) = refs[:n_t], refs[n_t : n_t + 3]
    switch_v, slope_v, exp_v, sems = refs[n_t + 3 :]
    rep, ten = lax.axis_index("replica"), lax.axis_index("tensor")
    r0 = pl.multiple_of((rep // cp) * nr, nr)
    copies = [
        pltpu.make_async_copy(src, dst, sems.at[i])
        for i, (src, dst) in enumerate(
            [
                (switch, switch_v),
                (slope, slope_v),
                (exp_ref.at[pl.ds(r0, nr), :], exp_v),
                (act, act_out),
                (lines, lines_out),
                (small, small_out),
            ]
        )
    ]
    for copy in copies:
        copy.start()
    copies[0].wait()
    copies[1].wait()
    v = switch_v[...].astype(F32)
    up = (slope_v[...].astype(F32) * (v * jax.nn.sigmoid(v))).astype(BF16)
    for k in range(n_t):
        outs[k][:B, :] = up
    copies[2].wait()
    nc = cols // cp
    for k in range(1, n_t):
        c0 = (ten ^ k) * cols + lax.rem(rep, cp) * nc
        for j in range(nc // 128):
            at = pl.multiple_of(c0 + j * 128, 128)
            outs[k][B + j * nr : B + (j + 1) * nr, :] = exp_v[:, pl.ds(at, 128)]
    for copy in copies[3:]:
        copy.wait()


def grads_body(n, act, after, *refs):
    ups, outs = refs[:n], refs[n:]
    up = jnp.concatenate([u[:B, :] for u in ups], axis=0)
    for c in range(0, act.shape[1], G):
        g = dot(up, act[:, c : c + G])
        for k in range(n):
            outs[k][:, c : c + G] = g[k * B : (k + 1) * B].astype(outs[k].dtype)


def bundle_body(n_t, keep, after, lines, *refs):
    parts, out = refs[: n_t - 1], refs[n_t - 1]
    n = parts[0].shape[0] - B
    for k in range(n_t - 1):
        out[k * n : (k + 1) * n, :] = parts[k][B:, :]
    blocks = lines.shape[1]
    rows = jnp.concatenate([lines[...].astype(F32), jnp.zeros((keep, 128 - blocks), F32)], axis=1)
    out[(n_t - 1) * n :, :] = jnp.concatenate([rows, jnp.zeros((16 - keep, 128), F32)], axis=0).astype(BF16)


def join_body(n, *refs):
    for i, ref in enumerate(refs[1 : n + 1]):
        refs[-1][i] = ref[...]


def own_body(keep, lines, small, p_ref, a_ref):
    blocks, nb = lines.shape[1], G // B
    rows = jnp.concatenate([lines[...].astype(F32), jnp.zeros((keep, 128 - blocks), F32)], axis=1)
    lane = lax.broadcasted_iota(jnp.int32, (nb * keep, 2 * B), 1).astype(F32)
    for g in range(blocks // nb):
        num = jnp.concatenate(
            [jnp.broadcast_to(rows[:, g * nb + j : g * nb + j + 1], (keep, 2 * B)) for j in range(nb)], axis=0
        )
        hot = jnp.concatenate(
            [jnp.where(lane == num, 1.0, 0.0), jnp.where(lane - B == num, 1.0, 0.0)], axis=0
        ).astype(BF16)
        a_ref[g * B : (g + 1) * B, :] = dot(hot, small[:, : 2 * B]).astype(BF16)
    rows = jnp.concatenate([rows] * (2 * B // keep), axis=0).T
    freq = lax.broadcasted_iota(jnp.int32, (B, 2 * B), 0).astype(F32)
    block = (lax.broadcasted_iota(jnp.int32, (1, 2 * B), 1) // keep) % nb
    term = lax.broadcasted_iota(jnp.int32, (B, 2 * B), 1) // (B // 2)
    for g in range(blocks // nb):
        num = rows[g * nb : g * nb + 1]
        for j in range(1, nb):
            num = jnp.where(block == j, rows[g * nb + j : g * nb + j + 1], num)
        hot = jnp.where(freq == num, 1.0, 0.0).astype(BF16)
        y = dot(small[:, 2 * B : 3 * B], hot)
        p = jnp.where(term == 3, 0.0, jnp.where(term == 1, y[B:], y[:B]))
        p_ref[:, g * 2 * B : (g + 1) * 2 * B] = p.astype(BF16)


def kept_body(ks, n_t, keep, vel, a_ref, tab, after, *refs):
    keep_rows(ks, n_t, keep, vel, a_ref, tab, refs[: len(ks)], *refs[-2:])


def keep_rows(ks, n_t, keep, vel, a_ref, tab, grads, send_ref, own_ref):
    cols = grads[0].shape[1]
    ng = cols // G
    lane_block = lax.broadcasted_iota(jnp.int32, (keep, G), 1) // B
    sel = []
    for n, k in enumerate(ks):
        c0 = (lax.axis_index("tensor") ^ k) * cols
        for i in range(ng):
            at = pl.multiple_of(c0 + i * G, G)
            moment = momentum_decay * vel[:, pl.ds(at, G)] + grads[n][:, i * G : (i + 1) * G].astype(F32)
            hi, lo = split(moment)
            y = dot(a_ref[pl.ds(pl.multiple_of(at // (G // B), B), B), :], jnp.concatenate([hi, lo], axis=0))
            y = y[: B // 2] + y[B // 2 :]
            got = y[:keep]
            for j in range(1, G // B):
                got = jnp.where(lane_block == j, y[j * keep : (j + 1) * keep], got)
            sel.append(got)
    hi, lo = split(jnp.concatenate(sel, axis=0))
    n = len(ks) * ng * keep
    y = dot(jnp.concatenate([hi, lo], axis=0), fwd(tab, 0))
    kept = (y[:n] + y[n:] + dot(hi, fwd(tab, 1))).astype(BF16)
    q = dot(kept, inv(tab, 0)) + dot(kept, inv(tab, 1))
    for n, k in enumerate(ks):
        c0 = pl.multiple_of((lax.axis_index("tensor") ^ k) * cols, G)
        part = jnp.concatenate([q[(n * ng + i) * keep : (n * ng + i + 1) * keep] for i in range(ng)], axis=1)
        own_ref[:, pl.ds(c0, cols)] = part
        send_ref[:, pl.ds(c0, cols)] = part.astype(BF16)


def return_body(n_t, keep, vel, p_ref, q, mask, tally, *refs):
    grads, (new_ref, w_ref, held, sems, mask_s, tally_s, small_sems) = refs[:n_t], refs[n_t:]
    fetches = [
        pltpu.make_async_copy(src, dst, small_sems.at[i])
        for i, (src, dst) in enumerate([(mask, mask_s), (tally, tally_s)])
    ]
    for copy in fetches:
        copy.start()
    cols = grads[0].shape[1]
    ng = cols // G
    lane_block = lax.broadcasted_iota(jnp.int32, (keep, G), 1) // B
    copies = []
    for k in range(n_t):
        c0 = pl.multiple_of((lax.axis_index("tensor") ^ k) * cols, G)
        for i in range(ng):
            at = pl.multiple_of(c0 + i * G, G)
            own = q[:, pl.ds(at, G)]
            spread = jnp.concatenate(
                [jnp.where(lane_block == j, own, 0.0) for j in range(G // B)], axis=0
            )
            hi, lo = split(spread)
            w = jnp.concatenate([hi, hi, lo, jnp.zeros_like(lo)], axis=0)
            back = dot(p_ref[:, pl.ds(pl.multiple_of(at // 2, 2 * B), 2 * B)], w)
            moment = momentum_decay * vel[:, pl.ds(at, G)] + grads[k][:, i * G : (i + 1) * G].astype(F32)
            held[:, pl.ds(at, G)] = moment - back
        cut = pl.ds(c0, cols)
        copies.append(pltpu.make_async_copy(held.at[:, cut], new_ref.at[:, cut], sems.at[k]))
        copies[-1].start()
    for copy in fetches:
        copy.wait()
    n_r = mask_s.shape[0]
    total, alive = jnp.float32(0), jnp.float32(0)
    for r in range(n_r):
        m = mask_s[r].astype(F32)
        total = total + m * tally_s[r].astype(F32)
        alive = alive + m
    half = n_r // 2
    place = (lax.broadcasted_iota(jnp.int32, (8, 2 * B), 1) // keep) % half
    scale = jnp.full((8, 2 * B), alive) / jnp.full((8, 2 * B), total)
    for h in range(2):
        w = jnp.zeros((8, 2 * B), F32)
        for i in range(half):
            r = lax.axis_index("replica") ^ (2 * i + h)
            w = jnp.where(place == i, mask_s[r].astype(F32) * tally_s[r].astype(F32), w)
        w_ref[h] = w * scale
    for copy in copies:
        copy.wait()


def places_body(keep, w_ref, small, bundles, *p_refs):
    n_r, last = bundles.shape[0], bundles.shape[1] - 16
    half, nb = n_r // 2, G // B
    rep = lax.axis_index("replica")
    freq = lax.broadcasted_iota(jnp.int32, (B, 2 * B), 0).astype(F32)
    lane = lax.broadcasted_iota(jnp.int32, (1, 2 * B), 1)
    block = lane // (half * keep)
    for h in range(2):
        hi_ref, lo_ref = p_refs[2 * h : 2 * h + 2]
        w = w_ref[h, :1, :]
        rows = [bundles[rep ^ (2 * i + h), last:, :].astype(F32)[:keep] for i in range(half)]
        rows = jnp.concatenate(rows * nb, axis=0).T
        for g in range(hi_ref.shape[1] // (2 * B)):
            num = rows[g * nb : g * nb + 1]
            for j in range(1, nb):
                num = jnp.where(block == j, rows[g * nb + j : g * nb + j + 1], num)
            hot = jnp.where(freq == num, 1.0, 0.0).astype(BF16)
            y = dot(small[:, 2 * B : 3 * B], hot)
            hi, lo = split((y[:B] + y[B:]) * w)
            hi_ref[:, g * 2 * B : (g + 1) * 2 * B] = hi
            lo_ref[:, g * 2 * B : (g + 1) * 2 * B] = lo


def spread_rows(p_hi, p_lo, own, ships, g):
    half, keep = ships.shape[0] + 1, ships.shape[1]
    cut = slice(g * G, (g + 1) * G)
    lane_block = lax.broadcasted_iota(jnp.int32, (half * keep, G), 1) // B
    s = [own[:, cut].astype(F32)] + [ships[i, :, cut].astype(F32) for i in range(half - 1)]
    s = jnp.concatenate(s, axis=0)
    w = jnp.concatenate(
        [jnp.where(lane_block == j, s, 0.0).astype(BF16) for j in range(G // B)], axis=0
    )
    cut = slice(g * 2 * B, (g + 1) * 2 * B)
    y = dot(jnp.concatenate([p_hi[:, cut], p_lo[:, cut]], axis=0), w)
    return y[:B] + y[B:]


def half_update_body(p_hi, p_lo, own, others, out):
    for g in range(out.shape[0] // B):
        out[g * B : (g + 1) * B, :] = spread_rows(p_hi, p_lo, own, others, g)


def update_body(chunk, half_sum, p_hi, p_lo, own, others, out, held, sems):
    ng = half_sum.shape[0] // B
    copies = []
    for c in range(0, ng, chunk):
        for g in range(c, c + chunk):
            held[:, g * G : (g + 1) * G] = half_sum[g * B : (g + 1) * B, :] + spread_rows(p_hi, p_lo, own, others, g)
        cut = pl.ds(c * G, chunk * G)
        copies.append(pltpu.make_async_copy(held.at[:, cut], out.at[:, cut], sems.at[c // chunk]))
        copies[-1].start()
    for copy in copies:
        copy.wait()


def input_grad_body(n_t, n_r, cp, exp_ref, bundles, *refs):
    ups, (out, held) = refs[:n_t], refs[n_t:]
    cols = out.shape[1]
    held[:B, :] = exp_ref[:, pl.ds(pl.multiple_of(lax.axis_index("tensor") * cols, 128), cols)]
    nc = cols // cp
    nr = B // (n_r // cp)
    tiles = nc // 128
    for r in range(n_r):
        r0, c0 = (r // cp) * nr, (r % cp) * nc
        for k in range(1, n_t):
            for j in range(tiles):
                at = ((k - 1) * tiles + j) * nr
                held[k * B + r0 : k * B + r0 + nr, c0 + j * 128 : c0 + (j + 1) * 128] = bundles[r, at : at + nr, :]
    up = jnp.concatenate([u[:B, :] for u in ups], axis=0).T
    for c in range(0, cols, G):
        out[:, c : c + G] = dot(up, held[:, c : c + G]).astype(BF16)


def per_device(n_t, n_r, act, switch, slope, exp, vel, lines, mask, tally):
    cols = act.shape[1]
    width = exp.shape[1]
    tok = act.shape[0]
    keep = lines.shape[3]
    blocks = width // B
    groups = width // G
    cp = 2
    rp = n_r // cp
    half = n_r // 2
    tab, small = constants()
    def trade(x, k):
        return lax.ppermute(x, "tensor", [(i, i ^ k) for i in range(n_t)])

    order = [*range(2, n_t), 1]

    def swap(x, m):
        return lax.ppermute(x, "replica", [(i, i ^ m) for i in range(n_r)])

    own = lines[0, 0].T
    tiles = cols // cp // 128
    nr = B // rp
    *parts, act, own, small = call(
        functools.partial(first_body, n_t, cp, cols, nr),
        [near((B, tok))]
        + [near((B + tiles * nr, 128))] * (n_t - 1)
        + [near(act.shape), near(own.shape, jnp.int32), near(small.shape)],
        (far(switch.T), far(slope.T), far(exp), far(act), far(own), far(small)),
        [ANY] * 6,
        [VM] * (n_t + 3),
        scratch=[
            pltpu.VMEM((B, tok), BF16),
            pltpu.VMEM((B, tok), BF16),
            pltpu.VMEM((nr, width), BF16),
            pltpu.SemaphoreType.DMA((6,)),
        ],
        nbytes=act.size * 4 + nr * width * 2,
        name="up_grads",
    )
    got = {k: trade(parts[k], k) for k in order}
    parts = [parts[0]] + [got[k] for k in range(1, n_t)]

    p_own, a_own = call(
        functools.partial(own_body, keep),
        [near((B, groups * 2 * B)), near((groups * B, 2 * B))],
        (own, small),
        [VM, VM],
        [VM, VM],
        name="own_places",
    )

    def grads_of(ks, after):
        return call(
            functools.partial(grads_body, len(ks)),
            [near((B, cols), BF16 if k else F32) for k in ks],
            (act, after, *[parts[k] for k in ks]),
            [VM, ANY] + [VM] * len(ks),
            [VM] * len(ks),
            name="weight_grads",
        )

    grads = {}
    for k in order[:-1]:
        (grads[k],) = grads_of([k], act)
    made, grads[0] = grads_of([order[-1], 0], a_own)
    grads[order[-1]] = made
    grads.update({k: trade(grads[k], k) for k in order})

    bundle = call(
        functools.partial(bundle_body, n_t, keep),
        near(((n_t - 1) * tiles * nr + 16, 128)),
        (made, own, *parts[1:]),
        [ANY] + [VM] * n_t,
        VM,
        name="bundle",
    )
    bundles = lax.all_gather(bundle, "replica", axis=0)

    rows = []
    for ks in ([k for k in range(n_t) if k != n_t - 1], [n_t - 1]):
        n = len(ks)
        rows = call(
            functools.partial(kept_body, ks, n_t, keep),
            [near((keep, width)), near((keep, width), F32)],
            (vel[0], a_own, tab, bundles, *[grads[k] for k in ks], *rows),
            [VM] * 3 + [ANY] + [VM] * (n + len(rows)),
            [VM] * 2,
            flops=6 * B * B * cols * n,
            nbytes=B * cols * 6 * n,
            name="kept_rows",
            alias={4 + n: 0, 5 + n: 1} if rows else {},
        )
    ship, q_own = rows

    new, shares = call(
        functools.partial(return_body, n_t, keep),
        [jax.ShapeDtypeStruct((B, width), F32), near((2, 8, 2 * B), F32)],
        (vel[0], p_own, q_own, far(mask), far(tally), *[grads[k] for k in range(n_t)]),
        [VM] * 3 + [ANY] * 2 + [VM] * n_t,
        [ANY, VM],
        scratch=[
            pltpu.VMEM((B, width), F32),
            pltpu.SemaphoreType.DMA((n_t,)),
            pltpu.SMEM((n_r,), jnp.int32),
            pltpu.SMEM((n_r,), jnp.int32),
            pltpu.SemaphoreType.DMA((2,)),
        ],
        flops=6 * B * B * width,
        nbytes=B * width * 10,
        name="new_momentums",
    )
    places = call(
        functools.partial(places_body, keep),
        [near((B, blocks * half * keep))] * 4,
        (shares, small, bundles),
        [VM] * 3,
        [VM] * 4,
        name="places",
    )
    input_grad = call(
        functools.partial(input_grad_body, n_t, n_r, cp),
        jax.ShapeDtypeStruct((tok, cols), BF16),
        (exp, bundles, *parts),
        [VM] * (2 + n_t),
        VM,
        scratch=[pltpu.VMEM((n_t * B, cols), BF16)],
        flops=2 * tok * n_t * B * cols,
        nbytes=(n_t * B * cols + tok * cols) * 2,
        name="input_grads",
    )

    ships = [ship] + [swap(ship, 2 * i) for i in range(1, half)]
    other_own = swap(ship, 1)
    others = call(
        functools.partial(join_body, half - 1),
        near((half - 1, keep, width)),
        (other_own, *ships[1:], far(new), far(input_grad), places[0]),
        [ANY] + [VM] * (half - 1) + [ANY] * 3,
        VM,
        name="join_kept",
    )
    other = swap(others, 1)
    half_sum = call(
        half_update_body,
        near((groups * B, G), F32),
        (*places[:2], ship, others),
        [VM] * 4,
        VM,
        name="half_updates",
    )
    chunk = 2 if groups % 2 == 0 else 1
    update = call(
        functools.partial(update_body, chunk),
        jax.ShapeDtypeStruct((B, width), F32),
        (half_sum, *places[2:], other_own, other),
        [VM] * 5,
        ANY,
        scratch=[
            pltpu.VMEM((B, width), F32),
            pltpu.SemaphoreType.DMA((groups // chunk,)),
        ],
        flops=8 * B * G * width,
        nbytes=B * width * 8,
        name="updates",
    )
    return input_grad, new[None], update


def per_device_plain(
    projection_inputs,
    switch_logits_raw,
    inner_neuron_slope,
    expansion_matrix,
    velocity_buffer,
    sent_spectral_lines,
    participant_mask,
    token_tallies,
):
    highest = lax.Precision.HIGHEST
    up_grad = (
        inner_neuron_slope.astype(jnp.float32) * jax.nn.silu(switch_logits_raw.astype(jnp.float32))
    ).astype(jnp.bfloat16)
    partial_terms = jnp.dot(up_grad, expansion_matrix, preferred_element_type=jnp.float32)
    input_grad = lax.psum_scatter(partial_terms, "tensor", scatter_dimension=1, tiled=True).astype(
        jnp.bfloat16
    )
    grad_w = lax.dot_general(
        up_grad,
        lax.all_gather(projection_inputs, "tensor", axis=1, tiled=True),
        (((0,), (0,)), ((), ())),
        preferred_element_type=jnp.float32,
    )
    row_total_count = expansion_matrix.shape[0] // 64
    col_count = expansion_matrix.shape[1] // 64
    moment = momentum_decay * velocity_buffer[0] + grad_w
    cosines = cosine_table()
    blocks = moment.reshape(row_total_count, 64, col_count, 64).transpose(0, 2, 1, 3)
    coefficients = jnp.einsum("fa,ijab,gb->ijfg", cosines, blocks, cosines, precision=highest)
    freq_ids = jnp.arange(64, dtype=jnp.int32)
    own_rows = sent_spectral_lines[0]
    chosen = (own_rows[..., None] == freq_ids).astype(jnp.float32)
    shipped = jnp.einsum("ijkf,ijfg->ijkg", chosen, coefficients, precision=highest).astype(
        jnp.bfloat16
    )
    spectrum = jnp.einsum("ijkf,ijkg->ijfg", chosen, shipped.astype(jnp.float32), precision=highest)
    returned = jnp.einsum("fa,ijfg,gb->ijab", cosines, spectrum, cosines, precision=highest)
    new_moment = moment - returned.transpose(0, 2, 1, 3).reshape(moment.shape)
    worker_burdens = participant_mask.astype(jnp.float32) * token_tallies.astype(jnp.float32)
    worker_fractions = worker_burdens * (
        jnp.sum(participant_mask.astype(jnp.float32)) / jnp.sum(worker_burdens)
    )
    myself = lax.axis_index("replica")
    combined = lax.psum(worker_fractions[myself] * spectrum, "replica")
    update = jnp.einsum("fa,ijfg,gb->ijab", cosines, combined, cosines, precision=highest)
    update = update.transpose(0, 2, 1, 3).reshape(moment.shape)
    return (input_grad, new_moment[None], update)


def solution(mesh):
    n_t, n_r = mesh.shape["tensor"], mesh.shape["replica"]

    def device(*args):
        act, exp, lines = args[0], args[3], args[5]
        fits = (
            act.shape[1] % G == 0
            and act.shape[0] % 128 == 0
            and exp.shape[0] == B
            and lines.shape[3] == 8
            and n_r == 8
            and n_t >= 2
            and n_t & (n_t - 1) == 0
        )
        if not fits:
            return per_device_plain(*args)
        return per_device(n_t, n_r, *args)

    return jax.shard_map(
        device,
        mesh=mesh,
        in_specs=(
            P("replica", "tensor"),
            P("replica", "tensor"),
            P("replica", "tensor"),
            P("tensor", None),
            P("replica", "tensor", None),
            P("replica", "tensor", None, None),
            P(),
            P(),
        ),
        out_specs=(P("replica", "tensor"), P("replica", "tensor", None), P("tensor", None)),
        check_vma=False,
    )
```

```python
import functools

import jax
import jax.numpy as jnp
import numpy as np
from jax import lax
from jax.experimental import pallas as pl
from jax.experimental.pallas import tpu as pltpu
from jax.sharding import PartitionSpec as P

momentum_decay = 0.9
B = 64
G = 256
F32 = jnp.float32
BF16 = jnp.bfloat16
VMEM_LIMIT = 24 * 1024 * 1024

VM = pl.BlockSpec(memory_space=pltpu.VMEM)
SM = pl.BlockSpec(memory_space=pltpu.SMEM)
ANY = pl.BlockSpec(memory_space=pl.ANY)


def cosine_table():
    freqs = jnp.arange(64, dtype=jnp.float32)[:, None]
    places = jnp.arange(64, dtype=jnp.float32)[None, :]
    cosines = jnp.cos(jnp.pi * (places + 0.5) * freqs / 64.0) * jnp.sqrt(2.0 / 64.0)
    return cosines.at[0].multiply(jnp.sqrt(0.5))


def cosine_np():
    f = np.arange(B)[:, None]
    a = np.arange(B)[None, :]
    c = np.cos(np.pi * (a + 0.5) * f / B) * np.sqrt(2.0 / B)
    c[0] *= np.sqrt(0.5)
    return c


def halves(c):
    hi = np.asarray(c, dtype=np.float32).astype(jnp.bfloat16)
    lo = (np.asarray(c, np.float64) - hi.astype(np.float64)).astype(np.float32).astype(jnp.bfloat16)
    return hi, lo


def constants():
    hi, lo = halves(cosine_np())
    eye = np.eye(G // B)
    kron = lambda x: np.kron(eye, np.asarray(x, np.float32)).astype(jnp.bfloat16)
    small = np.zeros((2 * B, 4 * B), jnp.bfloat16)
    for i, x in enumerate((hi, lo)):
        rows = slice(i * B, (i + 1) * B)
        small[rows, :B], small[rows, B : 2 * B], small[rows, 2 * B : 3 * B] = x, x, x.T
    return jnp.asarray(np.concatenate([kron(x) for x in (hi.T, lo.T, hi, lo)], axis=0)), jnp.asarray(small)


def fwd(tab, i):
    return tab[i * G : (i + 1) * G, :]


def inv(tab, i):
    return tab[(2 + i) * G : (3 + i) * G, :]


def dot(a, b):
    return jnp.dot(a, b, preferred_element_type=F32)


def split(x):
    hi = x.astype(BF16)
    return hi, (x - hi.astype(F32)).astype(BF16)


def near(shape, dtype=BF16):
    return pltpu.VMEM(shape, dtype)


def far(x):
    return pltpu.with_memory_space_constraint(x, pltpu.HBM)


def call(body, out_shape, ins, in_specs, out_specs, scratch=(), flops=0, nbytes=0, name=None, alias={}):
    return pl.pallas_call(
        body,
        out_shape=out_shape,
        in_specs=in_specs,
        out_specs=out_specs,
        scratch_shapes=scratch,
        input_output_aliases=alias,
        compiler_params=pltpu.CompilerParams(vmem_limit_bytes=VMEM_LIMIT),
        cost_estimate=pl.CostEstimate(flops=flops, bytes_accessed=nbytes, transcendentals=0),
        name=name,
    )(*ins)


def first_body(n_t, cp, cols, nr, switch, slope, exp_ref, act, lines, small, *refs):
    outs, (act_out, lines_out, small_out) = refs[:n_t], refs[n_t : n_t + 3]
    switch_v, slope_v, exp_v, sems = refs[n_t + 3 :]
    rep, ten = lax.axis_index("replica"), lax.axis_index("tensor")
    r0 = pl.multiple_of((rep // cp) * nr, nr)
    copies = [
        pltpu.make_async_copy(src, dst, sems.at[i])
        for i, (src, dst) in enumerate(
            [
                (switch, switch_v),
                (slope, slope_v),
                (exp_ref.at[pl.ds(r0, nr), :], exp_v),
                (act, act_out),
                (lines, lines_out),
                (small, small_out),
            ]
        )
    ]
    for copy in copies:
        copy.start()
    copies[0].wait()
    copies[1].wait()
    v = switch_v[...].astype(F32)
    up = (slope_v[...].astype(F32) * (v * jax.nn.sigmoid(v))).astype(BF16)
    for k in range(n_t):
        outs[k][:B, :] = up
    copies[2].wait()
    nc = cols // cp
    for k in range(1, n_t):
        c0 = (ten ^ k) * cols + lax.rem(rep, cp) * nc
        for j in range(nc // 128):
            at = pl.multiple_of(c0 + j * 128, 128)
            outs[k][B + j * nr : B + (j + 1) * nr, :] = exp_v[:, pl.ds(at, 128)]
    for copy in copies[3:]:
        copy.wait()


def grads_body(n, act, after, *refs):
    ups, outs = refs[:n], refs[n:]
    up = jnp.concatenate([u[:B, :] for u in ups], axis=0)
    for c in range(0, act.shape[1], G):
        g = dot(up, act[:, c : c + G])
        for k in range(n):
            outs[k][:, c : c + G] = g[k * B : (k + 1) * B].astype(outs[k].dtype)


def bundle_body(n_t, keep, after, lines, *refs):
    parts, out = refs[: n_t - 1], refs[n_t - 1]
    n = parts[0].shape[0] - B
    for k in range(n_t - 1):
        out[k * n : (k + 1) * n, :] = parts[k][B:, :]
    blocks = lines.shape[1]
    rows = jnp.concatenate([lines[...].astype(F32), jnp.zeros((keep, 128 - blocks), F32)], axis=1)
    out[(n_t - 1) * n :, :] = jnp.concatenate([rows, jnp.zeros((16 - keep, 128), F32)], axis=0).astype(BF16)


def join_body(n, *refs):
    core = lax.rem(lax.axis_index("replica"), 2)
    late, soon, *rest = refs[1 : n + 1]
    refs[-1][core] = soon[...]
    refs[-1][1 - core] = late[...]
    for i, ref in enumerate(rest):
        refs[-1][2 + i] = ref[...]


def own_body(keep, lines, small, p_ref, a_ref):
    blocks, nb = lines.shape[1], G // B
    rows = jnp.concatenate([lines[...].astype(F32), jnp.zeros((keep, 128 - blocks), F32)], axis=1)
    lane = lax.broadcasted_iota(jnp.int32, (nb * keep, 2 * B), 1).astype(F32)
    for g in range(blocks // nb):
        num = jnp.concatenate(
            [jnp.broadcast_to(rows[:, g * nb + j : g * nb + j + 1], (keep, 2 * B)) for j in range(nb)], axis=0
        )
        hot = jnp.concatenate(
            [jnp.where(lane == num, 1.0, 0.0), jnp.where(lane - B == num, 1.0, 0.0)], axis=0
        ).astype(BF16)
        a_ref[g * B : (g + 1) * B, :] = dot(hot, small[:, : 2 * B]).astype(BF16)
    rows = jnp.concatenate([rows] * (2 * B // keep), axis=0).T
    freq = lax.broadcasted_iota(jnp.int32, (B, 2 * B), 0).astype(F32)
    block = (lax.broadcasted_iota(jnp.int32, (1, 2 * B), 1) // keep) % nb
    term = lax.broadcasted_iota(jnp.int32, (B, 2 * B), 1) // (B // 2)
    for g in range(blocks // nb):
        num = rows[g * nb : g * nb + 1]
        for j in range(1, nb):
            num = jnp.where(block == j, rows[g * nb + j : g * nb + j + 1], num)
        hot = jnp.where(freq == num, 1.0, 0.0).astype(BF16)
        y = dot(small[:, 2 * B : 3 * B], hot)
        p = jnp.where(term == 3, 0.0, jnp.where(term == 1, y[B:], y[:B]))
        p_ref[:, g * 2 * B : (g + 1) * 2 * B] = p.astype(BF16)


def kept_body(ks, n_t, keep, vel, a_ref, tab, after, *refs):
    keep_rows(ks, n_t, keep, vel, a_ref, tab, refs[: len(ks)], *refs[-2:])


def keep_rows(ks, n_t, keep, vel, a_ref, tab, grads, send_ref, own_ref):
    cols = grads[0].shape[1]
    ng = cols // G
    lane_block = lax.broadcasted_iota(jnp.int32, (keep, G), 1) // B
    sel = []
    for n, k in enumerate(ks):
        c0 = (lax.axis_index("tensor") ^ k) * cols
        for i in range(ng):
            at = pl.multiple_of(c0 + i * G, G)
            moment = momentum_decay * vel[:, pl.ds(at, G)] + grads[n][:, i * G : (i + 1) * G].astype(F32)
            hi, lo = split(moment)
            y = dot(a_ref[pl.ds(pl.multiple_of(at // (G // B), B), B), :], jnp.concatenate([hi, lo], axis=0))
            y = y[: B // 2] + y[B // 2 :]
            got = y[:keep]
            for j in range(1, G // B):
                got = jnp.where(lane_block == j, y[j * keep : (j + 1) * keep], got)
            sel.append(got)
    hi, lo = split(jnp.concatenate(sel, axis=0))
    n = len(ks) * ng * keep
    y = dot(jnp.concatenate([hi, lo], axis=0), fwd(tab, 0))
    kept = (y[:n] + y[n:] + dot(hi, fwd(tab, 1))).astype(BF16)
    q = dot(kept, inv(tab, 0)) + dot(kept, inv(tab, 1))
    for n, k in enumerate(ks):
        c0 = pl.multiple_of((lax.axis_index("tensor") ^ k) * cols, G)
        part = jnp.concatenate([q[(n * ng + i) * keep : (n * ng + i + 1) * keep] for i in range(ng)], axis=1)
        own_ref[:, pl.ds(c0, cols)] = part
        send_ref[:, pl.ds(c0, cols)] = part.astype(BF16)


def return_body(n_t, keep, vel, p_ref, q, mask, tally, *refs):
    grads, (new_ref, w_ref, held, sems, mask_s, tally_s, small_sems) = refs[:n_t], refs[n_t:]
    fetches = [
        pltpu.make_async_copy(src, dst, small_sems.at[i])
        for i, (src, dst) in enumerate([(mask, mask_s), (tally, tally_s)])
    ]
    for copy in fetches:
        copy.start()
    cols = grads[0].shape[1]
    ng = cols // G
    lane_block = lax.broadcasted_iota(jnp.int32, (keep, G), 1) // B
    copies = []
    for k in range(n_t):
        c0 = pl.multiple_of((lax.axis_index("tensor") ^ k) * cols, G)
        for i in range(ng):
            at = pl.multiple_of(c0 + i * G, G)
            own = q[:, pl.ds(at, G)]
            spread = jnp.concatenate(
                [jnp.where(lane_block == j, own, 0.0) for j in range(G // B)], axis=0
            )
            hi, lo = split(spread)
            w = jnp.concatenate([hi, hi, lo, jnp.zeros_like(lo)], axis=0)
            back = dot(p_ref[:, pl.ds(pl.multiple_of(at // 2, 2 * B), 2 * B)], w)
            moment = momentum_decay * vel[:, pl.ds(at, G)] + grads[k][:, i * G : (i + 1) * G].astype(F32)
            held[:, pl.ds(at, G)] = moment - back
        cut = pl.ds(c0, cols)
        copies.append(pltpu.make_async_copy(held.at[:, cut], new_ref.at[:, cut], sems.at[k]))
        copies[-1].start()
    for copy in fetches:
        copy.wait()
    n_r = mask_s.shape[0]
    total, alive = jnp.float32(0), jnp.float32(0)
    for r in range(n_r):
        m = mask_s[r].astype(F32)
        total = total + m * tally_s[r].astype(F32)
        alive = alive + m
    half = n_r // 2
    place = (lax.broadcasted_iota(jnp.int32, (8, 2 * B), 1) // keep) % half
    scale = jnp.full((8, 2 * B), alive) / jnp.full((8, 2 * B), total)
    for h in range(2):
        w = jnp.zeros((8, 2 * B), F32)
        for i in range(half):
            r = lax.axis_index("replica") ^ (2 * i + h)
            w = jnp.where(place == i, mask_s[r].astype(F32) * tally_s[r].astype(F32), w)
        w_ref[h] = w * scale
    for copy in copies:
        copy.wait()


def places_body(keep, w_ref, small, bundles, *p_refs):
    n_r, last = bundles.shape[0], bundles.shape[1] - 16
    half, nb = n_r // 2, G // B
    rep = lax.axis_index("replica")
    freq = lax.broadcasted_iota(jnp.int32, (B, 2 * B), 0).astype(F32)
    lane = lax.broadcasted_iota(jnp.int32, (1, 2 * B), 1)
    block = lane // (half * keep)
    for h in range(2):
        hi_ref, lo_ref = p_refs[2 * h : 2 * h + 2]
        w = w_ref[h, :1, :]
        rows = [bundles[rep ^ (2 * i + h), last:, :].astype(F32)[:keep] for i in range(half)]
        rows = jnp.concatenate(rows * nb, axis=0).T
        for g in range(hi_ref.shape[1] // (2 * B)):
            num = rows[g * nb : g * nb + 1]
            for j in range(1, nb):
                num = jnp.where(block == j, rows[g * nb + j : g * nb + j + 1], num)
            hot = jnp.where(freq == num, 1.0, 0.0).astype(BF16)
            y = dot(small[:, 2 * B : 3 * B], hot)
            hi, lo = split((y[:B] + y[B:]) * w)
            hi_ref[:, g * 2 * B : (g + 1) * 2 * B] = hi
            lo_ref[:, g * 2 * B : (g + 1) * 2 * B] = lo


def spread_rows(p_hi, p_lo, own, ships, g):
    half, keep = ships.shape[0] + 1, ships.shape[1]
    cut = slice(g * G, (g + 1) * G)
    lane_block = lax.broadcasted_iota(jnp.int32, (half * keep, G), 1) // B
    s = [own[:, cut].astype(F32)] + [ships[i, :, cut].astype(F32) for i in range(half - 1)]
    s = jnp.concatenate(s, axis=0)
    w = jnp.concatenate(
        [jnp.where(lane_block == j, s, 0.0).astype(BF16) for j in range(G // B)], axis=0
    )
    cut = slice(g * 2 * B, (g + 1) * 2 * B)
    y = dot(jnp.concatenate([p_hi[:, cut], p_lo[:, cut]], axis=0), w)
    return y[:B] + y[B:]


def half_update_body(p_hi, p_lo, own, others, out):
    for g in range(out.shape[0] // B):
        out[g * B : (g + 1) * B, :] = spread_rows(p_hi, p_lo, own, others, g)


def update_body(chunk, half_sum, p_hi, p_lo, own, others, out, held, sems):
    ng = half_sum.shape[0] // B
    copies = []
    for c in range(0, ng, chunk):
        for g in range(c, c + chunk):
            held[:, g * G : (g + 1) * G] = half_sum[g * B : (g + 1) * B, :] + spread_rows(p_hi, p_lo, own, others, g)
        cut = pl.ds(c * G, chunk * G)
        copies.append(pltpu.make_async_copy(held.at[:, cut], out.at[:, cut], sems.at[c // chunk]))
        copies[-1].start()
    for copy in copies:
        copy.wait()


def input_grad_body(n_t, n_r, cp, exp_ref, bundles, *refs):
    ups, (out, held) = refs[:n_t], refs[n_t:]
    cols = out.shape[1]
    held[:B, :] = exp_ref[:, pl.ds(pl.multiple_of(lax.axis_index("tensor") * cols, 128), cols)]
    nc = cols // cp
    nr = B // (n_r // cp)
    tiles = nc // 128
    for r in range(n_r):
        r0, c0 = (r // cp) * nr, (r % cp) * nc
        for k in range(1, n_t):
            for j in range(tiles):
                at = ((k - 1) * tiles + j) * nr
                held[k * B + r0 : k * B + r0 + nr, c0 + j * 128 : c0 + (j + 1) * 128] = bundles[r, at : at + nr, :]
    up = jnp.concatenate([u[:B, :] for u in ups], axis=0).T
    for c in range(0, cols, G):
        out[:, c : c + G] = dot(up, held[:, c : c + G]).astype(BF16)


def per_device(n_t, n_r, act, switch, slope, exp, vel, lines, mask, tally):
    cols = act.shape[1]
    width = exp.shape[1]
    tok = act.shape[0]
    keep = lines.shape[3]
    blocks = width // B
    groups = width // G
    cp = 2
    rp = n_r // cp
    half = n_r // 2
    tab, small = constants()
    def trade(x, k):
        return lax.ppermute(x, "tensor", [(i, i ^ k) for i in range(n_t)])

    order = [*range(2, n_t), 1]

    def swap(x, m):
        return lax.ppermute(x, "replica", [(i, i ^ m) for i in range(n_r)])

    own = lines[0, 0].T
    tiles = cols // cp // 128
    nr = B // rp
    *parts, act, own, small = call(
        functools.partial(first_body, n_t, cp, cols, nr),
        [near((B, tok))]
        + [near((B + tiles * nr, 128))] * (n_t - 1)
        + [near(act.shape), near(own.shape, jnp.int32), near(small.shape)],
        (far(switch.T), far(slope.T), far(exp), far(act), far(own), far(small)),
        [ANY] * 6,
        [VM] * (n_t + 3),
        scratch=[
            pltpu.VMEM((B, tok), BF16),
            pltpu.VMEM((B, tok), BF16),
            pltpu.VMEM((nr, width), BF16),
            pltpu.SemaphoreType.DMA((6,)),
        ],
        nbytes=act.size * 4 + nr * width * 2,
        name="up_grads",
    )
    got = {k: trade(parts[k], k) for k in order}
    parts = [parts[0]] + [got[k] for k in range(1, n_t)]

    p_own, a_own = call(
        functools.partial(own_body, keep),
        [near((B, groups * 2 * B)), near((groups * B, 2 * B))],
        (own, small),
        [VM, VM],
        [VM, VM],
        name="own_places",
    )

    def grads_of(ks, after):
        return call(
            functools.partial(grads_body, len(ks)),
            [near((B, cols), BF16 if k else F32) for k in ks],
            (act, after, *[parts[k] for k in ks]),
            [VM, ANY] + [VM] * len(ks),
            [VM] * len(ks),
            name="weight_grads",
        )

    grads = {}
    for k in order[:-1]:
        (grads[k],) = grads_of([k], act)
    made, grads[0] = grads_of([order[-1], 0], a_own)
    grads[order[-1]] = made
    grads.update({k: trade(grads[k], k) for k in order})

    bundle = call(
        functools.partial(bundle_body, n_t, keep),
        near(((n_t - 1) * tiles * nr + 16, 128)),
        (made, own, *parts[1:]),
        [ANY] + [VM] * n_t,
        VM,
        name="bundle",
    )
    bundles = lax.all_gather(bundle, "replica", axis=0)

    rows = []
    for ks in ([k for k in range(n_t) if k != n_t - 1], [n_t - 1]):
        n = len(ks)
        rows = call(
            functools.partial(kept_body, ks, n_t, keep),
            [near((keep, width)), near((keep, width), F32)],
            (vel[0], a_own, tab, bundles, *[grads[k] for k in ks], *rows),
            [VM] * 3 + [ANY] + [VM] * (n + len(rows)),
            [VM] * 2,
            flops=6 * B * B * cols * n,
            nbytes=B * cols * 6 * n,
            name="kept_rows",
            alias={4 + n: 0, 5 + n: 1} if rows else {},
        )
    ship, q_own = rows

    new, shares = call(
        functools.partial(return_body, n_t, keep),
        [jax.ShapeDtypeStruct((B, width), F32), near((2, 8, 2 * B), F32)],
        (vel[0], p_own, q_own, far(mask), far(tally), *[grads[k] for k in range(n_t)]),
        [VM] * 3 + [ANY] * 2 + [VM] * n_t,
        [ANY, VM],
        scratch=[
            pltpu.VMEM((B, width), F32),
            pltpu.SemaphoreType.DMA((n_t,)),
            pltpu.SMEM((n_r,), jnp.int32),
            pltpu.SMEM((n_r,), jnp.int32),
            pltpu.SemaphoreType.DMA((2,)),
        ],
        flops=6 * B * B * width,
        nbytes=B * width * 10,
        name="new_momentums",
    )
    places = call(
        functools.partial(places_body, keep),
        [near((B, blocks * half * keep))] * 4,
        (shares, small, bundles),
        [VM] * 3,
        [VM] * 4,
        name="places",
    )
    input_grad = call(
        functools.partial(input_grad_body, n_t, n_r, cp),
        jax.ShapeDtypeStruct((tok, cols), BF16),
        (exp, bundles, *parts),
        [VM] * (2 + n_t),
        VM,
        scratch=[pltpu.VMEM((n_t * B, cols), BF16)],
        flops=2 * tok * n_t * B * cols,
        nbytes=(n_t * B * cols + tok * cols) * 2,
        name="input_grads",
    )

    crossed = [
        lax.ppermute(ship, "replica", [(r, r ^ (2, 4)[(r + turn) % 2]) for r in range(n_r)]) for turn in range(2)
    ]
    ships = [*reversed(crossed), swap(ship, 6)]
    other_own = swap(ship, 1)
    others = call(
        functools.partial(join_body, half - 1),
        near((half - 1, keep, width)),
        (other_own, *ships, far(new), far(input_grad), places[0]),
        [ANY] + [VM] * (half - 1) + [ANY] * 3,
        VM,
        name="join_kept",
    )
    other = swap(others, 1)
    half_sum = call(
        half_update_body,
        near((groups * B, G), F32),
        (*places[:2], ship, others),
        [VM] * 4,
        VM,
        name="half_updates",
    )
    chunk = 2 if groups % 2 == 0 else 1
    update = call(
        functools.partial(update_body, chunk),
        jax.ShapeDtypeStruct((B, width), F32),
        (half_sum, *places[2:], other_own, other),
        [VM] * 5,
        ANY,
        scratch=[
            pltpu.VMEM((B, width), F32),
            pltpu.SemaphoreType.DMA((groups // chunk,)),
        ],
        flops=8 * B * G * width,
        nbytes=B * width * 8,
        name="updates",
    )
    return input_grad, new[None], update


def per_device_plain(
    projection_inputs,
    switch_logits_raw,
    inner_neuron_slope,
    expansion_matrix,
    velocity_buffer,
    sent_spectral_lines,
    participant_mask,
    token_tallies,
):
    highest = lax.Precision.HIGHEST
    up_grad = (
        inner_neuron_slope.astype(jnp.float32) * jax.nn.silu(switch_logits_raw.astype(jnp.float32))
    ).astype(jnp.bfloat16)
    partial_terms = jnp.dot(up_grad, expansion_matrix, preferred_element_type=jnp.float32)
    input_grad = lax.psum_scatter(partial_terms, "tensor", scatter_dimension=1, tiled=True).astype(
        jnp.bfloat16
    )
    grad_w = lax.dot_general(
        up_grad,
        lax.all_gather(projection_inputs, "tensor", axis=1, tiled=True),
        (((0,), (0,)), ((), ())),
        preferred_element_type=jnp.float32,
    )
    row_total_count = expansion_matrix.shape[0] // 64
    col_count = expansion_matrix.shape[1] // 64
    moment = momentum_decay * velocity_buffer[0] + grad_w
    cosines = cosine_table()
    blocks = moment.reshape(row_total_count, 64, col_count, 64).transpose(0, 2, 1, 3)
    coefficients = jnp.einsum("fa,ijab,gb->ijfg", cosines, blocks, cosines, precision=highest)
    freq_ids = jnp.arange(64, dtype=jnp.int32)
    own_rows = sent_spectral_lines[0]
    chosen = (own_rows[..., None] == freq_ids).astype(jnp.float32)
    shipped = jnp.einsum("ijkf,ijfg->ijkg", chosen, coefficients, precision=highest).astype(
        jnp.bfloat16
    )
    spectrum = jnp.einsum("ijkf,ijkg->ijfg", chosen, shipped.astype(jnp.float32), precision=highest)
    returned = jnp.einsum("fa,ijfg,gb->ijab", cosines, spectrum, cosines, precision=highest)
    new_moment = moment - returned.transpose(0, 2, 1, 3).reshape(moment.shape)
    worker_burdens = participant_mask.astype(jnp.float32) * token_tallies.astype(jnp.float32)
    worker_fractions = worker_burdens * (
        jnp.sum(participant_mask.astype(jnp.float32)) / jnp.sum(worker_burdens)
    )
    myself = lax.axis_index("replica")
    combined = lax.psum(worker_fractions[myself] * spectrum, "replica")
    update = jnp.einsum("fa,ijfg,gb->ijab", cosines, combined, cosines, precision=highest)
    update = update.transpose(0, 2, 1, 3).reshape(moment.shape)
    return (input_grad, new_moment[None], update)


def solution(mesh):
    n_t, n_r = mesh.shape["tensor"], mesh.shape["replica"]

    def device(*args):
        act, exp, lines = args[0], args[3], args[5]
        fits = (
            act.shape[1] % G == 0
            and act.shape[0] % 128 == 0
            and exp.shape[0] == B
            and lines.shape[3] == 8
            and n_r == 8
            and n_t >= 2
            and n_t & (n_t - 1) == 0
        )
        if not fits:
            return per_device_plain(*args)
        return per_device(n_t, n_r, *args)

    return jax.shard_map(
        device,
        mesh=mesh,
        in_specs=(
            P("replica", "tensor"),
            P("replica", "tensor"),
            P("replica", "tensor"),
            P("tensor", None),
            P("replica", "tensor", None),
            P("replica", "tensor", None, None),
            P(),
            P(),
        ),
        out_specs=(P("replica", "tensor"), P("replica", "tensor", None), P("tensor", None)),
        check_vma=False,
    )
```

```python
import functools

import jax
import jax.numpy as jnp
import numpy as np
from jax import lax
from jax.experimental import pallas as pl
from jax.experimental.pallas import tpu as pltpu
from jax.sharding import PartitionSpec as P

momentum_decay = 0.9
B = 64
G = 256
F32 = jnp.float32
BF16 = jnp.bfloat16
VMEM_LIMIT = 24 * 1024 * 1024

VM = pl.BlockSpec(memory_space=pltpu.VMEM)
SM = pl.BlockSpec(memory_space=pltpu.SMEM)
ANY = pl.BlockSpec(memory_space=pl.ANY)


def cosine_table():
    freqs = jnp.arange(64, dtype=jnp.float32)[:, None]
    places = jnp.arange(64, dtype=jnp.float32)[None, :]
    cosines = jnp.cos(jnp.pi * (places + 0.5) * freqs / 64.0) * jnp.sqrt(2.0 / 64.0)
    return cosines.at[0].multiply(jnp.sqrt(0.5))


def cosine_np():
    f = np.arange(B)[:, None]
    a = np.arange(B)[None, :]
    c = np.cos(np.pi * (a + 0.5) * f / B) * np.sqrt(2.0 / B)
    c[0] *= np.sqrt(0.5)
    return c


def halves(c):
    hi = np.asarray(c, dtype=np.float32).astype(jnp.bfloat16)
    lo = (np.asarray(c, np.float64) - hi.astype(np.float64)).astype(np.float32).astype(jnp.bfloat16)
    return hi, lo


def constants():
    hi, lo = halves(cosine_np())
    eye = np.eye(G // B)
    kron = lambda x: np.kron(eye, np.asarray(x, np.float32)).astype(jnp.bfloat16)
    small = np.zeros((2 * B, 4 * B), jnp.bfloat16)
    for i, x in enumerate((hi, lo)):
        rows = slice(i * B, (i + 1) * B)
        small[rows, :B], small[rows, B : 2 * B], small[rows, 2 * B : 3 * B] = x, x, x.T
    return jnp.asarray(np.concatenate([kron(x) for x in (hi.T, lo.T, hi, lo)], axis=0)), jnp.asarray(small)


def fwd(tab, i):
    return tab[i * G : (i + 1) * G, :]


def inv(tab, i):
    return tab[(2 + i) * G : (3 + i) * G, :]


def dot(a, b):
    return jnp.dot(a, b, preferred_element_type=F32)


def split(x):
    hi = x.astype(BF16)
    return hi, (x - hi.astype(F32)).astype(BF16)


def near(shape, dtype=BF16):
    return pltpu.VMEM(shape, dtype)


def far(x):
    return pltpu.with_memory_space_constraint(x, pltpu.HBM)


def call(body, out_shape, ins, in_specs, out_specs, scratch=(), flops=0, nbytes=0, name=None, alias={}):
    return pl.pallas_call(
        body,
        out_shape=out_shape,
        in_specs=in_specs,
        out_specs=out_specs,
        scratch_shapes=scratch,
        input_output_aliases=alias,
        compiler_params=pltpu.CompilerParams(vmem_limit_bytes=VMEM_LIMIT),
        cost_estimate=pl.CostEstimate(flops=flops, bytes_accessed=nbytes, transcendentals=0),
        name=name,
    )(*ins)


def first_body(n_t, cp, cols, nr, switch, slope, exp_ref, act, lines, small, *refs):
    outs, (act_out, lines_out, small_out) = refs[:n_t], refs[n_t : n_t + 3]
    switch_v, slope_v, exp_v, sems = refs[n_t + 3 :]
    rep, ten = lax.axis_index("replica"), lax.axis_index("tensor")
    r0 = pl.multiple_of((rep // cp) * nr, nr)
    copies = [
        pltpu.make_async_copy(src, dst, sems.at[i])
        for i, (src, dst) in enumerate(
            [
                (switch, switch_v),
                (slope, slope_v),
                (exp_ref.at[pl.ds(r0, nr), :], exp_v),
                (act, act_out),
                (lines, lines_out),
                (small, small_out),
            ]
        )
    ]
    for copy in copies:
        copy.start()
    copies[0].wait()
    copies[1].wait()
    v = switch_v[...].astype(F32)
    up = (slope_v[...].astype(F32) * (v * jax.nn.sigmoid(v))).astype(BF16)
    for k in range(n_t):
        outs[k][:B, :] = up
    copies[2].wait()
    nc = cols // cp
    for k in range(1, n_t):
        c0 = (ten ^ k) * cols + lax.rem(rep, cp) * nc
        for j in range(nc // 128):
            at = pl.multiple_of(c0 + j * 128, 128)
            outs[k][B + j * nr : B + (j + 1) * nr, :] = exp_v[:, pl.ds(at, 128)]
    for copy in copies[3:]:
        copy.wait()


def grads_body(n, act, after, *refs):
    ups, outs = refs[:n], refs[n:]
    up = jnp.concatenate([u[:B, :] for u in ups], axis=0)
    for c in range(0, act.shape[1], G):
        g = dot(up, act[:, c : c + G])
        for k in range(n):
            outs[k][:, c : c + G] = g[k * B : (k + 1) * B].astype(outs[k].dtype)


def bundle_body(n_t, keep, after, lines, *refs):
    parts, out = refs[: n_t - 1], refs[n_t - 1]
    n = parts[0].shape[0] - B
    for k in range(n_t - 1):
        out[k * n : (k + 1) * n, :] = parts[k][B:, :]
    blocks = lines.shape[1]
    rows = jnp.concatenate([lines[...].astype(F32), jnp.zeros((keep, 128 - blocks), F32)], axis=1)
    out[(n_t - 1) * n :, :] = jnp.concatenate([rows, jnp.zeros((16 - keep, 128), F32)], axis=0).astype(BF16)


def join_body(n, *refs):
    for i, ref in enumerate(refs[1 : n + 1]):
        refs[-1][i] = ref[...]


def own_rows_body(keep, lines, small, a_ref):
    blocks, nb = lines.shape[1], G // B
    rows = jnp.concatenate([lines[...].astype(F32), jnp.zeros((keep, 128 - blocks), F32)], axis=1)
    lane = lax.broadcasted_iota(jnp.int32, (nb * keep, 2 * B), 1).astype(F32)
    for g in range(blocks // nb):
        num = jnp.concatenate(
            [jnp.broadcast_to(rows[:, g * nb + j : g * nb + j + 1], (keep, 2 * B)) for j in range(nb)], axis=0
        )
        hot = jnp.concatenate(
            [jnp.where(lane == num, 1.0, 0.0), jnp.where(lane - B == num, 1.0, 0.0)], axis=0
        ).astype(BF16)
        a_ref[g * B : (g + 1) * B, :] = dot(hot, small[:, : 2 * B]).astype(BF16)


def own_columns_body(keep, lines, small, after, p_ref):
    blocks, nb = lines.shape[1], G // B
    rows = jnp.concatenate([lines[...].astype(F32), jnp.zeros((keep, 128 - blocks), F32)], axis=1)
    rows = jnp.concatenate([rows] * (2 * B // keep), axis=0).T
    freq = lax.broadcasted_iota(jnp.int32, (B, 2 * B), 0).astype(F32)
    block = (lax.broadcasted_iota(jnp.int32, (1, 2 * B), 1) // keep) % nb
    term = lax.broadcasted_iota(jnp.int32, (B, 2 * B), 1) // (B // 2)
    for g in range(blocks // nb):
        num = rows[g * nb : g * nb + 1]
        for j in range(1, nb):
            num = jnp.where(block == j, rows[g * nb + j : g * nb + j + 1], num)
        hot = jnp.where(freq == num, 1.0, 0.0).astype(BF16)
        y = dot(small[:, 2 * B : 3 * B], hot)
        p = jnp.where(term == 3, 0.0, jnp.where(term == 1, y[B:], y[:B]))
        p_ref[:, g * 2 * B : (g + 1) * 2 * B] = p.astype(BF16)


def kept_body(ks, n_t, keep, vel, a_ref, tab, after, *refs):
    keep_rows(ks, n_t, keep, vel, a_ref, tab, refs[: len(ks)], *refs[-2:])


def keep_rows(ks, n_t, keep, vel, a_ref, tab, grads, send_ref, own_ref):
    cols = grads[0].shape[1]
    ng = cols // G
    lane_block = lax.broadcasted_iota(jnp.int32, (keep, G), 1) // B
    sel = []
    for n, k in enumerate(ks):
        c0 = (lax.axis_index("tensor") ^ k) * cols
        for i in range(ng):
            at = pl.multiple_of(c0 + i * G, G)
            moment = momentum_decay * vel[:, pl.ds(at, G)] + grads[n][:, i * G : (i + 1) * G].astype(F32)
            hi, lo = split(moment)
            y = dot(a_ref[pl.ds(pl.multiple_of(at // (G // B), B), B), :], jnp.concatenate([hi, lo], axis=0))
            y = y[: B // 2] + y[B // 2 :]
            got = y[:keep]
            for j in range(1, G // B):
                got = jnp.where(lane_block == j, y[j * keep : (j + 1) * keep], got)
            sel.append(got)
    hi, lo = split(jnp.concatenate(sel, axis=0))
    n = len(ks) * ng * keep
    y = dot(jnp.concatenate([hi, lo], axis=0), fwd(tab, 0))
    kept = (y[:n] + y[n:] + dot(hi, fwd(tab, 1))).astype(BF16)
    q = dot(kept, inv(tab, 0)) + dot(kept, inv(tab, 1))
    for n, k in enumerate(ks):
        c0 = pl.multiple_of((lax.axis_index("tensor") ^ k) * cols, G)
        part = jnp.concatenate([q[(n * ng + i) * keep : (n * ng + i + 1) * keep] for i in range(ng)], axis=1)
        own_ref[:, pl.ds(c0, cols)] = part
        send_ref[:, pl.ds(c0, cols)] = part.astype(BF16)


def return_body(n_t, keep, vel, p_ref, q, mask, tally, *refs):
    grads, (new_ref, w_ref, held, sems, mask_s, tally_s, small_sems) = refs[:n_t], refs[n_t:]
    fetches = [
        pltpu.make_async_copy(src, dst, small_sems.at[i])
        for i, (src, dst) in enumerate([(mask, mask_s), (tally, tally_s)])
    ]
    for copy in fetches:
        copy.start()
    cols = grads[0].shape[1]
    ng = cols // G
    lane_block = lax.broadcasted_iota(jnp.int32, (keep, G), 1) // B
    copies = []
    for k in range(n_t):
        c0 = pl.multiple_of((lax.axis_index("tensor") ^ k) * cols, G)
        for i in range(ng):
            at = pl.multiple_of(c0 + i * G, G)
            own = q[:, pl.ds(at, G)]
            spread = jnp.concatenate(
                [jnp.where(lane_block == j, own, 0.0) for j in range(G // B)], axis=0
            )
            hi, lo = split(spread)
            w = jnp.concatenate([hi, hi, lo, jnp.zeros_like(lo)], axis=0)
            back = dot(p_ref[:, pl.ds(pl.multiple_of(at // 2, 2 * B), 2 * B)], w)
            moment = momentum_decay * vel[:, pl.ds(at, G)] + grads[k][:, i * G : (i + 1) * G].astype(F32)
            held[:, pl.ds(at, G)] = moment - back
        cut = pl.ds(c0, cols)
        copies.append(pltpu.make_async_copy(held.at[:, cut], new_ref.at[:, cut], sems.at[k]))
        copies[-1].start()
    for copy in fetches:
        copy.wait()
    n_r = mask_s.shape[0]
    total, alive = jnp.float32(0), jnp.float32(0)
    for r in range(n_r):
        m = mask_s[r].astype(F32)
        total = total + m * tally_s[r].astype(F32)
        alive = alive + m
    half = n_r // 2
    place = (lax.broadcasted_iota(jnp.int32, (8, 2 * B), 1) // keep) % half
    scale = jnp.full((8, 2 * B), alive) / jnp.full((8, 2 * B), total)
    for h in range(2):
        w = jnp.zeros((8, 2 * B), F32)
        for i in range(half):
            r = lax.axis_index("replica") ^ (2 * i + h)
            w = jnp.where(place == i, mask_s[r].astype(F32) * tally_s[r].astype(F32), w)
        w_ref[h] = w * scale
    for copy in copies:
        copy.wait()


def places_body(keep, w_ref, small, bundles, *p_refs):
    n_r, last = bundles.shape[0], bundles.shape[1] - 16
    half, nb = n_r // 2, G // B
    rep = lax.axis_index("replica")
    freq = lax.broadcasted_iota(jnp.int32, (B, 2 * B), 0).astype(F32)
    lane = lax.broadcasted_iota(jnp.int32, (1, 2 * B), 1)
    block = lane // (half * keep)
    for h in range(2):
        hi_ref, lo_ref = p_refs[2 * h : 2 * h + 2]
        w = w_ref[h, :1, :]
        rows = [bundles[rep ^ (2 * i + h), last:, :].astype(F32)[:keep] for i in range(half)]
        rows = jnp.concatenate(rows * nb, axis=0).T
        for g in range(hi_ref.shape[1] // (2 * B)):
            num = rows[g * nb : g * nb + 1]
            for j in range(1, nb):
                num = jnp.where(block == j, rows[g * nb + j : g * nb + j + 1], num)
            hot = jnp.where(freq == num, 1.0, 0.0).astype(BF16)
            y = dot(small[:, 2 * B : 3 * B], hot)
            hi, lo = split((y[:B] + y[B:]) * w)
            hi_ref[:, g * 2 * B : (g + 1) * 2 * B] = hi
            lo_ref[:, g * 2 * B : (g + 1) * 2 * B] = lo


def spread_rows(p_hi, p_lo, own, ships, g):
    half, keep = ships.shape[0] + 1, ships.shape[1]
    cut = slice(g * G, (g + 1) * G)
    lane_block = lax.broadcasted_iota(jnp.int32, (half * keep, G), 1) // B
    s = [own[:, cut].astype(F32)] + [ships[i, :, cut].astype(F32) for i in range(half - 1)]
    s = jnp.concatenate(s, axis=0)
    w = jnp.concatenate(
        [jnp.where(lane_block == j, s, 0.0).astype(BF16) for j in range(G // B)], axis=0
    )
    cut = slice(g * 2 * B, (g + 1) * 2 * B)
    y = dot(jnp.concatenate([p_hi[:, cut], p_lo[:, cut]], axis=0), w)
    return y[:B] + y[B:]


def half_update_body(p_hi, p_lo, own, others, out):
    for g in range(out.shape[0] // B):
        out[g * B : (g + 1) * B, :] = spread_rows(p_hi, p_lo, own, others, g)


def update_body(chunk, half_sum, p_hi, p_lo, own, others, out, held, sems):
    ng = half_sum.shape[0] // B
    copies = []
    for c in range(0, ng, chunk):
        for g in range(c, c + chunk):
            held[:, g * G : (g + 1) * G] = half_sum[g * B : (g + 1) * B, :] + spread_rows(p_hi, p_lo, own, others, g)
        cut = pl.ds(c * G, chunk * G)
        copies.append(pltpu.make_async_copy(held.at[:, cut], out.at[:, cut], sems.at[c // chunk]))
        copies[-1].start()
    for copy in copies:
        copy.wait()


def input_grad_body(n_t, n_r, cp, exp_ref, bundles, *refs):
    ups, (out, held) = refs[:n_t], refs[n_t:]
    cols = out.shape[1]
    held[:B, :] = exp_ref[:, pl.ds(pl.multiple_of(lax.axis_index("tensor") * cols, 128), cols)]
    nc = cols // cp
    nr = B // (n_r // cp)
    tiles = nc // 128
    for r in range(n_r):
        r0, c0 = (r // cp) * nr, (r % cp) * nc
        for k in range(1, n_t):
            for j in range(tiles):
                at = ((k - 1) * tiles + j) * nr
                held[k * B + r0 : k * B + r0 + nr, c0 + j * 128 : c0 + (j + 1) * 128] = bundles[r, at : at + nr, :]
    up = jnp.concatenate([u[:B, :] for u in ups], axis=0).T
    for c in range(0, cols, G):
        out[:, c : c + G] = dot(up, held[:, c : c + G]).astype(BF16)


def per_device(n_t, n_r, act, switch, slope, exp, vel, lines, mask, tally):
    cols = act.shape[1]
    width = exp.shape[1]
    tok = act.shape[0]
    keep = lines.shape[3]
    blocks = width // B
    groups = width // G
    cp = 2
    rp = n_r // cp
    half = n_r // 2
    tab, small = constants()
    def trade(x, k):
        return lax.ppermute(x, "tensor", [(i, i ^ k) for i in range(n_t)])

    order = [*range(2, n_t), 1]

    def swap(x, m):
        return lax.ppermute(x, "replica", [(i, i ^ m) for i in range(n_r)])

    own = lines[0, 0].T
    tiles = cols // cp // 128
    nr = B // rp
    *parts, act, own, small = call(
        functools.partial(first_body, n_t, cp, cols, nr),
        [near((B, tok))]
        + [near((B + tiles * nr, 128))] * (n_t - 1)
        + [near(act.shape), near(own.shape, jnp.int32), near(small.shape)],
        (far(switch.T), far(slope.T), far(exp), far(act), far(own), far(small)),
        [ANY] * 6,
        [VM] * (n_t + 3),
        scratch=[
            pltpu.VMEM((B, tok), BF16),
            pltpu.VMEM((B, tok), BF16),
            pltpu.VMEM((nr, width), BF16),
            pltpu.SemaphoreType.DMA((6,)),
        ],
        nbytes=act.size * 4 + nr * width * 2,
        name="up_grads",
    )
    got = {k: trade(parts[k], k) for k in order}
    parts = [parts[0]] + [got[k] for k in range(1, n_t)]

    a_own = call(
        functools.partial(own_rows_body, keep),
        near((groups * B, 2 * B)),
        (own, small),
        [VM, VM],
        VM,
        name="own_rows",
    )

    def grads_of(ks, after):
        return call(
            functools.partial(grads_body, len(ks)),
            [near((B, cols), BF16 if k else F32) for k in ks],
            (act, after, *[parts[k] for k in ks]),
            [VM, ANY] + [VM] * len(ks),
            [VM] * len(ks),
            name="weight_grads",
        )

    grads = {}
    for k in order[:-1]:
        (grads[k],) = grads_of([k], act)
    made, grads[0] = grads_of([order[-1], 0], a_own)
    grads[order[-1]] = made
    grads.update({k: trade(grads[k], k) for k in order})

    bundle = call(
        functools.partial(bundle_body, n_t, keep),
        near(((n_t - 1) * tiles * nr + 16, 128)),
        (made, own, *parts[1:]),
        [ANY] + [VM] * n_t,
        VM,
        name="bundle",
    )
    bundles = lax.all_gather(bundle, "replica", axis=0)

    rows = []
    for ks in ([k for k in range(n_t) if k != n_t - 1], [n_t - 1]):
        n = len(ks)
        rows = call(
            functools.partial(kept_body, ks, n_t, keep),
            [near((keep, width)), near((keep, width), F32)],
            (vel[0], a_own, tab, bundles, *[grads[k] for k in ks], *rows),
            [VM] * 3 + [ANY] + [VM] * (n + len(rows)),
            [VM] * 2,
            flops=6 * B * B * cols * n,
            nbytes=B * cols * 6 * n,
            name="kept_rows",
            alias={4 + n: 0, 5 + n: 1} if rows else {},
        )
    ship, q_own = rows

    p_own = call(
        functools.partial(own_columns_body, keep),
        near((B, groups * 2 * B)),
        (own, small, q_own),
        [VM, VM, ANY],
        VM,
        name="own_columns",
    )
    new, shares = call(
        functools.partial(return_body, n_t, keep),
        [jax.ShapeDtypeStruct((B, width), F32), near((2, 8, 2 * B), F32)],
        (vel[0], p_own, q_own, far(mask), far(tally), *[grads[k] for k in range(n_t)]),
        [VM] * 3 + [ANY] * 2 + [VM] * n_t,
        [ANY, VM],
        scratch=[
            pltpu.VMEM((B, width), F32),
            pltpu.SemaphoreType.DMA((n_t,)),
            pltpu.SMEM((n_r,), jnp.int32),
            pltpu.SMEM((n_r,), jnp.int32),
            pltpu.SemaphoreType.DMA((2,)),
        ],
        flops=6 * B * B * width,
        nbytes=B * width * 10,
        name="new_momentums",
    )
    places = call(
        functools.partial(places_body, keep),
        [near((B, blocks * half * keep))] * 4,
        (shares, small, bundles),
        [VM] * 3,
        [VM] * 4,
        name="places",
    )
    input_grad = call(
        functools.partial(input_grad_body, n_t, n_r, cp),
        jax.ShapeDtypeStruct((tok, cols), BF16),
        (exp, bundles, *parts),
        [VM] * (2 + n_t),
        VM,
        scratch=[pltpu.VMEM((n_t * B, cols), BF16)],
        flops=2 * tok * n_t * B * cols,
        nbytes=(n_t * B * cols + tok * cols) * 2,
        name="input_grads",
    )

    ships = [ship] + [swap(ship, 2 * i) for i in range(1, half)]
    other_own = swap(ship, 1)
    others = call(
        functools.partial(join_body, half - 1),
        near((half - 1, keep, width)),
        (other_own, *ships[1:], far(new), far(input_grad), places[0]),
        [ANY] + [VM] * (half - 1) + [ANY] * 3,
        VM,
        name="join_kept",
    )
    other = swap(others, 1)
    half_sum = call(
        half_update_body,
        near((groups * B, G), F32),
        (*places[:2], ship, others),
        [VM] * 4,
        VM,
        name="half_updates",
    )
    chunk = 2 if groups % 2 == 0 else 1
    update = call(
        functools.partial(update_body, chunk),
        jax.ShapeDtypeStruct((B, width), F32),
        (half_sum, *places[2:], other_own, other),
        [VM] * 5,
        ANY,
        scratch=[
            pltpu.VMEM((B, width), F32),
            pltpu.SemaphoreType.DMA((groups // chunk,)),
        ],
        flops=8 * B * G * width,
        nbytes=B * width * 8,
        name="updates",
    )
    return input_grad, new[None], update


def per_device_plain(
    projection_inputs,
    switch_logits_raw,
    inner_neuron_slope,
    expansion_matrix,
    velocity_buffer,
    sent_spectral_lines,
    participant_mask,
    token_tallies,
):
    highest = lax.Precision.HIGHEST
    up_grad = (
        inner_neuron_slope.astype(jnp.float32) * jax.nn.silu(switch_logits_raw.astype(jnp.float32))
    ).astype(jnp.bfloat16)
    partial_terms = jnp.dot(up_grad, expansion_matrix, preferred_element_type=jnp.float32)
    input_grad = lax.psum_scatter(partial_terms, "tensor", scatter_dimension=1, tiled=True).astype(
        jnp.bfloat16
    )
    grad_w = lax.dot_general(
        up_grad,
        lax.all_gather(projection_inputs, "tensor", axis=1, tiled=True),
        (((0,), (0,)), ((), ())),
        preferred_element_type=jnp.float32,
    )
    row_total_count = expansion_matrix.shape[0] // 64
    col_count = expansion_matrix.shape[1] // 64
    moment = momentum_decay * velocity_buffer[0] + grad_w
    cosines = cosine_table()
    blocks = moment.reshape(row_total_count, 64, col_count, 64).transpose(0, 2, 1, 3)
    coefficients = jnp.einsum("fa,ijab,gb->ijfg", cosines, blocks, cosines, precision=highest)
    freq_ids = jnp.arange(64, dtype=jnp.int32)
    own_rows = sent_spectral_lines[0]
    chosen = (own_rows[..., None] == freq_ids).astype(jnp.float32)
    shipped = jnp.einsum("ijkf,ijfg->ijkg", chosen, coefficients, precision=highest).astype(
        jnp.bfloat16
    )
    spectrum = jnp.einsum("ijkf,ijkg->ijfg", chosen, shipped.astype(jnp.float32), precision=highest)
    returned = jnp.einsum("fa,ijfg,gb->ijab", cosines, spectrum, cosines, precision=highest)
    new_moment = moment - returned.transpose(0, 2, 1, 3).reshape(moment.shape)
    worker_burdens = participant_mask.astype(jnp.float32) * token_tallies.astype(jnp.float32)
    worker_fractions = worker_burdens * (
        jnp.sum(participant_mask.astype(jnp.float32)) / jnp.sum(worker_burdens)
    )
    myself = lax.axis_index("replica")
    combined = lax.psum(worker_fractions[myself] * spectrum, "replica")
    update = jnp.einsum("fa,ijfg,gb->ijab", cosines, combined, cosines, precision=highest)
    update = update.transpose(0, 2, 1, 3).reshape(moment.shape)
    return (input_grad, new_moment[None], update)


def solution(mesh):
    n_t, n_r = mesh.shape["tensor"], mesh.shape["replica"]

    def device(*args):
        act, exp, lines = args[0], args[3], args[5]
        fits = (
            act.shape[1] % G == 0
            and act.shape[0] % 128 == 0
            and exp.shape[0] == B
            and lines.shape[3] == 8
            and n_r == 8
            and n_t >= 2
            and n_t & (n_t - 1) == 0
        )
        if not fits:
            return per_device_plain(*args)
        return per_device(n_t, n_r, *args)

    return jax.shard_map(
        device,
        mesh=mesh,
        in_specs=(
            P("replica", "tensor"),
            P("replica", "tensor"),
            P("replica", "tensor"),
            P("tensor", None),
            P("replica", "tensor", None),
            P("replica", "tensor", None, None),
            P(),
            P(),
        ),
        out_specs=(P("replica", "tensor"), P("replica", "tensor", None), P("tensor", None)),
        check_vma=False,
    )
```

```python
import functools

import jax
import jax.numpy as jnp
import numpy as np
from jax import lax
from jax.experimental import pallas as pl
from jax.experimental.pallas import tpu as pltpu
from jax.sharding import PartitionSpec as P

momentum_decay = 0.9
B = 64
G = 256
F32 = jnp.float32
BF16 = jnp.bfloat16
VMEM_LIMIT = 24 * 1024 * 1024

VM = pl.BlockSpec(memory_space=pltpu.VMEM)
SM = pl.BlockSpec(memory_space=pltpu.SMEM)
ANY = pl.BlockSpec(memory_space=pl.ANY)


def cosine_table():
    freqs = jnp.arange(64, dtype=jnp.float32)[:, None]
    places = jnp.arange(64, dtype=jnp.float32)[None, :]
    cosines = jnp.cos(jnp.pi * (places + 0.5) * freqs / 64.0) * jnp.sqrt(2.0 / 64.0)
    return cosines.at[0].multiply(jnp.sqrt(0.5))


def cosine_np():
    f = np.arange(B)[:, None]
    a = np.arange(B)[None, :]
    c = np.cos(np.pi * (a + 0.5) * f / B) * np.sqrt(2.0 / B)
    c[0] *= np.sqrt(0.5)
    return c


def halves(c):
    hi = np.asarray(c, dtype=np.float32).astype(jnp.bfloat16)
    lo = (np.asarray(c, np.float64) - hi.astype(np.float64)).astype(np.float32).astype(jnp.bfloat16)
    return hi, lo


def constants():
    hi, lo = halves(cosine_np())
    eye = np.eye(G // B)
    kron = lambda x: np.kron(eye, np.asarray(x, np.float32)).astype(jnp.bfloat16)
    small = np.zeros((2 * B, 4 * B), jnp.bfloat16)
    for i, x in enumerate((hi, lo)):
        rows = slice(i * B, (i + 1) * B)
        small[rows, :B], small[rows, B : 2 * B], small[rows, 2 * B : 3 * B] = x, x, x.T
    return jnp.asarray(np.concatenate([kron(x) for x in (hi.T, lo.T, hi, lo)], axis=0)), jnp.asarray(small)


def fwd(tab, i):
    return tab[i * G : (i + 1) * G, :]


def inv(tab, i):
    return tab[(2 + i) * G : (3 + i) * G, :]


def dot(a, b):
    return jnp.dot(a, b, preferred_element_type=F32)


def split(x):
    hi = x.astype(BF16)
    return hi, (x - hi.astype(F32)).astype(BF16)


def near(shape, dtype=BF16):
    return pltpu.VMEM(shape, dtype)


def far(x):
    return pltpu.with_memory_space_constraint(x, pltpu.HBM)


def order_of(h):
    r = lax.axis_index("replica")
    if h == 0:
        return [r, r ^ 2, r ^ 4, r ^ 1]
    return [r ^ 3, r ^ 5, (r ^ 6) | 1, (r ^ 6) & ~1]


def call(body, out_shape, ins, in_specs, out_specs, scratch=(), flops=0, nbytes=0, name=None, alias={}):
    return pl.pallas_call(
        body,
        out_shape=out_shape,
        in_specs=in_specs,
        out_specs=out_specs,
        scratch_shapes=scratch,
        input_output_aliases=alias,
        compiler_params=pltpu.CompilerParams(vmem_limit_bytes=VMEM_LIMIT),
        cost_estimate=pl.CostEstimate(flops=flops, bytes_accessed=nbytes, transcendentals=0),
        name=name,
    )(*ins)


def first_body(n_t, cp, cols, nr, switch, slope, exp_ref, act, lines, small, *refs):
    outs, (act_out, lines_out, small_out) = refs[:n_t], refs[n_t : n_t + 3]
    switch_v, slope_v, exp_v, sems = refs[n_t + 3 :]
    rep, ten = lax.axis_index("replica"), lax.axis_index("tensor")
    r0 = pl.multiple_of((rep // cp) * nr, nr)
    copies = [
        pltpu.make_async_copy(src, dst, sems.at[i])
        for i, (src, dst) in enumerate(
            [
                (switch, switch_v),
                (slope, slope_v),
                (exp_ref.at[pl.ds(r0, nr), :], exp_v),
                (act, act_out),
                (lines, lines_out),
                (small, small_out),
            ]
        )
    ]
    for copy in copies:
        copy.start()
    copies[0].wait()
    copies[1].wait()
    v = switch_v[...].astype(F32)
    up = (slope_v[...].astype(F32) * (v * jax.nn.sigmoid(v))).astype(BF16)
    for k in range(n_t):
        outs[k][:B, :] = up
    copies[2].wait()
    nc = cols // cp
    for k in range(1, n_t):
        c0 = (ten ^ k) * cols + lax.rem(rep, cp) * nc
        for j in range(nc // 128):
            at = pl.multiple_of(c0 + j * 128, 128)
            outs[k][B + j * nr : B + (j + 1) * nr, :] = exp_v[:, pl.ds(at, 128)]
    for copy in copies[3:]:
        copy.wait()


def grads_body(n, act, after, *refs):
    ups, outs = refs[:n], refs[n:]
    up = jnp.concatenate([u[:B, :] for u in ups], axis=0)
    for c in range(0, act.shape[1], G):
        g = dot(up, act[:, c : c + G])
        for k in range(n):
            outs[k][:, c : c + G] = g[k * B : (k + 1) * B].astype(outs[k].dtype)


def bundle_body(n_t, keep, after, lines, *refs):
    parts, out = refs[: n_t - 1], refs[n_t - 1]
    n = parts[0].shape[0] - B
    for k in range(n_t - 1):
        out[k * n : (k + 1) * n, :] = parts[k][B:, :]
    blocks = lines.shape[1]
    rows = jnp.concatenate([lines[...].astype(F32), jnp.zeros((keep, 128 - blocks), F32)], axis=1)
    out[(n_t - 1) * n :, :] = jnp.concatenate([rows, jnp.zeros((16 - keep, 128), F32)], axis=0).astype(BF16)


def join_body(*refs):
    refs[-1][0] = refs[0][...]
    refs[-1][1] = refs[1][...]


def own_rows_body(keep, lines, small, a_ref):
    blocks, nb = lines.shape[1], G // B
    rows = jnp.concatenate([lines[...].astype(F32), jnp.zeros((keep, 128 - blocks), F32)], axis=1)
    lane = lax.broadcasted_iota(jnp.int32, (nb * keep, 2 * B), 1).astype(F32)
    for g in range(blocks // nb):
        num = jnp.concatenate(
            [jnp.broadcast_to(rows[:, g * nb + j : g * nb + j + 1], (keep, 2 * B)) for j in range(nb)], axis=0
        )
        hot = jnp.concatenate(
            [jnp.where(lane == num, 1.0, 0.0), jnp.where(lane - B == num, 1.0, 0.0)], axis=0
        ).astype(BF16)
        a_ref[g * B : (g + 1) * B, :] = dot(hot, small[:, : 2 * B]).astype(BF16)


def own_columns_body(keep, lines, small, after, p_ref):
    blocks, nb = lines.shape[1], G // B
    rows = jnp.concatenate([lines[...].astype(F32), jnp.zeros((keep, 128 - blocks), F32)], axis=1)
    rows = jnp.concatenate([rows] * (2 * B // keep), axis=0).T
    freq = lax.broadcasted_iota(jnp.int32, (B, 2 * B), 0).astype(F32)
    block = (lax.broadcasted_iota(jnp.int32, (1, 2 * B), 1) // keep) % nb
    term = lax.broadcasted_iota(jnp.int32, (B, 2 * B), 1) // (B // 2)
    for g in range(blocks // nb):
        num = rows[g * nb : g * nb + 1]
        for j in range(1, nb):
            num = jnp.where(block == j, rows[g * nb + j : g * nb + j + 1], num)
        hot = jnp.where(freq == num, 1.0, 0.0).astype(BF16)
        y = dot(small[:, 2 * B : 3 * B], hot)
        p = jnp.where(term == 3, 0.0, jnp.where(term == 1, y[B:], y[:B]))
        p_ref[:, g * 2 * B : (g + 1) * 2 * B] = p.astype(BF16)


def kept_body(ks, n_t, keep, vel, a_ref, tab, after, *refs):
    keep_rows(ks, n_t, keep, vel, a_ref, tab, refs[: len(ks)], *refs[-2:])


def keep_rows(ks, n_t, keep, vel, a_ref, tab, grads, send_ref, own_ref):
    cols = grads[0].shape[1]
    ng = cols // G
    lane_block = lax.broadcasted_iota(jnp.int32, (keep, G), 1) // B
    sel = []
    for n, k in enumerate(ks):
        c0 = (lax.axis_index("tensor") ^ k) * cols
        for i in range(ng):
            at = pl.multiple_of(c0 + i * G, G)
            moment = momentum_decay * vel[:, pl.ds(at, G)] + grads[n][:, i * G : (i + 1) * G].astype(F32)
            hi, lo = split(moment)
            y = dot(a_ref[pl.ds(pl.multiple_of(at // (G // B), B), B), :], jnp.concatenate([hi, lo], axis=0))
            y = y[: B // 2] + y[B // 2 :]
            got = y[:keep]
            for j in range(1, G // B):
                got = jnp.where(lane_block == j, y[j * keep : (j + 1) * keep], got)
            sel.append(got)
    hi, lo = split(jnp.concatenate(sel, axis=0))
    n = len(ks) * ng * keep
    y = dot(jnp.concatenate([hi, lo], axis=0), fwd(tab, 0))
    kept = (y[:n] + y[n:] + dot(hi, fwd(tab, 1))).astype(BF16)
    q = dot(kept, inv(tab, 0)) + dot(kept, inv(tab, 1))
    for n, k in enumerate(ks):
        c0 = pl.multiple_of((lax.axis_index("tensor") ^ k) * cols, G)
        part = jnp.concatenate([q[(n * ng + i) * keep : (n * ng + i + 1) * keep] for i in range(ng)], axis=1)
        own_ref[:, pl.ds(c0, cols)] = part
        send_ref[:, pl.ds(c0, cols)] = part.astype(BF16)


def return_body(n_t, keep, vel, p_ref, q, mask, tally, *refs):
    grads, (new_ref, w_ref, held, sems, mask_s, tally_s, small_sems) = refs[:n_t], refs[n_t:]
    fetches = [
        pltpu.make_async_copy(src, dst, small_sems.at[i])
        for i, (src, dst) in enumerate([(mask, mask_s), (tally, tally_s)])
    ]
    for copy in fetches:
        copy.start()
    cols = grads[0].shape[1]
    ng = cols // G
    lane_block = lax.broadcasted_iota(jnp.int32, (keep, G), 1) // B
    copies = []
    for k in range(n_t):
        c0 = pl.multiple_of((lax.axis_index("tensor") ^ k) * cols, G)
        for i in range(ng):
            at = pl.multiple_of(c0 + i * G, G)
            own = q[:, pl.ds(at, G)]
            spread = jnp.concatenate(
                [jnp.where(lane_block == j, own, 0.0) for j in range(G // B)], axis=0
            )
            hi, lo = split(spread)
            w = jnp.concatenate([hi, hi, lo, jnp.zeros_like(lo)], axis=0)
            back = dot(p_ref[:, pl.ds(pl.multiple_of(at // 2, 2 * B), 2 * B)], w)
            moment = momentum_decay * vel[:, pl.ds(at, G)] + grads[k][:, i * G : (i + 1) * G].astype(F32)
            held[:, pl.ds(at, G)] = moment - back
        cut = pl.ds(c0, cols)
        copies.append(pltpu.make_async_copy(held.at[:, cut], new_ref.at[:, cut], sems.at[k]))
        copies[-1].start()
    for copy in fetches:
        copy.wait()
    n_r = mask_s.shape[0]
    total, alive = jnp.float32(0), jnp.float32(0)
    for r in range(n_r):
        m = mask_s[r].astype(F32)
        total = total + m * tally_s[r].astype(F32)
        alive = alive + m
    half = n_r // 2
    place = (lax.broadcasted_iota(jnp.int32, (8, 2 * B), 1) // keep) % half
    scale = jnp.full((8, 2 * B), alive) / jnp.full((8, 2 * B), total)
    for h in range(2):
        w = jnp.zeros((8, 2 * B), F32)
        for i, r in enumerate(order_of(h)):
            w = jnp.where(place == i, mask_s[r].astype(F32) * tally_s[r].astype(F32), w)
        w_ref[h] = w * scale
    for copy in copies:
        copy.wait()


def places_body(keep, w_ref, small, bundles, *p_refs):
    n_r, last = bundles.shape[0], bundles.shape[1] - 16
    half, nb = n_r // 2, G // B
    freq = lax.broadcasted_iota(jnp.int32, (B, 2 * B), 0).astype(F32)
    lane = lax.broadcasted_iota(jnp.int32, (1, 2 * B), 1)
    block = lane // (half * keep)
    for h in range(2):
        hi_ref, lo_ref = p_refs[2 * h : 2 * h + 2]
        w = w_ref[h, :1, :]
        rows = [bundles[r, last:, :].astype(F32)[:keep] for r in order_of(h)]
        rows = jnp.concatenate(rows * nb, axis=0).T
        for g in range(hi_ref.shape[1] // (2 * B)):
            num = rows[g * nb : g * nb + 1]
            for j in range(1, nb):
                num = jnp.where(block == j, rows[g * nb + j : g * nb + j + 1], num)
            hot = jnp.where(freq == num, 1.0, 0.0).astype(BF16)
            y = dot(small[:, 2 * B : 3 * B], hot)
            hi, lo = split((y[:B] + y[B:]) * w)
            hi_ref[:, g * 2 * B : (g + 1) * 2 * B] = hi
            lo_ref[:, g * 2 * B : (g + 1) * 2 * B] = lo


def spread_rows(p_hi, p_lo, rows, g):
    s = jnp.concatenate(rows, axis=0)
    lane_block = lax.broadcasted_iota(jnp.int32, s.shape, 1) // B
    w = jnp.concatenate(
        [jnp.where(lane_block == j, s, 0.0).astype(BF16) for j in range(G // B)], axis=0
    )
    cut = slice(g * 2 * B, (g + 1) * 2 * B)
    y = dot(jnp.concatenate([p_hi[:, cut], p_lo[:, cut]], axis=0), w)
    return y[:B] + y[B:]


def half_update_body(p_hi, p_lo, own, near_two, other_own, out):
    for g in range(out.shape[0] // B):
        cut = slice(g * G, (g + 1) * G)
        rows = [x.astype(F32) for x in (own[:, cut], near_two[0, :, cut], near_two[1, :, cut], other_own[:, cut])]
        out[g * B : (g + 1) * B, :] = spread_rows(p_hi, p_lo, rows, g)


def update_body(chunk, half_sum, p_hi, p_lo, near_two, direct, relayed, out, held, sems):
    ng = half_sum.shape[0] // B
    second = lax.rem(lax.axis_index("replica"), 2) == 1
    copies = []
    for c in range(0, ng, chunk):
        for g in range(c, c + chunk):
            cut = slice(g * G, (g + 1) * G)
            rows = [near_two[i, :, cut].astype(F32) for i in range(2)]
            rows += [
                jnp.where(second, direct[i, :, cut].astype(F32), relayed[i, :, cut].astype(F32)) for i in range(2)
            ]
            held[:, cut] = half_sum[g * B : (g + 1) * B, :] + spread_rows(p_hi, p_lo, rows, g)
        cut = pl.ds(c * G, chunk * G)
        copies.append(pltpu.make_async_copy(held.at[:, cut], out.at[:, cut], sems.at[c // chunk]))
        copies[-1].start()
    for copy in copies:
        copy.wait()


def input_grad_body(n_t, n_r, cp, exp_ref, bundles, *refs):
    ups, (out, held) = refs[:n_t], refs[n_t:]
    cols = out.shape[1]
    held[:B, :] = exp_ref[:, pl.ds(pl.multiple_of(lax.axis_index("tensor") * cols, 128), cols)]
    nc = cols // cp
    nr = B // (n_r // cp)
    tiles = nc // 128
    for r in range(n_r):
        r0, c0 = (r // cp) * nr, (r % cp) * nc
        for k in range(1, n_t):
            for j in range(tiles):
                at = ((k - 1) * tiles + j) * nr
                held[k * B + r0 : k * B + r0 + nr, c0 + j * 128 : c0 + (j + 1) * 128] = bundles[r, at : at + nr, :]
    up = jnp.concatenate([u[:B, :] for u in ups], axis=0).T
    for c in range(0, cols, G):
        out[:, c : c + G] = dot(up, held[:, c : c + G]).astype(BF16)


def per_device(n_t, n_r, act, switch, slope, exp, vel, lines, mask, tally):
    cols = act.shape[1]
    width = exp.shape[1]
    tok = act.shape[0]
    keep = lines.shape[3]
    blocks = width // B
    groups = width // G
    cp = 2
    rp = n_r // cp
    half = n_r // 2
    tab, small = constants()
    def trade(x, k):
        return lax.ppermute(x, "tensor", [(i, i ^ k) for i in range(n_t)])

    order = [*range(2, n_t), 1]

    def swap(x, m):
        return lax.ppermute(x, "replica", [(i, i ^ m) for i in range(n_r)])

    own = lines[0, 0].T
    tiles = cols // cp // 128
    nr = B // rp
    *parts, act, own, small = call(
        functools.partial(first_body, n_t, cp, cols, nr),
        [near((B, tok))]
        + [near((B + tiles * nr, 128))] * (n_t - 1)
        + [near(act.shape), near(own.shape, jnp.int32), near(small.shape)],
        (far(switch.T), far(slope.T), far(exp), far(act), far(own), far(small)),
        [ANY] * 6,
        [VM] * (n_t + 3),
        scratch=[
            pltpu.VMEM((B, tok), BF16),
            pltpu.VMEM((B, tok), BF16),
            pltpu.VMEM((nr, width), BF16),
            pltpu.SemaphoreType.DMA((6,)),
        ],
        nbytes=act.size * 4 + nr * width * 2,
        name="up_grads",
    )
    got = {k: trade(parts[k], k) for k in order}
    parts = [parts[0]] + [got[k] for k in range(1, n_t)]

    a_own = call(
        functools.partial(own_rows_body, keep),
        near((groups * B, 2 * B)),
        (own, small),
        [VM, VM],
        VM,
        name="own_rows",
    )

    def grads_of(ks, after):
        return call(
            functools.partial(grads_body, len(ks)),
            [near((B, cols), BF16 if k else F32) for k in ks],
            (act, after, *[parts[k] for k in ks]),
            [VM, ANY] + [VM] * len(ks),
            [VM] * len(ks),
            name="weight_grads",
        )

    grads = {}
    for k in order[:-1]:
        (grads[k],) = grads_of([k], act)
    made, grads[0] = grads_of([order[-1], 0], a_own)
    grads[order[-1]] = made
    grads.update({k: trade(grads[k], k) for k in order})

    bundle = call(
        functools.partial(bundle_body, n_t, keep),
        near(((n_t - 1) * tiles * nr + 16, 128)),
        (made, own, *parts[1:]),
        [ANY] + [VM] * n_t,
        VM,
        name="bundle",
    )
    bundles = lax.all_gather(bundle, "replica", axis=0)

    rows = []
    for ks in ([k for k in range(n_t) if k != n_t - 1], [n_t - 1]):
        n = len(ks)
        rows = call(
            functools.partial(kept_body, ks, n_t, keep),
            [near((keep, width)), near((keep, width), F32)],
            (vel[0], a_own, tab, bundles, *[grads[k] for k in ks], *rows),
            [VM] * 3 + [ANY] + [VM] * (n + len(rows)),
            [VM] * 2,
            flops=6 * B * B * cols * n,
            nbytes=B * cols * 6 * n,
            name="kept_rows",
            alias={4 + n: 0, 5 + n: 1} if rows else {},
        )
    ship, q_own = rows

    p_own = call(
        functools.partial(own_columns_body, keep),
        near((B, groups * 2 * B)),
        (own, small, q_own),
        [VM, VM, ANY],
        VM,
        name="own_columns",
    )
    new, shares = call(
        functools.partial(return_body, n_t, keep),
        [jax.ShapeDtypeStruct((B, width), F32), near((2, 8, 2 * B), F32)],
        (vel[0], p_own, q_own, far(mask), far(tally), *[grads[k] for k in range(n_t)]),
        [VM] * 3 + [ANY] * 2 + [VM] * n_t,
        [ANY, VM],
        scratch=[
            pltpu.VMEM((B, width), F32),
            pltpu.SemaphoreType.DMA((n_t,)),
            pltpu.SMEM((n_r,), jnp.int32),
            pltpu.SMEM((n_r,), jnp.int32),
            pltpu.SemaphoreType.DMA((2,)),
        ],
        flops=6 * B * B * width,
        nbytes=B * width * 10,
        name="new_momentums",
    )
    places = call(
        functools.partial(places_body, keep),
        [near((B, blocks * half * keep))] * 4,
        (shares, small, bundles),
        [VM] * 3,
        [VM] * 4,
        name="places",
    )
    input_grad = call(
        functools.partial(input_grad_body, n_t, n_r, cp),
        jax.ShapeDtypeStruct((tok, cols), BF16),
        (exp, bundles, *parts),
        [VM] * (2 + n_t),
        VM,
        scratch=[pltpu.VMEM((n_t * B, cols), BF16)],
        flops=2 * tok * n_t * B * cols,
        nbytes=(n_t * B * cols + tok * cols) * 2,
        name="input_grads",
    )

    other_own = swap(ship, 1)
    pair = call(
        join_body,
        near((2, keep, width)),
        (ship, other_own),
        [VM] * 2,
        VM,
        name="join_cores",
    )
    direct = lax.ppermute(pair, "replica", [(r, r ^ 6) for r in range(n_r) if r % 2])
    beside = [swap(ship, 2), swap(ship, 4)]
    p_own = call(
        functools.partial(own_columns_body, keep),
        near((B, groups * 2 * B)),
        (own, small, q_own),
        [VM, VM, ANY],
        VM,
        name="own_columns",
    )
    new, shares = call(
        functools.partial(return_body, n_t, keep),
        [jax.ShapeDtypeStruct((B, width), F32), near((2, 8, 2 * B), F32)],
        (vel[0], p_own, q_own, far(mask), far(tally), *[grads[k] for k in range(n_t)]),
        [VM] * 3 + [ANY] * 2 + [VM] * n_t,
        [ANY, VM],
        scratch=[
            pltpu.VMEM((B, width), F32),
            pltpu.SemaphoreType.DMA((n_t,)),
            pltpu.SMEM((n_r,), jnp.int32),
            pltpu.SMEM((n_r,), jnp.int32),
            pltpu.SemaphoreType.DMA((2,)),
        ],
        flops=6 * B * B * width,
        nbytes=B * width * 10,
        name="new_momentums",
    )
    places = call(
        functools.partial(places_body, keep),
        [near((B, blocks * half * keep))] * 4,
        (shares, small, bundles),
        [VM] * 3,
        [VM] * 4,
        name="places",
    )
    input_grad = call(
        functools.partial(input_grad_body, n_t, n_r, cp),
        jax.ShapeDtypeStruct((tok, cols), BF16),
        (exp, bundles, *parts),
        [VM] * (2 + n_t),
        VM,
        scratch=[pltpu.VMEM((n_t * B, cols), BF16)],
        flops=2 * tok * n_t * B * cols,
        nbytes=(n_t * B * cols + tok * cols) * 2,
        name="input_grads",
    )

    ships = [ship] + [swap(ship, 2 * i) for i in range(1, half)]
    two = call(
        join_body,
        near((2, keep, width)),
        (*beside, far(new), far(input_grad), places[0]),
        [VM] * 2 + [ANY] * 3,
        VM,
        flops=1 << 30,
        name="join_kept",
    )
    other_two = swap(two, 1)
    relayed = lax.ppermute(direct, "replica", [(r, r ^ 1) for r in range(n_r) if r % 2])
    half_sum = call(
        half_update_body,
        near((groups * B, G), F32),
        (*places[:2], ship, two, other_own),
        [VM] * 5,
        VM,
        name="half_updates",
    )
    chunk = 2 if groups % 2 == 0 else 1
    update = call(
        functools.partial(update_body, chunk),
        jax.ShapeDtypeStruct((B, width), F32),
        (half_sum, *places[2:], other_two, direct, relayed),
        [VM] * 6,
        ANY,
        scratch=[
            pltpu.VMEM((B, width), F32),
            pltpu.SemaphoreType.DMA((groups // chunk,)),
        ],
        flops=8 * B * G * width,
        nbytes=B * width * 8,
        name="updates",
    )
    return input_grad, new[None], update


def per_device_plain(
    projection_inputs,
    switch_logits_raw,
    inner_neuron_slope,
    expansion_matrix,
    velocity_buffer,
    sent_spectral_lines,
    participant_mask,
    token_tallies,
):
    highest = lax.Precision.HIGHEST
    up_grad = (
        inner_neuron_slope.astype(jnp.float32) * jax.nn.silu(switch_logits_raw.astype(jnp.float32))
    ).astype(jnp.bfloat16)
    partial_terms = jnp.dot(up_grad, expansion_matrix, preferred_element_type=jnp.float32)
    input_grad = lax.psum_scatter(partial_terms, "tensor", scatter_dimension=1, tiled=True).astype(
        jnp.bfloat16
    )
    grad_w = lax.dot_general(
        up_grad,
        lax.all_gather(projection_inputs, "tensor", axis=1, tiled=True),
        (((0,), (0,)), ((), ())),
        preferred_element_type=jnp.float32,
    )
    row_total_count = expansion_matrix.shape[0] // 64
    col_count = expansion_matrix.shape[1] // 64
    moment = momentum_decay * velocity_buffer[0] + grad_w
    cosines = cosine_table()
    blocks = moment.reshape(row_total_count, 64, col_count, 64).transpose(0, 2, 1, 3)
    coefficients = jnp.einsum("fa,ijab,gb->ijfg", cosines, blocks, cosines, precision=highest)
    freq_ids = jnp.arange(64, dtype=jnp.int32)
    own_rows = sent_spectral_lines[0]
    chosen = (own_rows[..., None] == freq_ids).astype(jnp.float32)
    shipped = jnp.einsum("ijkf,ijfg->ijkg", chosen, coefficients, precision=highest).astype(
        jnp.bfloat16
    )
    spectrum = jnp.einsum("ijkf,ijkg->ijfg", chosen, shipped.astype(jnp.float32), precision=highest)
    returned = jnp.einsum("fa,ijfg,gb->ijab", cosines, spectrum, cosines, precision=highest)
    new_moment = moment - returned.transpose(0, 2, 1, 3).reshape(moment.shape)
    worker_burdens = participant_mask.astype(jnp.float32) * token_tallies.astype(jnp.float32)
    worker_fractions = worker_burdens * (
        jnp.sum(participant_mask.astype(jnp.float32)) / jnp.sum(worker_burdens)
    )
    myself = lax.axis_index("replica")
    combined = lax.psum(worker_fractions[myself] * spectrum, "replica")
    update = jnp.einsum("fa,ijfg,gb->ijab", cosines, combined, cosines, precision=highest)
    update = update.transpose(0, 2, 1, 3).reshape(moment.shape)
    return (input_grad, new_moment[None], update)


def solution(mesh):
    n_t, n_r = mesh.shape["tensor"], mesh.shape["replica"]

    def device(*args):
        act, exp, lines = args[0], args[3], args[5]
        fits = (
            act.shape[1] % G == 0
            and act.shape[0] % 128 == 0
            and exp.shape[0] == B
            and lines.shape[3] == 8
            and n_r == 8
            and n_t >= 2
            and n_t & (n_t - 1) == 0
        )
        if not fits:
            return per_device_plain(*args)
        return per_device(n_t, n_r, *args)

    return jax.shard_map(
        device,
        mesh=mesh,
        in_specs=(
            P("replica", "tensor"),
            P("replica", "tensor"),
            P("replica", "tensor"),
            P("tensor", None),
            P("replica", "tensor", None),
            P("replica", "tensor", None, None),
            P(),
            P(),
        ),
        out_specs=(P("replica", "tensor"), P("replica", "tensor", None), P("tensor", None)),
        check_vma=False,
    )
```

```python
import functools

import jax
import jax.numpy as jnp
import numpy as np
from jax import lax
from jax.experimental import pallas as pl
from jax.experimental.pallas import tpu as pltpu
from jax.sharding import PartitionSpec as P

momentum_decay = 0.9
B = 64
G = 256
F32 = jnp.float32
BF16 = jnp.bfloat16
VMEM_LIMIT = 24 * 1024 * 1024

VM = pl.BlockSpec(memory_space=pltpu.VMEM)
SM = pl.BlockSpec(memory_space=pltpu.SMEM)
ANY = pl.BlockSpec(memory_space=pl.ANY)


def cosine_table():
    freqs = jnp.arange(64, dtype=jnp.float32)[:, None]
    places = jnp.arange(64, dtype=jnp.float32)[None, :]
    cosines = jnp.cos(jnp.pi * (places + 0.5) * freqs / 64.0) * jnp.sqrt(2.0 / 64.0)
    return cosines.at[0].multiply(jnp.sqrt(0.5))


def cosine_np():
    f = np.arange(B)[:, None]
    a = np.arange(B)[None, :]
    c = np.cos(np.pi * (a + 0.5) * f / B) * np.sqrt(2.0 / B)
    c[0] *= np.sqrt(0.5)
    return c


def halves(c):
    hi = np.asarray(c, dtype=np.float32).astype(jnp.bfloat16)
    lo = (np.asarray(c, np.float64) - hi.astype(np.float64)).astype(np.float32).astype(jnp.bfloat16)
    return hi, lo


def constants():
    hi, lo = halves(cosine_np())
    eye = np.eye(G // B)
    kron = lambda x: np.kron(eye, np.asarray(x, np.float32)).astype(jnp.bfloat16)
    small = np.zeros((2 * B, 4 * B), jnp.bfloat16)
    for i, x in enumerate((hi, lo)):
        rows = slice(i * B, (i + 1) * B)
        small[rows, :B], small[rows, B : 2 * B], small[rows, 2 * B : 3 * B] = x, x, x.T
    return jnp.asarray(np.concatenate([kron(x) for x in (hi.T, lo.T, hi, lo)], axis=0)), jnp.asarray(small)


def fwd(tab, i):
    return tab[i * G : (i + 1) * G, :]


def inv(tab, i):
    return tab[(2 + i) * G : (3 + i) * G, :]


def dot(a, b):
    return jnp.dot(a, b, preferred_element_type=F32)


def split(x):
    hi = x.astype(BF16)
    return hi, (x - hi.astype(F32)).astype(BF16)


def near(shape, dtype=BF16):
    return pltpu.VMEM(shape, dtype)


def far(x):
    return pltpu.with_memory_space_constraint(x, pltpu.HBM)


def call(body, out_shape, ins, in_specs, out_specs, scratch=(), flops=0, nbytes=0, name=None, alias={}):
    return pl.pallas_call(
        body,
        out_shape=out_shape,
        in_specs=in_specs,
        out_specs=out_specs,
        scratch_shapes=scratch,
        input_output_aliases=alias,
        compiler_params=pltpu.CompilerParams(vmem_limit_bytes=VMEM_LIMIT),
        cost_estimate=pl.CostEstimate(flops=flops, bytes_accessed=nbytes, transcendentals=0),
        name=name,
    )(*ins)


def first_body(n_t, cp, cols, nr, switch, slope, exp_ref, act, lines, small, *refs):
    outs, (act_out, lines_out, small_out) = refs[:n_t], refs[n_t : n_t + 3]
    switch_v, slope_v, exp_v, sems = refs[n_t + 3 :]
    rep, ten = lax.axis_index("replica"), lax.axis_index("tensor")
    r0 = pl.multiple_of((rep // cp) * nr, nr)
    copies = [
        pltpu.make_async_copy(src, dst, sems.at[i])
        for i, (src, dst) in enumerate(
            [
                (switch, switch_v),
                (slope, slope_v),
                (exp_ref.at[pl.ds(r0, nr), :], exp_v),
                (act, act_out),
                (lines, lines_out),
                (small, small_out),
            ]
        )
    ]
    for copy in copies:
        copy.start()
    copies[0].wait()
    copies[1].wait()
    v = switch_v[...].astype(F32)
    up = (slope_v[...].astype(F32) * (v * jax.nn.sigmoid(v))).astype(BF16)
    for k in range(n_t):
        outs[k][:B, :] = up
    copies[2].wait()
    nc = cols // cp
    for k in range(1, n_t):
        c0 = (ten ^ k) * cols + lax.rem(rep, cp) * nc
        for j in range(nc // 128):
            at = pl.multiple_of(c0 + j * 128, 128)
            outs[k][B + j * nr : B + (j + 1) * nr, :] = exp_v[:, pl.ds(at, 128)]
    for copy in copies[3:]:
        copy.wait()


def grads_body(n, act, after, *refs):
    ups, outs = refs[:n], refs[n:]
    up = jnp.concatenate([u[:B, :] for u in ups], axis=0)
    for c in range(0, act.shape[1], G):
        g = dot(up, act[:, c : c + G])
        for k in range(n):
            outs[k][:, c : c + G] = g[k * B : (k + 1) * B].astype(outs[k].dtype)


def bundle_body(n_t, keep, after, lines, *refs):
    parts, out = refs[: n_t - 1], refs[n_t - 1]
    n = parts[0].shape[0] - B
    for k in range(n_t - 1):
        out[k * n : (k + 1) * n, :] = parts[k][B:, :]
    blocks = lines.shape[1]
    rows = jnp.concatenate([lines[...].astype(F32), jnp.zeros((keep, 128 - blocks), F32)], axis=1)
    out[(n_t - 1) * n :, :] = jnp.concatenate([rows, jnp.zeros((16 - keep, 128), F32)], axis=0).astype(BF16)


def join_body(n, *refs):
    for i, ref in enumerate(refs[1 : n + 1]):
        refs[-1][i] = ref[...]


def own_body(keep, lines, small, p_ref, a_ref):
    blocks, nb = lines.shape[1], G // B
    rows = jnp.concatenate([lines[...].astype(F32), jnp.zeros((keep, 128 - blocks), F32)], axis=1)
    lane = lax.broadcasted_iota(jnp.int32, (nb * keep, 2 * B), 1).astype(F32)
    for g in range(blocks // nb):
        num = jnp.concatenate(
            [jnp.broadcast_to(rows[:, g * nb + j : g * nb + j + 1], (keep, 2 * B)) for j in range(nb)], axis=0
        )
        hot = jnp.concatenate(
            [jnp.where(lane == num, 1.0, 0.0), jnp.where(lane - B == num, 1.0, 0.0)], axis=0
        ).astype(BF16)
        a_ref[g * B : (g + 1) * B, :] = dot(hot, small[:, : 2 * B]).astype(BF16)
    rows = jnp.concatenate([rows] * (2 * B // keep), axis=0).T
    freq = lax.broadcasted_iota(jnp.int32, (B, 2 * B), 0).astype(F32)
    block = (lax.broadcasted_iota(jnp.int32, (1, 2 * B), 1) // keep) % nb
    term = lax.broadcasted_iota(jnp.int32, (B, 2 * B), 1) // (B // 2)
    for g in range(blocks // nb):
        num = rows[g * nb : g * nb + 1]
        for j in range(1, nb):
            num = jnp.where(block == j, rows[g * nb + j : g * nb + j + 1], num)
        hot = jnp.where(freq == num, 1.0, 0.0).astype(BF16)
        y = dot(small[:, 2 * B : 3 * B], hot)
        p = jnp.where(term == 3, 0.0, jnp.where(term == 1, y[B:], y[:B]))
        p_ref[:, g * 2 * B : (g + 1) * 2 * B] = p.astype(BF16)


def selected(ks, n_t, keep, vel, a_ref, grads):
    cols = grads[0].shape[1]
    lane_block = lax.broadcasted_iota(jnp.int32, (keep, G), 1) // B
    for n, k in enumerate(ks):
        c0 = (lax.axis_index("tensor") ^ k) * cols
        for i in range(cols // G):
            at = pl.multiple_of(c0 + i * G, G)
            moment = momentum_decay * vel[:, pl.ds(at, G)] + grads[n][:, i * G : (i + 1) * G].astype(F32)
            hi, lo = split(moment)
            y = dot(a_ref[pl.ds(pl.multiple_of(at // (G // B), B), B), :], jnp.concatenate([hi, lo], axis=0))
            y = y[: B // 2] + y[B // 2 :]
            got = y[:keep]
            for j in range(1, G // B):
                got = jnp.where(lane_block == j, y[j * keep : (j + 1) * keep], got)
            yield at, got


def select_body(ks, n_t, keep, vel, a_ref, after, *refs):
    grads, sel_ref = refs[: len(ks)], refs[len(ks)]
    for at, got in selected(ks, n_t, keep, vel, a_ref, grads):
        sel_ref[:, pl.ds(at, G)] = got


def kept_body(before, ks, n_t, keep, vel, a_ref, tab, sel_ref, *refs):
    grads, (send_ref, own_ref) = refs[: len(ks)], refs[len(ks) :]
    cols = grads[0].shape[1]
    cells = []
    for k in before:
        c0 = (lax.axis_index("tensor") ^ k) * cols
        for i in range(cols // G):
            at = pl.multiple_of(c0 + i * G, G)
            cells.append((at, sel_ref[:, pl.ds(at, G)]))
    cells += list(selected(ks, n_t, keep, vel, a_ref, grads))
    n = len(cells) * keep
    hi, lo = split(jnp.concatenate([got for _, got in cells], axis=0))
    y = dot(jnp.concatenate([hi, lo], axis=0), fwd(tab, 0))
    kept = (y[:n] + y[n:] + dot(hi, fwd(tab, 1))).astype(BF16)
    q = dot(kept, inv(tab, 0)) + dot(kept, inv(tab, 1))
    for i, (at, _) in enumerate(cells):
        part = q[i * keep : (i + 1) * keep]
        own_ref[:, pl.ds(at, G)] = part
        send_ref[:, pl.ds(at, G)] = part.astype(BF16)


def return_body(n_t, keep, vel, p_ref, q, mask, tally, *refs):
    grads, (new_ref, w_ref, held, sems, mask_s, tally_s, small_sems) = refs[:n_t], refs[n_t:]
    fetches = [
        pltpu.make_async_copy(src, dst, small_sems.at[i])
        for i, (src, dst) in enumerate([(mask, mask_s), (tally, tally_s)])
    ]
    for copy in fetches:
        copy.start()
    cols = grads[0].shape[1]
    ng = cols // G
    lane_block = lax.broadcasted_iota(jnp.int32, (keep, G), 1) // B
    copies = []
    for k in range(n_t):
        c0 = pl.multiple_of((lax.axis_index("tensor") ^ k) * cols, G)
        for i in range(ng):
            at = pl.multiple_of(c0 + i * G, G)
            own = q[:, pl.ds(at, G)]
            spread = jnp.concatenate(
                [jnp.where(lane_block == j, own, 0.0) for j in range(G // B)], axis=0
            )
            hi, lo = split(spread)
            w = jnp.concatenate([hi, hi, lo, jnp.zeros_like(lo)], axis=0)
            back = dot(p_ref[:, pl.ds(pl.multiple_of(at // 2, 2 * B), 2 * B)], w)
            moment = momentum_decay * vel[:, pl.ds(at, G)] + grads[k][:, i * G : (i + 1) * G].astype(F32)
            held[:, pl.ds(at, G)] = moment - back
        cut = pl.ds(c0, cols)
        copies.append(pltpu.make_async_copy(held.at[:, cut], new_ref.at[:, cut], sems.at[k]))
        copies[-1].start()
    for copy in fetches:
        copy.wait()
    n_r = mask_s.shape[0]
    total, alive = jnp.float32(0), jnp.float32(0)
    for r in range(n_r):
        m = mask_s[r].astype(F32)
        total = total + m * tally_s[r].astype(F32)
        alive = alive + m
    half = n_r // 2
    place = (lax.broadcasted_iota(jnp.int32, (8, 2 * B), 1) // keep) % half
    scale = jnp.full((8, 2 * B), alive) / jnp.full((8, 2 * B), total)
    for h in range(2):
        w = jnp.zeros((8, 2 * B), F32)
        for i in range(half):
            r = lax.axis_index("replica") ^ (2 * i + h)
            w = jnp.where(place == i, mask_s[r].astype(F32) * tally_s[r].astype(F32), w)
        w_ref[h] = w * scale
    for copy in copies:
        copy.wait()


def places_body(keep, w_ref, small, bundles, *p_refs):
    n_r, last = bundles.shape[0], bundles.shape[1] - 16
    half, nb = n_r // 2, G // B
    rep = lax.axis_index("replica")
    freq = lax.broadcasted_iota(jnp.int32, (B, 2 * B), 0).astype(F32)
    lane = lax.broadcasted_iota(jnp.int32, (1, 2 * B), 1)
    block = lane // (half * keep)
    for h in range(2):
        hi_ref, lo_ref = p_refs[2 * h : 2 * h + 2]
        w = w_ref[h, :1, :]
        rows = [bundles[rep ^ (2 * i + h), last:, :].astype(F32)[:keep] for i in range(half)]
        rows = jnp.concatenate(rows * nb, axis=0).T
        for g in range(hi_ref.shape[1] // (2 * B)):
            num = rows[g * nb : g * nb + 1]
            for j in range(1, nb):
                num = jnp.where(block == j, rows[g * nb + j : g * nb + j + 1], num)
            hot = jnp.where(freq == num, 1.0, 0.0).astype(BF16)
            y = dot(small[:, 2 * B : 3 * B], hot)
            hi, lo = split((y[:B] + y[B:]) * w)
            hi_ref[:, g * 2 * B : (g + 1) * 2 * B] = hi
            lo_ref[:, g * 2 * B : (g + 1) * 2 * B] = lo


def spread_rows(p_hi, p_lo, own, ships, g):
    half, keep = ships.shape[0] + 1, ships.shape[1]
    cut = slice(g * G, (g + 1) * G)
    lane_block = lax.broadcasted_iota(jnp.int32, (half * keep, G), 1) // B
    s = [own[:, cut].astype(F32)] + [ships[i, :, cut].astype(F32) for i in range(half - 1)]
    s = jnp.concatenate(s, axis=0)
    w = jnp.concatenate(
        [jnp.where(lane_block == j, s, 0.0).astype(BF16) for j in range(G // B)], axis=0
    )
    cut = slice(g * 2 * B, (g + 1) * 2 * B)
    y = dot(jnp.concatenate([p_hi[:, cut], p_lo[:, cut]], axis=0), w)
    return y[:B] + y[B:]


def half_update_body(p_hi, p_lo, own, others, out):
    for g in range(out.shape[0] // B):
        out[g * B : (g + 1) * B, :] = spread_rows(p_hi, p_lo, own, others, g)


def update_body(chunk, half_sum, p_hi, p_lo, own, others, out, held, sems):
    ng = half_sum.shape[0] // B
    copies = []
    for c in range(0, ng, chunk):
        for g in range(c, c + chunk):
            held[:, g * G : (g + 1) * G] = half_sum[g * B : (g + 1) * B, :] + spread_rows(p_hi, p_lo, own, others, g)
        cut = pl.ds(c * G, chunk * G)
        copies.append(pltpu.make_async_copy(held.at[:, cut], out.at[:, cut], sems.at[c // chunk]))
        copies[-1].start()
    for copy in copies:
        copy.wait()


def input_grad_body(n_t, n_r, cp, exp_ref, bundles, *refs):
    ups, (out, held) = refs[:n_t], refs[n_t:]
    cols = out.shape[1]
    held[:B, :] = exp_ref[:, pl.ds(pl.multiple_of(lax.axis_index("tensor") * cols, 128), cols)]
    nc = cols // cp
    nr = B // (n_r // cp)
    tiles = nc // 128
    for r in range(n_r):
        r0, c0 = (r // cp) * nr, (r % cp) * nc
        for k in range(1, n_t):
            for j in range(tiles):
                at = ((k - 1) * tiles + j) * nr
                held[k * B + r0 : k * B + r0 + nr, c0 + j * 128 : c0 + (j + 1) * 128] = bundles[r, at : at + nr, :]
    up = jnp.concatenate([u[:B, :] for u in ups], axis=0).T
    for c in range(0, cols, G):
        out[:, c : c + G] = dot(up, held[:, c : c + G]).astype(BF16)


def per_device(n_t, n_r, act, switch, slope, exp, vel, lines, mask, tally):
    cols = act.shape[1]
    width = exp.shape[1]
    tok = act.shape[0]
    keep = lines.shape[3]
    blocks = width // B
    groups = width // G
    cp = 2
    rp = n_r // cp
    half = n_r // 2
    tab, small = constants()
    def trade(x, k):
        return lax.ppermute(x, "tensor", [(i, i ^ k) for i in range(n_t)])

    order = [*range(2, n_t), 1]

    def swap(x, m):
        return lax.ppermute(x, "replica", [(i, i ^ m) for i in range(n_r)])

    own = lines[0, 0].T
    tiles = cols // cp // 128
    nr = B // rp
    *parts, act, own, small = call(
        functools.partial(first_body, n_t, cp, cols, nr),
        [near((B, tok))]
        + [near((B + tiles * nr, 128))] * (n_t - 1)
        + [near(act.shape), near(own.shape, jnp.int32), near(small.shape)],
        (far(switch.T), far(slope.T), far(exp), far(act), far(own), far(small)),
        [ANY] * 6,
        [VM] * (n_t + 3),
        scratch=[
            pltpu.VMEM((B, tok), BF16),
            pltpu.VMEM((B, tok), BF16),
            pltpu.VMEM((nr, width), BF16),
            pltpu.SemaphoreType.DMA((6,)),
        ],
        nbytes=act.size * 4 + nr * width * 2,
        name="up_grads",
    )
    got = {k: trade(parts[k], k) for k in order}
    parts = [parts[0]] + [got[k] for k in range(1, n_t)]

    p_own, a_own = call(
        functools.partial(own_body, keep),
        [near((B, groups * 2 * B)), near((groups * B, 2 * B))],
        (own, small),
        [VM, VM],
        [VM, VM],
        name="own_places",
    )

    def grads_of(ks, after):
        return call(
            functools.partial(grads_body, len(ks)),
            [near((B, cols), BF16 if k else F32) for k in ks],
            (act, after, *[parts[k] for k in ks]),
            [VM, ANY] + [VM] * len(ks),
            [VM] * len(ks),
            name="weight_grads",
        )

    grads = {}
    for k in order[:-1]:
        (grads[k],) = grads_of([k], act)
    made, grads[0] = grads_of([order[-1], 0], a_own)
    grads[order[-1]] = made
    grads.update({k: trade(grads[k], k) for k in order})

    bundle = call(
        functools.partial(bundle_body, n_t, keep),
        near(((n_t - 1) * tiles * nr + 16, 128)),
        (made, own, *parts[1:]),
        [ANY] + [VM] * n_t,
        VM,
        name="bundle",
    )
    bundles = lax.all_gather(bundle, "replica", axis=0)

    before, last = [k for k in range(n_t) if k != n_t - 1], [n_t - 1]
    sel = call(
        functools.partial(select_body, before, n_t, keep),
        near((keep, width), F32),
        (vel[0], a_own, bundles, *[grads[k] for k in before]),
        [VM] * 2 + [ANY] + [VM] * len(before),
        VM,
        flops=6 * B * B * cols * len(before),
        nbytes=B * cols * 6 * len(before),
        name="selected_rows",
    )
    ship, q_own = call(
        functools.partial(kept_body, before, last, n_t, keep),
        [near((keep, width)), near((keep, width), F32)],
        (vel[0], a_own, tab, sel, *[grads[k] for k in last]),
        [VM] * (4 + len(last)),
        [VM] * 2,
        flops=6 * B * B * cols,
        nbytes=B * cols * 6,
        name="kept_rows",
    )

    new, shares = call(
        functools.partial(return_body, n_t, keep),
        [jax.ShapeDtypeStruct((B, width), F32), near((2, 8, 2 * B), F32)],
        (vel[0], p_own, q_own, far(mask), far(tally), *[grads[k] for k in range(n_t)]),
        [VM] * 3 + [ANY] * 2 + [VM] * n_t,
        [ANY, VM],
        scratch=[
            pltpu.VMEM((B, width), F32),
            pltpu.SemaphoreType.DMA((n_t,)),
            pltpu.SMEM((n_r,), jnp.int32),
            pltpu.SMEM((n_r,), jnp.int32),
            pltpu.SemaphoreType.DMA((2,)),
        ],
        flops=6 * B * B * width,
        nbytes=B * width * 10,
        name="new_momentums",
    )
    places = call(
        functools.partial(places_body, keep),
        [near((B, blocks * half * keep))] * 4,
        (shares, small, bundles),
        [VM] * 3,
        [VM] * 4,
        name="places",
    )
    input_grad = call(
        functools.partial(input_grad_body, n_t, n_r, cp),
        jax.ShapeDtypeStruct((tok, cols), BF16),
        (exp, bundles, *parts),
        [VM] * (2 + n_t),
        VM,
        scratch=[pltpu.VMEM((n_t * B, cols), BF16)],
        flops=2 * tok * n_t * B * cols,
        nbytes=(n_t * B * cols + tok * cols) * 2,
        name="input_grads",
    )

    ships = [ship] + [swap(ship, 2 * i) for i in range(1, half)]
    other_own = swap(ship, 1)
    others = call(
        functools.partial(join_body, half - 1),
        near((half - 1, keep, width)),
        (other_own, *ships[1:], far(new), far(input_grad), places[0]),
        [ANY] + [VM] * (half - 1) + [ANY] * 3,
        VM,
        name="join_kept",
    )
    other = swap(others, 1)
    half_sum = call(
        half_update_body,
        near((groups * B, G), F32),
        (*places[:2], ship, others),
        [VM] * 4,
        VM,
        name="half_updates",
    )
    chunk = 2 if groups % 2 == 0 else 1
    update = call(
        functools.partial(update_body, chunk),
        jax.ShapeDtypeStruct((B, width), F32),
        (half_sum, *places[2:], other_own, other),
        [VM] * 5,
        ANY,
        scratch=[
            pltpu.VMEM((B, width), F32),
            pltpu.SemaphoreType.DMA((groups // chunk,)),
        ],
        flops=8 * B * G * width,
        nbytes=B * width * 8,
        name="updates",
    )
    return input_grad, new[None], update


def per_device_plain(
    projection_inputs,
    switch_logits_raw,
    inner_neuron_slope,
    expansion_matrix,
    velocity_buffer,
    sent_spectral_lines,
    participant_mask,
    token_tallies,
):
    highest = lax.Precision.HIGHEST
    up_grad = (
        inner_neuron_slope.astype(jnp.float32) * jax.nn.silu(switch_logits_raw.astype(jnp.float32))
    ).astype(jnp.bfloat16)
    partial_terms = jnp.dot(up_grad, expansion_matrix, preferred_element_type=jnp.float32)
    input_grad = lax.psum_scatter(partial_terms, "tensor", scatter_dimension=1, tiled=True).astype(
        jnp.bfloat16
    )
    grad_w = lax.dot_general(
        up_grad,
        lax.all_gather(projection_inputs, "tensor", axis=1, tiled=True),
        (((0,), (0,)), ((), ())),
        preferred_element_type=jnp.float32,
    )
    row_total_count = expansion_matrix.shape[0] // 64
    col_count = expansion_matrix.shape[1] // 64
    moment = momentum_decay * velocity_buffer[0] + grad_w
    cosines = cosine_table()
    blocks = moment.reshape(row_total_count, 64, col_count, 64).transpose(0, 2, 1, 3)
    coefficients = jnp.einsum("fa,ijab,gb->ijfg", cosines, blocks, cosines, precision=highest)
    freq_ids = jnp.arange(64, dtype=jnp.int32)
    own_rows = sent_spectral_lines[0]
    chosen = (own_rows[..., None] == freq_ids).astype(jnp.float32)
    shipped = jnp.einsum("ijkf,ijfg->ijkg", chosen, coefficients, precision=highest).astype(
        jnp.bfloat16
    )
    spectrum = jnp.einsum("ijkf,ijkg->ijfg", chosen, shipped.astype(jnp.float32), precision=highest)
    returned = jnp.einsum("fa,ijfg,gb->ijab", cosines, spectrum, cosines, precision=highest)
    new_moment = moment - returned.transpose(0, 2, 1, 3).reshape(moment.shape)
    worker_burdens = participant_mask.astype(jnp.float32) * token_tallies.astype(jnp.float32)
    worker_fractions = worker_burdens * (
        jnp.sum(participant_mask.astype(jnp.float32)) / jnp.sum(worker_burdens)
    )
    myself = lax.axis_index("replica")
    combined = lax.psum(worker_fractions[myself] * spectrum, "replica")
    update = jnp.einsum("fa,ijfg,gb->ijab", cosines, combined, cosines, precision=highest)
    update = update.transpose(0, 2, 1, 3).reshape(moment.shape)
    return (input_grad, new_moment[None], update)


def solution(mesh):
    n_t, n_r = mesh.shape["tensor"], mesh.shape["replica"]

    def device(*args):
        act, exp, lines = args[0], args[3], args[5]
        fits = (
            act.shape[1] % G == 0
            and act.shape[0] % 128 == 0
            and exp.shape[0] == B
            and lines.shape[3] == 8
            and n_r == 8
            and n_t >= 2
            and n_t & (n_t - 1) == 0
        )
        if not fits:
            return per_device_plain(*args)
        return per_device(n_t, n_r, *args)

    return jax.shard_map(
        device,
        mesh=mesh,
        in_specs=(
            P("replica", "tensor"),
            P("replica", "tensor"),
            P("replica", "tensor"),
            P("tensor", None),
            P("replica", "tensor", None),
            P("replica", "tensor", None, None),
            P(),
            P(),
        ),
        out_specs=(P("replica", "tensor"), P("replica", "tensor", None), P("tensor", None)),
        check_vma=False,
    )
```

```python
import functools

import jax
import jax.numpy as jnp
import numpy as np
from jax import lax
from jax.experimental import pallas as pl
from jax.experimental.pallas import tpu as pltpu
from jax.sharding import PartitionSpec as P

momentum_decay = 0.9
B = 64
G = 256
F32 = jnp.float32
BF16 = jnp.bfloat16
VMEM_LIMIT = 24 * 1024 * 1024

VM = pl.BlockSpec(memory_space=pltpu.VMEM)
SM = pl.BlockSpec(memory_space=pltpu.SMEM)
ANY = pl.BlockSpec(memory_space=pl.ANY)


def cosine_table():
    freqs = jnp.arange(64, dtype=jnp.float32)[:, None]
    places = jnp.arange(64, dtype=jnp.float32)[None, :]
    cosines = jnp.cos(jnp.pi * (places + 0.5) * freqs / 64.0) * jnp.sqrt(2.0 / 64.0)
    return cosines.at[0].multiply(jnp.sqrt(0.5))


def cosine_np():
    f = np.arange(B)[:, None]
    a = np.arange(B)[None, :]
    c = np.cos(np.pi * (a + 0.5) * f / B) * np.sqrt(2.0 / B)
    c[0] *= np.sqrt(0.5)
    return c


def halves(c):
    hi = np.asarray(c, dtype=np.float32).astype(jnp.bfloat16)
    lo = (np.asarray(c, np.float64) - hi.astype(np.float64)).astype(np.float32).astype(jnp.bfloat16)
    return hi, lo


def constants():
    hi, lo = halves(cosine_np())
    eye = np.eye(G // B)
    kron = lambda x: np.kron(eye, np.asarray(x, np.float32)).astype(jnp.bfloat16)
    small = np.zeros((2 * B, 4 * B), jnp.bfloat16)
    for i, x in enumerate((hi, lo)):
        rows = slice(i * B, (i + 1) * B)
        small[rows, :B], small[rows, B : 2 * B], small[rows, 2 * B : 3 * B] = x, x, x.T
    return jnp.asarray(np.concatenate([kron(x) for x in (hi.T, lo.T, hi, lo)], axis=0)), jnp.asarray(small)


def fwd(tab, i):
    return tab[i * G : (i + 1) * G, :]


def inv(tab, i):
    return tab[(2 + i) * G : (3 + i) * G, :]


def dot(a, b):
    return jnp.dot(a, b, preferred_element_type=F32)


def split(x):
    hi = x.astype(BF16)
    return hi, (x - hi.astype(F32)).astype(BF16)


def near(shape, dtype=BF16):
    return pltpu.VMEM(shape, dtype)


def far(x):
    return pltpu.with_memory_space_constraint(x, pltpu.HBM)


def call(body, out_shape, ins, in_specs, out_specs, scratch=(), flops=0, nbytes=0, name=None, alias={}):
    return pl.pallas_call(
        body,
        out_shape=out_shape,
        in_specs=in_specs,
        out_specs=out_specs,
        scratch_shapes=scratch,
        input_output_aliases=alias,
        compiler_params=pltpu.CompilerParams(vmem_limit_bytes=VMEM_LIMIT),
        cost_estimate=pl.CostEstimate(flops=flops, bytes_accessed=nbytes, transcendentals=0),
        name=name,
    )(*ins)


def first_body(n_t, cp, cols, nr, switch, slope, exp_ref, act, lines, small, *refs):
    outs, (act_out, lines_out, small_out) = refs[:n_t], refs[n_t : n_t + 3]
    switch_v, slope_v, exp_v, sems = refs[n_t + 3 :]
    rep, ten = lax.axis_index("replica"), lax.axis_index("tensor")
    r0 = pl.multiple_of((rep // cp) * nr, nr)
    copies = [
        pltpu.make_async_copy(src, dst, sems.at[i])
        for i, (src, dst) in enumerate(
            [
                (switch, switch_v),
                (slope, slope_v),
                (exp_ref.at[pl.ds(r0, nr), :], exp_v),
                (act, act_out),
                (lines, lines_out),
                (small, small_out),
            ]
        )
    ]
    for copy in copies:
        copy.start()
    copies[0].wait()
    copies[1].wait()
    v = switch_v[...].astype(F32)
    up = (slope_v[...].astype(F32) * (v * jax.nn.sigmoid(v))).astype(BF16)
    for k in range(n_t):
        outs[k][:B, :] = up
    copies[2].wait()
    nc = cols // cp
    for k in range(1, n_t):
        c0 = (ten ^ k) * cols + lax.rem(rep, cp) * nc
        for j in range(nc // 128):
            at = pl.multiple_of(c0 + j * 128, 128)
            outs[k][B + j * nr : B + (j + 1) * nr, :] = exp_v[:, pl.ds(at, 128)]
    for copy in copies[3:]:
        copy.wait()


def grads_body(n, act, after, *refs):
    ups, outs = refs[:n], refs[n:]
    up = jnp.concatenate([u[:B, :] for u in ups], axis=0)
    for c in range(0, act.shape[1], G):
        g = dot(up, act[:, c : c + G])
        for k in range(n):
            outs[k][:, c : c + G] = g[k * B : (k + 1) * B].astype(outs[k].dtype)


def bundle_body(n_t, keep, after, lines, *refs):
    parts, out = refs[: n_t - 1], refs[n_t - 1]
    n = parts[0].shape[0] - B
    for k in range(n_t - 1):
        out[k * n : (k + 1) * n, :] = parts[k][B:, :]
    blocks = lines.shape[1]
    rows = jnp.concatenate([lines[...].astype(F32), jnp.zeros((keep, 128 - blocks), F32)], axis=1)
    out[(n_t - 1) * n :, :] = jnp.concatenate([rows, jnp.zeros((16 - keep, 128), F32)], axis=0).astype(BF16)


def join_body(n, *refs):
    first, *rest, second = refs[1 : n + 1]
    for i, ref in enumerate([first, second, *rest]):
        refs[-1][i] = ref[...]


def own_body(keep, lines, small, p_ref, a_ref):
    blocks, nb = lines.shape[1], G // B
    rows = jnp.concatenate([lines[...].astype(F32), jnp.zeros((keep, 128 - blocks), F32)], axis=1)
    lane = lax.broadcasted_iota(jnp.int32, (nb * keep, 2 * B), 1).astype(F32)
    for g in range(blocks // nb):
        num = jnp.concatenate(
            [jnp.broadcast_to(rows[:, g * nb + j : g * nb + j + 1], (keep, 2 * B)) for j in range(nb)], axis=0
        )
        hot = jnp.concatenate(
            [jnp.where(lane == num, 1.0, 0.0), jnp.where(lane - B == num, 1.0, 0.0)], axis=0
        ).astype(BF16)
        a_ref[g * B : (g + 1) * B, :] = dot(hot, small[:, : 2 * B]).astype(BF16)
    rows = jnp.concatenate([rows] * (2 * B // keep), axis=0).T
    freq = lax.broadcasted_iota(jnp.int32, (B, 2 * B), 0).astype(F32)
    block = (lax.broadcasted_iota(jnp.int32, (1, 2 * B), 1) // keep) % nb
    term = lax.broadcasted_iota(jnp.int32, (B, 2 * B), 1) // (B // 2)
    for g in range(blocks // nb):
        num = rows[g * nb : g * nb + 1]
        for j in range(1, nb):
            num = jnp.where(block == j, rows[g * nb + j : g * nb + j + 1], num)
        hot = jnp.where(freq == num, 1.0, 0.0).astype(BF16)
        y = dot(small[:, 2 * B : 3 * B], hot)
        p = jnp.where(term == 3, 0.0, jnp.where(term == 1, y[B:], y[:B]))
        p_ref[:, g * 2 * B : (g + 1) * 2 * B] = p.astype(BF16)


def kept_body(ks, n_t, keep, vel, a_ref, tab, after, *refs):
    keep_rows(ks, n_t, keep, vel, a_ref, tab, refs[: len(ks)], *refs[-2:])


def keep_rows(ks, n_t, keep, vel, a_ref, tab, grads, send_ref, own_ref):
    cols = grads[0].shape[1]
    ng = cols // G
    lane_block = lax.broadcasted_iota(jnp.int32, (keep, G), 1) // B
    sel = []
    for n, k in enumerate(ks):
        c0 = (lax.axis_index("tensor") ^ k) * cols
        for i in range(ng):
            at = pl.multiple_of(c0 + i * G, G)
            moment = momentum_decay * vel[:, pl.ds(at, G)] + grads[n][:, i * G : (i + 1) * G].astype(F32)
            hi, lo = split(moment)
            y = dot(a_ref[pl.ds(pl.multiple_of(at // (G // B), B), B), :], jnp.concatenate([hi, lo], axis=0))
            y = y[: B // 2] + y[B // 2 :]
            got = y[:keep]
            for j in range(1, G // B):
                got = jnp.where(lane_block == j, y[j * keep : (j + 1) * keep], got)
            sel.append(got)
    hi, lo = split(jnp.concatenate(sel, axis=0))
    n = len(ks) * ng * keep
    y = dot(jnp.concatenate([hi, lo], axis=0), fwd(tab, 0))
    kept = (y[:n] + y[n:] + dot(hi, fwd(tab, 1))).astype(BF16)
    q = dot(kept, inv(tab, 0)) + dot(kept, inv(tab, 1))
    for n, k in enumerate(ks):
        c0 = pl.multiple_of((lax.axis_index("tensor") ^ k) * cols, G)
        part = jnp.concatenate([q[(n * ng + i) * keep : (n * ng + i + 1) * keep] for i in range(ng)], axis=1)
        own_ref[:, pl.ds(c0, cols)] = part
        send_ref[:, pl.ds(c0, cols)] = part.astype(BF16)


def return_body(n_t, keep, vel, p_ref, q, mask, tally, *refs):
    grads, (new_ref, w_ref, held, sems, mask_s, tally_s, small_sems) = refs[:n_t], refs[n_t:]
    fetches = [
        pltpu.make_async_copy(src, dst, small_sems.at[i])
        for i, (src, dst) in enumerate([(mask, mask_s), (tally, tally_s)])
    ]
    for copy in fetches:
        copy.start()
    cols = grads[0].shape[1]
    ng = cols // G
    lane_block = lax.broadcasted_iota(jnp.int32, (keep, G), 1) // B
    copies = []
    for k in range(n_t):
        c0 = pl.multiple_of((lax.axis_index("tensor") ^ k) * cols, G)
        for i in range(ng):
            at = pl.multiple_of(c0 + i * G, G)
            own = q[:, pl.ds(at, G)]
            spread = jnp.concatenate(
                [jnp.where(lane_block == j, own, 0.0) for j in range(G // B)], axis=0
            )
            hi, lo = split(spread)
            w = jnp.concatenate([hi, hi, lo, jnp.zeros_like(lo)], axis=0)
            back = dot(p_ref[:, pl.ds(pl.multiple_of(at // 2, 2 * B), 2 * B)], w)
            moment = momentum_decay * vel[:, pl.ds(at, G)] + grads[k][:, i * G : (i + 1) * G].astype(F32)
            held[:, pl.ds(at, G)] = moment - back
        cut = pl.ds(c0, cols)
        copies.append(pltpu.make_async_copy(held.at[:, cut], new_ref.at[:, cut], sems.at[k]))
        copies[-1].start()
    for copy in fetches:
        copy.wait()
    n_r = mask_s.shape[0]
    total, alive = jnp.float32(0), jnp.float32(0)
    for r in range(n_r):
        m = mask_s[r].astype(F32)
        total = total + m * tally_s[r].astype(F32)
        alive = alive + m
    half = n_r // 2
    place = (lax.broadcasted_iota(jnp.int32, (8, 2 * B), 1) // keep) % half
    scale = jnp.full((8, 2 * B), alive) / jnp.full((8, 2 * B), total)
    for h in range(2):
        w = jnp.zeros((8, 2 * B), F32)
        for i in range(half):
            r = lax.axis_index("replica") ^ (2 * i + h)
            w = jnp.where(place == i, mask_s[r].astype(F32) * tally_s[r].astype(F32), w)
        w_ref[h] = w * scale
    for copy in copies:
        copy.wait()


def places_body(keep, w_ref, small, bundles, *p_refs):
    n_r, last = bundles.shape[0], bundles.shape[1] - 16
    half, nb = n_r // 2, G // B
    rep = lax.axis_index("replica")
    freq = lax.broadcasted_iota(jnp.int32, (B, 2 * B), 0).astype(F32)
    lane = lax.broadcasted_iota(jnp.int32, (1, 2 * B), 1)
    block = lane // (half * keep)
    for h in range(2):
        hi_ref, lo_ref = p_refs[2 * h : 2 * h + 2]
        w = w_ref[h, :1, :]
        rows = [bundles[rep ^ (2 * i + h), last:, :].astype(F32)[:keep] for i in range(half)]
        rows = jnp.concatenate(rows * nb, axis=0).T
        for g in range(hi_ref.shape[1] // (2 * B)):
            num = rows[g * nb : g * nb + 1]
            for j in range(1, nb):
                num = jnp.where(block == j, rows[g * nb + j : g * nb + j + 1], num)
            hot = jnp.where(freq == num, 1.0, 0.0).astype(BF16)
            y = dot(small[:, 2 * B : 3 * B], hot)
            hi, lo = split((y[:B] + y[B:]) * w)
            hi_ref[:, g * 2 * B : (g + 1) * 2 * B] = hi
            lo_ref[:, g * 2 * B : (g + 1) * 2 * B] = lo


def spread_rows(p_hi, p_lo, own, ships, g):
    half, keep = ships.shape[0] + 1, ships.shape[1]
    cut = slice(g * G, (g + 1) * G)
    lane_block = lax.broadcasted_iota(jnp.int32, (half * keep, G), 1) // B
    s = [own[:, cut].astype(F32)] + [ships[i, :, cut].astype(F32) for i in range(half - 1)]
    s = jnp.concatenate(s, axis=0)
    w = jnp.concatenate(
        [jnp.where(lane_block == j, s, 0.0).astype(BF16) for j in range(G // B)], axis=0
    )
    cut = slice(g * 2 * B, (g + 1) * 2 * B)
    y = dot(jnp.concatenate([p_hi[:, cut], p_lo[:, cut]], axis=0), w)
    return y[:B] + y[B:]


def half_update_body(p_hi, p_lo, own, others, out):
    for g in range(out.shape[0] // B):
        out[g * B : (g + 1) * B, :] = spread_rows(p_hi, p_lo, own, others, g)


def update_body(chunk, half_sum, p_hi, p_lo, own, others, out, held, sems):
    ng = half_sum.shape[0] // B
    copies = []
    for c in range(0, ng, chunk):
        for g in range(c, c + chunk):
            held[:, g * G : (g + 1) * G] = half_sum[g * B : (g + 1) * B, :] + spread_rows(p_hi, p_lo, own, others, g)
        cut = pl.ds(c * G, chunk * G)
        copies.append(pltpu.make_async_copy(held.at[:, cut], out.at[:, cut], sems.at[c // chunk]))
        copies[-1].start()
    for copy in copies:
        copy.wait()


def input_grad_body(n_t, n_r, cp, exp_ref, bundles, *refs):
    ups, (out, held) = refs[:n_t], refs[n_t:]
    cols = out.shape[1]
    held[:B, :] = exp_ref[:, pl.ds(pl.multiple_of(lax.axis_index("tensor") * cols, 128), cols)]
    nc = cols // cp
    nr = B // (n_r // cp)
    tiles = nc // 128
    for r in range(n_r):
        r0, c0 = (r // cp) * nr, (r % cp) * nc
        for k in range(1, n_t):
            for j in range(tiles):
                at = ((k - 1) * tiles + j) * nr
                held[k * B + r0 : k * B + r0 + nr, c0 + j * 128 : c0 + (j + 1) * 128] = bundles[r, at : at + nr, :]
    up = jnp.concatenate([u[:B, :] for u in ups], axis=0).T
    for c in range(0, cols, G):
        out[:, c : c + G] = dot(up, held[:, c : c + G]).astype(BF16)


def per_device(n_t, n_r, act, switch, slope, exp, vel, lines, mask, tally):
    cols = act.shape[1]
    width = exp.shape[1]
    tok = act.shape[0]
    keep = lines.shape[3]
    blocks = width // B
    groups = width // G
    cp = 2
    rp = n_r // cp
    half = n_r // 2
    tab, small = constants()
    def trade(x, k):
        return lax.ppermute(x, "tensor", [(i, i ^ k) for i in range(n_t)])

    order = [*range(2, n_t), 1]

    def swap(x, m):
        return lax.ppermute(x, "replica", [(i, i ^ m) for i in range(n_r)])

    own = lines[0, 0].T
    tiles = cols // cp // 128
    nr = B // rp
    *parts, act, own, small = call(
        functools.partial(first_body, n_t, cp, cols, nr),
        [near((B, tok))]
        + [near((B + tiles * nr, 128))] * (n_t - 1)
        + [near(act.shape), near(own.shape, jnp.int32), near(small.shape)],
        (far(switch.T), far(slope.T), far(exp), far(act), far(own), far(small)),
        [ANY] * 6,
        [VM] * (n_t + 3),
        scratch=[
            pltpu.VMEM((B, tok), BF16),
            pltpu.VMEM((B, tok), BF16),
            pltpu.VMEM((nr, width), BF16),
            pltpu.SemaphoreType.DMA((6,)),
        ],
        nbytes=act.size * 4 + nr * width * 2,
        name="up_grads",
    )
    got = {k: trade(parts[k], k) for k in order}
    parts = [parts[0]] + [got[k] for k in range(1, n_t)]

    p_own, a_own = call(
        functools.partial(own_body, keep),
        [near((B, groups * 2 * B)), near((groups * B, 2 * B))],
        (own, small),
        [VM, VM],
        [VM, VM],
        name="own_places",
    )

    def grads_of(ks, after):
        return call(
            functools.partial(grads_body, len(ks)),
            [near((B, cols), BF16 if k else F32) for k in ks],
            (act, after, *[parts[k] for k in ks]),
            [VM, ANY] + [VM] * len(ks),
            [VM] * len(ks),
            name="weight_grads",
        )

    grads = {}
    for k in order[:-1]:
        (grads[k],) = grads_of([k], act)
    made, grads[0] = grads_of([order[-1], 0], a_own)
    grads[order[-1]] = made
    grads.update({k: trade(grads[k], k) for k in order})

    bundle = call(
        functools.partial(bundle_body, n_t, keep),
        near(((n_t - 1) * tiles * nr + 16, 128)),
        (made, own, *parts[1:]),
        [ANY] + [VM] * n_t,
        VM,
        name="bundle",
    )
    bundles = lax.all_gather(bundle, "replica", axis=0)

    rows = []
    for ks in ([k for k in range(n_t) if k != n_t - 1], [n_t - 1]):
        n = len(ks)
        rows = call(
            functools.partial(kept_body, ks, n_t, keep),
            [near((keep, width)), near((keep, width), F32)],
            (vel[0], a_own, tab, bundles, *[grads[k] for k in ks], *rows),
            [VM] * 3 + [ANY] + [VM] * (n + len(rows)),
            [VM] * 2,
            flops=6 * B * B * cols * n,
            nbytes=B * cols * 6 * n,
            name="kept_rows",
            alias={4 + n: 0, 5 + n: 1} if rows else {},
        )
    ship, q_own = rows

    new, shares = call(
        functools.partial(return_body, n_t, keep),
        [jax.ShapeDtypeStruct((B, width), F32), near((2, 8, 2 * B), F32)],
        (vel[0], p_own, q_own, far(mask), far(tally), *[grads[k] for k in range(n_t)]),
        [VM] * 3 + [ANY] * 2 + [VM] * n_t,
        [ANY, VM],
        scratch=[
            pltpu.VMEM((B, width), F32),
            pltpu.SemaphoreType.DMA((n_t,)),
            pltpu.SMEM((n_r,), jnp.int32),
            pltpu.SMEM((n_r,), jnp.int32),
            pltpu.SemaphoreType.DMA((2,)),
        ],
        flops=6 * B * B * width,
        nbytes=B * width * 10,
        name="new_momentums",
    )
    places = call(
        functools.partial(places_body, keep),
        [near((B, blocks * half * keep))] * 4,
        (shares, small, bundles),
        [VM] * 3,
        [VM] * 4,
        name="places",
    )
    input_grad = call(
        functools.partial(input_grad_body, n_t, n_r, cp),
        jax.ShapeDtypeStruct((tok, cols), BF16),
        (exp, bundles, *parts),
        [VM] * (2 + n_t),
        VM,
        scratch=[pltpu.VMEM((n_t * B, cols), BF16)],
        flops=2 * tok * n_t * B * cols,
        nbytes=(n_t * B * cols + tok * cols) * 2,
        name="input_grads",
    )

    ships = [ship] + [swap(ship, 2 * i) for i in range(1, half)]
    other_own = swap(ship, 1)
    others = call(
        functools.partial(join_body, half - 1),
        near((half - 1, keep, width)),
        (other_own, ships[1], *ships[3:], ships[2], far(new), far(input_grad), places[0]),
        [ANY] + [VM] * (half - 1) + [ANY] * 3,
        VM,
        name="join_kept",
    )
    other = swap(others, 1)
    half_sum = call(
        half_update_body,
        near((groups * B, G), F32),
        (*places[:2], ship, others),
        [VM] * 4,
        VM,
        name="half_updates",
    )
    chunk = 2 if groups % 2 == 0 else 1
    update = call(
        functools.partial(update_body, chunk),
        jax.ShapeDtypeStruct((B, width), F32),
        (half_sum, *places[2:], other_own, other),
        [VM] * 5,
        ANY,
        scratch=[
            pltpu.VMEM((B, width), F32),
            pltpu.SemaphoreType.DMA((groups // chunk,)),
        ],
        flops=8 * B * G * width,
        nbytes=B * width * 8,
        name="updates",
    )
    return input_grad, new[None], update


def per_device_plain(
    projection_inputs,
    switch_logits_raw,
    inner_neuron_slope,
    expansion_matrix,
    velocity_buffer,
    sent_spectral_lines,
    participant_mask,
    token_tallies,
):
    highest = lax.Precision.HIGHEST
    up_grad = (
        inner_neuron_slope.astype(jnp.float32) * jax.nn.silu(switch_logits_raw.astype(jnp.float32))
    ).astype(jnp.bfloat16)
    partial_terms = jnp.dot(up_grad, expansion_matrix, preferred_element_type=jnp.float32)
    input_grad = lax.psum_scatter(partial_terms, "tensor", scatter_dimension=1, tiled=True).astype(
        jnp.bfloat16
    )
    grad_w = lax.dot_general(
        up_grad,
        lax.all_gather(projection_inputs, "tensor", axis=1, tiled=True),
        (((0,), (0,)), ((), ())),
        preferred_element_type=jnp.float32,
    )
    row_total_count = expansion_matrix.shape[0] // 64
    col_count = expansion_matrix.shape[1] // 64
    moment = momentum_decay * velocity_buffer[0] + grad_w
    cosines = cosine_table()
    blocks = moment.reshape(row_total_count, 64, col_count, 64).transpose(0, 2, 1, 3)
    coefficients = jnp.einsum("fa,ijab,gb->ijfg", cosines, blocks, cosines, precision=highest)
    freq_ids = jnp.arange(64, dtype=jnp.int32)
    own_rows = sent_spectral_lines[0]
    chosen = (own_rows[..., None] == freq_ids).astype(jnp.float32)
    shipped = jnp.einsum("ijkf,ijfg->ijkg", chosen, coefficients, precision=highest).astype(
        jnp.bfloat16
    )
    spectrum = jnp.einsum("ijkf,ijkg->ijfg", chosen, shipped.astype(jnp.float32), precision=highest)
    returned = jnp.einsum("fa,ijfg,gb->ijab", cosines, spectrum, cosines, precision=highest)
    new_moment = moment - returned.transpose(0, 2, 1, 3).reshape(moment.shape)
    worker_burdens = participant_mask.astype(jnp.float32) * token_tallies.astype(jnp.float32)
    worker_fractions = worker_burdens * (
        jnp.sum(participant_mask.astype(jnp.float32)) / jnp.sum(worker_burdens)
    )
    myself = lax.axis_index("replica")
    combined = lax.psum(worker_fractions[myself] * spectrum, "replica")
    update = jnp.einsum("fa,ijfg,gb->ijab", cosines, combined, cosines, precision=highest)
    update = update.transpose(0, 2, 1, 3).reshape(moment.shape)
    return (input_grad, new_moment[None], update)


def solution(mesh):
    n_t, n_r = mesh.shape["tensor"], mesh.shape["replica"]

    def device(*args):
        act, exp, lines = args[0], args[3], args[5]
        fits = (
            act.shape[1] % G == 0
            and act.shape[0] % 128 == 0
            and exp.shape[0] == B
            and lines.shape[3] == 8
            and n_r == 8
            and n_t >= 2
            and n_t & (n_t - 1) == 0
        )
        if not fits:
            return per_device_plain(*args)
        return per_device(n_t, n_r, *args)

    return jax.shard_map(
        device,
        mesh=mesh,
        in_specs=(
            P("replica", "tensor"),
            P("replica", "tensor"),
            P("replica", "tensor"),
            P("tensor", None),
            P("replica", "tensor", None),
            P("replica", "tensor", None, None),
            P(),
            P(),
        ),
        out_specs=(P("replica", "tensor"), P("replica", "tensor", None), P("tensor", None)),
        check_vma=False,
    )
```

```python
import functools

import jax
import jax.numpy as jnp
import numpy as np
from jax import lax
from jax.experimental import pallas as pl
from jax.experimental.pallas import tpu as pltpu
from jax.sharding import PartitionSpec as P

momentum_decay = 0.9
B = 64
G = 256
F32 = jnp.float32
BF16 = jnp.bfloat16
VMEM_LIMIT = 24 * 1024 * 1024

VM = pl.BlockSpec(memory_space=pltpu.VMEM)
SM = pl.BlockSpec(memory_space=pltpu.SMEM)
ANY = pl.BlockSpec(memory_space=pl.ANY)


def cosine_table():
    freqs = jnp.arange(64, dtype=jnp.float32)[:, None]
    places = jnp.arange(64, dtype=jnp.float32)[None, :]
    cosines = jnp.cos(jnp.pi * (places + 0.5) * freqs / 64.0) * jnp.sqrt(2.0 / 64.0)
    return cosines.at[0].multiply(jnp.sqrt(0.5))


def cosine_np():
    f = np.arange(B)[:, None]
    a = np.arange(B)[None, :]
    c = np.cos(np.pi * (a + 0.5) * f / B) * np.sqrt(2.0 / B)
    c[0] *= np.sqrt(0.5)
    return c


def halves(c):
    hi = np.asarray(c, dtype=np.float32).astype(jnp.bfloat16)
    lo = (np.asarray(c, np.float64) - hi.astype(np.float64)).astype(np.float32).astype(jnp.bfloat16)
    return hi, lo


def constants():
    hi, lo = halves(cosine_np())
    eye = np.eye(G // B)
    kron = lambda x: np.kron(eye, np.asarray(x, np.float32)).astype(jnp.bfloat16)
    small = np.zeros((2 * B, 4 * B), jnp.bfloat16)
    for i, x in enumerate((hi, lo)):
        rows = slice(i * B, (i + 1) * B)
        small[rows, :B], small[rows, B : 2 * B], small[rows, 2 * B : 3 * B] = x, x, x.T
    return jnp.asarray(np.concatenate([kron(x) for x in (hi.T, lo.T, hi, lo)], axis=0)), jnp.asarray(small)


def fwd(tab, i):
    return tab[i * G : (i + 1) * G, :]


def inv(tab, i):
    return tab[(2 + i) * G : (3 + i) * G, :]


def dot(a, b):
    return jnp.dot(a, b, preferred_element_type=F32)


def split(x):
    hi = x.astype(BF16)
    return hi, (x - hi.astype(F32)).astype(BF16)


def near(shape, dtype=BF16):
    return pltpu.VMEM(shape, dtype)


def far(x):
    return pltpu.with_memory_space_constraint(x, pltpu.HBM)


def call(body, out_shape, ins, in_specs, out_specs, scratch=(), flops=0, nbytes=0, name=None, alias={}):
    return pl.pallas_call(
        body,
        out_shape=out_shape,
        in_specs=in_specs,
        out_specs=out_specs,
        scratch_shapes=scratch,
        input_output_aliases=alias,
        compiler_params=pltpu.CompilerParams(vmem_limit_bytes=VMEM_LIMIT),
        cost_estimate=pl.CostEstimate(flops=flops, bytes_accessed=nbytes, transcendentals=0),
        name=name,
    )(*ins)


def first_body(n_t, cp, cols, nr, switch, slope, exp_ref, act, lines, small, *refs):
    outs, (act_out, lines_out, small_out) = refs[:n_t], refs[n_t : n_t + 3]
    switch_v, slope_v, exp_v, sems = refs[n_t + 3 :]
    rep, ten = lax.axis_index("replica"), lax.axis_index("tensor")
    r0 = pl.multiple_of((rep // cp) * nr, nr)
    copies = [
        pltpu.make_async_copy(src, dst, sems.at[i])
        for i, (src, dst) in enumerate(
            [
                (switch, switch_v),
                (slope, slope_v),
                (exp_ref.at[pl.ds(r0, nr), :], exp_v),
                (act, act_out),
                (lines, lines_out),
                (small, small_out),
            ]
        )
    ]
    for copy in copies:
        copy.start()
    copies[0].wait()
    copies[1].wait()
    v = switch_v[...].astype(F32)
    up = (slope_v[...].astype(F32) * (v * jax.nn.sigmoid(v))).astype(BF16)
    for k in range(n_t):
        outs[k][:B, :] = up
    copies[2].wait()
    nc = cols // cp
    for k in range(1, n_t):
        c0 = (ten ^ k) * cols + lax.rem(rep, cp) * nc
        for j in range(nc // 128):
            at = pl.multiple_of(c0 + j * 128, 128)
            outs[k][B + j * nr : B + (j + 1) * nr, :] = exp_v[:, pl.ds(at, 128)]
    for copy in copies[3:]:
        copy.wait()


def grads_body(n, act, after, *refs):
    ups, outs = refs[:n], refs[n:]
    up = jnp.concatenate([u[:B, :] for u in ups], axis=0)
    for c in range(0, act.shape[1], G):
        g = dot(up, act[:, c : c + G])
        for k in range(n):
            outs[k][:, c : c + G] = g[k * B : (k + 1) * B].astype(outs[k].dtype)


def bundle_body(n_t, keep, after, lines, *refs):
    parts, out = refs[: n_t - 1], refs[n_t - 1]
    n = parts[0].shape[0] - B
    for k in range(n_t - 1):
        out[k * n : (k + 1) * n, :] = parts[k][B:, :]
    blocks = lines.shape[1]
    rows = jnp.concatenate([lines[...].astype(F32), jnp.zeros((keep, 128 - blocks), F32)], axis=1)
    out[(n_t - 1) * n :, :] = jnp.concatenate([rows, jnp.zeros((16 - keep, 128), F32)], axis=0).astype(BF16)


def join_body(n, *refs):
    for i, ref in enumerate(refs[1 : n + 1]):
        refs[-1][i] = ref[...]


def own_body(keep, lines, small, p_ref, a_ref):
    blocks, nb = lines.shape[1], G // B
    rows = jnp.concatenate([lines[...].astype(F32), jnp.zeros((keep, 128 - blocks), F32)], axis=1)
    lane = lax.broadcasted_iota(jnp.int32, (nb * keep, 2 * B), 1).astype(F32)
    for g in range(blocks // nb):
        num = jnp.concatenate(
            [jnp.broadcast_to(rows[:, g * nb + j : g * nb + j + 1], (keep, 2 * B)) for j in range(nb)], axis=0
        )
        hot = jnp.concatenate(
            [jnp.where(lane == num, 1.0, 0.0), jnp.where(lane - B == num, 1.0, 0.0)], axis=0
        ).astype(BF16)
        a_ref[g * B : (g + 1) * B, :] = dot(hot, small[:, : 2 * B]).astype(BF16)
    rows = jnp.concatenate([rows] * (2 * B // keep), axis=0).T
    freq = lax.broadcasted_iota(jnp.int32, (B, 2 * B), 0).astype(F32)
    block = (lax.broadcasted_iota(jnp.int32, (1, 2 * B), 1) // keep) % nb
    term = lax.broadcasted_iota(jnp.int32, (B, 2 * B), 1) // (B // 2)
    for g in range(blocks // nb):
        num = rows[g * nb : g * nb + 1]
        for j in range(1, nb):
            num = jnp.where(block == j, rows[g * nb + j : g * nb + j + 1], num)
        hot = jnp.where(freq == num, 1.0, 0.0).astype(BF16)
        y = dot(small[:, 2 * B : 3 * B], hot)
        p = jnp.where(term == 3, 0.0, jnp.where(term == 1, y[B:], y[:B]))
        p_ref[:, g * 2 * B : (g + 1) * 2 * B] = p.astype(BF16)


def kept_body(ks, n_t, keep, vel, a_ref, tab, after, *refs):
    keep_rows(ks, n_t, keep, vel, a_ref, tab, refs[: len(ks)], *refs[-2:])


def keep_rows(ks, n_t, keep, vel, a_ref, tab, grads, send_ref, own_ref):
    cols = grads[0].shape[1]
    ng = cols // G
    lane_block = lax.broadcasted_iota(jnp.int32, (keep, G), 1) // B
    sel = []
    for n, k in enumerate(ks):
        c0 = (lax.axis_index("tensor") ^ k) * cols
        for i in range(ng):
            at = pl.multiple_of(c0 + i * G, G)
            moment = momentum_decay * vel[:, pl.ds(at, G)] + grads[n][:, i * G : (i + 1) * G].astype(F32)
            hi, lo = split(moment)
            y = dot(a_ref[pl.ds(pl.multiple_of(at // (G // B), B), B), :], jnp.concatenate([hi, lo], axis=0))
            y = y[: B // 2] + y[B // 2 :]
            got = y[:keep]
            for j in range(1, G // B):
                got = jnp.where(lane_block == j, y[j * keep : (j + 1) * keep], got)
            sel.append(got)
    hi, lo = split(jnp.concatenate(sel, axis=0))
    n = len(ks) * ng * keep
    y = dot(jnp.concatenate([hi, lo], axis=0), fwd(tab, 0))
    kept = (y[:n] + y[n:] + dot(hi, fwd(tab, 1))).astype(BF16)
    q = dot(kept, inv(tab, 0)) + dot(kept, inv(tab, 1))
    for n, k in enumerate(ks):
        c0 = pl.multiple_of((lax.axis_index("tensor") ^ k) * cols, G)
        part = jnp.concatenate([q[(n * ng + i) * keep : (n * ng + i + 1) * keep] for i in range(ng)], axis=1)
        own_ref[:, pl.ds(c0, cols)] = part
        send_ref[:, pl.ds(c0, cols)] = part.astype(BF16)


def return_body(n_t, keep, vel, p_ref, q, mask, tally, *refs):
    grads, (new_ref, w_ref, held, sems, mask_s, tally_s, small_sems) = refs[:n_t], refs[n_t:]
    fetches = [
        pltpu.make_async_copy(src, dst, small_sems.at[i])
        for i, (src, dst) in enumerate([(mask, mask_s), (tally, tally_s)])
    ]
    for copy in fetches:
        copy.start()
    cols = grads[0].shape[1]
    ng = cols // G
    lane_block = lax.broadcasted_iota(jnp.int32, (keep, G), 1) // B
    copies = []
    for k in range(n_t):
        c0 = pl.multiple_of((lax.axis_index("tensor") ^ k) * cols, G)
        for i in range(ng):
            at = pl.multiple_of(c0 + i * G, G)
            own = q[:, pl.ds(at, G)]
            spread = jnp.concatenate(
                [jnp.where(lane_block == j, own, 0.0) for j in range(G // B)], axis=0
            )
            hi, lo = split(spread)
            w = jnp.concatenate([hi, hi, lo, jnp.zeros_like(lo)], axis=0)
            back = dot(p_ref[:, pl.ds(pl.multiple_of(at // 2, 2 * B), 2 * B)], w)
            moment = momentum_decay * vel[:, pl.ds(at, G)] + grads[k][:, i * G : (i + 1) * G].astype(F32)
            held[:, pl.ds(at, G)] = moment - back
        cut = pl.ds(c0, cols)
        copies.append(pltpu.make_async_copy(held.at[:, cut], new_ref.at[:, cut], sems.at[k]))
        copies[-1].start()
    for copy in fetches:
        copy.wait()
    n_r = mask_s.shape[0]
    total, alive = jnp.float32(0), jnp.float32(0)
    for r in range(n_r):
        m = mask_s[r].astype(F32)
        total = total + m * tally_s[r].astype(F32)
        alive = alive + m
    half = n_r // 2
    place = (lax.broadcasted_iota(jnp.int32, (8, 2 * B), 1) // keep) % half
    scale = jnp.full((8, 2 * B), alive) / jnp.full((8, 2 * B), total)
    for h in range(2):
        w = jnp.zeros((8, 2 * B), F32)
        for i in range(half):
            r = lax.axis_index("replica") ^ (2 * i + h)
            w = jnp.where(place == i, mask_s[r].astype(F32) * tally_s[r].astype(F32), w)
        w_ref[h] = w * scale
    for copy in copies:
        copy.wait()


def places_body(keep, w_ref, small, bundles, *p_refs):
    n_r, last = bundles.shape[0], bundles.shape[1] - 16
    half, nb = n_r // 2, G // B
    rep = lax.axis_index("replica")
    freq = lax.broadcasted_iota(jnp.int32, (B, 2 * B), 0).astype(F32)
    lane = lax.broadcasted_iota(jnp.int32, (1, 2 * B), 1)
    block = lane // (half * keep)
    for h in range(2):
        hi_ref, lo_ref = p_refs[2 * h : 2 * h + 2]
        w = w_ref[h, :1, :]
        rows = [bundles[rep ^ (2 * i + h), last:, :].astype(F32)[:keep] for i in range(half)]
        rows = jnp.concatenate(rows * nb, axis=0).T
        for g in range(hi_ref.shape[1] // (2 * B)):
            num = rows[g * nb : g * nb + 1]
            for j in range(1, nb):
                num = jnp.where(block == j, rows[g * nb + j : g * nb + j + 1], num)
            hot = jnp.where(freq == num, 1.0, 0.0).astype(BF16)
            y = dot(small[:, 2 * B : 3 * B], hot)
            hi, lo = split((y[:B] + y[B:]) * w)
            hi_ref[:, g * 2 * B : (g + 1) * 2 * B] = hi
            lo_ref[:, g * 2 * B : (g + 1) * 2 * B] = lo


def spread_rows(p_hi, p_lo, own, ships, g):
    half, keep = ships.shape[0] + 1, ships.shape[1]
    cut = slice(g * G, (g + 1) * G)
    lane_block = lax.broadcasted_iota(jnp.int32, (half * keep, G), 1) // B
    s = [own[:, cut].astype(F32)] + [ships[i, :, cut].astype(F32) for i in range(half - 1)]
    s = jnp.concatenate(s, axis=0)
    s = s.astype(BF16)
    w = jnp.concatenate(
        [s * jnp.where(lane_block == j, 1.0, 0.0).astype(BF16) for j in range(G // B)], axis=0
    )
    cut = slice(g * 2 * B, (g + 1) * 2 * B)
    y = dot(jnp.concatenate([p_hi[:, cut], p_lo[:, cut]], axis=0), w)
    return y[:B] + y[B:]


def half_update_body(p_hi, p_lo, own, others, out):
    for g in range(out.shape[0] // B):
        out[g * B : (g + 1) * B, :] = spread_rows(p_hi, p_lo, own, others, g)


def update_body(chunk, half_sum, p_hi, p_lo, own, others, out, held, sems):
    ng = half_sum.shape[0] // B
    copies = []
    for c in range(0, ng, chunk):
        for g in range(c, c + chunk):
            held[:, g * G : (g + 1) * G] = half_sum[g * B : (g + 1) * B, :] + spread_rows(p_hi, p_lo, own, others, g)
        cut = pl.ds(c * G, chunk * G)
        copies.append(pltpu.make_async_copy(held.at[:, cut], out.at[:, cut], sems.at[c // chunk]))
        copies[-1].start()
    for copy in copies:
        copy.wait()


def input_grad_body(n_t, n_r, cp, exp_ref, bundles, *refs):
    ups, (out, held) = refs[:n_t], refs[n_t:]
    cols = out.shape[1]
    held[:B, :] = exp_ref[:, pl.ds(pl.multiple_of(lax.axis_index("tensor") * cols, 128), cols)]
    nc = cols // cp
    nr = B // (n_r // cp)
    tiles = nc // 128
    for r in range(n_r):
        r0, c0 = (r // cp) * nr, (r % cp) * nc
        for k in range(1, n_t):
            for j in range(tiles):
                at = ((k - 1) * tiles + j) * nr
                held[k * B + r0 : k * B + r0 + nr, c0 + j * 128 : c0 + (j + 1) * 128] = bundles[r, at : at + nr, :]
    up = jnp.concatenate([u[:B, :] for u in ups], axis=0).T
    for c in range(0, cols, G):
        out[:, c : c + G] = dot(up, held[:, c : c + G]).astype(BF16)


def per_device(n_t, n_r, act, switch, slope, exp, vel, lines, mask, tally):
    cols = act.shape[1]
    width = exp.shape[1]
    tok = act.shape[0]
    keep = lines.shape[3]
    blocks = width // B
    groups = width // G
    cp = 2
    rp = n_r // cp
    half = n_r // 2
    tab, small = constants()
    def trade(x, k):
        return lax.ppermute(x, "tensor", [(i, i ^ k) for i in range(n_t)])

    order = [*range(2, n_t), 1]

    def swap(x, m):
        return lax.ppermute(x, "replica", [(i, i ^ m) for i in range(n_r)])

    own = lines[0, 0].T
    tiles = cols // cp // 128
    nr = B // rp
    *parts, act, own, small = call(
        functools.partial(first_body, n_t, cp, cols, nr),
        [near((B, tok))]
        + [near((B + tiles * nr, 128))] * (n_t - 1)
        + [near(act.shape), near(own.shape, jnp.int32), near(small.shape)],
        (far(switch.T), far(slope.T), far(exp), far(act), far(own), far(small)),
        [ANY] * 6,
        [VM] * (n_t + 3),
        scratch=[
            pltpu.VMEM((B, tok), BF16),
            pltpu.VMEM((B, tok), BF16),
            pltpu.VMEM((nr, width), BF16),
            pltpu.SemaphoreType.DMA((6,)),
        ],
        nbytes=act.size * 4 + nr * width * 2,
        name="up_grads",
    )
    got = {k: trade(parts[k], k) for k in order}
    parts = [parts[0]] + [got[k] for k in range(1, n_t)]

    p_own, a_own = call(
        functools.partial(own_body, keep),
        [near((B, groups * 2 * B)), near((groups * B, 2 * B))],
        (own, small),
        [VM, VM],
        [VM, VM],
        name="own_places",
    )

    def grads_of(ks, after):
        return call(
            functools.partial(grads_body, len(ks)),
            [near((B, cols), BF16 if k else F32) for k in ks],
            (act, after, *[parts[k] for k in ks]),
            [VM, ANY] + [VM] * len(ks),
            [VM] * len(ks),
            name="weight_grads",
        )

    grads = {}
    for k in order[:-1]:
        (grads[k],) = grads_of([k], act)
    made, grads[0] = grads_of([order[-1], 0], a_own)
    grads[order[-1]] = made
    grads.update({k: trade(grads[k], k) for k in order})

    bundle = call(
        functools.partial(bundle_body, n_t, keep),
        near(((n_t - 1) * tiles * nr + 16, 128)),
        (made, own, *parts[1:]),
        [ANY] + [VM] * n_t,
        VM,
        name="bundle",
    )
    bundles = lax.all_gather(bundle, "replica", axis=0)

    rows = []
    for ks in ([k for k in range(n_t) if k != n_t - 1], [n_t - 1]):
        n = len(ks)
        rows = call(
            functools.partial(kept_body, ks, n_t, keep),
            [near((keep, width)), near((keep, width), F32)],
            (vel[0], a_own, tab, bundles, *[grads[k] for k in ks], *rows),
            [VM] * 3 + [ANY] + [VM] * (n + len(rows)),
            [VM] * 2,
            flops=6 * B * B * cols * n,
            nbytes=B * cols * 6 * n,
            name="kept_rows",
            alias={4 + n: 0, 5 + n: 1} if rows else {},
        )
    ship, q_own = rows

    new, shares = call(
        functools.partial(return_body, n_t, keep),
        [jax.ShapeDtypeStruct((B, width), F32), near((2, 8, 2 * B), F32)],
        (vel[0], p_own, q_own, far(mask), far(tally), *[grads[k] for k in range(n_t)]),
        [VM] * 3 + [ANY] * 2 + [VM] * n_t,
        [ANY, VM],
        scratch=[
            pltpu.VMEM((B, width), F32),
            pltpu.SemaphoreType.DMA((n_t,)),
            pltpu.SMEM((n_r,), jnp.int32),
            pltpu.SMEM((n_r,), jnp.int32),
            pltpu.SemaphoreType.DMA((2,)),
        ],
        flops=6 * B * B * width,
        nbytes=B * width * 10,
        name="new_momentums",
    )
    places = call(
        functools.partial(places_body, keep),
        [near((B, blocks * half * keep))] * 4,
        (shares, small, bundles),
        [VM] * 3,
        [VM] * 4,
        name="places",
    )
    input_grad = call(
        functools.partial(input_grad_body, n_t, n_r, cp),
        jax.ShapeDtypeStruct((tok, cols), BF16),
        (exp, bundles, *parts),
        [VM] * (2 + n_t),
        VM,
        scratch=[pltpu.VMEM((n_t * B, cols), BF16)],
        flops=2 * tok * n_t * B * cols,
        nbytes=(n_t * B * cols + tok * cols) * 2,
        name="input_grads",
    )

    ships = [ship] + [swap(ship, 2 * i) for i in range(1, half)]
    other_own = swap(ship, 1)
    others = call(
        functools.partial(join_body, half - 1),
        near((half - 1, keep, width)),
        (other_own, *ships[1:], far(new), far(input_grad), places[0]),
        [ANY] + [VM] * (half - 1) + [ANY] * 3,
        VM,
        name="join_kept",
    )
    other = swap(others, 1)
    half_sum = call(
        half_update_body,
        near((groups * B, G), F32),
        (*places[:2], ship, others),
        [VM] * 4,
        VM,
        name="half_updates",
    )
    chunk = 2 if groups % 2 == 0 else 1
    update = call(
        functools.partial(update_body, chunk),
        jax.ShapeDtypeStruct((B, width), F32),
        (half_sum, *places[2:], other_own, other),
        [VM] * 5,
        ANY,
        scratch=[
            pltpu.VMEM((B, width), F32),
            pltpu.SemaphoreType.DMA((groups // chunk,)),
        ],
        flops=8 * B * G * width,
        nbytes=B * width * 8,
        name="updates",
    )
    return input_grad, new[None], update


def per_device_plain(
    projection_inputs,
    switch_logits_raw,
    inner_neuron_slope,
    expansion_matrix,
    velocity_buffer,
    sent_spectral_lines,
    participant_mask,
    token_tallies,
):
    highest = lax.Precision.HIGHEST
    up_grad = (
        inner_neuron_slope.astype(jnp.float32) * jax.nn.silu(switch_logits_raw.astype(jnp.float32))
    ).astype(jnp.bfloat16)
    partial_terms = jnp.dot(up_grad, expansion_matrix, preferred_element_type=jnp.float32)
    input_grad = lax.psum_scatter(partial_terms, "tensor", scatter_dimension=1, tiled=True).astype(
        jnp.bfloat16
    )
    grad_w = lax.dot_general(
        up_grad,
        lax.all_gather(projection_inputs, "tensor", axis=1, tiled=True),
        (((0,), (0,)), ((), ())),
        preferred_element_type=jnp.float32,
    )
    row_total_count = expansion_matrix.shape[0] // 64
    col_count = expansion_matrix.shape[1] // 64
    moment = momentum_decay * velocity_buffer[0] + grad_w
    cosines = cosine_table()
    blocks = moment.reshape(row_total_count, 64, col_count, 64).transpose(0, 2, 1, 3)
    coefficients = jnp.einsum("fa,ijab,gb->ijfg", cosines, blocks, cosines, precision=highest)
    freq_ids = jnp.arange(64, dtype=jnp.int32)
    own_rows = sent_spectral_lines[0]
    chosen = (own_rows[..., None] == freq_ids).astype(jnp.float32)
    shipped = jnp.einsum("ijkf,ijfg->ijkg", chosen, coefficients, precision=highest).astype(
        jnp.bfloat16
    )
    spectrum = jnp.einsum("ijkf,ijkg->ijfg", chosen, shipped.astype(jnp.float32), precision=highest)
    returned = jnp.einsum("fa,ijfg,gb->ijab", cosines, spectrum, cosines, precision=highest)
    new_moment = moment - returned.transpose(0, 2, 1, 3).reshape(moment.shape)
    worker_burdens = participant_mask.astype(jnp.float32) * token_tallies.astype(jnp.float32)
    worker_fractions = worker_burdens * (
        jnp.sum(participant_mask.astype(jnp.float32)) / jnp.sum(worker_burdens)
    )
    myself = lax.axis_index("replica")
    combined = lax.psum(worker_fractions[myself] * spectrum, "replica")
    update = jnp.einsum("fa,ijfg,gb->ijab", cosines, combined, cosines, precision=highest)
    update = update.transpose(0, 2, 1, 3).reshape(moment.shape)
    return (input_grad, new_moment[None], update)


def solution(mesh):
    n_t, n_r = mesh.shape["tensor"], mesh.shape["replica"]

    def device(*args):
        act, exp, lines = args[0], args[3], args[5]
        fits = (
            act.shape[1] % G == 0
            and act.shape[0] % 128 == 0
            and exp.shape[0] == B
            and lines.shape[3] == 8
            and n_r == 8
            and n_t >= 2
            and n_t & (n_t - 1) == 0
        )
        if not fits:
            return per_device_plain(*args)
        return per_device(n_t, n_r, *args)

    return jax.shard_map(
        device,
        mesh=mesh,
        in_specs=(
            P("replica", "tensor"),
            P("replica", "tensor"),
            P("replica", "tensor"),
            P("tensor", None),
            P("replica", "tensor", None),
            P("replica", "tensor", None, None),
            P(),
            P(),
        ),
        out_specs=(P("replica", "tensor"), P("replica", "tensor", None), P("tensor", None)),
        check_vma=False,
    )
```

```python
import functools

import jax
import jax.numpy as jnp
import numpy as np
from jax import lax
from jax.experimental import pallas as pl
from jax.experimental.pallas import tpu as pltpu
from jax.sharding import PartitionSpec as P

momentum_decay = 0.9
B = 64
G = 256
F32 = jnp.float32
BF16 = jnp.bfloat16
VMEM_LIMIT = 24 * 1024 * 1024

VM = pl.BlockSpec(memory_space=pltpu.VMEM)
SM = pl.BlockSpec(memory_space=pltpu.SMEM)
ANY = pl.BlockSpec(memory_space=pl.ANY)


def cosine_table():
    freqs = jnp.arange(64, dtype=jnp.float32)[:, None]
    places = jnp.arange(64, dtype=jnp.float32)[None, :]
    cosines = jnp.cos(jnp.pi * (places + 0.5) * freqs / 64.0) * jnp.sqrt(2.0 / 64.0)
    return cosines.at[0].multiply(jnp.sqrt(0.5))


def cosine_np():
    f = np.arange(B)[:, None]
    a = np.arange(B)[None, :]
    c = np.cos(np.pi * (a + 0.5) * f / B) * np.sqrt(2.0 / B)
    c[0] *= np.sqrt(0.5)
    return c


def halves(c):
    hi = np.asarray(c, dtype=np.float32).astype(jnp.bfloat16)
    lo = (np.asarray(c, np.float64) - hi.astype(np.float64)).astype(np.float32).astype(jnp.bfloat16)
    return hi, lo


def constants():
    hi, lo = halves(cosine_np())
    eye = np.eye(G // B)
    kron = lambda x: np.kron(eye, np.asarray(x, np.float32)).astype(jnp.bfloat16)
    small = np.zeros((2 * B, 4 * B), jnp.bfloat16)
    for i, x in enumerate((hi, lo)):
        rows = slice(i * B, (i + 1) * B)
        small[rows, :B], small[rows, B : 2 * B], small[rows, 2 * B : 3 * B] = x, x, x.T
    return jnp.asarray(np.concatenate([kron(x) for x in (hi.T, lo.T, hi, lo)], axis=0)), jnp.asarray(small)


def fwd(tab, i):
    return tab[i * G : (i + 1) * G, :]


def inv(tab, i):
    return tab[(2 + i) * G : (3 + i) * G, :]


def dot(a, b):
    return jnp.dot(a, b, preferred_element_type=F32)


def split(x):
    hi = x.astype(BF16)
    return hi, (x - hi.astype(F32)).astype(BF16)


def near(shape, dtype=BF16):
    return pltpu.VMEM(shape, dtype)


def far(x):
    return pltpu.with_memory_space_constraint(x, pltpu.HBM)


def call(body, out_shape, ins, in_specs, out_specs, scratch=(), flops=0, nbytes=0, name=None, alias={}):
    return pl.pallas_call(
        body,
        out_shape=out_shape,
        in_specs=in_specs,
        out_specs=out_specs,
        scratch_shapes=scratch,
        input_output_aliases=alias,
        compiler_params=pltpu.CompilerParams(vmem_limit_bytes=VMEM_LIMIT),
        cost_estimate=pl.CostEstimate(flops=flops, bytes_accessed=nbytes, transcendentals=0),
        name=name,
    )(*ins)


def first_body(n_t, cp, cols, nr, switch, slope, exp_ref, act, lines, small, *refs):
    outs, (act_out, lines_out, small_out) = refs[:n_t], refs[n_t : n_t + 3]
    switch_v, slope_v, exp_v, sems = refs[n_t + 3 :]
    rep, ten = lax.axis_index("replica"), lax.axis_index("tensor")
    r0 = pl.multiple_of((rep // cp) * nr, nr)
    copies = [
        pltpu.make_async_copy(src, dst, sems.at[i])
        for i, (src, dst) in enumerate(
            [
                (switch, switch_v),
                (slope, slope_v),
                (exp_ref.at[pl.ds(r0, nr), :], exp_v),
                (act, act_out),
                (lines, lines_out),
                (small, small_out),
            ]
        )
    ]
    for copy in copies:
        copy.start()
    copies[0].wait()
    copies[1].wait()
    v = switch_v[...].astype(F32)
    up = (slope_v[...].astype(F32) * (v * jax.nn.sigmoid(v))).astype(BF16)
    for k in range(n_t):
        outs[k][:B, :] = up
    copies[2].wait()
    nc = cols // cp
    for k in range(1, n_t):
        c0 = (ten ^ k) * cols + lax.rem(rep, cp) * nc
        for j in range(nc // 128):
            at = pl.multiple_of(c0 + j * 128, 128)
            outs[k][B + j * nr : B + (j + 1) * nr, :] = exp_v[:, pl.ds(at, 128)]
    for copy in copies[3:]:
        copy.wait()


def grads_body(n, act, after, *refs):
    ups, outs = refs[:n], refs[n:]
    up = jnp.concatenate([u[:B, :] for u in ups], axis=0)
    for c in range(0, act.shape[1], G):
        g = dot(up, act[:, c : c + G])
        for k in range(n):
            outs[k][:, c : c + G] = g[k * B : (k + 1) * B].astype(outs[k].dtype)


def bundle_body(n_t, keep, after, lines, *refs):
    parts, out = refs[: n_t - 1], refs[n_t - 1]
    n = parts[0].shape[0] - B
    for k in range(n_t - 1):
        out[k * n : (k + 1) * n, :] = parts[k][B:, :]
    blocks = lines.shape[1]
    rows = jnp.concatenate([lines[...].astype(F32), jnp.zeros((keep, 128 - blocks), F32)], axis=1)
    out[(n_t - 1) * n :, :] = jnp.concatenate([rows, jnp.zeros((16 - keep, 128), F32)], axis=0).astype(BF16)


def join_body(n, *refs):
    for i, ref in enumerate(refs[1 : n + 1]):
        refs[-1][i] = ref[...]


def own_body(keep, lines, small, p_ref, a_ref):
    blocks, nb = lines.shape[1], G // B
    rows = jnp.concatenate([lines[...].astype(F32), jnp.zeros((keep, 128 - blocks), F32)], axis=1)
    lane = lax.broadcasted_iota(jnp.int32, (nb * keep, 2 * B), 1).astype(F32)
    for g in range(blocks // nb):
        num = jnp.concatenate(
            [jnp.broadcast_to(rows[:, g * nb + j : g * nb + j + 1], (keep, 2 * B)) for j in range(nb)], axis=0
        )
        hot = jnp.concatenate(
            [jnp.where(lane == num, 1.0, 0.0), jnp.where(lane - B == num, 1.0, 0.0)], axis=0
        ).astype(BF16)
        a_ref[g * B : (g + 1) * B, :] = dot(hot, small[:, : 2 * B]).astype(BF16)
    rows = jnp.concatenate([rows] * (2 * B // keep), axis=0).T
    freq = lax.broadcasted_iota(jnp.int32, (B, 2 * B), 0).astype(F32)
    block = (lax.broadcasted_iota(jnp.int32, (1, 2 * B), 1) // keep) % nb
    term = lax.broadcasted_iota(jnp.int32, (B, 2 * B), 1) // (B // 2)
    for g in range(blocks // nb):
        num = rows[g * nb : g * nb + 1]
        for j in range(1, nb):
            num = jnp.where(block == j, rows[g * nb + j : g * nb + j + 1], num)
        hot = jnp.where(freq == num, 1.0, 0.0).astype(BF16)
        y = dot(small[:, 2 * B : 3 * B], hot)
        p = jnp.where(term == 3, 0.0, jnp.where(term == 1, y[B:], y[:B]))
        p_ref[:, g * 2 * B : (g + 1) * 2 * B] = p.astype(BF16)


def kept_body(ks, n_t, keep, vel, a_ref, tab, after, *refs):
    keep_rows(ks, n_t, keep, vel, a_ref, tab, refs[: len(ks)], *refs[-2:])


def keep_rows(ks, n_t, keep, vel, a_ref, tab, grads, send_ref, own_ref):
    cols = grads[0].shape[1]
    ng = cols // G
    lane_block = lax.broadcasted_iota(jnp.int32, (keep, G), 1) // B
    sel = []
    for n, k in enumerate(ks):
        c0 = (lax.axis_index("tensor") ^ k) * cols
        for i in range(ng):
            at = pl.multiple_of(c0 + i * G, G)
            moment = momentum_decay * vel[:, pl.ds(at, G)] + grads[n][:, i * G : (i + 1) * G].astype(F32)
            hi, lo = split(moment)
            y = dot(a_ref[pl.ds(pl.multiple_of(at // (G // B), B), B), :], jnp.concatenate([hi, lo], axis=0))
            y = y[: B // 2] + y[B // 2 :]
            got = y[:keep]
            for j in range(1, G // B):
                got = jnp.where(lane_block == j, y[j * keep : (j + 1) * keep], got)
            sel.append(got)
    hi, lo = split(jnp.concatenate(sel, axis=0))
    n = len(ks) * ng * keep
    y = dot(jnp.concatenate([hi, lo], axis=0), fwd(tab, 0))
    kept = (y[:n] + y[n:] + dot(hi, fwd(tab, 1))).astype(BF16)
    q = dot(kept, inv(tab, 0)) + dot(kept, inv(tab, 1))
    for n, k in enumerate(ks):
        c0 = pl.multiple_of((lax.axis_index("tensor") ^ k) * cols, G)
        part = jnp.concatenate([q[(n * ng + i) * keep : (n * ng + i + 1) * keep] for i in range(ng)], axis=1)
        own_ref[:, pl.ds(c0, cols)] = part
        send_ref[:, pl.ds(c0, cols)] = part.astype(BF16)


def return_body(n_t, keep, vel, p_ref, q, mask, tally, *refs):
    grads, (new_ref, w_ref, held, sems, mask_s, tally_s, small_sems) = refs[:n_t], refs[n_t:]
    fetches = [
        pltpu.make_async_copy(src, dst, small_sems.at[i])
        for i, (src, dst) in enumerate([(mask, mask_s), (tally, tally_s)])
    ]
    for copy in fetches:
        copy.start()
    cols = grads[0].shape[1]
    ng = cols // G
    lane_block = lax.broadcasted_iota(jnp.int32, (keep, G), 1) // B
    copies = []
    for k in range(n_t):
        c0 = pl.multiple_of((lax.axis_index("tensor") ^ k) * cols, G)
        for i in range(ng):
            at = pl.multiple_of(c0 + i * G, G)
            own = q[:, pl.ds(at, G)]
            spread = jnp.concatenate(
                [jnp.where(lane_block == j, own, 0.0) for j in range(G // B)], axis=0
            )
            hi, lo = split(spread)
            w = jnp.concatenate([hi, hi, lo, jnp.zeros_like(lo)], axis=0)
            back = dot(p_ref[:, pl.ds(pl.multiple_of(at // 2, 2 * B), 2 * B)], w)
            moment = momentum_decay * vel[:, pl.ds(at, G)] + grads[k][:, i * G : (i + 1) * G].astype(F32)
            held[:, pl.ds(at, G)] = moment - back
        cut = pl.ds(c0, cols)
        copies.append(pltpu.make_async_copy(held.at[:, cut], new_ref.at[:, cut], sems.at[k]))
        copies[-1].start()
    for copy in fetches:
        copy.wait()
    n_r = mask_s.shape[0]
    total, alive = jnp.float32(0), jnp.float32(0)
    for r in range(n_r):
        m = mask_s[r].astype(F32)
        total = total + m * tally_s[r].astype(F32)
        alive = alive + m
    half = n_r // 2
    place = (lax.broadcasted_iota(jnp.int32, (8, 2 * B), 1) // keep) % half
    scale = jnp.full((8, 2 * B), alive) / jnp.full((8, 2 * B), total)
    for h in range(2):
        w = jnp.zeros((8, 2 * B), F32)
        for i in range(half):
            r = lax.axis_index("replica") ^ (2 * i + h)
            w = jnp.where(place == i, mask_s[r].astype(F32) * tally_s[r].astype(F32), w)
        w_ref[h] = w * scale
    for copy in copies:
        copy.wait()


def places_body(keep, w_ref, small, bundles, *p_refs):
    n_r, last = bundles.shape[0], bundles.shape[1] - 16
    half, nb = n_r // 2, G // B
    rep = lax.axis_index("replica")
    freq = lax.broadcasted_iota(jnp.int32, (B, 2 * B), 0).astype(F32)
    lane = lax.broadcasted_iota(jnp.int32, (1, 2 * B), 1)
    block = lane // (half * keep)
    for h in range(2):
        hi_ref, lo_ref = p_refs[2 * h : 2 * h + 2]
        w = w_ref[h, :1, :]
        rows = [bundles[rep ^ (2 * i + h), last:, :].astype(F32)[:keep] for i in range(half)]
        rows = jnp.concatenate(rows * nb, axis=0).T
        for g in range(hi_ref.shape[1] // (2 * B)):
            num = rows[g * nb : g * nb + 1]
            for j in range(1, nb):
                num = jnp.where(block == j, rows[g * nb + j : g * nb + j + 1], num)
            hot = jnp.where(freq == num, 1.0, 0.0).astype(BF16)
            y = dot(small[:, 2 * B : 3 * B], hot)
            hi, lo = split((y[:B] + y[B:]) * w)
            hi_ref[:, g * 2 * B : (g + 1) * 2 * B] = hi
            lo_ref[:, g * 2 * B : (g + 1) * 2 * B] = lo


def spread_rows(p_hi, p_lo, own, ships, g):
    half, keep = ships.shape[0] + 1, ships.shape[1]
    cut = slice(g * G, (g + 1) * G)
    lane_block = lax.broadcasted_iota(jnp.int32, (half * keep, G), 1) // B
    s = [own[:, cut].astype(F32)] + [ships[i, :, cut].astype(F32) for i in range(half - 1)]
    s = jnp.concatenate(s, axis=0)
    w = jnp.concatenate(
        [jnp.where(lane_block == j, s, 0.0).astype(BF16) for j in range(G // B)], axis=0
    )
    cut = slice(g * 2 * B, (g + 1) * 2 * B)
    y = dot(jnp.concatenate([p_hi[:, cut], p_lo[:, cut]], axis=0), w)
    return y[:B] + y[B:]


def half_update_body(p_hi, p_lo, own, others, out):
    for g in range(out.shape[0] // B):
        out[g * B : (g + 1) * B, :] = spread_rows(p_hi, p_lo, own, others, g)


def update_body(chunk, half_sum, p_hi, p_lo, own, others, out, held, sems):
    ng = half_sum.shape[0] // B
    copies = []
    for c in range(0, ng, chunk):
        for g in range(c, c + chunk):
            held[:, g * G : (g + 1) * G] = half_sum[g * B : (g + 1) * B, :] + spread_rows(p_hi, p_lo, own, others, g)
        cut = pl.ds(c * G, chunk * G)
        copies.append(pltpu.make_async_copy(held.at[:, cut], out.at[:, cut], sems.at[c // chunk]))
        copies[-1].start()
    for copy in copies:
        copy.wait()


def input_grad_body(n_t, n_r, cp, exp_ref, bundles, *refs):
    ups, (out, held) = refs[:n_t], refs[n_t:]
    cols = out.shape[1]
    held[:B, :] = exp_ref[:, pl.ds(pl.multiple_of(lax.axis_index("tensor") * cols, 128), cols)]
    nc = cols // cp
    nr = B // (n_r // cp)
    tiles = nc // 128
    for r in range(n_r):
        r0, c0 = (r // cp) * nr, (r % cp) * nc
        for k in range(1, n_t):
            for j in range(tiles):
                at = ((k - 1) * tiles + j) * nr
                held[k * B + r0 : k * B + r0 + nr, c0 + j * 128 : c0 + (j + 1) * 128] = bundles[r, at : at + nr, :]
    up = jnp.concatenate([u[:B, :] for u in ups], axis=0).T
    for c in range(0, cols, G):
        out[:, c : c + G] = dot(up, held[:, c : c + G]).astype(BF16)


def per_device(n_t, n_r, act, switch, slope, exp, vel, lines, mask, tally):
    cols = act.shape[1]
    width = exp.shape[1]
    tok = act.shape[0]
    keep = lines.shape[3]
    blocks = width // B
    groups = width // G
    cp = 2
    rp = n_r // cp
    half = n_r // 2
    tab, small = constants()
    def trade(x, k):
        return lax.ppermute(x, "tensor", [(i, i ^ k) for i in range(n_t)])

    order = [*range(2, n_t), 1]

    def swap(x, m):
        return lax.ppermute(x, "replica", [(i, i ^ m) for i in range(n_r)])

    own = lines[0, 0].T
    tiles = cols // cp // 128
    nr = B // rp
    *parts, act, own, small = call(
        functools.partial(first_body, n_t, cp, cols, nr),
        [near((B, tok))]
        + [near((B + tiles * nr, 128))] * (n_t - 1)
        + [near(act.shape), near(own.shape, jnp.int32), near(small.shape)],
        (far(switch.T), far(slope.T), far(exp), far(act), far(own), far(small)),
        [ANY] * 6,
        [VM] * (n_t + 3),
        scratch=[
            pltpu.VMEM((B, tok), BF16),
            pltpu.VMEM((B, tok), BF16),
            pltpu.VMEM((nr, width), BF16),
            pltpu.SemaphoreType.DMA((6,)),
        ],
        nbytes=act.size * 4 + nr * width * 2,
        name="up_grads",
    )
    got = {k: trade(parts[k], k) for k in order}
    parts = [parts[0]] + [got[k] for k in range(1, n_t)]

    p_own, a_own = call(
        functools.partial(own_body, keep),
        [near((B, groups * 2 * B)), near((groups * B, 2 * B))],
        (own, small),
        [VM, VM],
        [VM, VM],
        name="own_places",
    )

    def grads_of(ks, after):
        return call(
            functools.partial(grads_body, len(ks)),
            [near((B, cols), BF16 if k else F32) for k in ks],
            (act, after, *[parts[k] for k in ks]),
            [VM, ANY] + [VM] * len(ks),
            [VM] * len(ks),
            name="weight_grads",
        )

    grads = {}
    for k in order[:-1]:
        (grads[k],) = grads_of([k], act)
    made, grads[0] = grads_of([order[-1], 0], a_own)
    grads[order[-1]] = made
    grads.update({k: trade(grads[k], k) for k in order})

    bundle = call(
        functools.partial(bundle_body, n_t, keep),
        near(((n_t - 1) * tiles * nr + 16, 128)),
        (made, own, *parts[1:]),
        [ANY] + [VM] * n_t,
        VM,
        name="bundle",
    )
    bundles = lax.all_gather(bundle, "replica", axis=0)

    rows = []
    for ks in ([k for k in range(n_t) if k != n_t - 1], [n_t - 1]):
        n = len(ks)
        rows = call(
            functools.partial(kept_body, ks, n_t, keep),
            [near((keep, width)), near((keep, width), F32)],
            (vel[0], a_own, tab, bundles, *[grads[k] for k in ks], *rows),
            [VM] * 3 + [ANY] + [VM] * (n + len(rows)),
            [VM] * 2,
            flops=6 * B * B * cols * n,
            nbytes=B * cols * 6 * n,
            name="kept_rows",
            alias={4 + n: 0, 5 + n: 1} if rows else {},
        )
    ship, q_own = rows

    new, shares = call(
        functools.partial(return_body, n_t, keep),
        [jax.ShapeDtypeStruct((B, width), F32), near((2, 8, 2 * B), F32)],
        (vel[0], p_own, q_own, far(mask), far(tally), *[grads[k] for k in range(n_t)]),
        [VM] * 3 + [ANY] * 2 + [VM] * n_t,
        [ANY, VM],
        scratch=[
            pltpu.VMEM((B, width), F32),
            pltpu.SemaphoreType.DMA((n_t,)),
            pltpu.SMEM((n_r,), jnp.int32),
            pltpu.SMEM((n_r,), jnp.int32),
            pltpu.SemaphoreType.DMA((2,)),
        ],
        flops=6 * B * B * width,
        nbytes=B * width * 10,
        name="new_momentums",
    )
    places = call(
        functools.partial(places_body, keep),
        [near((B, blocks * half * keep))] * 4,
        (shares, small, bundles),
        [VM] * 3,
        [VM] * 4,
        name="places",
    )
    input_grad = call(
        functools.partial(input_grad_body, n_t, n_r, cp),
        jax.ShapeDtypeStruct((tok, cols), BF16),
        (exp, bundles, *parts),
        [VM] * (2 + n_t),
        VM,
        scratch=[pltpu.VMEM((n_t * B, cols), BF16)],
        flops=2 * tok * n_t * B * cols,
        nbytes=(n_t * B * cols + tok * cols) * 2,
        name="input_grads",
    )

    ships = [ship] + [swap(ship, 2 * i) for i in range(1, half)]
    other_own = swap(ship, 1)
    others = call(
        functools.partial(join_body, half - 1),
        near((half - 1, keep, width)),
        (other_own, *ships[1:], far(new), far(input_grad), places[0]),
        [ANY] + [VM] * (half - 1) + [ANY] * 3,
        VM,
        name="join_kept",
    )
    other = swap(others, 1)
    half_sum = call(
        half_update_body,
        near((groups * B, G), F32),
        (*places[:2], ship, others),
        [VM] * 4,
        VM,
        name="half_updates",
    )
    chunk = next(c for c in (4, 2, 1) if groups % c == 0)
    update = call(
        functools.partial(update_body, chunk),
        jax.ShapeDtypeStruct((B, width), F32),
        (half_sum, *places[2:], other_own, other),
        [VM] * 5,
        ANY,
        scratch=[
            pltpu.VMEM((B, width), F32),
            pltpu.SemaphoreType.DMA((groups // chunk,)),
        ],
        flops=8 * B * G * width,
        nbytes=B * width * 8,
        name="updates",
    )
    return input_grad, new[None], update


def per_device_plain(
    projection_inputs,
    switch_logits_raw,
    inner_neuron_slope,
    expansion_matrix,
    velocity_buffer,
    sent_spectral_lines,
    participant_mask,
    token_tallies,
):
    highest = lax.Precision.HIGHEST
    up_grad = (
        inner_neuron_slope.astype(jnp.float32) * jax.nn.silu(switch_logits_raw.astype(jnp.float32))
    ).astype(jnp.bfloat16)
    partial_terms = jnp.dot(up_grad, expansion_matrix, preferred_element_type=jnp.float32)
    input_grad = lax.psum_scatter(partial_terms, "tensor", scatter_dimension=1, tiled=True).astype(
        jnp.bfloat16
    )
    grad_w = lax.dot_general(
        up_grad,
        lax.all_gather(projection_inputs, "tensor", axis=1, tiled=True),
        (((0,), (0,)), ((), ())),
        preferred_element_type=jnp.float32,
    )
    row_total_count = expansion_matrix.shape[0] // 64
    col_count = expansion_matrix.shape[1] // 64
    moment = momentum_decay * velocity_buffer[0] + grad_w
    cosines = cosine_table()
    blocks = moment.reshape(row_total_count, 64, col_count, 64).transpose(0, 2, 1, 3)
    coefficients = jnp.einsum("fa,ijab,gb->ijfg", cosines, blocks, cosines, precision=highest)
    freq_ids = jnp.arange(64, dtype=jnp.int32)
    own_rows = sent_spectral_lines[0]
    chosen = (own_rows[..., None] == freq_ids).astype(jnp.float32)
    shipped = jnp.einsum("ijkf,ijfg->ijkg", chosen, coefficients, precision=highest).astype(
        jnp.bfloat16
    )
    spectrum = jnp.einsum("ijkf,ijkg->ijfg", chosen, shipped.astype(jnp.float32), precision=highest)
    returned = jnp.einsum("fa,ijfg,gb->ijab", cosines, spectrum, cosines, precision=highest)
    new_moment = moment - returned.transpose(0, 2, 1, 3).reshape(moment.shape)
    worker_burdens = participant_mask.astype(jnp.float32) * token_tallies.astype(jnp.float32)
    worker_fractions = worker_burdens * (
        jnp.sum(participant_mask.astype(jnp.float32)) / jnp.sum(worker_burdens)
    )
    myself = lax.axis_index("replica")
    combined = lax.psum(worker_fractions[myself] * spectrum, "replica")
    update = jnp.einsum("fa,ijfg,gb->ijab", cosines, combined, cosines, precision=highest)
    update = update.transpose(0, 2, 1, 3).reshape(moment.shape)
    return (input_grad, new_moment[None], update)


def solution(mesh):
    n_t, n_r = mesh.shape["tensor"], mesh.shape["replica"]

    def device(*args):
        act, exp, lines = args[0], args[3], args[5]
        fits = (
            act.shape[1] % G == 0
            and act.shape[0] % 128 == 0
            and exp.shape[0] == B
            and lines.shape[3] == 8
            and n_r == 8
            and n_t >= 2
            and n_t & (n_t - 1) == 0
        )
        if not fits:
            return per_device_plain(*args)
        return per_device(n_t, n_r, *args)

    return jax.shard_map(
        device,
        mesh=mesh,
        in_specs=(
            P("replica", "tensor"),
            P("replica", "tensor"),
            P("replica", "tensor"),
            P("tensor", None),
            P("replica", "tensor", None),
            P("replica", "tensor", None, None),
            P(),
            P(),
        ),
        out_specs=(P("replica", "tensor"), P("replica", "tensor", None), P("tensor", None)),
        check_vma=False,
    )
```
